32 devices in a mesh: grp: 4 (over z), shard: 8 (over y, x, core).
Axes of the slice: x: 2, y: 2, z: 4, core: 2. Of those that a mesh axis runs over, the one named last changes fastest.
Arguments:
- video: bfloat16 [2, 32, 393, 768], P(None, ('grp', 'shard')), may hold values from -6 to 6
- cotangent: bfloat16 [2, 32, 393, 768], P(None, ('grp', 'shard')), may hold values from -6 to 6
- live: int32 [2, 32], P(None, ('grp', 'shard')), may hold values 0 or 1
- time_entry: bfloat16 [768, 2304], P('shard'), may hold values from -0.21875 to 0.21875
- time_exit: bfloat16 [768, 768], P('shard'), may hold values from -0.4375 to 0.4375
- time_mixer: bfloat16 [768, 768], P('shard'), may hold values from -0.21875 to 0.21875
- space_entry: bfloat16 [768, 2304], P('shard'), may hold values from -0.21875 to 0.21875
- space_exit: bfloat16 [768, 768], P('shard'), may hold values from -0.875 to 0.875
- hidden_expand: bfloat16 [768, 3072], P('shard'), may hold values from -0.21875 to 0.21875
- hidden_reduce: bfloat16 [3072, 768], P('shard'), may hold values from -0.109375 to 0.109375
- bias_rows: bfloat16 [8, 768], P(None, 'shard'), may hold values from -3 to 3
- hidden_bias: bfloat16 [3072], P('shard'), may hold values from -3 to 3
- norm_gain: bfloat16 [3, 768], P(None, 'shard'), may hold values from 0.5 to 1.5
- norm_shift: bfloat16 [3, 768], P(None, 'shard'), may hold values from -3 to 3
Outputs:
- block_output: bfloat16 [2, 32, 393, 768], P(None, ('grp', 'shard'))
- input_grad: bfloat16 [2, 32, 393, 768], P(None, ('grp', 'shard'))
- grad_time_entry: float32 [768, 2304], P('shard')
- grad_time_exit: float32 [768, 768], P('shard')
- grad_time_mixer: float32 [768, 768], P('shard')
- grad_space_entry: float32 [768, 2304], P('shard')
- grad_space_exit: float32 [768, 768], P('shard')
- grad_hidden_expand: float32 [768, 3072], P('shard')
- grad_hidden_reduce: float32 [3072, 768], P('shard')
- grad_bias_rows: float32 [8, 768], P(None, 'shard')
- grad_hidden_bias: float32 [3072], P('shard')
- grad_norm_gain: float32 [3, 768], P(None, 'shard')
- grad_norm_shift: float32 [3, 768], P(None, 'shard')
The draws below stay inside these ranges and needn't reach their ends.
Inputs may be any that keep to these rules, and one draw needn't show every extreme that they name: `live`: 1 where a slot of a micro-batch holds a clip, 0 where it is empty.
All inputs are finite; a program needn't handle non-finite values. No bound on the sum of `live` on one device may be relied on, other than what follows from the above.
Results may differ from the reference program's by a relative error of at most 0.017.
Values may be sent and summed in bfloat16 or wider, within the bound.
No kernel may reach another device: no remote copies, remote signals or barrier semaphores. Data moves between devices by JAX's collectives and lax.ppermute only.
A program may use at most 256 MiB of HBM per device.

```python
import jax
import jax.numpy as jnp
from jax import lax

D = 768
HEADS = 12
HD = 64
FF = 3072
FRAMES = 2
PLACES = 196
MB = 2
TOK = 393
SLOTS = 32


def plant(values, key, low, high):
    dims = values.shape
    place = [jax.random.randint(jax.random.fold_in(key, axis), (), 0, dims[axis]) for axis in range(len(dims))]
    values = values.at[tuple(place)].set(low)
    longest = dims.index(max(dims))
    place[longest] = (place[longest] + 1) % dims[longest]
    return values.at[tuple(place)].set(high)


def level_of(rng, shape, split, least, high):
    loudness = 1.0
    for position, shards_of in split:
        draws = jax.random.uniform(jax.random.fold_in(jax.random.fold_in(rng, 6), position), (shards_of,), jnp.float32, least / len(split), high / len(split))
        loudness = loudness * jnp.repeat(jnp.exp(draws), shape[position] // shards_of).reshape((-1,) + (1,) * (len(shape) - 1 - position))
    return loudness


def noise(key, shape, scale, reach, shards=(), dtype=jnp.bfloat16):
    drawn = scale * jax.random.normal(key, shape, jnp.float32)
    if shards:
        drawn = drawn * level_of(key, shape, shards, -0.22, 0.18)
    return jnp.clip(drawn, -reach, reach).astype(dtype)


def setup_inputs(seed: int = 0) -> dict:
    keys = jax.random.split(jax.random.key(seed), 15)
    return {
        "video": noise(keys[0], (MB, SLOTS, TOK, D), 1.0, 6.0, ((1, 32),)),
        "cotangent": noise(keys[1], (MB, SLOTS, TOK, D), 1.0, 6.0, ((1, 32),)),
        "live": plant((jax.random.randint(keys[2], (MB, SLOTS), 0, 8) < 5).astype(jnp.int32), jax.random.fold_in(keys[2], 1), 0, 1),
        "time_entry": noise(keys[3], (D, 3 * D), D ** -0.5, 0.21875, ((0, 8),)),
        "time_exit": noise(keys[4], (D, D), (D // 4) ** -0.5, 0.4375, ((0, 8),)),
        "time_mixer": noise(keys[5], (D, D), D ** -0.5, 0.21875, ((0, 8),)),
        "space_entry": noise(keys[6], (D, 3 * D), D ** -0.5, 0.21875, ((0, 8),)),
        "space_exit": noise(keys[7], (D, D), (D // 16) ** -0.5, 0.875, ((0, 8),)),
        "hidden_expand": noise(keys[8], (D, FF), D ** -0.5, 0.21875, ((0, 8),)),
        "hidden_reduce": noise(keys[9], (FF, D), FF ** -0.5, 0.109375, ((0, 8),)),
        "bias_rows": noise(keys[10], (8, D), 0.5, 3.0, ((1, 8),)),
        "hidden_bias": noise(keys[11], (FF,), 0.5, 3.0, ((0, 8),)),
        "norm_gain": jnp.clip(1.0 + 0.1 * jax.random.normal(keys[12], (3, D), jnp.float32), 0.5, 1.5).astype(jnp.bfloat16),
        "norm_shift": noise(keys[13], (3, D), 0.5, 3.0, ((1, 8),)),
    }


@jax.custom_vjp
def low(v):
    return lax.optimization_barrier(v.astype(jnp.bfloat16)).astype(jnp.float32)

@jax.custom_vjp
def low_back(v):
    return v

def low_keep(v):
    return (low(v), None)

def low_pass(kept, grad):
    return (grad,)

def back_keep(v):
    return (v, None)

def back_low(kept, grad):
    return (low(grad),)
low.defvjp(low_keep, low_pass)
low_back.defvjp(back_keep, back_low)
EPSILON = 1e-06

def both_ways(tensor):
    return low_back(low(tensor))

def layer_norm(activations, gain_row, shift_row):
    center = activations - lax.optimization_barrier(jnp.mean(activations, axis=-1, keepdims=True))
    return center * lax.rsqrt(lax.optimization_barrier(jnp.mean(center * center, axis=-1, keepdims=True)) + EPSILON) * gain_row + shift_row

def product(first_op, second_op):
    return jnp.dot(first_op, second_op, precision=lax.Precision.HIGHEST)

def attention(queries, key_part, values):
    scores = low_back(jnp.einsum('bhqd,bhkd->bhqk', queries, key_part, precision=lax.Precision.HIGHEST) * HD ** (-0.5))
    row_peak = lax.optimization_barrier(jnp.max(scores, axis=-1, keepdims=True))
    powered = jnp.exp(scores - row_peak)
    soft_weights = low(powered / lax.optimization_barrier(jnp.sum(powered, axis=-1, keepdims=True)))
    return both_ways(jnp.einsum('bhqk,bhkd->bhqd', soft_weights, values, precision=lax.Precision.HIGHEST))

def to_time(matrix):
    return matrix.reshape(FRAMES, PLACES, HEADS, HD).transpose(1, 2, 0, 3)

def to_space(matrix):
    class_rows = jnp.broadcast_to(matrix[:1][None], (FRAMES, 1, D))
    framed = jnp.concatenate([class_rows, matrix[1:].reshape(FRAMES, PLACES, D)], axis=1)
    return framed.reshape(FRAMES, 1 + PLACES, HEADS, HD).transpose(0, 2, 1, 3)

def forward(clip_rows, time_entry, time_exit, time_mixer, space_entry, space_exit, hidden_expand, hidden_reduce, bias_rows, hidden_bias, norm_gain, norm_shift):
    patches = clip_rows[1:]
    normed = low(layer_norm(patches, norm_gain[0], norm_shift[0]))
    packed = product(normed, time_entry)
    queries = both_ways(packed[:, :D] + bias_rows[0])
    key_part = both_ways(packed[:, D:2 * D])
    values = both_ways(packed[:, 2 * D:] + bias_rows[1])
    mixture = attention(to_time(queries), to_time(key_part), to_time(values))
    mixture = mixture.transpose(2, 0, 1, 3).reshape(FRAMES * PLACES, D)
    exit_rows = both_ways(product(mixture, time_exit) + bias_rows[2])
    branch = low_back(product(exit_rows, time_mixer) + bias_rows[3])
    whole_rows = jnp.concatenate([clip_rows[:1], patches + branch], axis=0)
    normed = low(layer_norm(whole_rows, norm_gain[1], norm_shift[1]))
    packed = product(normed, space_entry)
    queries = both_ways(packed[:, :D] + bias_rows[4])
    key_part = both_ways(packed[:, D:2 * D])
    values = both_ways(packed[:, 2 * D:] + bias_rows[5])
    mixture = attention(to_space(queries), to_space(key_part), to_space(values))
    mixture = mixture.transpose(0, 2, 1, 3).reshape(FRAMES * (1 + PLACES), D)
    branch = low_back(product(mixture, space_exit) + bias_rows[6]).reshape(FRAMES, 1 + PLACES, D)
    update = jnp.concatenate([lax.optimization_barrier(jnp.mean(branch[:, 0], axis=0, keepdims=True)), branch[:, 1:].reshape(FRAMES * PLACES, D)], axis=0)
    after_space = whole_rows + update
    normed = low(layer_norm(after_space, norm_gain[2], norm_shift[2]))
    inner_rows = low_back(product(normed, hidden_expand) + hidden_bias)
    active = low(jax.nn.gelu(inner_rows, approximate=False))
    return after_space + low_back(product(active, hidden_reduce) + bias_rows[7])

def reference(video, cotangent, live, time_entry, time_exit, time_mixer, space_entry, space_exit, hidden_expand, hidden_reduce, bias_rows, hidden_bias, norm_gain, norm_shift):
    weights = tuple((weight.astype(jnp.float32) for weight in (time_entry, time_exit, time_mixer, space_entry, space_exit, hidden_expand, hidden_reduce, bias_rows, hidden_bias, norm_gain, norm_shift)))
    clip_batch = video.reshape(MB * SLOTS, TOK, D).astype(jnp.float32)
    grads_in = cotangent.reshape(MB * SLOTS, TOK, D).astype(jnp.float32)
    live_flags = live.reshape(MB * SLOTS).astype(jnp.float32)

    def one_clip(totals, inputs):
        clip_rows, grad_out, live_flag = inputs
        result, pullback = jax.vjp(forward, clip_rows, *weights)
        gradients = pullback(grad_out * live_flag)
        totals = tuple((running + increment for running, increment in zip(totals, gradients[1:])))
        return (totals, ((result * live_flag).astype(jnp.bfloat16), gradients[0].astype(jnp.bfloat16)))
    initial = tuple((jnp.zeros(weight.shape, jnp.float32) for weight in weights))
    totals, (outputs, input_grads) = lax.scan(one_clip, initial, (clip_batch, grads_in, live_flags))
    return (outputs.reshape(MB, SLOTS, TOK, D), input_grads.reshape(MB, SLOTS, TOK, D), totals[0], totals[1], totals[2], totals[3], totals[4], totals[5], totals[6], totals[7], totals[8], totals[9], totals[10])
```

```python
import functools

import jax
import jax.numpy as jnp
from jax import lax
from jax.experimental import pallas as pl
from jax.experimental.pallas import tpu as pltpu
from jax.sharding import PartitionSpec as P

FRAMES = 2
PLACES = 196
HD = 64
EPSILON = 1e-06
BLOCK = 208
EDGE = 192
CLASS = PLACES - EDGE
CHUNK = 64
WIDE = 256
BF = jnp.bfloat16
F32 = jnp.float32
VMEM_LIMIT = 60 * 1024 * 1024


def nn(a, b):
    return lax.dot_general(a, b, (((1,), (0,)), ((), ())), preferred_element_type=F32)


def nt(a, b):
    return lax.dot_general(a, b, (((1,), (1,)), ((), ())), preferred_element_type=F32)


def tn(a, b):
    return lax.dot_general(a, b, (((0,), (0,)), ((), ())), preferred_element_type=F32)


def loop(count, body):
    def step(i, carry):
        body(i)
        return carry

    lax.fori_loop(0, count, step, 0)


def rows_of(i, size):
    return pl.ds(pl.multiple_of(i * size, size), size)


def cols_of(i, size, base=0):
    return pl.ds(pl.multiple_of(base + i * size, 128), size)


def unit(x):
    center = x - jnp.mean(x, axis=-1, keepdims=True)
    factor = lax.rsqrt(jnp.mean(center * center, axis=-1, keepdims=True) + EPSILON)
    return center * factor, factor


def norm_chunks(src, dst, gain, shift):
    def body(i):
        at = rows_of(i, CHUNK)
        w, _ = unit(src[at, :].astype(F32))
        dst[at, :] = (w * gain + shift).astype(BF)

    loop(src.shape[0] // CHUNK, body)


def fold(x):
    return jnp.sum(x.reshape(x.shape[0] // 8, 8, x.shape[1]), axis=0)


def norm_back_chunks(gn_ref, x_ref, gain, base_of, store):
    columns = x_ref.shape[1]

    def body(i, carry):
        gain_sum, shift_sum = carry
        at = rows_of(i, CHUNK)
        gn = gn_ref[at, :]
        w, factor = unit(x_ref[at, :].astype(F32))
        scaled = gn * gain
        plain = jnp.mean(scaled, axis=-1, keepdims=True)
        cross = jnp.mean(scaled * w, axis=-1, keepdims=True)
        store(at, base_of(at) + factor * (scaled - plain - w * cross))
        return gain_sum + fold(gn * w), shift_sum + fold(gn)

    zero = jnp.zeros((8, columns), F32)
    gain_sum, shift_sum = lax.fori_loop(0, x_ref.shape[0] // CHUNK, body, (zero, zero))
    return jnp.sum(gain_sum, axis=0, keepdims=True), jnp.sum(shift_sum, axis=0, keepdims=True)


def column_sums(ref, start, size):
    def body(i, total):
        return total + fold(ref[rows_of(i, CHUNK), start : start + size].astype(F32))

    total = lax.fori_loop(0, ref.shape[0] // CHUNK, body, jnp.zeros((8, size), F32))
    return jnp.sum(total, axis=0, keepdims=True)


def head_map(columns):
    feature = lax.broadcasted_iota(jnp.int32, (columns, 128), 0) // HD
    head = lax.broadcasted_iota(jnp.int32, (columns, 128), 1)
    return (feature == head).astype(BF)


def split_store(high, low, at, value):
    top = value.astype(BF)
    high[at, :] = top
    low[at, :] = (value - top.astype(F32)).astype(BF)


def row_in_block(i, size, columns):
    return (i * size + lax.broadcasted_iota(jnp.int32, (size, columns), 0)) % BLOCK


def load(loads, sems):
    copies = [pltpu.make_async_copy(s, d, sems.at[n]) for n, (s, d) in enumerate(loads)]
    for copy in copies:
        copy.start()
    return copies


def wait(copies):
    for copy in copies:
        copy.wait()


def time_forward(x_ref, small_ref, w_ref, nt_ref, qkv_ref, o_ref, e_ref, p_ref, y_ref, w, high, low, sems):
    columns = x_ref.shape[1]
    copies = load([(w_ref, w)], sems)
    norm_chunks(x_ref, nt_ref, small_ref[12:13, :], small_ref[15:16, :])
    wait(copies)
    zero_bias = jnp.zeros((1, columns), F32)
    for part, bias in enumerate((small_ref[0:1, :], zero_bias, small_ref[1:2, :])):
        for j in range(columns // WIDE):
            at = slice(j * WIDE, (j + 1) * WIDE)
            to = slice(part * columns + j * WIDE, part * columns + (j + 1) * WIDE)
            qkv_ref[:, to] = (nn(nt_ref[...], w[:, to]) + bias[:, at]).astype(BF)
    heads = head_map(columns)
    small = 16
    for clip in range(x_ref.shape[0] // (FRAMES * BLOCK)):
        first = clip * FRAMES * BLOCK

        def products(i, first=first):
            at = [pl.ds(pl.multiple_of(first + f * BLOCK + i * small, small), small) for f in range(FRAMES)]
            q = [qkv_ref[a, 0:columns].astype(F32) for a in at]
            k = [qkv_ref[a, columns : 2 * columns].astype(F32) for a in at]
            for f in range(FRAMES):
                for g in range(FRAMES):
                    to = pl.ds(pl.multiple_of((f * FRAMES + g) * BLOCK + i * small, small), small)
                    split_store(high, low, to, q[f] * k[g])

        loop(BLOCK // small, products)
        scores = (nn(high[...], heads) + nn(low[...], heads)) * HD ** (-0.5)
        s = [scores[n * BLOCK : (n + 1) * BLOCK, :] for n in range(4)]
        for f in range(FRAMES):
            peak = jnp.maximum(s[2 * f], s[2 * f + 1])
            powered = [jnp.exp(s[2 * f] - peak), jnp.exp(s[2 * f + 1] - peak)]
            total = powered[0] + powered[1]
            for g in range(FRAMES):
                to = slice(clip * 4 * BLOCK + (2 * f + g) * BLOCK, clip * 4 * BLOCK + (2 * f + g + 1) * BLOCK)
                p_ref[to, :] = powered[g] / total
        spread = p_ref[clip * 4 * BLOCK : (clip + 1) * 4 * BLOCK, :].astype(BF)
        for j in range(columns // WIDE):
            at = slice(j * WIDE, (j + 1) * WIDE)
            high[:, at] = nt(spread, heads[at, :]).astype(BF)

        def mixture(i, first=first):
            at = [pl.ds(pl.multiple_of(first + f * BLOCK + i * small, small), small) for f in range(FRAMES)]
            v = [qkv_ref[a, 2 * columns : 3 * columns].astype(F32) for a in at]
            for f in range(FRAMES):
                total = 0.0
                for g in range(FRAMES):
                    p = high[pl.ds(pl.multiple_of((f * FRAMES + g) * BLOCK + i * small, small), small), :]
                    total = total + p.astype(F32) * v[g]
                o_ref[at[f], :] = total.astype(BF)

        loop(BLOCK // small, mixture)
    for j in range(columns // WIDE):
        at = slice(j * WIDE, (j + 1) * WIDE)
        from_w = slice(3 * columns + j * WIDE, 3 * columns + (j + 1) * WIDE)
        e_ref[:, at] = (nn(o_ref[...], w[:, from_w]) + small_ref[2:3, at]).astype(BF)
    patch = row_in_block(0, x_ref.shape[0], WIDE) < PLACES
    for j in range(columns // WIDE):
        at = slice(j * WIDE, (j + 1) * WIDE)
        from_w = slice(4 * columns + j * WIDE, 4 * columns + (j + 1) * WIDE)
        branch = nn(e_ref[...], w[:, from_w]) + small_ref[3:4, at]
        y_ref[:, at] = x_ref[:, at].astype(F32) + jnp.where(patch, branch, 0.0)


def half_masks():
    lane = lax.broadcasted_iota(jnp.int32, (1, 128), 1)
    return (lane < HD).astype(BF), (lane >= HD).astype(BF)


def space_forward(y_ref, small_ref, w_ref, ns_ref, qkv_ref, p_ref, o_ref, z_ref, w, sems):
    columns = y_ref.shape[1]
    blocks = y_ref.shape[0] // BLOCK
    pairs = columns // 128
    copies = load([(w_ref, w)], sems)
    norm_chunks(y_ref, ns_ref, small_ref[13:14, :], small_ref[16:17, :])
    wait(copies)
    zero_bias = jnp.zeros((1, columns), F32)
    for part, bias in enumerate((small_ref[4:5, :], zero_bias, small_ref[5:6, :])):
        for j in range(columns // WIDE):
            at = slice(j * WIDE, (j + 1) * WIDE)
            to = slice(part * columns + j * WIDE, part * columns + (j + 1) * WIDE)
            qkv_ref[:, to] = (nn(ns_ref[...], w[:, to]) + bias[:, at]).astype(BF)
    masks = half_masks()
    first = lax.broadcasted_iota(jnp.int32, (BLOCK, 128), 1) < HD
    column = lax.broadcasted_iota(jnp.int32, (1, BLOCK), 1)
    hidden = jnp.where(column <= PLACES, 0.0, -1e30)

    def attend(n):
        block, pair = n // pairs, n % pairs
        at = rows_of(block, BLOCK)
        q = qkv_ref[at, cols_of(pair, 128)]
        k = qkv_ref[at, cols_of(pair, 128, columns)]
        v = qkv_ref[at, cols_of(pair, 128, 2 * columns)]
        outs = []
        for half in range(2):
            scores = nt(q * masks[half], k) * HD ** (-0.5) + hidden
            powered = jnp.exp(scores - jnp.max(scores, axis=-1, keepdims=True))
            weights = (powered * (1.0 / jnp.sum(powered, axis=-1, keepdims=True))).astype(BF)
            p_ref[2 * n + half] = weights
            outs.append(nn(weights, v))
        o_ref[at, cols_of(pair, 128)] = jnp.where(first, outs[0], outs[1]).astype(BF)

    loop(blocks * pairs, attend)
    is_class = lax.broadcasted_iota(jnp.int32, (BLOCK - EDGE, WIDE), 0) == CLASS
    for j in range(columns // WIDE):
        at = slice(j * WIDE, (j + 1) * WIDE)
        from_w = slice(3 * columns + j * WIDE, 3 * columns + (j + 1) * WIDE)
        branch = nn(o_ref[...], w[:, from_w]) + small_ref[6:7, at]
        z_ref[:, at] = y_ref[:, at] + branch
        for clip in range(blocks // FRAMES):
            edges = [slice((clip * FRAMES + f) * BLOCK + EDGE, (clip * FRAMES + f + 1) * BLOCK) for f in range(FRAMES)]
            mean = (branch[edges[0], :] + branch[edges[1], :]) * (1.0 / FRAMES)
            for edge in edges:
                z_ref[edge, at] = y_ref[edge, at] + jnp.where(is_class, mean, branch[edge, :])


def gelu_both(h):
    cdf = 0.5 * (1.0 + lax.erf(h * 0.5**0.5))
    density = jnp.exp(h * h * -0.5) * 0.3989422804014327
    return h * cdf, cdf + h * density


def feed(z_ref, g_ref, small_ref, hb_ref, we_ref, wr_ref, out_ref, gz_ref, sums_ref, ghb_ref, dwe_ref, dwr_ref, we, wr, nm, a, gh, gn, sems):
    columns = z_ref.shape[1]
    units = we.shape[1]
    copies = load([(we_ref, we), (wr_ref, wr)], sems)
    norm_chunks(z_ref, nm, small_ref[14:15, :], small_ref[17:18, :])
    wait(copies)

    def inner(j):
        at = cols_of(j, WIDE)
        h = nn(nm[...], we[:, at]) + hb_ref[0:1, at]
        active, slope = gelu_both(h)
        a[:, at] = active.astype(BF)
        gh[:, at] = (nt(g_ref[...], wr[rows_of(j, WIDE), :]) * slope).astype(BF)

    loop(units // WIDE, inner)

    def outer(j):
        at = cols_of(j, WIDE)
        dwr_ref[rows_of(j, WIDE), :] = tn(a[:, at], g_ref[...]).astype(BF)
        block = gh[:, at]
        dwe_ref[:, at] = tn(nm[...], block).astype(BF)
        ghb_ref[0:1, at] = jnp.sum(block.astype(F32), axis=0, keepdims=True)

    loop(units // WIDE, outer)
    for j in range(columns // WIDE):
        at = slice(j * WIDE, (j + 1) * WIDE)
        gn[:, at] = nt(gh[...], we[at, :])
        out_ref[:, at] = (z_ref[:, at] + (nn(a[...], wr[:, at]) + small_ref[7:8, at])).astype(BF)

    def store(rows, value):
        gz_ref[rows, :] = value

    gain_sum, shift_sum = norm_back_chunks(
        gn, z_ref, small_ref[14:15, :], lambda rows: g_ref[rows, :].astype(F32), store
    )
    sums_ref[0:1, :] = column_sums(g_ref, 0, columns)
    sums_ref[1:2, :] = gain_sum
    sums_ref[2:3, :] = shift_sum


def space_backward(gz_ref, y_ref, ns_ref, qkv_ref, p_ref, o_ref, small_ref, w_ref, gy_ref, sums_ref, dw_ref, w, gbs, go, gqkv, gn, sems):
    columns = y_ref.shape[1]
    rows = y_ref.shape[0]
    clips = rows // (BLOCK * FRAMES)
    pairs = columns // 128
    copies = load([(w_ref, w)], sems)

    def lower(i):
        at = rows_of(i, CHUNK)
        gbs[at, :] = gz_ref[at, :].astype(BF)

    loop(rows // CHUNK, lower)
    is_class = lax.broadcasted_iota(jnp.int32, (BLOCK - EDGE, columns), 0) == CLASS
    for clip in range(clips):
        edges = [slice((clip * FRAMES + f) * BLOCK + EDGE, (clip * FRAMES + f + 1) * BLOCK) for f in range(FRAMES)]
        share = gz_ref[edges[0], :] * (1.0 / FRAMES)
        for edge in edges:
            gbs[edge, :] = jnp.where(is_class, share, gz_ref[edge, :]).astype(BF)
    wait(copies)
    for j in range(columns // WIDE):
        at = slice(j * WIDE, (j + 1) * WIDE)
        go[:, at] = nt(gbs[...], w[at, 3 * columns : 4 * columns]).astype(BF)
        dw_ref[:, 3 * columns + j * WIDE : 3 * columns + (j + 1) * WIDE] = tn(o_ref[...], gbs[:, at]).astype(BF)
    masks = half_masks()
    first = lax.broadcasted_iota(jnp.int32, (BLOCK, 128), 1) < HD
    class_row = lax.broadcasted_iota(jnp.int32, (BLOCK, 128), 0) == PLACES

    def attend(n):
        clip, pair = n // pairs, n % pairs
        found = []
        for f in range(FRAMES):
            block = clip * FRAMES + f
            at = rows_of(block, BLOCK)
            q = qkv_ref[at, cols_of(pair, 128)]
            k = qkv_ref[at, cols_of(pair, 128, columns)]
            v = qkv_ref[at, cols_of(pair, 128, 2 * columns)]
            grad = go[at, cols_of(pair, 128)]
            parts = []
            for half in range(2):
                p = p_ref[2 * (block * pairs + pair) + half]
                gp = nt(grad * masks[half], v)
                weights = p.astype(F32)
                shared = jnp.sum(gp * weights, axis=-1, keepdims=True)
                gs = (weights * (gp - shared)).astype(BF)
                parts.append((nn(gs, k), tn(gs, q), tn(p, grad)))
            scale = HD ** (-0.5)
            found.append(
                [jnp.where(first, left, right) * s for left, right, s in zip(*parts, (scale, scale, 1.0))]
            )
        for part in range(3):
            one, two = found[0][part], found[1][part]
            one = jnp.where(class_row, one + two, one)
            two = jnp.where(class_row, 0.0, two)
            to = cols_of(pair, 128, part * columns)
            gqkv[rows_of(clip * FRAMES, BLOCK), to] = one.astype(BF)
            gqkv[rows_of(clip * FRAMES + 1, BLOCK), to] = two.astype(BF)

    loop(clips * pairs, attend)
    for j in range(3 * columns // WIDE):
        at = slice(j * WIDE, (j + 1) * WIDE)
        dw_ref[:, at] = tn(ns_ref[...], gqkv[:, at]).astype(BF)
    for j in range(columns // WIDE):
        at = slice(j * WIDE, (j + 1) * WIDE)
        gn[:, at] = nt(gqkv[...], w[at, 0 : 3 * columns])

    def store(at, value):
        gy_ref[at, :] = value

    gain_sum, shift_sum = norm_back_chunks(gn, y_ref, small_ref[13:14, :], lambda at: gz_ref[at, :], store)
    sums_ref[0:1, :] = column_sums(gqkv, 0, columns)
    sums_ref[1:2, :] = column_sums(gqkv, 2 * columns, columns)
    sums_ref[2:3, :] = column_sums(gbs, 0, columns)
    sums_ref[3:4, :] = gain_sum
    sums_ref[4:5, :] = shift_sum


def time_backward(gy_ref, x_ref, nt_ref, qkv_ref, p_ref, o_ref, e_ref, small_ref, w_ref, gx_ref, sums_ref, dw_ref, w, grt, get, go, gqkv, gn, high, low, sems):
    columns = x_ref.shape[1]
    rows = x_ref.shape[0]
    copies = load([(w_ref, w)], sems)

    def lower(i):
        at = rows_of(i, CHUNK)
        patch = row_in_block(i, CHUNK, columns) < PLACES
        grt[at, :] = jnp.where(patch, gy_ref[at, :], 0.0).astype(BF)

    loop(rows // CHUNK, lower)
    wait(copies)
    for j in range(columns // WIDE):
        at = slice(j * WIDE, (j + 1) * WIDE)
        get[:, at] = nt(grt[...], w[at, 4 * columns : 5 * columns]).astype(BF)
        dw_ref[:, 4 * columns + j * WIDE : 4 * columns + (j + 1) * WIDE] = tn(e_ref[...], grt[:, at]).astype(BF)
    for j in range(columns // WIDE):
        at = slice(j * WIDE, (j + 1) * WIDE)
        go[:, at] = nt(get[...], w[at, 3 * columns : 4 * columns]).astype(BF)
        dw_ref[:, 3 * columns + j * WIDE : 3 * columns + (j + 1) * WIDE] = tn(o_ref[...], get[:, at]).astype(BF)
    heads = head_map(columns)
    small = 16
    scale = HD ** (-0.5)
    for clip in range(rows // (FRAMES * BLOCK)):
        start = clip * FRAMES * BLOCK

        def products(i, start=start):
            at = [pl.ds(pl.multiple_of(start + f * BLOCK + i * small, small), small) for f in range(FRAMES)]
            grad = [go[a, :].astype(F32) for a in at]
            v = [qkv_ref[a, 2 * columns : 3 * columns].astype(F32) for a in at]
            for f in range(FRAMES):
                for g in range(FRAMES):
                    to = pl.ds(pl.multiple_of((f * FRAMES + g) * BLOCK + i * small, small), small)
                    split_store(high, low, to, grad[f] * v[g])

        loop(BLOCK // small, products)
        gp_all = nn(high[...], heads) + nn(low[...], heads)
        gp = [gp_all[n * BLOCK : (n + 1) * BLOCK, :] for n in range(4)]
        p_all = p_ref[clip * 4 * BLOCK : (clip + 1) * 4 * BLOCK, :]
        p = [p_all[n * BLOCK : (n + 1) * BLOCK, :] for n in range(4)]
        gs = []
        for f in range(FRAMES):
            shared = gp[2 * f] * p[2 * f] + gp[2 * f + 1] * p[2 * f + 1]
            for g in range(FRAMES):
                gs.append((p[2 * f + g] * (gp[2 * f + g] - shared)).astype(BF))
        gs = jnp.concatenate(gs, axis=0)
        spread = p_all.astype(BF)
        for j in range(columns // WIDE):
            at = slice(j * WIDE, (j + 1) * WIDE)
            high[:, at] = nt(spread, heads[at, :]).astype(BF)
            low[:, at] = nt(gs, heads[at, :]).astype(BF)

        def gather(i, start=start):
            at = [pl.ds(pl.multiple_of(start + f * BLOCK + i * small, small), small) for f in range(FRAMES)]
            to = [pl.ds(pl.multiple_of(n * BLOCK + i * small, small), small) for n in range(4)]
            q = [qkv_ref[a, 0:columns].astype(F32) for a in at]
            k = [qkv_ref[a, columns : 2 * columns].astype(F32) for a in at]
            grad = [go[a, :].astype(F32) for a in at]
            s = [low[t, :].astype(F32) for t in to]
            w8 = [high[t, :].astype(F32) for t in to]
            for f in range(FRAMES):
                gqkv[at[f], 0:columns] = ((s[2 * f] * k[0] + s[2 * f + 1] * k[1]) * scale).astype(BF)
                gqkv[at[f], columns : 2 * columns] = ((s[f] * q[0] + s[2 + f] * q[1]) * scale).astype(BF)
                gqkv[at[f], 2 * columns : 3 * columns] = (w8[f] * grad[0] + w8[2 + f] * grad[1]).astype(BF)

        loop(BLOCK // small, gather)
    for j in range(3 * columns // WIDE):
        at = slice(j * WIDE, (j + 1) * WIDE)
        dw_ref[:, at] = tn(nt_ref[...], gqkv[:, at]).astype(BF)
    for j in range(columns // WIDE):
        at = slice(j * WIDE, (j + 1) * WIDE)
        gn[:, at] = nt(gqkv[...], w[at, 0 : 3 * columns])

    def store(at, value):
        gx_ref[at, :] = value.astype(BF)

    gain_sum, shift_sum = norm_back_chunks(gn, x_ref, small_ref[12:13, :], lambda at: gy_ref[at, :], store)
    sums_ref[0:1, :] = column_sums(gqkv, 0, columns)
    sums_ref[1:2, :] = column_sums(gqkv, 2 * columns, columns)
    sums_ref[2:3, :] = column_sums(get, 0, columns)
    sums_ref[3:4, :] = column_sums(grt, 0, columns)
    sums_ref[4:5, :] = gain_sum
    sums_ref[5:6, :] = shift_sum


IN_VMEM = pl.BlockSpec(memory_space=pltpu.VMEM)
IN_ANY = pl.BlockSpec(memory_space=pl.ANY)


def call(body, operands, spaces, outs, scratch, flops, name):
    moved = sum(o.size * o.dtype.itemsize for o in operands) + sum(
        functools.reduce(lambda a, b: a * b, s) * jnp.dtype(d).itemsize for s, d in outs
    )
    return pl.pallas_call(
        body,
        out_shape=[jax.ShapeDtypeStruct(s, d) for s, d in outs],
        in_specs=[IN_ANY if space else IN_VMEM for space in spaces],
        out_specs=[IN_VMEM] * len(outs),
        scratch_shapes=scratch,
        compiler_params=pltpu.CompilerParams(vmem_limit_bytes=VMEM_LIMIT),
        cost_estimate=pl.CostEstimate(flops=flops, bytes_accessed=moved, transcendentals=0),
        name=name,
    )(*operands)


def pack_rows(tokens, once):
    clips, _, columns = tokens.shape
    frames = []
    for f in range(FRAMES):
        places = tokens[:, 1 + f * PLACES : 1 + (f + 1) * PLACES]
        head = tokens[:, :1] if f == 0 or not once else jnp.zeros_like(tokens[:, :1])
        frames.append(jnp.concatenate([places, head, jnp.zeros((clips, BLOCK - PLACES - 1, columns), tokens.dtype)], axis=1))
    return jnp.stack(frames, axis=1).reshape(clips * FRAMES * BLOCK, columns)


def unpack_rows(rows, clips):
    framed = rows.reshape(clips, FRAMES, BLOCK, rows.shape[-1])
    return jnp.concatenate(
        [framed[:, 0, PLACES : PLACES + 1]] + [framed[:, f, :PLACES] for f in range(FRAMES)], axis=1
    )


def layer(x, g, small, hb, wt, ws, we, wr):
    rows, columns = x.shape
    units = we.shape[1]
    blocks = rows // BLOCK
    pairs = columns // 128
    act = ((rows, columns), BF)
    act3 = ((rows, 3 * columns), BF)
    wide = ((rows, columns), F32)
    probs = ((rows * FRAMES, 128), F32)
    sums = ((8, columns), F32)
    square = 2 * rows * columns * columns
    dma = pltpu.SemaphoreType.DMA
    normed_t, qkv_t, o_t, e_t, p_t, y = call(
        time_forward, (x, small, wt), (0, 0, 1), [act, act3, act, act, probs, wide],
        [pltpu.VMEM(wt.shape, BF), pltpu.VMEM((4 * BLOCK, columns), BF), pltpu.VMEM((4 * BLOCK, columns), BF), dma((8,))],
        5 * square, "time_forward",
    )
    normed_s, qkv_s, p_s, o_s, z = call(
        space_forward, (y, small, ws), (0, 0, 1),
        [act, act3, ((2 * blocks * pairs, BLOCK, BLOCK), BF), act, wide],
        [pltpu.VMEM(ws.shape, BF), dma((8,))], 5 * square, "space_forward",
    )
    out, gz, sums_f, ghb, dwe, dwr = call(
        feed, (z, g, small, hb, we, wr), (0, 0, 0, 0, 1, 1),
        [act, wide, sums, ((8, units), F32), (we.shape, BF), (wr.shape, BF)],
        [pltpu.VMEM(we.shape, BF), pltpu.VMEM(wr.shape, BF), pltpu.VMEM((rows, columns), BF),
         pltpu.VMEM((rows, units), BF), pltpu.VMEM((rows, units), BF), pltpu.VMEM((rows, columns), F32), dma((8,))],
        24 * square, "feed",
    )
    gy, sums_s, dws = call(
        space_backward, (gz, y, normed_s, qkv_s, p_s, o_s, small, ws), (0, 0, 0, 0, 0, 0, 0, 1),
        [wide, sums, (ws.shape, BF)],
        [pltpu.VMEM(ws.shape, BF), pltpu.VMEM((rows, columns), BF), pltpu.VMEM((rows, columns), BF),
         pltpu.VMEM((rows, 3 * columns), BF), pltpu.VMEM((rows, columns), F32), dma((8,))],
        10 * square, "space_backward",
    )
    gx, sums_t, dwt = call(
        time_backward, (gy, x, normed_t, qkv_t, p_t, o_t, e_t, small, wt), (0,) * 8 + (1,),
        [act, sums, (wt.shape, BF)],
        [pltpu.VMEM(wt.shape, BF)] + [pltpu.VMEM((rows, columns), BF)] * 3
        + [pltpu.VMEM((rows, 3 * columns), BF), pltpu.VMEM((rows, columns), F32)]
        + [pltpu.VMEM((4 * BLOCK, columns), BF)] * 2 + [dma((8,))],
        10 * square, "time_backward",
    )
    return out, gx, dwt, dws, dwe, dwr, sums_t, sums_s, sums_f, ghb


def local(video, cotangent, live, time_entry, time_exit, time_mixer, space_entry, space_exit, hidden_expand, hidden_reduce, bias_rows, hidden_bias, norm_gain, norm_shift):
    clips, _, tokens, columns = video.shape
    shards = lax.axis_size("shard")
    mine = lax.axis_index("shard")
    part = columns // shards

    def gather(value):
        return lax.all_gather(value, "shard", axis=0, tiled=True)

    packed = jnp.concatenate([bias_rows, hidden_bias.reshape(-1, part), norm_gain, norm_shift], axis=0)
    n_hidden = hidden_bias.shape[0] // part
    spread = lax.all_gather(packed, "shard", axis=0)
    by_rows = jnp.concatenate(
        [
            spread[:, :8].transpose(1, 0, 2).reshape(8, columns),
            spread[:, 8 : 8 + n_hidden].reshape(-1, columns),
            spread[:, 8 + n_hidden :].transpose(1, 0, 2).reshape(6, columns),
        ],
        axis=0,
    ).astype(F32)
    units = hidden_bias.shape[0] * shards
    small = jnp.pad(by_rows, ((0, 6), (0, 0)))
    hb = jnp.pad(spread[:, 8 : 8 + n_hidden].reshape(1, units).astype(F32), ((0, 7), (0, 0)))
    wt = gather(jnp.concatenate([time_entry, time_exit, time_mixer], axis=1))
    ws = gather(jnp.concatenate([space_entry, space_exit], axis=1))
    we = gather(hidden_expand)
    wr = gather(hidden_reduce)
    flags = live.astype(BF)[:, :, None]
    x = pack_rows(video[:, 0], False)
    g = pack_rows(cotangent[:, 0] * flags, True)
    out, gx, dwt, dws, dwe, dwr, sums_t, sums_s, sums_f, ghb = layer(x, g, small, hb, wt, ws, we, wr)

    def reduce(value):
        kept = lax.psum_scatter(value, "shard", scatter_dimension=0, tiled=True)
        return lax.psum(kept, "grp").astype(F32)

    rt, rs, re, rr = reduce(dwt), reduce(dws), reduce(dwe), reduce(dwr)
    sums = jnp.concatenate([sums_t[0:4], sums_s[0:3], sums_f[0:1], ghb[0:1].reshape(-1, columns), sums_t[4:5], sums_s[3:4], sums_f[1:2], sums_t[5:6], sums_s[4:5], sums_f[2:3]], axis=0)
    sums = lax.psum(sums, ("grp", "shard"))
    cut = lax.dynamic_slice_in_dim(sums, mine * part, part, axis=1)
    rows_hidden = lax.dynamic_slice_in_dim(sums[8:12].reshape(-1), mine * hidden_bias.shape[0], hidden_bias.shape[0])
    return (
        (unpack_rows(out, clips) * flags)[:, None],
        unpack_rows(gx, clips)[:, None],
        rt[:, : 3 * columns],
        rt[:, 3 * columns : 4 * columns],
        rt[:, 4 * columns :],
        rs[:, : 3 * columns],
        rs[:, 3 * columns :],
        re,
        rr,
        cut[0:8],
        rows_hidden,
        cut[12:15],
        cut[15:18],
    )


def solution(mesh):
    clips = P(None, ("grp", "shard"), None, None)
    rows = P("shard", None)
    cols = P(None, "shard")
    return jax.shard_map(
        local,
        mesh=mesh,
        in_specs=(clips, clips, P(None, ("grp", "shard"))) + (rows,) * 7 + (cols, P("shard"), cols, cols),
        out_specs=(clips, clips) + (rows,) * 7 + (cols, P("shard"), cols, cols),
        check_vma=False,
    )
```

```python
import functools
import math

import jax
import jax.numpy as jnp
from jax import lax
from jax.experimental import pallas as pl
from jax.experimental.pallas import tpu as pltpu
from jax.sharding import PartitionSpec as P

FRAMES = 2
PLACES = 196
HD = 64
EPSILON = 1e-06
BLOCK = 208
EDGE = 192
CLASS = PLACES - EDGE
CHUNK = 64
WIDE = 256
BF = jnp.bfloat16
F32 = jnp.float32
VMEM_LIMIT = 60 * 1024 * 1024


def nn(a, b):
    return lax.dot_general(a, b, (((1,), (0,)), ((), ())), preferred_element_type=F32)


def nt(a, b):
    return lax.dot_general(a, b, (((1,), (1,)), ((), ())), preferred_element_type=F32)


def tn(a, b):
    return lax.dot_general(a, b, (((0,), (0,)), ((), ())), preferred_element_type=F32)


def loop(count, body):
    def step(i, carry):
        body(i)
        return carry

    lax.fori_loop(0, count, step, 0)


def rows_of(i, size):
    return pl.ds(pl.multiple_of(i * size, size), size)


def cols_of(i, size, base=0):
    return pl.ds(pl.multiple_of(base + i * size, 128), size)


def unit(x):
    center = x - jnp.mean(x, axis=-1, keepdims=True)
    factor = lax.rsqrt(jnp.mean(center * center, axis=-1, keepdims=True) + EPSILON)
    return center * factor, factor


def norm_chunks(src, dst, gain, shift):
    def body(i):
        at = rows_of(i, CHUNK)
        w, _ = unit(src[at, :].astype(F32))
        dst[at, :] = (w * gain + shift).astype(BF)

    loop(src.shape[0] // CHUNK, body)


def fold(x):
    return jnp.sum(x.reshape(x.shape[0] // 8, 8, x.shape[1]), axis=0)


def norm_back_chunks(gn_ref, x_ref, gain, base_of, store):
    columns = x_ref.shape[1]

    def body(i, carry):
        gain_sum, shift_sum = carry
        at = rows_of(i, CHUNK)
        gn = gn_ref[at, :]
        w, factor = unit(x_ref[at, :].astype(F32))
        scaled = gn * gain
        plain = jnp.mean(scaled, axis=-1, keepdims=True)
        cross = jnp.mean(scaled * w, axis=-1, keepdims=True)
        store(at, base_of(at) + factor * (scaled - plain - w * cross))
        return gain_sum + fold(gn * w), shift_sum + fold(gn)

    zero = jnp.zeros((8, columns), F32)
    gain_sum, shift_sum = lax.fori_loop(0, x_ref.shape[0] // CHUNK, body, (zero, zero))
    return jnp.sum(gain_sum, axis=0, keepdims=True), jnp.sum(shift_sum, axis=0, keepdims=True)


def column_sums(ref, start, size):
    def body(i, total):
        return total + fold(ref[rows_of(i, CHUNK), start : start + size].astype(F32))

    total = lax.fori_loop(0, ref.shape[0] // CHUNK, body, jnp.zeros((8, size), F32))
    return jnp.sum(total, axis=0, keepdims=True)


def head_map(columns):
    feature = lax.broadcasted_iota(jnp.int32, (columns, 128), 0) // HD
    head = lax.broadcasted_iota(jnp.int32, (columns, 128), 1)
    return (feature == head).astype(BF)


def split_store(high, low, at, value):
    top = value.astype(BF)
    high[at, :] = top
    low[at, :] = (value - top.astype(F32)).astype(BF)


def row_in_block(i, size, columns):
    return (i * size + lax.broadcasted_iota(jnp.int32, (size, columns), 0)) % BLOCK


def start(pairs, sems):
    copies = [pltpu.make_async_copy(s, d, sems.at[n]) for n, (s, d) in enumerate(pairs)]
    for copy in copies:
        copy.start()
    return copies


def wait(copies):
    for copy in copies:
        copy.wait()


def piece_views(bufs):
    rows = bufs[2].shape[0]
    return [b.at[k * rows : (k + 1) * rows] for b in bufs for k in range(b.shape[0] // rows)]


def rows_at(place, rows, share=1, k=0):
    return pl.ds(pl.multiple_of((place * share + k) * rows, 16), rows)


def load(bufs, place_ref, w, sems):
    if len(bufs) == 1:
        return start([(bufs[0], w)], sems)
    views = piece_views(bufs)
    rows = views[0].shape[0]
    return start([(v, w.at[rows_at(place_ref[n], rows), :]) for n, v in enumerate(views)], sems)


def load_feed(bufs, place_ref, we, wr, sems):
    if len(bufs) == 2:
        return start([(bufs[0], we), (bufs[1], wr)], sems)
    views = piece_views(bufs)
    rows, units = views[0].shape[0], we.shape[1]
    columns = wr.shape[1]
    share = units // columns
    pairs = [(v.at[:, 0:units], we.at[rows_at(place_ref[n], rows), :]) for n, v in enumerate(views)]
    for n, v in enumerate(views):
        for k in range(share):
            to = rows_at(place_ref[n], rows, share, k)
            pairs.append((v.at[:, units + k * columns : units + (k + 1) * columns], wr.at[to, :]))
    return start(pairs, sems)


def store_pieces(dw, outs, place_ref, sems):
    if len(outs) == 1:
        return start([(dw, outs[0])], sems)
    rows = outs[0].shape[1]
    pairs = []
    for side, out in enumerate(outs):
        for m in range(out.shape[0]):
            pairs.append((dw.at[rows_at(place_ref[8 + side * 4 + m], rows), :], out.at[m]))
    return start(pairs, sems)


def store_feed(dwe, dwr, outs, whole, place_ref, sems):
    if whole:
        return start([(dwe, outs[0]), (dwr, outs[1])], sems)
    rows, units, columns = outs[0].shape[1], dwe.shape[1], dwr.shape[1]
    share = units // columns
    pairs = []
    for side, out in enumerate(outs):
        for m in range(out.shape[0]):
            place = place_ref[8 + side * 4 + m]
            pairs.append((dwe.at[rows_at(place, rows), :], out.at[m, :, 0:units]))
            for k in range(share):
                source = dwr.at[rows_at(place, rows, share, k), :]
                pairs.append((source, out.at[m, :, units + k * columns : units + (k + 1) * columns]))
    return start(pairs, sems)


def time_forward(nb, place_ref, x_ref, small_ref, *refs):
    bufs, (nt_ref, qkv_ref, o_ref, e_ref, p_ref, y_ref, w, high, low, sems) = refs[:nb], refs[nb:]
    columns = x_ref.shape[1]
    copies = load(bufs, place_ref, w, sems)
    norm_chunks(x_ref, nt_ref, small_ref[12:13, :], small_ref[15:16, :])
    wait(copies)
    zero_bias = jnp.zeros((1, columns), F32)
    for part, bias in enumerate((small_ref[0:1, :], zero_bias, small_ref[1:2, :])):
        for j in range(columns // WIDE):
            at = slice(j * WIDE, (j + 1) * WIDE)
            to = slice(part * columns + j * WIDE, part * columns + (j + 1) * WIDE)
            qkv_ref[:, to] = (nn(nt_ref[...], w[:, to]) + bias[:, at]).astype(BF)
    heads = head_map(columns)
    small = 16
    for clip in range(x_ref.shape[0] // (FRAMES * BLOCK)):
        first = clip * FRAMES * BLOCK

        def products(i, first=first):
            at = [pl.ds(pl.multiple_of(first + f * BLOCK + i * small, small), small) for f in range(FRAMES)]
            q = [qkv_ref[a, 0:columns].astype(F32) for a in at]
            k = [qkv_ref[a, columns : 2 * columns].astype(F32) for a in at]
            for f in range(FRAMES):
                for g in range(FRAMES):
                    to = pl.ds(pl.multiple_of((f * FRAMES + g) * BLOCK + i * small, small), small)
                    split_store(high, low, to, q[f] * k[g])

        loop(BLOCK // small, products)
        scores = (nn(high[...], heads) + nn(low[...], heads)) * HD ** (-0.5)
        s = [scores[n * BLOCK : (n + 1) * BLOCK, :] for n in range(4)]
        for f in range(FRAMES):
            peak = jnp.maximum(s[2 * f], s[2 * f + 1])
            powered = [jnp.exp(s[2 * f] - peak), jnp.exp(s[2 * f + 1] - peak)]
            total = powered[0] + powered[1]
            for g in range(FRAMES):
                to = slice(clip * 4 * BLOCK + (2 * f + g) * BLOCK, clip * 4 * BLOCK + (2 * f + g + 1) * BLOCK)
                p_ref[to, :] = powered[g] / total
        spread = p_ref[clip * 4 * BLOCK : (clip + 1) * 4 * BLOCK, :].astype(BF)
        for j in range(columns // WIDE):
            at = slice(j * WIDE, (j + 1) * WIDE)
            high[:, at] = nt(spread, heads[at, :]).astype(BF)

        def mixture(i, first=first):
            at = [pl.ds(pl.multiple_of(first + f * BLOCK + i * small, small), small) for f in range(FRAMES)]
            v = [qkv_ref[a, 2 * columns : 3 * columns].astype(F32) for a in at]
            for f in range(FRAMES):
                total = 0.0
                for g in range(FRAMES):
                    p = high[pl.ds(pl.multiple_of((f * FRAMES + g) * BLOCK + i * small, small), small), :]
                    total = total + p.astype(F32) * v[g]
                o_ref[at[f], :] = total.astype(BF)

        loop(BLOCK // small, mixture)
    for j in range(columns // WIDE):
        at = slice(j * WIDE, (j + 1) * WIDE)
        from_w = slice(3 * columns + j * WIDE, 3 * columns + (j + 1) * WIDE)
        e_ref[:, at] = (nn(o_ref[...], w[:, from_w]) + small_ref[2:3, at]).astype(BF)
    patch = row_in_block(0, x_ref.shape[0], WIDE) < PLACES
    for j in range(columns // WIDE):
        at = slice(j * WIDE, (j + 1) * WIDE)
        from_w = slice(4 * columns + j * WIDE, 4 * columns + (j + 1) * WIDE)
        branch = nn(e_ref[...], w[:, from_w]) + small_ref[3:4, at]
        y_ref[:, at] = x_ref[:, at].astype(F32) + jnp.where(patch, branch, 0.0)


def half_masks():
    lane = lax.broadcasted_iota(jnp.int32, (1, 128), 1)
    return (lane < HD).astype(BF), (lane >= HD).astype(BF)


def space_forward(nb, place_ref, y_ref, small_ref, *refs):
    bufs, (ns_ref, qkv_ref, p_ref, o_ref, z_ref, w, sems) = refs[:nb], refs[nb:]
    columns = y_ref.shape[1]
    blocks = y_ref.shape[0] // BLOCK
    pairs = columns // 128
    copies = load(bufs, place_ref, w, sems)
    norm_chunks(y_ref, ns_ref, small_ref[13:14, :], small_ref[16:17, :])
    wait(copies)
    zero_bias = jnp.zeros((1, columns), F32)
    for part, bias in enumerate((small_ref[4:5, :], zero_bias, small_ref[5:6, :])):
        for j in range(columns // WIDE):
            at = slice(j * WIDE, (j + 1) * WIDE)
            to = slice(part * columns + j * WIDE, part * columns + (j + 1) * WIDE)
            qkv_ref[:, to] = (nn(ns_ref[...], w[:, to]) + bias[:, at]).astype(BF)
    masks = half_masks()
    first = lax.broadcasted_iota(jnp.int32, (BLOCK, 128), 1) < HD
    column = lax.broadcasted_iota(jnp.int32, (1, BLOCK), 1)
    hidden = jnp.where(column <= PLACES, 0.0, -1e30)

    def attend(n):
        block, pair = n // pairs, n % pairs
        at = rows_of(block, BLOCK)
        q = qkv_ref[at, cols_of(pair, 128)]
        k = qkv_ref[at, cols_of(pair, 128, columns)]
        v = qkv_ref[at, cols_of(pair, 128, 2 * columns)]
        outs = []
        for half in range(2):
            scores = nt(q * masks[half], k) * HD ** (-0.5) + hidden
            powered = jnp.exp(scores - jnp.max(scores, axis=-1, keepdims=True))
            weights = (powered * (1.0 / jnp.sum(powered, axis=-1, keepdims=True))).astype(BF)
            p_ref[2 * n + half] = weights
            outs.append(nn(weights, v))
        o_ref[at, cols_of(pair, 128)] = jnp.where(first, outs[0], outs[1]).astype(BF)

    loop(blocks * pairs, attend)
    is_class = lax.broadcasted_iota(jnp.int32, (BLOCK - EDGE, WIDE), 0) == CLASS
    for j in range(columns // WIDE):
        at = slice(j * WIDE, (j + 1) * WIDE)
        from_w = slice(3 * columns + j * WIDE, 3 * columns + (j + 1) * WIDE)
        branch = nn(o_ref[...], w[:, from_w]) + small_ref[6:7, at]
        z_ref[:, at] = y_ref[:, at] + branch
        for clip in range(blocks // FRAMES):
            edges = [slice((clip * FRAMES + f) * BLOCK + EDGE, (clip * FRAMES + f + 1) * BLOCK) for f in range(FRAMES)]
            mean = (branch[edges[0], :] + branch[edges[1], :]) * (1.0 / FRAMES)
            for edge in edges:
                z_ref[edge, at] = y_ref[edge, at] + jnp.where(is_class, mean, branch[edge, :])


def gelu_both(h):
    cdf = 0.5 * (1.0 + lax.erf(h * 0.5**0.5))
    density = jnp.exp(h * h * -0.5) * 0.3989422804014327
    return h * cdf, cdf + h * density


def feed(nb, place_ref, z_ref, g_ref, small_ref, hb_ref, *refs):
    bufs, (out_ref, gz_ref, sums_ref, ghb_ref, *outs) = refs[:nb], refs[nb : nb + 6]
    we, wr, dwe_ref, dwr_ref, nm, a, gh, gn, sems, out_sems = refs[nb + 6 :]
    columns = z_ref.shape[1]
    units = we.shape[1]
    copies = load_feed(bufs, place_ref, we, wr, sems)
    norm_chunks(z_ref, nm, small_ref[14:15, :], small_ref[17:18, :])
    wait(copies)

    def inner(j):
        at = cols_of(j, WIDE)
        h = nn(nm[...], we[:, at]) + hb_ref[0:1, at]
        active, slope = gelu_both(h)
        a[:, at] = active.astype(BF)
        gh[:, at] = (nt(g_ref[...], wr[rows_of(j, WIDE), :]) * slope).astype(BF)

    loop(units // WIDE, inner)

    def outer(j):
        at = cols_of(j, WIDE)
        dwr_ref[rows_of(j, WIDE), :] = tn(a[:, at], g_ref[...]).astype(BF)
        block = gh[:, at]
        dwe_ref[:, at] = tn(nm[...], block).astype(BF)
        ghb_ref[0:1, at] = jnp.sum(block.astype(F32), axis=0, keepdims=True)

    loop(units // WIDE, outer)
    copies = store_feed(dwe_ref, dwr_ref, outs, nb == 2, place_ref, out_sems)
    for j in range(columns // WIDE):
        at = slice(j * WIDE, (j + 1) * WIDE)
        gn[:, at] = nt(gh[...], we[at, :])
        out_ref[:, at] = (z_ref[:, at] + (nn(a[...], wr[:, at]) + small_ref[7:8, at])).astype(BF)

    def store(rows, value):
        gz_ref[rows, :] = value

    gain_sum, shift_sum = norm_back_chunks(
        gn, z_ref, small_ref[14:15, :], lambda rows: g_ref[rows, :].astype(F32), store
    )
    sums_ref[0:1, :] = column_sums(g_ref, 0, columns)
    sums_ref[1:2, :] = gain_sum
    sums_ref[2:3, :] = shift_sum
    wait(copies)


def space_backward(nb, no, place_ref, gz_ref, y_ref, ns_ref, qkv_ref, p_ref, o_ref, small_ref, *refs):
    bufs, (gy_ref, sums_ref, *outs) = refs[:nb], refs[nb : nb + 2 + no]
    w, dw_ref, gbs, go, gqkv, gn, sems, out_sems = refs[nb + 2 + no :]
    columns = y_ref.shape[1]
    rows = y_ref.shape[0]
    clips = rows // (BLOCK * FRAMES)
    pairs = columns // 128
    copies = load(bufs, place_ref, w, sems)

    def lower(i):
        at = rows_of(i, CHUNK)
        gbs[at, :] = gz_ref[at, :].astype(BF)

    loop(rows // CHUNK, lower)
    is_class = lax.broadcasted_iota(jnp.int32, (BLOCK - EDGE, columns), 0) == CLASS
    for clip in range(clips):
        edges = [slice((clip * FRAMES + f) * BLOCK + EDGE, (clip * FRAMES + f + 1) * BLOCK) for f in range(FRAMES)]
        share = gz_ref[edges[0], :] * (1.0 / FRAMES)
        for edge in edges:
            gbs[edge, :] = jnp.where(is_class, share, gz_ref[edge, :]).astype(BF)
    wait(copies)
    for j in range(columns // WIDE):
        at = slice(j * WIDE, (j + 1) * WIDE)
        go[:, at] = nt(gbs[...], w[at, 3 * columns : 4 * columns]).astype(BF)
        dw_ref[:, 3 * columns + j * WIDE : 3 * columns + (j + 1) * WIDE] = tn(o_ref[...], gbs[:, at]).astype(BF)
    masks = half_masks()
    first = lax.broadcasted_iota(jnp.int32, (BLOCK, 128), 1) < HD
    class_row = lax.broadcasted_iota(jnp.int32, (BLOCK, 128), 0) == PLACES

    def attend(n):
        clip, pair = n // pairs, n % pairs
        found = []
        for f in range(FRAMES):
            block = clip * FRAMES + f
            at = rows_of(block, BLOCK)
            q = qkv_ref[at, cols_of(pair, 128)]
            k = qkv_ref[at, cols_of(pair, 128, columns)]
            v = qkv_ref[at, cols_of(pair, 128, 2 * columns)]
            grad = go[at, cols_of(pair, 128)]
            parts = []
            for half in range(2):
                p = p_ref[2 * (block * pairs + pair) + half]
                gp = nt(grad * masks[half], v)
                weights = p.astype(F32)
                shared = jnp.sum(gp * weights, axis=-1, keepdims=True)
                gs = (weights * (gp - shared)).astype(BF)
                parts.append((nn(gs, k), tn(gs, q), tn(p, grad)))
            scale = HD ** (-0.5)
            found.append(
                [jnp.where(first, left, right) * s for left, right, s in zip(*parts, (scale, scale, 1.0))]
            )
        for part in range(3):
            one, two = found[0][part], found[1][part]
            one = jnp.where(class_row, one + two, one)
            two = jnp.where(class_row, 0.0, two)
            to = cols_of(pair, 128, part * columns)
            gqkv[rows_of(clip * FRAMES, BLOCK), to] = one.astype(BF)
            gqkv[rows_of(clip * FRAMES + 1, BLOCK), to] = two.astype(BF)

    loop(clips * pairs, attend)
    for j in range(3 * columns // WIDE):
        at = slice(j * WIDE, (j + 1) * WIDE)
        dw_ref[:, at] = tn(ns_ref[...], gqkv[:, at]).astype(BF)
    copies = store_pieces(dw_ref, outs, place_ref, out_sems)
    for j in range(columns // WIDE):
        at = slice(j * WIDE, (j + 1) * WIDE)
        gn[:, at] = nt(gqkv[...], w[at, 0 : 3 * columns])

    def store(at, value):
        gy_ref[at, :] = value

    gain_sum, shift_sum = norm_back_chunks(gn, y_ref, small_ref[13:14, :], lambda at: gz_ref[at, :], store)
    sums_ref[0:1, :] = column_sums(gqkv, 0, columns)
    sums_ref[1:2, :] = column_sums(gqkv, 2 * columns, columns)
    sums_ref[2:3, :] = column_sums(gbs, 0, columns)
    sums_ref[3:4, :] = gain_sum
    sums_ref[4:5, :] = shift_sum
    wait(copies)


def time_backward(nb, no, place_ref, gy_ref, x_ref, nt_ref, qkv_ref, p_ref, o_ref, e_ref, small_ref, *refs):
    bufs, (gx_ref, sums_ref, *outs) = refs[:nb], refs[nb : nb + 2 + no]
    w, dw_ref, grt, get, go, gqkv, gn, high, low, sems, out_sems = refs[nb + 2 + no :]
    columns = x_ref.shape[1]
    rows = x_ref.shape[0]
    copies = load(bufs, place_ref, w, sems)

    def lower(i):
        at = rows_of(i, CHUNK)
        patch = row_in_block(i, CHUNK, columns) < PLACES
        grt[at, :] = jnp.where(patch, gy_ref[at, :], 0.0).astype(BF)

    loop(rows // CHUNK, lower)
    wait(copies)
    for j in range(columns // WIDE):
        at = slice(j * WIDE, (j + 1) * WIDE)
        get[:, at] = nt(grt[...], w[at, 4 * columns : 5 * columns]).astype(BF)
        dw_ref[:, 4 * columns + j * WIDE : 4 * columns + (j + 1) * WIDE] = tn(e_ref[...], grt[:, at]).astype(BF)
    for j in range(columns // WIDE):
        at = slice(j * WIDE, (j + 1) * WIDE)
        go[:, at] = nt(get[...], w[at, 3 * columns : 4 * columns]).astype(BF)
        dw_ref[:, 3 * columns + j * WIDE : 3 * columns + (j + 1) * WIDE] = tn(o_ref[...], get[:, at]).astype(BF)
    heads = head_map(columns)
    small = 16
    scale = HD ** (-0.5)
    for clip in range(rows // (FRAMES * BLOCK)):
        start = clip * FRAMES * BLOCK

        def products(i, start=start):
            at = [pl.ds(pl.multiple_of(start + f * BLOCK + i * small, small), small) for f in range(FRAMES)]
            grad = [go[a, :].astype(F32) for a in at]
            v = [qkv_ref[a, 2 * columns : 3 * columns].astype(F32) for a in at]
            for f in range(FRAMES):
                for g in range(FRAMES):
                    to = pl.ds(pl.multiple_of((f * FRAMES + g) * BLOCK + i * small, small), small)
                    split_store(high, low, to, grad[f] * v[g])

        loop(BLOCK // small, products)
        gp_all = nn(high[...], heads) + nn(low[...], heads)
        gp = [gp_all[n * BLOCK : (n + 1) * BLOCK, :] for n in range(4)]
        p_all = p_ref[clip * 4 * BLOCK : (clip + 1) * 4 * BLOCK, :]
        p = [p_all[n * BLOCK : (n + 1) * BLOCK, :] for n in range(4)]
        gs = []
        for f in range(FRAMES):
            shared = gp[2 * f] * p[2 * f] + gp[2 * f + 1] * p[2 * f + 1]
            for g in range(FRAMES):
                gs.append((p[2 * f + g] * (gp[2 * f + g] - shared)).astype(BF))
        gs = jnp.concatenate(gs, axis=0)
        spread = p_all.astype(BF)
        for j in range(columns // WIDE):
            at = slice(j * WIDE, (j + 1) * WIDE)
            high[:, at] = nt(spread, heads[at, :]).astype(BF)
            low[:, at] = nt(gs, heads[at, :]).astype(BF)

        def gather(i, start=start):
            at = [pl.ds(pl.multiple_of(start + f * BLOCK + i * small, small), small) for f in range(FRAMES)]
            to = [pl.ds(pl.multiple_of(n * BLOCK + i * small, small), small) for n in range(4)]
            q = [qkv_ref[a, 0:columns].astype(F32) for a in at]
            k = [qkv_ref[a, columns : 2 * columns].astype(F32) for a in at]
            grad = [go[a, :].astype(F32) for a in at]
            s = [low[t, :].astype(F32) for t in to]
            w8 = [high[t, :].astype(F32) for t in to]
            for f in range(FRAMES):
                gqkv[at[f], 0:columns] = ((s[2 * f] * k[0] + s[2 * f + 1] * k[1]) * scale).astype(BF)
                gqkv[at[f], columns : 2 * columns] = ((s[f] * q[0] + s[2 + f] * q[1]) * scale).astype(BF)
                gqkv[at[f], 2 * columns : 3 * columns] = (w8[f] * grad[0] + w8[2 + f] * grad[1]).astype(BF)

        loop(BLOCK // small, gather)
    for j in range(3 * columns // WIDE):
        at = slice(j * WIDE, (j + 1) * WIDE)
        dw_ref[:, at] = tn(nt_ref[...], gqkv[:, at]).astype(BF)
    copies = store_pieces(dw_ref, outs, place_ref, out_sems)
    for j in range(columns // WIDE):
        at = slice(j * WIDE, (j + 1) * WIDE)
        gn[:, at] = nt(gqkv[...], w[at, 0 : 3 * columns])

    def store(at, value):
        gx_ref[at, :] = value.astype(BF)

    gain_sum, shift_sum = norm_back_chunks(gn, x_ref, small_ref[12:13, :], lambda at: gy_ref[at, :], store)
    sums_ref[0:1, :] = column_sums(gqkv, 0, columns)
    sums_ref[1:2, :] = column_sums(gqkv, 2 * columns, columns)
    sums_ref[2:3, :] = column_sums(get, 0, columns)
    sums_ref[3:4, :] = column_sums(grt, 0, columns)
    sums_ref[4:5, :] = gain_sum
    sums_ref[5:6, :] = shift_sum
    wait(copies)


SPACES = {
    "v": pl.BlockSpec(memory_space=pltpu.VMEM),
    "a": pl.BlockSpec(memory_space=pl.ANY),
    "s": pl.BlockSpec(memory_space=pltpu.SMEM),
}


def call(body, operands, spaces, outs, out_spaces, scratch, flops, name):
    moved = sum(o.size * o.dtype.itemsize for o in operands)
    moved += sum(math.prod(s) * jnp.dtype(d).itemsize for s, d in outs)
    return pl.pallas_call(
        body,
        out_shape=[jax.ShapeDtypeStruct(s, d) for s, d in outs],
        in_specs=[SPACES[space] for space in spaces],
        out_specs=[SPACES[space] for space in out_spaces],
        scratch_shapes=scratch,
        compiler_params=pltpu.CompilerParams(vmem_limit_bytes=VMEM_LIMIT),
        cost_estimate=pl.CostEstimate(flops=flops, bytes_accessed=moved, transcendentals=0),
        name=name,
    )(*operands)


def pack_rows(tokens, once):
    clips, _, columns = tokens.shape
    frames = []
    for f in range(FRAMES):
        places = tokens[:, 1 + f * PLACES : 1 + (f + 1) * PLACES]
        head = tokens[:, :1] if f == 0 or not once else jnp.zeros_like(tokens[:, :1])
        frames.append(jnp.concatenate([places, head, jnp.zeros((clips, BLOCK - PLACES - 1, columns), tokens.dtype)], axis=1))
    return jnp.stack(frames, axis=1).reshape(clips * FRAMES * BLOCK, columns)


def unpack_rows(rows, clips):
    framed = rows.reshape(clips, FRAMES, BLOCK, rows.shape[-1])
    return jnp.concatenate(
        [framed[:, 0, PLACES : PLACES + 1]] + [framed[:, f, :PLACES] for f in range(FRAMES)], axis=1
    )


class Layer:
    def __init__(self, rows, columns, units, shards, pieced, place):
        self.rows, self.columns, self.units = rows, columns, units
        self.pieced, self.place = pieced, place
        self.piece = columns // shards
        self.act = ((rows, columns), BF)
        self.act3 = ((rows, 3 * columns), BF)
        self.wide = ((rows, columns), F32)
        self.sums = ((8, columns), F32)
        self.square = 2 * rows * columns * columns

    def grads(self, width):
        if self.pieced:
            return [((4, self.piece, width), BF)] * 2
        return [((self.columns, width), BF)]

    def vmem(self, *shapes):
        return [pltpu.VMEM(s, d) for s, d in shapes]

    def sems(self, count):
        return [pltpu.SemaphoreType.DMA((count,))]

    def time_forward(self, x, small, bufs):
        c, n = self.columns, len(bufs)
        quad = ((4 * BLOCK, c), BF)
        return call(
            functools.partial(time_forward, n), (self.place, x, small, *bufs), "svv" + "a" * n,
            [self.act, self.act3, self.act, self.act, ((self.rows * FRAMES, 128), F32), self.wide], "v" * 6,
            self.vmem(((c, 5 * c), BF), quad, quad) + self.sems(8), 5 * self.square, "time_forward",
        )

    def space_forward(self, y, small, bufs):
        c, n = self.columns, len(bufs)
        probs = ((self.rows // BLOCK * (c // 128) * 2, BLOCK, BLOCK), BF)
        return call(
            functools.partial(space_forward, n), (self.place, y, small, *bufs), "svv" + "a" * n,
            [self.act, self.act3, probs, self.act, self.wide], "v" * 5,
            self.vmem(((c, 4 * c), BF)) + self.sems(8), 5 * self.square, "space_forward",
        )

    def feed(self, z, g, small, hb, bufs):
        c, u, n = self.columns, self.units, len(bufs)
        outs = self.grads(u + u) if self.pieced else [((c, u), BF), ((u, c), BF)]
        return call(
            functools.partial(feed, n), (self.place, z, g, small, hb, *bufs), "svvvv" + "a" * n,
            [self.act, self.wide, self.sums, ((8, u), F32)] + outs, "vvvv" + "a" * len(outs),
            self.vmem(((c, u), BF), ((u, c), BF), ((c, u), BF), ((u, c), BF), self.act, ((self.rows, u), BF), ((self.rows, u), BF), self.wide)
            + self.sems(64) + self.sems(64), 24 * self.square, "feed",
        )

    def space_backward(self, gz, y, normed, qkv, p, o, small, bufs):
        c, n = self.columns, len(bufs)
        outs = self.grads(4 * c)
        return call(
            functools.partial(space_backward, n, len(outs)), (self.place, gz, y, normed, qkv, p, o, small, *bufs), "s" + "v" * 7 + "a" * n,
            [self.wide, self.sums] + outs, "vv" + "a" * len(outs),
            self.vmem(((c, 4 * c), BF), ((c, 4 * c), BF), self.act, self.act, self.act3, self.wide) + self.sems(8) + self.sems(8),
            10 * self.square, "space_backward",
        )

    def time_backward(self, gy, x, normed, qkv, p, o, e, small, bufs):
        c, n = self.columns, len(bufs)
        outs = self.grads(5 * c)
        quad = ((4 * BLOCK, c), BF)
        return call(
            functools.partial(time_backward, n, len(outs)), (self.place, gy, x, normed, qkv, p, o, e, small, *bufs), "s" + "v" * 8 + "a" * n,
            [self.act, self.sums] + outs, "vv" + "a" * len(outs),
            self.vmem(((c, 5 * c), BF), ((c, 5 * c), BF), self.act, self.act, self.act, self.act3, self.wide, quad, quad) + self.sems(8) + self.sems(8),
            10 * self.square, "time_backward",
        )


BOTH = ("grp", "shard")


def permute(value, target):
    shards = lax.axis_size("shard")
    pairs = [(z * shards + s, z * shards + target(s)) for z in range(lax.axis_size("grp")) for s in range(shards)]
    return lax.ppermute(value, BOTH, pairs)


def to_sibling(value):
    return permute(value, lambda s: s ^ 1)


def along_x(value):
    return permute(value, lambda s: s ^ 2)


def along_y(value):
    return permute(value, lambda s: s ^ 4)


def gather_start(own):
    return jnp.concatenate([own, to_sibling(own)], axis=0)


def gather_hop(both):
    return permute(both, lambda s: s ^ (2 if s % 2 == 0 else 4))


def gather_rest(both, hop):
    second = permute(hop[: hop.shape[0] // 2], lambda s: s ^ (4 if s % 2 == 0 else 2))
    return (both, hop, second, to_sibling(hop), to_sibling(second))


def places(s):
    near = jnp.where(s % 2 == 0, 2, 4)
    far = 6 - near
    gathered = [s, s ^ 1, s ^ near, s ^ near ^ 1, s ^ 6, s ^ 1 ^ far, s ^ far, s ^ 7]
    kept = [s, s ^ 2, s ^ 4, s ^ 6]
    return jnp.stack(gathered + kept + [k ^ 1 for k in kept]).astype(jnp.int32)


def reduce_pieces(keep, give):
    summed = keep + to_sibling(give)
    own, west, north, far = summed[0], summed[1], summed[2], summed[3]
    half = own.shape[0] // 2
    got_x = along_x(jnp.stack([far[:half], west[:half]]))
    got_y = along_y(jnp.stack([far[half:], north[half:]]))
    last_x = along_x(west[half:] + got_y[0])
    last_y = along_y(north[:half] + got_x[0])
    wide = own.astype(F32)
    low_half = wide[:half] + got_x[1].astype(F32) + last_y.astype(F32)
    high_half = wide[half:] + got_y[1].astype(F32) + last_x.astype(F32)
    return jnp.concatenate([low_half, high_half], axis=0).astype(BF)


def local(video, cotangent, live, time_entry, time_exit, time_mixer, space_entry, space_exit, hidden_expand, hidden_reduce, bias_rows, hidden_bias, norm_gain, norm_shift):
    clips, _, tokens, columns = video.shape
    shards, groups = lax.axis_size("shard"), lax.axis_size("grp")
    mine = lax.axis_index("shard")
    part = columns // shards
    units = hidden_bias.shape[0] * shards
    share = units // columns
    pieced = shards == 8

    own_t = jnp.concatenate([time_entry, time_exit, time_mixer], axis=1)
    own_s = jnp.concatenate([space_entry, space_exit], axis=1)
    if pieced:
        own_f = jnp.concatenate([hidden_expand] + [hidden_reduce[k * part : (k + 1) * part] for k in range(share)], axis=1)
        both_t = gather_start(own_t)
        hop_t = gather_hop(both_t)
        both_s, both_f = gather_start(own_s), gather_start(own_f)
        both_s, hop_t = lax.optimization_barrier((both_s, hop_t))
        wt = gather_rest(both_t, hop_t)
        hop_s = gather_hop(both_s)
        both_f, hop_s = lax.optimization_barrier((both_f, hop_s))
        ws = gather_rest(both_s, hop_s)
        wf = gather_rest(both_f, gather_hop(both_f))
        place = places(mine)
    else:
        wt, ws, we, wr = (lax.all_gather(v, "shard", axis=0, tiled=True) for v in (own_t, own_s, hidden_expand, hidden_reduce))
        wt, ws, wf = (wt,), (ws,), (we, wr)
        place = jnp.zeros((16,), jnp.int32)

    packed = jnp.concatenate([bias_rows, hidden_bias.reshape(-1, part), norm_gain, norm_shift], axis=0)
    spread = lax.all_gather(packed, "shard", axis=0)
    by_rows = jnp.concatenate(
        [
            spread[:, :8].transpose(1, 0, 2).reshape(8, columns),
            spread[:, 8 : 8 + share].reshape(-1, columns),
            spread[:, 8 + share :].transpose(1, 0, 2).reshape(6, columns),
        ],
        axis=0,
    ).astype(F32)
    small = jnp.pad(by_rows, ((0, 6), (0, 0)))
    hb = jnp.pad(spread[:, 8 : 8 + share].reshape(1, units).astype(F32), ((0, 7), (0, 0)))
    flags = live.astype(BF)[:, :, None]
    x = pack_rows(video[:, 0], False)
    g = pack_rows(cotangent[:, 0] * flags, True)

    net = Layer(x.shape[0], columns, units, shards, pieced, place)
    normed_t, qkv_t, o_t, e_t, p_t, y = net.time_forward(x, small, wt)
    normed_s, qkv_s, p_s, o_s, z = net.space_forward(y, small, ws)
    out, gz, sums_f, ghb, *grad_f = net.feed(z, g, small, hb, wf)
    gy, sums_s, *grad_s = net.space_backward(gz, y, normed_s, qkv_s, p_s, o_s, small, ws)
    gx, sums_t, *grad_t = net.time_backward(gy, x, normed_t, qkv_t, p_t, o_t, e_t, small, wt)

    if pieced:
        kept_f = lax.psum(reduce_pieces(*grad_f), "grp")
        kept_s, kept_f = lax.optimization_barrier((reduce_pieces(*grad_s), kept_f))
        kept_s = lax.psum(kept_s, "grp")
        kept_t, kept_s = lax.optimization_barrier((reduce_pieces(*grad_t), kept_s))
        kept_t = lax.psum(kept_t, "grp")
        rt, rs, rf = (v.astype(F32) for v in (kept_t, kept_s, kept_f))
        re = rf[:, :units]
        rr = jnp.concatenate([rf[:, units + k * columns : units + (k + 1) * columns] for k in range(share)], axis=0)
    else:
        rt, rs, re, rr = (
            lax.psum(lax.psum_scatter(v, "shard", scatter_dimension=0, tiled=True), "grp").astype(F32)
            for v in (*grad_t, *grad_s, *grad_f)
        )
    sums = jnp.concatenate(
        [sums_t[0:4], sums_s[0:3], sums_f[0:1], ghb[0:1].reshape(-1, columns), sums_t[4:5], sums_s[3:4], sums_f[1:2], sums_t[5:6], sums_s[4:5], sums_f[2:3]],
        axis=0,
    )
    sums = lax.psum(sums, ("grp", "shard"))
    cut = lax.dynamic_slice_in_dim(sums, mine * part, part, axis=1)
    rows_hidden = lax.dynamic_slice_in_dim(sums[8 : 8 + share].reshape(-1), mine * hidden_bias.shape[0], hidden_bias.shape[0])
    last = 8 + share
    return (
        (unpack_rows(out, clips) * flags)[:, None],
        unpack_rows(gx, clips)[:, None],
        rt[:, : 3 * columns],
        rt[:, 3 * columns : 4 * columns],
        rt[:, 4 * columns :],
        rs[:, : 3 * columns],
        rs[:, 3 * columns :],
        re,
        rr,
        cut[0:8],
        rows_hidden,
        cut[last : last + 3],
        cut[last + 3 : last + 6],
    )


def solution(mesh):
    clips = P(None, ("grp", "shard"), None, None)
    rows = P("shard", None)
    cols = P(None, "shard")
    return jax.shard_map(
        local,
        mesh=mesh,
        in_specs=(clips, clips, P(None, ("grp", "shard"))) + (rows,) * 7 + (cols, P("shard"), cols, cols),
        out_specs=(clips, clips) + (rows,) * 7 + (cols, P("shard"), cols, cols),
        check_vma=False,
    )
```

```python
import functools
import math

import jax
import jax.numpy as jnp
from jax import lax
from jax.experimental import pallas as pl
from jax.experimental.pallas import tpu as pltpu
from jax.sharding import PartitionSpec as P

FRAMES = 2
PLACES = 196
HD = 64
EPSILON = 1e-06
BLOCK = 208
EDGE = 192
CLASS = PLACES - EDGE
CHUNK = 2 * BLOCK
WIDE = 256
BF = jnp.bfloat16
F32 = jnp.float32
SMALL = 32
MICRO = 4_000_000_000
VMEM_LIMIT = 60 * 1024 * 1024


def nn(a, b):
    return lax.dot_general(a, b, (((1,), (0,)), ((), ())), preferred_element_type=F32)


def nt(a, b):
    return lax.dot_general(a, b, (((1,), (1,)), ((), ())), preferred_element_type=F32)


def tn(a, b):
    return lax.dot_general(a, b, (((0,), (0,)), ((), ())), preferred_element_type=F32)


def loop(count, body):
    def step(i, carry):
        body(i)
        return carry

    lax.fori_loop(0, count, step, 0)


def rows_of(i, size):
    return pl.ds(pl.multiple_of(i * size, size), size)


def cols_of(i, size, base=0):
    return pl.ds(pl.multiple_of(base + i * size, 128), size)


def unit(x):
    center = x - jnp.mean(x, axis=-1, keepdims=True)
    factor = lax.rsqrt(jnp.mean(center * center, axis=-1, keepdims=True) + EPSILON)
    return center * factor, factor


def norm_chunks(src, dst, gain, shift):
    def body(i):
        at = rows_of(i, CHUNK)
        w, _ = unit(src[at, :].astype(F32))
        dst[at, :] = (w * gain + shift).astype(BF)

    loop(src.shape[0] // CHUNK, body)


def fold(x):
    return jnp.sum(x.reshape(x.shape[0] // 8, 8, x.shape[1]), axis=0)


def norm_back_chunks(gn_ref, x_ref, gain, base_of, store):
    columns = x_ref.shape[1]

    def body(i, carry):
        gain_sum, shift_sum = carry
        at = rows_of(i, CHUNK)
        gn = gn_ref[at, :]
        w, factor = unit(x_ref[at, :].astype(F32))
        scaled = gn * gain
        plain = jnp.mean(scaled, axis=-1, keepdims=True)
        cross = jnp.mean(scaled * w, axis=-1, keepdims=True)
        store(at, base_of(at) + factor * (scaled - plain - w * cross))
        return gain_sum + fold(gn * w), shift_sum + fold(gn)

    zero = jnp.zeros((8, columns), F32)
    gain_sum, shift_sum = lax.fori_loop(0, x_ref.shape[0] // CHUNK, body, (zero, zero))
    return jnp.sum(gain_sum, axis=0, keepdims=True), jnp.sum(shift_sum, axis=0, keepdims=True)


def column_sums(ref, start, size):
    def body(i, total):
        return total + fold(ref[rows_of(i, CHUNK), start : start + size].astype(F32))

    total = lax.fori_loop(0, ref.shape[0] // CHUNK, body, jnp.zeros((8, size), F32))
    return jnp.sum(total, axis=0, keepdims=True)


def head_map(columns):
    feature = lax.broadcasted_iota(jnp.int32, (columns, 128), 0) // HD
    head = lax.broadcasted_iota(jnp.int32, (columns, 128), 1)
    return (feature == head).astype(BF)


def head_sums(a_ref, a_rows, a_base, b_ref, b_rows, b_base, heads):
    total = None
    for j in range(heads.shape[0] // WIDE):
        a = a_ref[a_rows, a_base + j * WIDE : a_base + (j + 1) * WIDE].astype(F32)
        b = b_ref[b_rows, b_base + j * WIDE : b_base + (j + 1) * WIDE].astype(F32)
        top = (a * b).astype(BF)
        rest = (a * b - top.astype(F32)).astype(BF)
        part = heads[j * WIDE : (j + 1) * WIDE, :]
        term = nn(top, part) + nn(rest, part)
        total = term if total is None else total + term
    return total


def row_in_block(i, size, columns):
    return (i * size + lax.broadcasted_iota(jnp.int32, (size, columns), 0)) % BLOCK


def start(pairs, sems):
    copies = [pltpu.make_async_copy(s, d, sems.at[n]) for n, (s, d) in enumerate(pairs)]
    for copy in copies:
        copy.start()
    return copies


def wait(copies):
    for copy in copies:
        copy.wait()


def piece_views(bufs):
    rows = bufs[2].shape[0]
    return [b.at[k * rows : (k + 1) * rows] for b in bufs for k in range(b.shape[0] // rows)]


def rows_at(place, rows, share=1, k=0):
    return pl.ds(pl.multiple_of((place * share + k) * rows, 16), rows)


def load(bufs, place_ref, w, sems):
    if len(bufs) == 1:
        return start([(bufs[0], w)], sems)
    views = piece_views(bufs)
    rows = views[0].shape[0]
    return start([(v, w.at[rows_at(place_ref[n], rows), :]) for n, v in enumerate(views)], sems)


ORDER = ((3, 0), (1, 0), (3, 1), (2, 1), (1, 1), (2, 0), (0, 0), (0, 1))


def store_pieces(dw, outs, place_ref, sems, share=1):
    if len(outs) == 1:
        return start([(dw, outs[0])], sems)
    half, columns = outs[0].shape[1], dw.shape[1]
    pairs = []
    for side, out in enumerate(outs):
        for n, (chip, top) in enumerate(ORDER):
            place = place_ref[8 + side * 4 + chip]
            for k in range(share):
                source = dw.at[pl.ds(pl.multiple_of(((place * share + k) * 2 + top) * half, 16), half), :]
                pairs.append((source, out.at[n, :, k * columns : (k + 1) * columns]))
    return start(pairs, sems)


def piece_select(piece, rows, columns):
    lane = lax.broadcasted_iota(jnp.int32, (128, columns), 0)
    column = lax.broadcasted_iota(jnp.int32, (128, columns), 1)
    return ((lane < rows) & (column == piece * rows + lane)).astype(BF)


def spread_small(w, small_ref, hb_ref):
    columns = small_ref.shape[1]
    rows = columns // 8
    start = w.shape[1] - 128
    total = jnp.zeros((SMALL, columns), F32)
    for piece in range(8):
        block = w[piece * rows : piece * rows + SMALL, start:]
        total = total + nn(block, piece_select(piece, rows, columns))
        wide = block.astype(F32)
        for r in range(3):
            at = (piece * 3 + r) * 128
            hb_ref[0:1, at : at + 128] = wide[8 + r : 9 + r, :]
    small_ref[...] = total


def gather_small(dw, sums):
    sums_t, sums_s, sums_f, ghb = sums
    columns = sums_t.shape[1]
    rows = columns // 8
    start = dw.shape[1] - 128
    zero = jnp.zeros((3, columns), F32)
    order = [sums_t[0:4, :], sums_s[0:3, :], sums_f[0:1, :], zero, sums_t[4:5, :], sums_s[3:4, :], sums_f[1:2, :]]
    order += [sums_t[5:6, :], sums_s[4:5, :], sums_f[2:3, :], jnp.zeros((SMALL - 17, columns), F32)]
    values = jnp.concatenate(order, axis=0).astype(BF)
    for piece in range(8):
        block = nt(values, piece_select(piece, rows, columns))
        hidden = [ghb[0:1, (piece * 3 + r) * 128 : (piece * 3 + r + 1) * 128] for r in range(3)]
        block = jnp.concatenate([block[0:8, :]] + hidden + [block[11:, :]], axis=0)
        dw[piece * rows : piece * rows + SMALL, start:] = block.astype(BF)
        dw[piece * rows + SMALL : (piece + 1) * rows, start:] = jnp.zeros((rows - SMALL, 128), BF)


def load_feed(bufs, place_ref, we, wr, sems):
    if len(bufs) == 2:
        return start([(bufs[0], we)], sems), start([(bufs[1], wr)], sems.at[8:])
    views = piece_views(bufs)
    rows, units, columns = views[0].shape[0], we.shape[1], wr.shape[1]
    share = units // columns
    first = start([(v.at[:, 0:units], we.at[rows_at(place_ref[n], rows), :]) for n, v in enumerate(views)], sems)
    pairs = []
    for n, v in enumerate(views):
        for k in range(share):
            to = rows_at(place_ref[n], rows, share, k)
            pairs.append((v.at[:, units + k * columns : units + (k + 1) * columns], wr.at[to, :]))
    return first, start(pairs, sems.at[8:])


class Late:
    def __init__(self, source, target, sem):
        self.target = target
        self.copy = pltpu.make_async_copy(source, target, sem)
        self.copy.start()

    def get(self):
        if self.copy is not None:
            self.copy.wait()
            self.copy = None
        return self.target


class Early:
    def __init__(self, ref, target, sem):
        self.ref = ref
        self.copy = pltpu.make_async_copy(ref, target, sem)

    def send(self):
        self.copy.start()


SPACES = {
    "v": pl.BlockSpec(memory_space=pltpu.VMEM),
    "a": pl.BlockSpec(memory_space=pl.ANY),
    "l": pl.BlockSpec(memory_space=pl.ANY),
    "e": pl.BlockSpec(memory_space=pl.ANY),
    "s": pl.BlockSpec(memory_space=pltpu.SMEM),
}


def call(body, operands, spaces, outs, out_spaces, scratch, micros, name):
    late = [n for n, space in enumerate(spaces) if space == "l"]
    early = [n for n, space in enumerate(out_spaces) if space == "e"]
    n_in, n_out, n_scratch = len(operands), len(outs), len(scratch)

    def kernel(*refs):
        ins, refs = list(refs[:n_in]), refs[n_in:]
        results, refs = list(refs[:n_out]), refs[n_out:]
        own, refs = refs[:n_scratch], refs[n_scratch:]
        held, refs = refs[: len(late)], refs[len(late) :]
        filled, refs = refs[: len(early)], refs[len(early) :]
        late_sems, early_sems = refs
        for k, n in enumerate(late):
            ins[n] = Late(ins[n], held[k], late_sems.at[k])
        for k, n in enumerate(early):
            results[n] = Early(filled[k], results[n], early_sems.at[k])
        body(ins, results, own)
        for n in late:
            ins[n].get()
        for n in early:
            results[n].copy.wait()

    more = [pltpu.VMEM(operands[n].shape, operands[n].dtype) for n in late]
    more += [pltpu.VMEM(*outs[n]) for n in early]
    more += [pltpu.SemaphoreType.DMA((max(1, len(late)),)), pltpu.SemaphoreType.DMA((max(1, len(early)),))]
    return pl.pallas_call(
        kernel,
        out_shape=[jax.ShapeDtypeStruct(s, d) for s, d in outs],
        in_specs=[SPACES[space] for space in spaces],
        out_specs=[SPACES[space] for space in out_spaces],
        scratch_shapes=list(scratch) + more,
        compiler_params=pltpu.CompilerParams(vmem_limit_bytes=VMEM_LIMIT),
        cost_estimate=pl.CostEstimate(flops=micros * MICRO, bytes_accessed=0, transcendentals=0),
        name=name,
    )(*operands)


def blocks_of(count):
    return [slice(j * WIDE, (j + 1) * WIDE) for j in range(count // WIDE)]


def shifted(at, base):
    return slice(at.start + base, at.stop + base)


def entry(normed, w, qkv, query_bias, value_bias):
    columns = normed.shape[1]
    for part, bias in enumerate((query_bias, None, value_bias)):
        for at in blocks_of(columns):
            to = shifted(at, part * columns)
            packed = nn(normed[...], w[:, to])
            qkv[:, to] = (packed if bias is None else packed + bias[:, at]).astype(BF)


def time_forward(n, ins, results, own):
    place_ref, x_ref, *rest = ins
    given, bufs = rest[: len(rest) - n], rest[len(rest) - n :]
    nt_out, qkv_out, o_out, e_out, p_out, y_ref, small_ref, hb_ref = results
    w, sems = own
    columns = x_ref.shape[1]
    wait(load(bufs, place_ref, w, sems))
    if given:
        small_ref[...] = given[0][...]
        hb_ref[...] = given[1][...]
    else:
        spread_small(w, small_ref, hb_ref)
    norm_chunks(x_ref, nt_out.ref, small_ref[11:12, :], small_ref[14:15, :])
    nt_out.send()
    qkv_ref, o_ref, e_ref, p_ref = qkv_out.ref, o_out.ref, e_out.ref, p_out.ref
    entry(nt_out.ref, w, qkv_ref, small_ref[0:1, :], small_ref[1:2, :])
    qkv_out.send()
    heads = head_map(columns)
    for clip in range(x_ref.shape[0] // (FRAMES * BLOCK)):
        at = [slice((clip * FRAMES + f) * BLOCK, (clip * FRAMES + f + 1) * BLOCK) for f in range(FRAMES)]
        weights = []
        for f in range(FRAMES):
            s = [head_sums(qkv_ref, at[f], 0, qkv_ref, at[g], columns, heads) * HD ** (-0.5) for g in range(FRAMES)]
            peak = jnp.maximum(s[0], s[1])
            powered = [jnp.exp(score - peak) for score in s]
            inverse = 1.0 / (powered[0] + powered[1])
            for g in range(FRAMES):
                m = (clip * FRAMES + f) * FRAMES + g
                p = powered[g] * inverse
                p_ref[m * BLOCK : (m + 1) * BLOCK, :] = p
                weights.append(p.astype(BF))
        for to in blocks_of(columns):
            v = [qkv_ref[a, shifted(to, 2 * columns)].astype(F32) for a in at]
            for f in range(FRAMES):
                spread = [nt(weights[FRAMES * f + g], heads[to, :]) for g in range(FRAMES)]
                o_ref[at[f], to] = (spread[0] * v[0] + spread[1] * v[1]).astype(BF)
    p_out.send()
    o_out.send()
    for at in blocks_of(columns):
        e_ref[:, at] = (nn(o_ref[...], w[:, shifted(at, 3 * columns)]) + small_ref[2:3, at]).astype(BF)
    e_out.send()
    patch = row_in_block(0, x_ref.shape[0], WIDE) < PLACES
    for at in blocks_of(columns):
        branch = nn(e_ref[...], w[:, shifted(at, 4 * columns)]) + small_ref[3:4, at]
        y_ref[:, at] = x_ref[:, at].astype(F32) + jnp.where(patch, branch, 0.0)


def half_masks():
    lane = lax.broadcasted_iota(jnp.int32, (1, 128), 1)
    return (lane < HD).astype(BF), (lane >= HD).astype(BF)


def space_forward(n, ins, results, own):
    place_ref, y_ref, small_ref, *bufs = ins
    ns_out, qkv_out, p_out, o_out, z_ref = results
    w, sems = own
    columns = y_ref.shape[1]
    blocks = y_ref.shape[0] // BLOCK
    pairs = columns // 128
    copies = load(bufs, place_ref, w, sems)
    norm_chunks(y_ref, ns_out.ref, small_ref[12:13, :], small_ref[15:16, :])
    ns_out.send()
    wait(copies)
    qkv_ref, p_ref, o_ref = qkv_out.ref, p_out.ref, o_out.ref
    entry(ns_out.ref, w, qkv_ref, small_ref[4:5, :], small_ref[5:6, :])
    qkv_out.send()
    masks = half_masks()
    first = lax.broadcasted_iota(jnp.int32, (BLOCK, 128), 1) < HD
    column = lax.broadcasted_iota(jnp.int32, (1, BLOCK), 1)
    hidden = jnp.where(column <= PLACES, 0.0, -1e30)

    def attend(block):
        at = rows_of(block, BLOCK)
        columns_of = [[slice(part * columns + k * 128, part * columns + (k + 1) * 128) for k in range(pairs)] for part in range(3)]
        scores = []
        for k in range(pairs):
            query, key = qkv_ref[at, columns_of[0][k]], qkv_ref[at, columns_of[1][k]]
            scores += [nt(query * mask, key) * HD ** (-0.5) + hidden for mask in masks]
        powered = [jnp.exp(s - jnp.max(s, axis=-1, keepdims=True)) for s in scores]
        weights = [(e * (1.0 / jnp.sum(e, axis=-1, keepdims=True))).astype(BF) for e in powered]
        for k in range(pairs):
            value = qkv_ref[at, columns_of[2][k]]
            for half in range(2):
                p_ref[(block * pairs + k) * 2 + half] = weights[2 * k + half]
            mixed = jnp.where(first, nn(weights[2 * k], value), nn(weights[2 * k + 1], value))
            o_ref[at, columns_of[0][k]] = mixed.astype(BF)

    loop(blocks, attend)
    p_out.send()
    o_out.send()
    is_class = lax.broadcasted_iota(jnp.int32, (BLOCK - EDGE, WIDE), 0) == CLASS
    for at in blocks_of(columns):
        branch = nn(o_ref[...], w[:, shifted(at, 3 * columns)]) + small_ref[6:7, at]
        z_ref[:, at] = y_ref[:, at] + branch
        for clip in range(blocks // FRAMES):
            edges = [slice((clip * FRAMES + f) * BLOCK + EDGE, (clip * FRAMES + f + 1) * BLOCK) for f in range(FRAMES)]
            mean = (branch[edges[0], :] + branch[edges[1], :]) * (1.0 / FRAMES)
            for edge in edges:
                z_ref[edge, at] = y_ref[edge, at] + jnp.where(is_class, mean, branch[edge, :])


def gelu_both(h):
    cdf = 0.5 * (1.0 + lax.erf(h * 0.5**0.5))
    density = jnp.exp(h * h * -0.5) * 0.3989422804014327
    return h * cdf, cdf + h * density


def feed(ins, results, own):
    place_ref, z_ref, g_ref, small_ref, hb_ref, *bufs = ins
    out_ref, gh_out, sums_ref, ghb_ref, dwr_out, *outs = results
    we, wr, dwe, nm, a, sems, out_sems = own
    gh, dwr = gh_out.ref, dwr_out.ref
    columns = z_ref.shape[1]
    units = we.shape[1]
    copies, more = load_feed(bufs, place_ref, we, wr, sems)
    norm_chunks(z_ref, nm, small_ref[13:14, :], small_ref[16:17, :])
    wait(copies + more)

    def inner(j):
        at = cols_of(j, WIDE)
        h = nn(nm[...], we[:, at]) + hb_ref[0:1, at]
        active, slope = gelu_both(h)
        a[:, at] = active.astype(BF)
        gh[:, at] = (nt(g_ref[...], wr[rows_of(j, WIDE), :]) * slope).astype(BF)

    loop(units // WIDE, inner)
    gh_out.send()

    def left(j):
        dwr[rows_of(j, WIDE), :] = tn(a[:, cols_of(j, WIDE)], g_ref[...]).astype(BF)

    loop(units // WIDE, left)
    dwr_out.send()

    def right(j):
        at = cols_of(j, WIDE)
        block = gh[:, at]
        dwe[:, at] = tn(nm[...], block).astype(BF)
        ghb_ref[0:1, at] = jnp.sum(block.astype(F32), axis=0, keepdims=True)

    loop(units // WIDE, right)
    copies = store_pieces(dwe, outs, place_ref, out_sems)
    for at in blocks_of(columns):
        out_ref[:, at] = (z_ref[:, at] + (nn(a[...], wr[:, at]) + small_ref[7:8, at])).astype(BF)
    sums_ref[0:1, :] = column_sums(g_ref, 0, columns)
    wait(copies)


def norm_backward(row, n, ins, results, own):
    place_ref, gh_ref, x_in, base_in, small_ref, *bufs = ins
    gz_ref, sums_ref = results
    w, gn, sems = own
    columns = gz_ref.shape[1]
    views = [b.at[:, 0 : w.shape[1]] for b in bufs]
    wait(load(views, place_ref, w, sems))
    for at in blocks_of(columns):
        gn[:, at] = nt(gh_ref[...], w[at, :])
    x_ref, base = x_in.get(), base_in.get()

    def store(at, value):
        gz_ref[at, :] = value

    gain_sum, shift_sum = norm_back_chunks(
        gn, x_ref, small_ref[row : row + 1, :], lambda at: base[at, :].astype(F32), store
    )
    sums_ref[0:1, :] = gain_sum
    sums_ref[1:2, :] = shift_sum


def space_backward(n, ins, results, own):
    place_ref, gz_ref, ns_in, qkv_in, p_in, o_in, *rest = ins
    bufs = rest[:n]
    gqkv_out, sums_ref, *outs = results
    w, dw_ref, gbs, go, sems, out_sems = own
    columns = gz_ref.shape[1]
    rows = gz_ref.shape[0]
    clips = rows // (BLOCK * FRAMES)
    pairs = columns // 128
    copies = load([b.at[:, 3 * columns : 4 * columns] for b in bufs], place_ref, w, sems)

    def lower(i):
        at = rows_of(i, CHUNK)
        gbs[at, :] = gz_ref[at, :].astype(BF)

    loop(rows // CHUNK, lower)
    is_class = lax.broadcasted_iota(jnp.int32, (BLOCK - EDGE, columns), 0) == CLASS
    for clip in range(clips):
        edges = [slice((clip * FRAMES + f) * BLOCK + EDGE, (clip * FRAMES + f + 1) * BLOCK) for f in range(FRAMES)]
        share = gz_ref[edges[0], :] * (1.0 / FRAMES)
        for edge in edges:
            gbs[edge, :] = jnp.where(is_class, share, gz_ref[edge, :]).astype(BF)
    wait(copies)
    for at in blocks_of(columns):
        go[:, at] = nt(gbs[...], w[at, :]).astype(BF)
    o_ref, qkv_ref, p_ref, gqkv = o_in.get(), qkv_in.get(), p_in.get(), gqkv_out.ref
    for at in blocks_of(columns):
        dw_ref[:, shifted(at, 3 * columns)] = tn(o_ref[...], gbs[:, at]).astype(BF)
    masks = half_masks()
    first = lax.broadcasted_iota(jnp.int32, (BLOCK, 128), 1) < HD
    class_row = lax.broadcasted_iota(jnp.int32, (BLOCK - EDGE, 128), 0) == CLASS
    together = 2

    def attend(step):
        parts = []
        for u in range(together):
            clip, pair = (step * together + u) // pairs, (step * together + u) % pairs
            for f in range(FRAMES):
                block = clip * FRAMES + f
                at = rows_of(block, BLOCK)
                q, k, v = (qkv_ref[at, cols_of(pair, 128, part * columns)] for part in range(3))
                grad = go[at, cols_of(pair, 128)]
                parts += [(q, k, v, grad, mask, p_ref[2 * (block * pairs + pair) + half]) for half, mask in enumerate(masks)]
        gp = [nt(grad * mask, v) for _, _, v, grad, mask, _ in parts]
        p = [part[5].astype(F32) for part in parts]
        shared = [jnp.sum(a * b, axis=-1, keepdims=True) for a, b in zip(gp, p)]
        gs = [(b * (a - c)).astype(BF) for a, b, c in zip(gp, p, shared)]
        scale = HD ** (-0.5)
        gq = [nn(a, part[1]) * scale for a, part in zip(gs, parts)]
        gv = [tn(part[5], part[3]) for part in parts]
        gk = [tn(a, part[0]) * scale for a, part in zip(gs, parts)]
        for u in range(together):
            clip, pair = (step * together + u) // pairs, (step * together + u) % pairs
            for part, values in enumerate((gq, gk, gv)):
                to = cols_of(pair, 128, part * columns)
                one, two = (jnp.where(first, values[4 * u + 2 * f], values[4 * u + 2 * f + 1]) for f in range(FRAMES))
                top = pl.multiple_of(clip * FRAMES * BLOCK, 16)
                gqkv[pl.ds(top, EDGE), to] = one[:EDGE].astype(BF)
                gqkv[pl.ds(top + BLOCK, EDGE), to] = two[:EDGE].astype(BF)
                both = jnp.where(class_row, one[EDGE:] + two[EDGE:], one[EDGE:])
                gqkv[pl.ds(top + EDGE, BLOCK - EDGE), to] = both.astype(BF)
                rest = jnp.where(class_row, 0.0, two[EDGE:])
                gqkv[pl.ds(top + BLOCK + EDGE, BLOCK - EDGE), to] = rest.astype(BF)

    loop(clips * pairs // together, attend)
    gqkv_out.send()
    ns_ref = ns_in.get()
    for at in blocks_of(3 * columns):
        dw_ref[:, at] = tn(ns_ref[...], gqkv[:, at]).astype(BF)
    copies = store_pieces(dw_ref, outs, place_ref, out_sems)
    sums_ref[0:1, :] = column_sums(gqkv, 0, columns)
    sums_ref[1:2, :] = column_sums(gqkv, 2 * columns, columns)
    sums_ref[2:3, :] = column_sums(gbs, 0, columns)
    wait(copies)


def time_backward(n, ins, results, own):
    place_ref, gy_ref, x_in, nt_in, qkv_in, p_in, o_in, e_in, small_ref, *others = ins
    others, bufs = others[: len(others) - n], others[len(others) - n :]
    gx_ref, sums_ref, *outs = results
    w, dw_ref, grt, get, go, gqkv, gn, sems, out_sems = own
    columns = gy_ref.shape[1]
    rows = gy_ref.shape[0]
    copies = load(bufs, place_ref, w, sems)

    def lower(i):
        at = rows_of(i, CHUNK)
        patch = row_in_block(i, CHUNK, columns) < PLACES
        grt[at, :] = jnp.where(patch, gy_ref[at, :], 0.0).astype(BF)

    loop(rows // CHUNK, lower)
    wait(copies)
    for at in blocks_of(columns):
        get[:, at] = nt(grt[...], w[at, 4 * columns : 5 * columns]).astype(BF)
    for at in blocks_of(columns):
        go[:, at] = nt(get[...], w[at, 3 * columns : 4 * columns]).astype(BF)
    e_ref, o_ref = e_in.get(), o_in.get()
    for at in blocks_of(columns):
        dw_ref[:, shifted(at, 4 * columns)] = tn(e_ref[...], grt[:, at]).astype(BF)
    for at in blocks_of(columns):
        dw_ref[:, shifted(at, 3 * columns)] = tn(o_ref[...], get[:, at]).astype(BF)
    qkv_ref, p_ref = qkv_in.get(), p_in.get()
    heads = head_map(columns)
    for clip in range(rows // (FRAMES * BLOCK)):
        at = [slice((clip * FRAMES + f) * BLOCK, (clip * FRAMES + f + 1) * BLOCK) for f in range(FRAMES)]
        gs, kept = [], []
        for f in range(FRAMES):
            gp = [head_sums(go, at[f], 0, qkv_ref, at[g], 2 * columns, heads) for g in range(FRAMES)]
            first = ((clip * FRAMES + f) * FRAMES) * BLOCK
            p = [p_ref[first + g * BLOCK : first + (g + 1) * BLOCK, :] for g in range(FRAMES)]
            shared = gp[0] * p[0] + gp[1] * p[1]
            gs += [(p[g] * (gp[g] - shared)).astype(BF) for g in range(FRAMES)]
            kept += [p[g].astype(BF) for g in range(FRAMES)]
        for block in blocks_of(columns):
            to = [shifted(block, part * columns) for part in range(3)]
            q, k = ([qkv_ref[a, to[part]].astype(F32) for a in at] for part in range(2))
            grad = [go[a, block].astype(F32) for a in at]
            scaled = heads[block, :] * BF(HD ** (-0.5))
            spread = [nt(value, scaled) for value in gs]
            for f in range(FRAMES):
                gqkv[at[f], to[0]] = (spread[2 * f] * k[0] + spread[2 * f + 1] * k[1]).astype(BF)
                gqkv[at[f], to[1]] = (spread[f] * q[0] + spread[2 + f] * q[1]).astype(BF)
            spread = [nt(value, heads[block, :]) for value in kept]
            for f in range(FRAMES):
                gqkv[at[f], to[2]] = (spread[f] * grad[0] + spread[2 + f] * grad[1]).astype(BF)
    nt_ref = nt_in.get()
    for at in blocks_of(3 * columns):
        dw_ref[:, at] = tn(nt_ref[...], gqkv[:, at]).astype(BF)
    main = slice(0, 5 * columns)
    copies = store_pieces(dw_ref.at[:, main], [out.at[..., main] for out in outs], place_ref, out_sems)
    for at in blocks_of(columns):
        gn[:, at] = nt(gqkv[...], w[at, 0 : 3 * columns])
    x_ref = x_in.get()

    def store(at, value):
        gx_ref[at, :] = value.astype(BF)

    gain_sum, shift_sum = norm_back_chunks(gn, x_ref, small_ref[11:12, :], lambda at: gy_ref[at, :], store)
    sums_ref[0:1, :] = column_sums(gqkv, 0, columns)
    sums_ref[1:2, :] = column_sums(gqkv, 2 * columns, columns)
    sums_ref[2:3, :] = column_sums(get, 0, columns)
    sums_ref[3:4, :] = column_sums(grt, 0, columns)
    sums_ref[4:5, :] = gain_sum
    sums_ref[5:6, :] = shift_sum
    wait(copies)
    if others:
        gather_small(dw_ref, (sums_ref, *others))
        last = slice(5 * columns, 5 * columns + 128)
        wait(store_pieces(dw_ref.at[:, last], [out.at[..., last] for out in outs], place_ref, out_sems))


def pack_rows(tokens, once):
    clips, _, columns = tokens.shape
    frames = []
    for f in range(FRAMES):
        places = tokens[:, 1 + f * PLACES : 1 + (f + 1) * PLACES]
        head = tokens[:, :1] if f == 0 or not once else jnp.zeros_like(tokens[:, :1])
        frames.append(jnp.concatenate([places, head, jnp.zeros((clips, BLOCK - PLACES - 1, columns), tokens.dtype)], axis=1))
    return jnp.stack(frames, axis=1).reshape(clips * FRAMES * BLOCK, columns)


def unpack_rows(rows, clips):
    framed = rows.reshape(clips, FRAMES, BLOCK, rows.shape[-1])
    return jnp.concatenate(
        [framed[:, 0, PLACES : PLACES + 1]] + [framed[:, f, :PLACES] for f in range(FRAMES)], axis=1
    )


class Layer:
    def __init__(self, rows, columns, units, shards, pieced, place):
        self.rows, self.columns, self.units = rows, columns, units
        self.pieced, self.place = pieced, place
        self.piece = columns // shards
        self.act = ((rows, columns), BF)
        self.act3 = ((rows, 3 * columns), BF)
        self.tall = ((rows, units), BF)
        self.wide = ((rows, columns), F32)
        self.sums = ((8, columns), F32)

    def grads(self, width):
        if self.pieced:
            return [((8, self.piece // 2, width), BF)] * 2
        return [((self.columns, width), BF)]

    def vmem(self, *shapes):
        return [pltpu.VMEM(s, d) for s, d in shapes]

    def sems(self, *counts):
        return [pltpu.SemaphoreType.DMA((count,)) for count in counts]

    def time_forward(self, x, given, bufs):
        c, n = self.columns, len(bufs)
        extra = [((SMALL, c), F32), ((8, self.units), F32)]
        return call(
            functools.partial(time_forward, n), (self.place, x, *given, *bufs), "sv" + "v" * len(given) + "a" * n,
            [self.act, self.act3, self.act, self.act, ((self.rows * FRAMES, 128), F32), self.wide] + extra, "eeeeevvv",
            self.vmem(((c, bufs[0].shape[1]), BF)) + self.sems(8), 14, "time_forward",
        )

    def space_forward(self, y, small, bufs):
        c, n = self.columns, len(bufs)
        probs = ((self.rows // BLOCK * (c // 128) * 2, BLOCK, BLOCK), BF)
        return call(
            functools.partial(space_forward, n), (self.place, y, small, *bufs), "svv" + "a" * n,
            [self.act, self.act3, probs, self.act, self.wide], "eeeev",
            self.vmem(((c, 4 * c), BF)) + self.sems(8), 16, "space_forward",
        )

    def feed(self, z, g, small, hb, bufs):
        c, u, n = self.columns, self.units, len(bufs)
        outs = self.grads(u)
        return call(
            feed, (self.place, z, g, small, hb, *bufs), "svvvv" + "a" * n,
            [self.act, self.tall, self.sums, ((8, u), F32), ((u, c), BF)] + outs, "vevve" + "a" * len(outs),
            self.vmem(((c, u), BF), ((u, c), BF), ((c, u), BF), self.act, self.tall) + self.sems(40, 16), 38, "feed",
        )

    def norm_backward(self, row, gh, x, base, small, bufs, name):
        c, n, wide = self.columns, len(bufs), gh.shape[1]
        return call(
            functools.partial(norm_backward, row, n), (self.place, gh, x, base, small, *bufs), "svllv" + "a" * n,
            [self.wide, self.sums], "vv", self.vmem(((c, wide), BF), self.wide) + self.sems(8), 10, name,
        )

    def space_backward(self, gz, normed, qkv, p, o, bufs):
        c, n = self.columns, len(bufs)
        outs = self.grads(4 * c)
        return call(
            functools.partial(space_backward, n), (self.place, gz, normed, qkv, p, o, *bufs), "svllll" + "a" * n,
            [self.act3, self.sums] + outs, "ev" + "a" * len(outs),
            self.vmem(((c, c), BF), ((c, 4 * c), BF), self.act, self.act) + self.sems(8, 16), 20, "space_backward",
        )

    def time_backward(self, gy, x, normed, qkv, p, o, e, small, others, bufs):
        c, n = self.columns, len(bufs)
        width = bufs[0].shape[1]
        outs = self.grads(width)
        return call(
            functools.partial(time_backward, n), (self.place, gy, x, normed, qkv, p, o, e, small, *others, *bufs),
            "svllllllv" + "v" * len(others) + "a" * n, [self.act, self.sums] + outs, "vv" + "a" * len(outs),
            self.vmem(((c, width), BF), ((c, width), BF), self.act, self.act, self.act, self.act3, self.wide) + self.sems(8, 16),
            24, "time_backward",
        )


BOTH = ("grp", "shard")


def permute(value, target):
    shards = lax.axis_size("shard")
    pairs = [(z * shards + s, z * shards + target(s)) for z in range(lax.axis_size("grp")) for s in range(shards)]
    return lax.ppermute(value, BOTH, pairs)


def to_sibling(value):
    return permute(value, lambda s: s ^ 1)


def along_x(value):
    return permute(value, lambda s: s ^ 2)


def along_y(value):
    return permute(value, lambda s: s ^ 4)


def gather_start(own):
    return jnp.concatenate([own, to_sibling(own)], axis=0)


def gather_hop(both):
    return permute(both, lambda s: s ^ (2 if s % 2 == 0 else 4))


def gather_second(hop):
    return permute(hop[: hop.shape[0] // 2], lambda s: s ^ (4 if s % 2 == 0 else 2))


def places(s):
    near = jnp.where(s % 2 == 0, 2, 4)
    far = 6 - near
    gathered = [s, s ^ 1, s ^ near, s ^ near ^ 1, s ^ 6, s ^ 1 ^ far, s ^ far, s ^ 7]
    kept = [s, s ^ 2, s ^ 4, s ^ 6]
    return jnp.stack(gathered + kept + [k ^ 1 for k in kept]).astype(jnp.int32)


def total(*terms):
    return sum(t.astype(F32) for t in terms).astype(BF)


class Reduction:
    def __init__(self, keep, give):
        self.keep = keep
        self.got = to_sibling(give)

    def own(self, start, stop):
        return self.keep[start:stop], self.got[start:stop]

    def first(self):
        return total(*self.own(0, 2)), total(*self.own(2, 4))

    def cross(self, sent):
        self.from_x, self.from_y = along_x(sent[0]), along_y(sent[1])

    def second(self):
        return total(*self.own(4, 5), self.from_y[:1]), total(*self.own(5, 6), self.from_x[:1])

    def cross_again(self, sent):
        self.last_x, self.last_y = along_x(sent[0]), along_y(sent[1])

    def finish(self):
        top = total(*self.own(6, 7), self.from_x[1:], self.last_y)
        bottom = total(*self.own(7, 8), self.from_y[1:], self.last_x)
        return top[0], bottom[0]


def tie(*values):
    leaves, shape = jax.tree.flatten(values)
    return jax.tree.unflatten(shape, lax.optimization_barrier(tuple(leaves)))


def swap_z(value):
    shards = lax.axis_size("shard")
    pairs = [(z * shards + s, (z ^ 1) * shards + s) for z in range(lax.axis_size("grp")) for s in range(shards)]
    return lax.ppermute(value, BOTH, pairs)


def sum_groups(halves, even):
    top, bottom = halves
    held = total(jnp.where(even, top, bottom), swap_z(jnp.where(even, bottom, top)))
    held = total(held, lax.ppermute(held, "grp", [(z, z ^ 2) for z in range(4)]))
    other = swap_z(held)
    return jnp.concatenate([jnp.where(even, held, other), jnp.where(even, other, held)], axis=0)


def local(video, cotangent, live, time_entry, time_exit, time_mixer, space_entry, space_exit, hidden_expand, hidden_reduce, bias_rows, hidden_bias, norm_gain, norm_shift):
    clips, _, tokens, columns = video.shape
    shards, groups = lax.axis_size("shard"), lax.axis_size("grp")
    mine = lax.axis_index("shard")
    part = columns // shards
    units = hidden_bias.shape[0] * shards
    share = units // columns
    pieced = shards == 8 and groups == 4

    def gather(value):
        return lax.all_gather(value, "shard", axis=0, tiled=True)

    flags = live.astype(BF)[:, :, None]
    x = pack_rows(video[:, 0], False)
    g = pack_rows(cotangent[:, 0] * flags, True)
    own_t = jnp.concatenate([time_entry, time_exit, time_mixer], axis=1)
    own_s = jnp.concatenate([space_entry, space_exit], axis=1)
    if pieced:
        narrow = jnp.concatenate([norm_gain, norm_shift], axis=0)
        narrow = jnp.concatenate(
            [jnp.pad(bias_rows, ((0, 0), (0, 128 - part))), hidden_bias.reshape(-1, 128), jnp.pad(narrow, ((0, 0), (0, 128 - part)))], axis=0
        )
        own_t = jnp.concatenate([own_t, jnp.pad(narrow, ((0, part - narrow.shape[0]), (0, 0)))], axis=1)
        own_f = jnp.concatenate([hidden_expand] + [hidden_reduce[k * part : (k + 1) * part] for k in range(share)], axis=1)
        net = Layer(x.shape[0], columns, units, shards, pieced, places(mine))
        both_t = gather_start(own_t)
        both_s, both_f = gather_start(own_s), gather_start(own_f)
        hop_t, both_s, both_f, x, g = tie(gather_hop(both_t), both_s, both_f, x, g)
        second_t, both_s, both_f = tie(gather_second(hop_t), both_s, both_f)
        wt = (both_t, hop_t, second_t, to_sibling(hop_t), to_sibling(second_t))
        hop_s = gather_hop(both_s)
        normed_t, qkv_t, o_t, e_t, p_t, y, small, hb = net.time_forward(x, (), wt)
        hop_s, y, both_f = tie(hop_s, y, both_f)
        second_s = gather_second(hop_s)
        hop_f = gather_hop(both_f)
        ws = (both_s, hop_s, second_s, to_sibling(hop_s), to_sibling(second_s))
        normed_s, qkv_s, p_s, o_s, z = net.space_forward(y, small, ws)
        hop_f, z = tie(hop_f, z)
        second_f = gather_second(hop_f)
        wf = (both_f, hop_f, second_f, to_sibling(hop_f), to_sibling(second_f))
    else:
        net = Layer(x.shape[0], columns, units, shards, pieced, jnp.zeros((16,), jnp.int32))
        packed = jnp.concatenate([bias_rows, norm_gain, norm_shift], axis=0)
        spread = lax.all_gather(packed, "shard", axis=0).transpose(1, 0, 2).reshape(-1, columns).astype(F32)
        small = jnp.concatenate([spread[:8], jnp.zeros((3, columns), F32), spread[8:], jnp.zeros((SMALL - 17, columns), F32)], axis=0)
        given = (small, jnp.pad(gather(hidden_bias).astype(F32)[None], ((0, 7), (0, 0))))
        wt, ws, wf = (gather(own_t),), (gather(own_s),), (gather(hidden_expand), gather(hidden_reduce))
        normed_t, qkv_t, o_t, e_t, p_t, y, small, hb = net.time_forward(x, given, wt)
        normed_s, qkv_s, p_s, o_s, z = net.space_forward(y, small, ws)

    out, gh, sums_f, ghb, grad_r, *grad_e = net.feed(z, g, small, hb, wf)
    gz, norm_f = net.norm_backward(13, gh, z, g, small, wf if pieced else wf[:1], "feed_norm")
    if pieced:
        sum_e = Reduction(*grad_e)
        sent_e, gz = tie(sum_e.first(), gz)
        sum_e.cross(sent_e)
    gqkv, sums_s, *grad_s = net.space_backward(gz, normed_s, qkv_s, p_s, o_s, ws)
    if pieced:
        sum_s = Reduction(*grad_s)
        sent_e, gqkv = tie(sum_e.second(), gqkv)
        sum_e.cross_again(sent_e)
    gy, norm_s = net.norm_backward(12, gqkv, y, gz, small, ws, "space_norm")
    if pieced:
        kept_e, sent_s, gy = tie(sum_e.finish(), sum_s.first(), gy)
        sum_s.cross(sent_s)
        sums_s = jnp.concatenate([sums_s[0:3], norm_s[0:2], sums_s[5:]], axis=0)
        sums_f = jnp.concatenate([sums_f[0:1], norm_f[0:2], sums_f[3:]], axis=0)
    others = (sums_s, sums_f, ghb) if pieced else ()
    gx, sums_t, *grad_t = net.time_backward(gy, x, normed_t, qkv_t, p_t, o_t, e_t, small, others, wt)

    if pieced:
        even = lax.axis_index("grp") % 2 == 0
        kept_r = lax.psum_scatter(grad_r, "shard", scatter_dimension=0, tiled=True)
        re, rr = lax.psum((jnp.concatenate(kept_e, axis=0), kept_r), "grp")
        sum_t = Reduction(*grad_t)
        _, gx = tie(kept_r, gx)
        sent_s, sent_t = tie(sum_s.second(), sum_t.first())
        sum_s.cross_again(sent_s)
        sum_t.cross(sent_t)
        kept_s, sent_t = tie(sum_s.finish(), sum_t.second())
        sum_t.cross_again(sent_t)
        rs = sum_groups(kept_s, even).astype(F32)
        rt = sum_groups(sum_t.finish(), even)
        re, rr, rt = (v.astype(F32) for v in tie(re, rr, rt))
        narrow = rt[:, 5 * columns :]
        biases, rows_hidden = narrow[0:8, :part], narrow[8:11].reshape(-1)
        gains, shifts = narrow[11:14, :part], narrow[14:17, :part]
    else:
        re, rr, rs, rt = (
            lax.psum(lax.psum_scatter(v, "shard", scatter_dimension=0, tiled=True), "grp").astype(F32)
            for v in (*grad_e, grad_r, *grad_s, *grad_t)
        )
        rows = [sums_t[0:4], sums_s[0:3], sums_f[0:1], sums_t[4:5], norm_s[0:1], norm_f[0:1], sums_t[5:6], norm_s[1:2], norm_f[1:2]]
        cut = lax.dynamic_slice_in_dim(lax.psum(jnp.concatenate(rows, axis=0), BOTH), mine * part, part, axis=1)
        biases, gains, shifts = cut[0:8], cut[8:11], cut[11:14]
        rows_hidden = lax.dynamic_slice_in_dim(lax.psum(ghb[0], BOTH), mine * hidden_bias.shape[0], hidden_bias.shape[0])
    return (
        (unpack_rows(out, clips) * flags)[:, None],
        unpack_rows(gx, clips)[:, None],
        rt[:, : 3 * columns],
        rt[:, 3 * columns : 4 * columns],
        rt[:, 4 * columns : 5 * columns],
        rs[:, : 3 * columns],
        rs[:, 3 * columns :],
        re,
        rr,
        biases,
        rows_hidden,
        gains,
        shifts,
    )


def solution(mesh):
    clips = P(None, ("grp", "shard"), None, None)
    rows = P("shard", None)
    cols = P(None, "shard")
    return jax.shard_map(
        local,
        mesh=mesh,
        in_specs=(clips, clips, P(None, ("grp", "shard"))) + (rows,) * 7 + (cols, P("shard"), cols, cols),
        out_specs=(clips, clips) + (rows,) * 7 + (cols, P("shard"), cols, cols),
        check_vma=False,
    )
```

```python
import functools
import math

import jax
import jax.numpy as jnp
from jax import lax
from jax.experimental import pallas as pl
from jax.experimental.pallas import tpu as pltpu
from jax.sharding import PartitionSpec as P

FRAMES = 2
PLACES = 196
HD = 64
EPSILON = 1e-06
BLOCK = 208
EDGE = 192
CLASS = PLACES - EDGE
CHUNK = 2 * BLOCK
WIDE = 256
BF = jnp.bfloat16
F32 = jnp.float32
SMALL = 32
MICRO = 4_000_000_000
SPARE = 12 * 1024 * 1024
VMEM_LIMIT = 60 * 1024 * 1024


def nn(a, b):
    return lax.dot_general(a, b, (((1,), (0,)), ((), ())), preferred_element_type=F32)


def nt(a, b):
    return lax.dot_general(a, b, (((1,), (1,)), ((), ())), preferred_element_type=F32)


def tn(a, b):
    return lax.dot_general(a, b, (((0,), (0,)), ((), ())), preferred_element_type=F32)


def loop(count, body):
    for i in range(count):
        body(i)


def rows_of(i, size):
    return slice(i * size, (i + 1) * size)


def cols_of(i, size, base=0):
    return slice(base + i * size, base + (i + 1) * size)


def unit(x):
    center = x - jnp.mean(x, axis=-1, keepdims=True)
    factor = lax.rsqrt(jnp.mean(center * center, axis=-1, keepdims=True) + EPSILON)
    return center * factor, factor


def norm_chunks(src, dst, gain, shift):
    def body(i):
        at = rows_of(i, CHUNK)
        w, _ = unit(src[at, :].astype(F32))
        dst[at, :] = (w * gain + shift).astype(BF)

    loop(src.shape[0] // CHUNK, body)


def fold(x):
    return jnp.sum(x.reshape(x.shape[0] // 8, 8, x.shape[1]), axis=0)


def norm_back_chunks(gn_ref, x_ref, gain, base_of, store):
    columns = x_ref.shape[1]

    def body(i, carry):
        gain_sum, shift_sum = carry
        at = rows_of(i, CHUNK)
        gn = gn_ref[at, :]
        w, factor = unit(x_ref[at, :].astype(F32))
        scaled = gn * gain
        plain = jnp.mean(scaled, axis=-1, keepdims=True)
        cross = jnp.mean(scaled * w, axis=-1, keepdims=True)
        store(at, base_of(at) + factor * (scaled - plain - w * cross))
        return gain_sum + fold(gn * w), shift_sum + fold(gn)

    zero = jnp.zeros((8, columns), F32)
    gain_sum, shift_sum = zero, zero
    for i in range(x_ref.shape[0] // CHUNK):
        gain_sum, shift_sum = body(i, (gain_sum, shift_sum))
    return jnp.sum(gain_sum, axis=0, keepdims=True), jnp.sum(shift_sum, axis=0, keepdims=True)


def column_sums(ref, start, size):
    def body(i, total):
        return total + fold(ref[rows_of(i, CHUNK), start : start + size].astype(F32))

    total = jnp.zeros((8, size), F32)
    for i in range(ref.shape[0] // CHUNK):
        total = body(i, total)
    return jnp.sum(total, axis=0, keepdims=True)


def head_map(columns):
    feature = lax.broadcasted_iota(jnp.int32, (columns, 128), 0) // HD
    head = lax.broadcasted_iota(jnp.int32, (columns, 128), 1)
    return (feature == head).astype(BF)


def head_sums(a_ref, a_rows, a_base, b_ref, b_rows, b_base, heads):
    total = None
    for j in range(heads.shape[0] // WIDE):
        a = a_ref[a_rows, a_base + j * WIDE : a_base + (j + 1) * WIDE].astype(F32)
        b = b_ref[b_rows, b_base + j * WIDE : b_base + (j + 1) * WIDE].astype(F32)
        top = (a * b).astype(BF)
        rest = (a * b - top.astype(F32)).astype(BF)
        part = heads[j * WIDE : (j + 1) * WIDE, :]
        term = nn(top, part) + nn(rest, part)
        total = term if total is None else total + term
    return total


def row_in_block(i, size, columns):
    return (i * size + lax.broadcasted_iota(jnp.int32, (size, columns), 0)) % BLOCK


def start(pairs, sems):
    copies = [pltpu.make_async_copy(s, d, sems.at[n]) for n, (s, d) in enumerate(pairs)]
    for copy in copies:
        copy.start()
    return copies


def wait(copies):
    for copy in copies:
        copy.wait()


def piece_views(bufs):
    rows = bufs[2].shape[0]
    return [b.at[k * rows : (k + 1) * rows] for b in bufs for k in range(b.shape[0] // rows)]


def rows_at(place, rows, share=1, k=0):
    return pl.ds(pl.multiple_of((place * share + k) * rows, 16), rows)


def load(bufs, place_ref, w, sems):
    if len(bufs) == 1:
        return start([(bufs[0], w)], sems)
    views = piece_views(bufs)
    rows = views[0].shape[0]
    return start([(v, w.at[rows_at(place_ref[n], rows), :]) for n, v in enumerate(views)], sems)


ORDER = ((3, 0), (1, 0), (3, 1), (2, 1), (1, 1), (2, 0), (0, 0), (0, 1))


def store_pieces(dw, outs, place_ref, sems, share=1, base=0):
    if len(outs) == 1:
        return start([(dw, outs[0])], sems)
    half, columns = outs[0].shape[1], dw.shape[1]
    pairs = []
    for side, out in enumerate(outs):
        for n, (chip, top) in enumerate(ORDER):
            place = place_ref[8 + side * 4 + chip]
            for k in range(share):
                source = dw.at[pl.ds(pl.multiple_of(((place * share + k) * 2 + top) * half, 16), half), :]
                pairs.append((source, out.at[n, :, base + k * columns : base + (k + 1) * columns]))
    return start(pairs, sems)


def piece_select(piece, rows, columns):
    lane = lax.broadcasted_iota(jnp.int32, (128, columns), 0)
    column = lax.broadcasted_iota(jnp.int32, (128, columns), 1)
    return ((lane < rows) & (column == piece * rows + lane)).astype(BF)


def spread_small(w, small_ref, hb_ref):
    columns = small_ref.shape[1]
    rows = columns // 8
    start = w.shape[1] - 128
    total = jnp.zeros((SMALL, columns), F32)
    for piece in range(8):
        block = w[piece * rows : piece * rows + SMALL, start:]
        total = total + nn(block, piece_select(piece, rows, columns))
        wide = block.astype(F32)
        for r in range(3):
            at = (piece * 3 + r) * 128
            hb_ref[0:1, at : at + 128] = wide[8 + r : 9 + r, :]
    small_ref[...] = total


def gather_small(dw, sums):
    sums_t, sums_s, sums_f, ghb = sums
    columns = sums_t.shape[1]
    rows = columns // 8
    start = dw.shape[1] - 128
    zero = jnp.zeros((3, columns), F32)
    order = [sums_t[0:4, :], sums_s[0:3, :], sums_f[0:1, :], zero, sums_t[4:5, :], sums_s[3:4, :], sums_f[1:2, :]]
    order += [sums_t[5:6, :], sums_s[4:5, :], sums_f[2:3, :], jnp.zeros((SMALL - 17, columns), F32)]
    values = jnp.concatenate(order, axis=0).astype(BF)
    for piece in range(8):
        block = nt(values, piece_select(piece, rows, columns))
        hidden = [ghb[0:1, (piece * 3 + r) * 128 : (piece * 3 + r + 1) * 128] for r in range(3)]
        block = jnp.concatenate([block[0:8, :]] + hidden + [block[11:, :]], axis=0)
        dw[piece * rows : piece * rows + SMALL, start:] = block.astype(BF)
        dw[piece * rows + SMALL : (piece + 1) * rows, start:] = jnp.zeros((rows - SMALL, 128), BF)


def load_feed(bufs, place_ref, we, wr, sems):
    if len(bufs) == 2:
        return start([(bufs[0], we)], sems), start([(bufs[1], wr)], sems.at[8:])
    views = piece_views(bufs)
    rows, units, columns = views[0].shape[0], we.shape[1], wr.shape[1]
    share = units // columns
    first = start([(v.at[:, 0:units], we.at[rows_at(place_ref[n], rows), :]) for n, v in enumerate(views)], sems)
    pairs = []
    for n, v in enumerate(views):
        for k in range(share):
            to = rows_at(place_ref[n], rows, share, k)
            pairs.append((v.at[:, units + k * columns : units + (k + 1) * columns], wr.at[to, :]))
    return first, start(pairs, sems.at[8:])


class Late:
    def __init__(self, source, target, sem):
        self.target = target
        self.copy = pltpu.make_async_copy(source, target, sem)
        self.copy.start()

    def get(self):
        if self.copy is not None:
            self.copy.wait()
            self.copy = None
        return self.target


class Early:
    def __init__(self, ref, target, sem):
        self.ref = ref
        self.copy = pltpu.make_async_copy(ref, target, sem)

    def send(self):
        self.copy.start()


SPACES = {
    "v": pl.BlockSpec(memory_space=pltpu.VMEM),
    "a": pl.BlockSpec(memory_space=pl.ANY),
    "l": pl.BlockSpec(memory_space=pl.ANY),
    "e": pl.BlockSpec(memory_space=pl.ANY),
    "s": pl.BlockSpec(memory_space=pltpu.SMEM),
}


def call(body, operands, spaces, outs, out_spaces, scratch, micros, name, tight=True):
    late = [n for n, space in enumerate(spaces) if space == "l"]
    early = [n for n, space in enumerate(out_spaces) if space == "e"]
    n_in, n_out, n_scratch = len(operands), len(outs), len(scratch)

    def kernel(*refs):
        ins, refs = list(refs[:n_in]), refs[n_in:]
        results, refs = list(refs[:n_out]), refs[n_out:]
        own, refs = refs[:n_scratch], refs[n_scratch:]
        held, refs = refs[: len(late)], refs[len(late) :]
        filled, refs = refs[: len(early)], refs[len(early) :]
        late_sems, early_sems = refs
        for k, n in enumerate(late):
            ins[n] = Late(ins[n], held[k], late_sems.at[k])
        for k, n in enumerate(early):
            results[n] = Early(filled[k], results[n], early_sems.at[k])
        body(ins, results, own)
        for n in late:
            ins[n].get()
        for n in early:
            results[n].copy.wait()

    held = [operands[n].size * operands[n].dtype.itemsize for n, space in enumerate(spaces) if space in "vl"]
    held += [math.prod(outs[n][0]) * jnp.dtype(outs[n][1]).itemsize for n, space in enumerate(out_spaces) if space in "ve"]
    held += [math.prod(ref.shape) * jnp.dtype(ref.dtype).itemsize for ref in scratch if "semaphore" not in str(ref.memory_space)]
    limit = min(VMEM_LIMIT, sum(held) + SPARE) if tight else VMEM_LIMIT
    more = [pltpu.VMEM(operands[n].shape, operands[n].dtype) for n in late]
    more += [pltpu.VMEM(*outs[n]) for n in early]
    more += [pltpu.SemaphoreType.DMA((max(1, len(late)),)), pltpu.SemaphoreType.DMA((max(1, len(early)),))]
    return pl.pallas_call(
        kernel,
        out_shape=[jax.ShapeDtypeStruct(s, d) for s, d in outs],
        in_specs=[SPACES[space] for space in spaces],
        out_specs=[SPACES[space] for space in out_spaces],
        scratch_shapes=list(scratch) + more,
        compiler_params=pltpu.CompilerParams(vmem_limit_bytes=limit),
        cost_estimate=pl.CostEstimate(flops=micros * MICRO, bytes_accessed=0, transcendentals=0),
        name=name,
    )(*operands)


def blocks_of(count):
    return [slice(j * WIDE, (j + 1) * WIDE) for j in range(count // WIDE)]


def shifted(at, base):
    return slice(at.start + base, at.stop + base)


def entry(normed, w, qkv, query_bias, value_bias):
    columns = normed.shape[1]
    for part, bias in enumerate((query_bias, None, value_bias)):
        for at in blocks_of(columns):
            to = shifted(at, part * columns)
            packed = nn(normed[...], w[:, to])
            qkv[:, to] = (packed if bias is None else packed + bias[:, at]).astype(BF)


def time_forward(n, ins, results, own):
    place_ref, x_ref, *rest = ins
    given, bufs = rest[: len(rest) - n], rest[len(rest) - n :]
    nt_out, qkv_out, o_out, e_out, p_out, y_ref, small_ref, hb_ref = results
    w, sems = own
    columns = x_ref.shape[1]
    wait(load(bufs, place_ref, w, sems))
    if given:
        small_ref[...] = given[0][...]
        hb_ref[...] = given[1][...]
    else:
        spread_small(w, small_ref, hb_ref)
    norm_chunks(x_ref, nt_out.ref, small_ref[11:12, :], small_ref[14:15, :])
    nt_out.send()
    qkv_ref, o_ref, e_ref, p_ref = qkv_out.ref, o_out.ref, e_out.ref, p_out.ref
    entry(nt_out.ref, w, qkv_ref, small_ref[0:1, :], small_ref[1:2, :])
    qkv_out.send()
    heads = head_map(columns)
    for clip in range(x_ref.shape[0] // (FRAMES * BLOCK)):
        at = [slice((clip * FRAMES + f) * BLOCK, (clip * FRAMES + f + 1) * BLOCK) for f in range(FRAMES)]
        weights = []
        for f in range(FRAMES):
            s = [head_sums(qkv_ref, at[f], 0, qkv_ref, at[g], columns, heads) * HD ** (-0.5) for g in range(FRAMES)]
            peak = jnp.maximum(s[0], s[1])
            powered = [jnp.exp(score - peak) for score in s]
            inverse = 1.0 / (powered[0] + powered[1])
            for g in range(FRAMES):
                m = (clip * FRAMES + f) * FRAMES + g
                p = powered[g] * inverse
                p_ref[m * BLOCK : (m + 1) * BLOCK, :] = p
                weights.append(p.astype(BF))
        for to in blocks_of(columns):
            v = [qkv_ref[a, shifted(to, 2 * columns)].astype(F32) for a in at]
            for f in range(FRAMES):
                spread = [nt(weights[FRAMES * f + g], heads[to, :]) for g in range(FRAMES)]
                o_ref[at[f], to] = (spread[0] * v[0] + spread[1] * v[1]).astype(BF)
    p_out.send()
    o_out.send()
    for at in blocks_of(columns):
        e_ref[:, at] = (nn(o_ref[...], w[:, shifted(at, 3 * columns)]) + small_ref[2:3, at]).astype(BF)
    e_out.send()
    patch = row_in_block(0, x_ref.shape[0], WIDE) < PLACES
    for at in blocks_of(columns):
        branch = nn(e_ref[...], w[:, shifted(at, 4 * columns)]) + small_ref[3:4, at]
        y_ref[:, at] = x_ref[:, at].astype(F32) + jnp.where(patch, branch, 0.0)


def half_masks():
    lane = lax.broadcasted_iota(jnp.int32, (1, 128), 1)
    return (lane < HD).astype(BF), (lane >= HD).astype(BF)


def space_forward(n, ins, results, own):
    place_ref, y_ref, small_ref, *bufs = ins
    ns_out, qkv_out, p_out, o_out, z_ref = results
    w, sems = own
    columns = y_ref.shape[1]
    blocks = y_ref.shape[0] // BLOCK
    pairs = columns // 128
    copies = load(bufs, place_ref, w, sems)
    norm_chunks(y_ref, ns_out.ref, small_ref[12:13, :], small_ref[15:16, :])
    ns_out.send()
    wait(copies)
    qkv_ref, p_ref, o_ref = qkv_out.ref, p_out.ref, o_out.ref
    entry(ns_out.ref, w, qkv_ref, small_ref[4:5, :], small_ref[5:6, :])
    qkv_out.send()
    masks = half_masks()
    first = lax.broadcasted_iota(jnp.int32, (BLOCK, 128), 1) < HD
    column = lax.broadcasted_iota(jnp.int32, (1, BLOCK), 1)
    hidden = jnp.where(column <= PLACES, 0.0, -1e30)

    def attend(block):
        at = rows_of(block, BLOCK)
        columns_of = [[slice(part * columns + k * 128, part * columns + (k + 1) * 128) for k in range(pairs)] for part in range(3)]
        scores = []
        for k in range(pairs):
            query, key = qkv_ref[at, columns_of[0][k]], qkv_ref[at, columns_of[1][k]]
            scores += [nt(query * mask, key) * HD ** (-0.5) + hidden for mask in masks]
        powered = [jnp.exp(s - jnp.max(s, axis=-1, keepdims=True)) for s in scores]
        weights = [(e * (1.0 / jnp.sum(e, axis=-1, keepdims=True))).astype(BF) for e in powered]
        for k in range(pairs):
            value = qkv_ref[at, columns_of[2][k]]
            for half in range(2):
                p_ref[(block * pairs + k) * 2 + half] = weights[2 * k + half]
            mixed = jnp.where(first, nn(weights[2 * k], value), nn(weights[2 * k + 1], value))
            o_ref[at, columns_of[0][k]] = mixed.astype(BF)

    loop(blocks, attend)
    p_out.send()
    o_out.send()
    is_class = lax.broadcasted_iota(jnp.int32, (BLOCK - EDGE, WIDE), 0) == CLASS
    for at in blocks_of(columns):
        branch = nn(o_ref[...], w[:, shifted(at, 3 * columns)]) + small_ref[6:7, at]
        z_ref[:, at] = y_ref[:, at] + branch
        for clip in range(blocks // FRAMES):
            edges = [slice((clip * FRAMES + f) * BLOCK + EDGE, (clip * FRAMES + f + 1) * BLOCK) for f in range(FRAMES)]
            mean = (branch[edges[0], :] + branch[edges[1], :]) * (1.0 / FRAMES)
            for edge in edges:
                z_ref[edge, at] = y_ref[edge, at] + jnp.where(is_class, mean, branch[edge, :])


def gelu_both(h):
    cdf = 0.5 * (1.0 + lax.erf(h * 0.5**0.5))
    density = jnp.exp(h * h * -0.5) * 0.3989422804014327
    return h * cdf, cdf + h * density


def feed_out(ins, results, own):
    place_ref, z_ref, g_ref, small_ref, hb_ref, *bufs = ins
    out_ref, nm_out, gh_out, *outs = results
    we, wr, dwr, a, sems, out_sems = own
    nm, gh = nm_out.ref, gh_out.ref
    columns = z_ref.shape[1]
    units = we.shape[1]
    copies, more = load_feed(bufs, place_ref, we, wr, sems)
    norm_chunks(z_ref, nm, small_ref[13:14, :], small_ref[16:17, :])
    nm_out.send()
    wait(copies + more)

    def inner(j):
        at = cols_of(j, WIDE)
        h = nn(nm[...], we[:, at]) + hb_ref[0:1, at]
        active, slope = gelu_both(h)
        a[:, at] = active.astype(BF)
        gh[:, at] = (nt(g_ref[...], wr[rows_of(j, WIDE), :]) * slope).astype(BF)

    loop(units // WIDE, inner)
    gh_out.send()

    def left(j):
        dwr[rows_of(j, WIDE), :] = tn(a[:, cols_of(j, WIDE)], g_ref[...]).astype(BF)

    loop(units // WIDE, left)
    copies = store_pieces(dwr, outs, place_ref, out_sems, units // columns)
    for at in blocks_of(columns):
        out_ref[:, at] = (z_ref[:, at] + (nn(a[...], wr[:, at]) + small_ref[7:8, at])).astype(BF)
    wait(copies)


def feed_in(ins, results, own):
    place_ref, gh, nm, g_in = ins
    sums_ref, ghb_ref, *outs = results
    dwe, out_sems = own
    units = gh.shape[1]

    def right(j):
        at = cols_of(j, WIDE)
        block = gh[:, at]
        dwe[:, at] = tn(nm[...], block).astype(BF)
        ghb_ref[0:1, at] = jnp.sum(block.astype(F32), axis=0, keepdims=True)

    loop(units // WIDE, right)
    copies = store_pieces(dwe, outs, place_ref, out_sems)
    sums_ref[0:1, :] = column_sums(g_in.get(), 0, nm.shape[1])
    wait(copies)


def norm_backward(row, n, ins, results, own):
    place_ref, gh_ref, x_in, base_in, small_ref, *bufs = ins
    gz_ref, sums_ref = results
    w, gn, sems = own
    columns = gz_ref.shape[1]
    views = [b.at[:, 0 : w.shape[1]] for b in bufs]
    wait(load(views, place_ref, w, sems))
    for at in blocks_of(columns):
        gn[:, at] = nt(gh_ref[...], w[at, :])
    x_ref, base = x_in.get(), base_in.get()

    def store(at, value):
        gz_ref[at, :] = value

    gain_sum, shift_sum = norm_back_chunks(
        gn, x_ref, small_ref[row : row + 1, :], lambda at: base[at, :].astype(F32), store
    )
    sums_ref[0:1, :] = gain_sum
    sums_ref[1:2, :] = shift_sum


def space_backward(n, ins, results, own):
    place_ref, gz_ref, ns_in, qkv_in, p_in, o_in, *rest = ins
    bufs = rest[:n]
    gqkv_out, sums_ref, *outs = results
    w, dw_ref, gbs, go, sems, out_sems = own
    columns = gz_ref.shape[1]
    rows = gz_ref.shape[0]
    clips = rows // (BLOCK * FRAMES)
    pairs = columns // 128
    copies = load([b.at[:, 3 * columns : 4 * columns] for b in bufs], place_ref, w, sems)

    def lower(i):
        at = rows_of(i, CHUNK)
        gbs[at, :] = gz_ref[at, :].astype(BF)

    loop(rows // CHUNK, lower)
    is_class = lax.broadcasted_iota(jnp.int32, (BLOCK - EDGE, columns), 0) == CLASS
    for clip in range(clips):
        edges = [slice((clip * FRAMES + f) * BLOCK + EDGE, (clip * FRAMES + f + 1) * BLOCK) for f in range(FRAMES)]
        share = gz_ref[edges[0], :] * (1.0 / FRAMES)
        for edge in edges:
            gbs[edge, :] = jnp.where(is_class, share, gz_ref[edge, :]).astype(BF)
    wait(copies)
    for at in blocks_of(columns):
        go[:, at] = nt(gbs[...], w[at, :]).astype(BF)
    o_ref, qkv_ref, p_ref, gqkv = o_in.get(), qkv_in.get(), p_in.get(), gqkv_out.ref
    for at in blocks_of(columns):
        dw_ref[:, shifted(at, 3 * columns)] = tn(o_ref[...], gbs[:, at]).astype(BF)
    masks = half_masks()
    first = lax.broadcasted_iota(jnp.int32, (BLOCK, 128), 1) < HD
    class_row = lax.broadcasted_iota(jnp.int32, (BLOCK - EDGE, 128), 0) == CLASS
    together = 2

    def attend(step):
        parts = []
        for u in range(together):
            clip, pair = (step * together + u) // pairs, (step * together + u) % pairs
            for f in range(FRAMES):
                block = clip * FRAMES + f
                at = rows_of(block, BLOCK)
                q, k, v = (qkv_ref[at, cols_of(pair, 128, part * columns)] for part in range(3))
                grad = go[at, cols_of(pair, 128)]
                parts += [(q, k, v, grad, mask, p_ref[2 * (block * pairs + pair) + half]) for half, mask in enumerate(masks)]
        gp = [nt(grad * mask, v) for _, _, v, grad, mask, _ in parts]
        p = [part[5].astype(F32) for part in parts]
        shared = [jnp.sum(a * b, axis=-1, keepdims=True) for a, b in zip(gp, p)]
        gs = [(b * (a - c)).astype(BF) for a, b, c in zip(gp, p, shared)]
        scale = HD ** (-0.5)
        gq = [nn(a, part[1]) * scale for a, part in zip(gs, parts)]
        gv = [tn(part[5], part[3]) for part in parts]
        gk = [tn(a, part[0]) * scale for a, part in zip(gs, parts)]
        for u in range(together):
            clip, pair = (step * together + u) // pairs, (step * together + u) % pairs
            for part, values in enumerate((gq, gk, gv)):
                to = cols_of(pair, 128, part * columns)
                one, two = (jnp.where(first, values[4 * u + 2 * f], values[4 * u + 2 * f + 1]) for f in range(FRAMES))
                top = clip * FRAMES * BLOCK
                gqkv[pl.ds(top, EDGE), to] = one[:EDGE].astype(BF)
                gqkv[pl.ds(top + BLOCK, EDGE), to] = two[:EDGE].astype(BF)
                both = jnp.where(class_row, one[EDGE:] + two[EDGE:], one[EDGE:])
                gqkv[pl.ds(top + EDGE, BLOCK - EDGE), to] = both.astype(BF)
                rest = jnp.where(class_row, 0.0, two[EDGE:])
                gqkv[pl.ds(top + BLOCK + EDGE, BLOCK - EDGE), to] = rest.astype(BF)

    loop(clips * pairs // together, attend)
    gqkv_out.send()
    ns_ref = ns_in.get()
    for at in blocks_of(3 * columns):
        dw_ref[:, at] = tn(ns_ref[...], gqkv[:, at]).astype(BF)
    copies = store_pieces(dw_ref, outs, place_ref, out_sems)
    sums_ref[0:1, :] = column_sums(gqkv, 0, columns)
    sums_ref[1:2, :] = column_sums(gqkv, 2 * columns, columns)
    sums_ref[2:3, :] = column_sums(gbs, 0, columns)
    wait(copies)


def mixer_backward(n, ins, results, own):
    place_ref, gy_ref, o_in, e_in, *bufs = ins
    go_out, sums_ref, *outs = results
    w, dw_ref, grt, get, sems, out_sems = own
    columns = gy_ref.shape[1]
    rows = gy_ref.shape[0]
    copies = load([b.at[:, 3 * columns : 5 * columns] for b in bufs], place_ref, w, sems)

    def lower(i):
        at = rows_of(i, CHUNK)
        patch = row_in_block(i, CHUNK, columns) < PLACES
        grt[at, :] = jnp.where(patch, gy_ref[at, :], 0.0).astype(BF)

    loop(rows // CHUNK, lower)
    wait(copies)
    go = go_out.ref
    for at in blocks_of(columns):
        get[:, at] = nt(grt[...], w[at, columns : 2 * columns]).astype(BF)
    e_ref, o_ref = e_in.get(), o_in.get()
    for at in blocks_of(columns):
        dw_ref[:, shifted(at, columns)] = tn(e_ref[...], grt[:, at]).astype(BF)
    for at in blocks_of(columns):
        dw_ref[:, at] = tn(o_ref[...], get[:, at]).astype(BF)
    copies = store_pieces(dw_ref, outs, place_ref, out_sems)
    for at in blocks_of(columns):
        go[:, at] = nt(get[...], w[at, 0:columns]).astype(BF)
    go_out.send()
    sums_ref[2:3, :] = column_sums(get, 0, columns)
    sums_ref[3:4, :] = column_sums(grt, 0, columns)
    wait(copies)


def time_backward(n, ins, results, own):
    place_ref, go, qkv_ref, p_ref, nt_in, x_in, gy_in, small_ref, before, *others = ins
    others, bufs = others[: len(others) - n], others[len(others) - n :]
    gx_ref, sums_ref, *outs = results
    w, dw_ref, gqkv, gn, sems, out_sems = own
    columns = gx_ref.shape[1]
    rows = gx_ref.shape[0]
    copies = load([b.at[:, 0 : 3 * columns] for b in bufs], place_ref, w, sems)
    heads = head_map(columns)
    for clip in range(rows // (FRAMES * BLOCK)):
        at = [slice((clip * FRAMES + f) * BLOCK, (clip * FRAMES + f + 1) * BLOCK) for f in range(FRAMES)]
        gs, kept = [], []
        for f in range(FRAMES):
            gp = [head_sums(go, at[f], 0, qkv_ref, at[g], 2 * columns, heads) for g in range(FRAMES)]
            first = ((clip * FRAMES + f) * FRAMES) * BLOCK
            p = [p_ref[first + g * BLOCK : first + (g + 1) * BLOCK, :] for g in range(FRAMES)]
            shared = gp[0] * p[0] + gp[1] * p[1]
            gs += [(p[g] * (gp[g] - shared)).astype(BF) for g in range(FRAMES)]
            kept += [p[g].astype(BF) for g in range(FRAMES)]
        for block in blocks_of(columns):
            to = [shifted(block, part * columns) for part in range(3)]
            q, k = ([qkv_ref[a, to[part]].astype(F32) for a in at] for part in range(2))
            grad = [go[a, block].astype(F32) for a in at]
            scaled = heads[block, :] * BF(HD ** (-0.5))
            spread = [nt(value, scaled) for value in gs]
            for f in range(FRAMES):
                gqkv[at[f], to[0]] = (spread[2 * f] * k[0] + spread[2 * f + 1] * k[1]).astype(BF)
                gqkv[at[f], to[1]] = (spread[f] * q[0] + spread[2 + f] * q[1]).astype(BF)
            spread = [nt(value, heads[block, :]) for value in kept]
            for f in range(FRAMES):
                gqkv[at[f], to[2]] = (spread[f] * grad[0] + spread[2 + f] * grad[1]).astype(BF)
    nt_ref = nt_in.get()
    for at in blocks_of(3 * columns):
        dw_ref[:, at] = tn(nt_ref[...], gqkv[:, at]).astype(BF)
    main = slice(0, 3 * columns)
    stores = store_pieces(dw_ref.at[:, main], [out.at[..., main] for out in outs], place_ref, out_sems)
    wait(copies)
    for at in blocks_of(columns):
        gn[:, at] = nt(gqkv[...], w[at, :])
    x_ref, gy_ref = x_in.get(), gy_in.get()

    def store(at, value):
        gx_ref[at, :] = value.astype(BF)

    gain_sum, shift_sum = norm_back_chunks(gn, x_ref, small_ref[11:12, :], lambda at: gy_ref[at, :], store)
    sums_ref[0:1, :] = column_sums(gqkv, 0, columns)
    sums_ref[1:2, :] = column_sums(gqkv, 2 * columns, columns)
    sums_ref[2:4, :] = before[2:4, :]
    sums_ref[4:5, :] = gain_sum
    sums_ref[5:6, :] = shift_sum
    wait(stores)
    if others:
        gather_small(dw_ref, (sums_ref, *others))
        last = slice(3 * columns, 3 * columns + 128)
        wait(store_pieces(dw_ref.at[:, last], [out.at[..., last] for out in outs], place_ref, out_sems))


def pack_rows(tokens, once):
    clips, _, columns = tokens.shape
    frames = []
    for f in range(FRAMES):
        places = tokens[:, 1 + f * PLACES : 1 + (f + 1) * PLACES]
        head = tokens[:, :1] if f == 0 or not once else jnp.zeros_like(tokens[:, :1])
        frames.append(jnp.concatenate([places, head, jnp.zeros((clips, BLOCK - PLACES - 1, columns), tokens.dtype)], axis=1))
    return jnp.stack(frames, axis=1).reshape(clips * FRAMES * BLOCK, columns)


def unpack_rows(rows, clips):
    framed = rows.reshape(clips, FRAMES, BLOCK, rows.shape[-1])
    return jnp.concatenate(
        [framed[:, 0, PLACES : PLACES + 1]] + [framed[:, f, :PLACES] for f in range(FRAMES)], axis=1
    )


class Layer:
    def __init__(self, rows, columns, units, shards, pieced, place):
        self.rows, self.columns, self.units = rows, columns, units
        self.pieced, self.place = pieced, place
        self.piece = columns // shards
        self.act = ((rows, columns), BF)
        self.act3 = ((rows, 3 * columns), BF)
        self.tall = ((rows, units), BF)
        self.wide = ((rows, columns), F32)
        self.sums = ((8, columns), F32)

    def grads(self, width):
        if self.pieced:
            return [((8, self.piece // 2, width), BF)] * 2
        return [((self.columns, width), BF)]

    def vmem(self, *shapes):
        return [pltpu.VMEM(s, d) for s, d in shapes]

    def sems(self, *counts):
        return [pltpu.SemaphoreType.DMA((count,)) for count in counts]

    def time_forward(self, x, given, bufs):
        c, n = self.columns, len(bufs)
        extra = [((SMALL, c), F32), ((8, self.units), F32)]
        return call(
            functools.partial(time_forward, n), (self.place, x, *given, *bufs), "sv" + "v" * len(given) + "a" * n,
            [self.act, self.act3, self.act, self.act, ((self.rows * FRAMES, 128), F32), self.wide] + extra, "eeeeevvv",
            self.vmem(((c, bufs[0].shape[1]), BF)) + self.sems(8), 14, "time_forward", False,
        )

    def space_forward(self, y, small, bufs):
        c, n = self.columns, len(bufs)
        probs = ((self.rows // BLOCK * (c // 128) * 2, BLOCK, BLOCK), BF)
        return call(
            functools.partial(space_forward, n), (self.place, y, small, *bufs), "svv" + "a" * n,
            [self.act, self.act3, probs, self.act, self.wide], "eeeev",
            self.vmem(((c, 4 * c), BF)) + self.sems(8), 16, "space_forward", False,
        )

    def feed_out(self, z, g, small, hb, bufs):
        c, u, n = self.columns, self.units, len(bufs)
        outs = self.grads(u) if self.pieced else [((u, c), BF)]
        return call(
            feed_out, (self.place, z, g, small, hb, *bufs), "svvvv" + "a" * n,
            [self.act, self.act, self.tall] + outs, "vee" + "a" * len(outs),
            self.vmem(((c, u), BF), ((u, c), BF), ((u, c), BF), self.tall) + self.sems(40, 64), 30, "feed_out", False,
        )

    def feed_in(self, gh, normed, g):
        c, u = self.columns, self.units
        outs = self.grads(u)
        return call(
            feed_in, (self.place, gh, normed, g), "svvl", [self.sums, ((8, u), F32)] + outs, "vv" + "a" * len(outs),
            self.vmem(((c, u), BF)) + self.sems(16), 8, "feed_in",
        )

    def norm_backward(self, row, gh, x, base, small, bufs, name):
        c, n, wide = self.columns, len(bufs), gh.shape[1]
        return call(
            functools.partial(norm_backward, row, n), (self.place, gh, x, base, small, *bufs), "svllv" + "a" * n,
            [self.wide, self.sums], "vv", self.vmem(((c, wide), BF), self.wide) + self.sems(8), 10, name,
        )

    def space_backward(self, gz, normed, qkv, p, o, bufs):
        c, n = self.columns, len(bufs)
        outs = self.grads(4 * c)
        return call(
            functools.partial(space_backward, n), (self.place, gz, normed, qkv, p, o, *bufs), "svllll" + "a" * n,
            [self.act3, self.sums] + outs, "ev" + "a" * len(outs),
            self.vmem(((c, c), BF), ((c, 4 * c), BF), self.act, self.act) + self.sems(8, 16), 20, "space_backward",
        )

    def mixer_backward(self, gy, o, e, bufs):
        c, n = self.columns, len(bufs)
        outs = self.grads(2 * c)
        return call(
            functools.partial(mixer_backward, n), (self.place, gy, o, e, *bufs), "svll" + "a" * n,
            [self.act, self.sums] + outs, "ev" + "a" * len(outs),
            self.vmem(((c, 2 * c), BF), ((c, 2 * c), BF), self.act, self.act) + self.sems(8, 16), 8, "mixer_backward",
        )

    def time_backward(self, go, qkv, p, normed, x, gy, small, before, others, bufs):
        c, n = self.columns, len(bufs)
        width = 3 * c + (128 if others else 0)
        outs = self.grads(width)
        return call(
            functools.partial(time_backward, n), (self.place, go, qkv, p, normed, x, gy, small, before, *others, *bufs),
            "svvvlllvv" + "v" * len(others) + "a" * n, [self.act, self.sums] + outs, "vv" + "a" * len(outs),
            self.vmem(((c, 3 * c), BF), ((c, width), BF), self.act3, self.wide) + self.sems(8, 16), 20, "time_backward",
        )


BOTH = ("grp", "shard")


def permute(value, target):
    shards = lax.axis_size("shard")
    pairs = [(z * shards + s, z * shards + target(s)) for z in range(lax.axis_size("grp")) for s in range(shards)]
    return lax.ppermute(value, BOTH, pairs)


def to_sibling(value):
    return permute(value, lambda s: s ^ 1)


def along_x(value):
    return permute(value, lambda s: s ^ 2)


def along_y(value):
    return permute(value, lambda s: s ^ 4)


def gather_start(own):
    return jnp.concatenate([own, to_sibling(own)], axis=0)


def gather_hop(both):
    return permute(both, lambda s: s ^ (2 if s % 2 == 0 else 4))


def gather_second(hop):
    return permute(hop[: hop.shape[0] // 2], lambda s: s ^ (4 if s % 2 == 0 else 2))


def places(s):
    near = jnp.where(s % 2 == 0, 2, 4)
    far = 6 - near
    gathered = [s, s ^ 1, s ^ near, s ^ near ^ 1, s ^ 6, s ^ 1 ^ far, s ^ far, s ^ 7]
    kept = [s, s ^ 2, s ^ 4, s ^ 6]
    return jnp.stack(gathered + kept + [k ^ 1 for k in kept]).astype(jnp.int32)


def total(*terms):
    return sum(t.astype(F32) for t in terms).astype(BF)


class Reduction:
    def __init__(self, keep, give):
        self.keep = keep
        self.got = to_sibling(give)

    def own(self, start, stop):
        return self.keep[start:stop], self.got[start:stop]

    def first(self):
        return total(*self.own(0, 2)), total(*self.own(2, 4))

    def cross(self, sent):
        self.from_x, self.from_y = along_x(sent[0]), along_y(sent[1])

    def second(self):
        return total(*self.own(4, 5), self.from_y[:1]), total(*self.own(5, 6), self.from_x[:1])

    def cross_again(self, sent):
        self.last_x, self.last_y = along_x(sent[0]), along_y(sent[1])

    def finish(self):
        top = total(*self.own(6, 7), self.from_x[1:], self.last_y)
        bottom = total(*self.own(7, 8), self.from_y[1:], self.last_x)
        return top[0], bottom[0]


def beside(*values):
    return jnp.concatenate([v[n : n + 1] for v in values for n in range(v.shape[0])], axis=2)


def apart(value, widths):
    stops = [sum(widths[: n + 1]) for n in range(len(widths))]
    return [value[..., stop - width : stop] for stop, width in zip(stops, widths)]


def tie(*values):
    leaves, shape = jax.tree.flatten(values)
    return jax.tree.unflatten(shape, lax.optimization_barrier(tuple(leaves)))


def swap_z(value):
    shards = lax.axis_size("shard")
    pairs = [(z * shards + s, (z ^ 1) * shards + s) for z in range(lax.axis_size("grp")) for s in range(shards)]
    return lax.ppermute(value, BOTH, pairs)


def across_pairs(value):
    return lax.ppermute(value, "grp", [(z, z ^ 2) for z in range(4)])


def inward(value):
    return lax.ppermute(value, "grp", [(0, 1), (3, 2)])


def across(value):
    return lax.ppermute(value, "grp", [(1, 2), (2, 1)])


def outward(value):
    return lax.ppermute(value, "grp", [(1, 0), (2, 3)])


def local(video, cotangent, live, time_entry, time_exit, time_mixer, space_entry, space_exit, hidden_expand, hidden_reduce, bias_rows, hidden_bias, norm_gain, norm_shift):
    clips, _, tokens, columns = video.shape
    shards, groups = lax.axis_size("shard"), lax.axis_size("grp")
    mine = lax.axis_index("shard")
    part = columns // shards
    units = hidden_bias.shape[0] * shards
    share = units // columns
    pieced = shards == 8 and groups == 4

    def gather(value):
        return lax.all_gather(value, "shard", axis=0, tiled=True)

    flags = live.astype(BF)[:, :, None]

    own_t = jnp.concatenate([time_entry, time_exit, time_mixer], axis=1)
    own_s = jnp.concatenate([space_entry, space_exit], axis=1)
    if pieced:
        narrow = jnp.concatenate([norm_gain, norm_shift], axis=0)
        narrow = jnp.concatenate(
            [jnp.pad(bias_rows, ((0, 0), (0, 128 - part))), hidden_bias.reshape(-1, 128), jnp.pad(narrow, ((0, 0), (0, 128 - part)))], axis=0
        )
        own_t = jnp.concatenate([own_t, jnp.pad(narrow, ((0, part - narrow.shape[0]), (0, 0)))], axis=1)
        own_f = jnp.concatenate([hidden_expand] + [hidden_reduce[k * part : (k + 1) * part] for k in range(share)], axis=1)
        net = Layer(clips * FRAMES * BLOCK, columns, units, shards, pieced, places(mine))
        both_t = gather_start(own_t)
        both_t, video, own_s, own_f = tie(both_t, video, own_s, own_f)
        hop_t = gather_hop(both_t)
        x = pack_rows(video[:, 0], False)
        both_s, both_f = gather_start(own_s), gather_start(own_f)
        hop_t, both_s, both_f, x = tie(hop_t, both_s, both_f, x)
        second_t, both_s, both_f = tie(gather_second(hop_t), both_s, both_f)
        wt = (both_t, hop_t, second_t, to_sibling(hop_t), to_sibling(second_t))
        hop_s, hop_f = gather_hop(both_s), gather_hop(both_f)
        normed_t, qkv_t, o_t, e_t, p_t, y, small, hb = net.time_forward(x, (), wt)
        hop_s, y, cotangent = tie(hop_s, y, cotangent)
        g = pack_rows(cotangent[:, 0] * flags, True)
        second_s = gather_second(hop_s)
        ws = (both_s, hop_s, second_s, to_sibling(hop_s), to_sibling(second_s))
        hop_f, y, ws, g = tie(hop_f, y, ws, g)
        normed_s, qkv_s, p_s, o_s, z = net.space_forward(y, small, ws)
        second_f, z = tie(gather_second(hop_f), z)
        wf = (both_f, hop_f, second_f, to_sibling(hop_f), to_sibling(second_f))
    else:
        x, g = pack_rows(video[:, 0], False), pack_rows(cotangent[:, 0] * flags, True)
        net = Layer(clips * FRAMES * BLOCK, columns, units, shards, pieced, jnp.zeros((16,), jnp.int32))
        packed = jnp.concatenate([bias_rows, norm_gain, norm_shift], axis=0)
        spread = lax.all_gather(packed, "shard", axis=0).transpose(1, 0, 2).reshape(-1, columns).astype(F32)
        small = jnp.concatenate([spread[:8], jnp.zeros((3, columns), F32), spread[8:], jnp.zeros((SMALL - 17, columns), F32)], axis=0)
        given = (small, jnp.pad(gather(hidden_bias).astype(F32)[None], ((0, 7), (0, 0))))
        wt, ws, wf = (gather(own_t),), (gather(own_s),), (gather(hidden_expand), gather(hidden_reduce))
        normed_t, qkv_t, o_t, e_t, p_t, y, small, hb = net.time_forward(x, given, wt)
        normed_s, qkv_s, p_s, o_s, z = net.space_forward(y, small, ws)

    out, normed_f, gh, *grad_r = net.feed_out(z, g, small, hb, wf)
    if pieced:
        sum_r = Reduction(*grad_r)
    sums_f, ghb, *grad_e = net.feed_in(gh, normed_f, g)
    if pieced:
        sum_e = Reduction(*grad_e)
        sent_r, gh, ghb, sums_f, sum_e.keep = tie(sum_r.first(), gh, ghb, sums_f, sum_e.keep)
        sum_r.cross(sent_r)
    gz, norm_f = net.norm_backward(13, gh, z, g, small, wf if pieced else wf[:1], "feed_norm")
    if pieced:
        sent_r, sent_e, gz, norm_f = tie(sum_r.second(), sum_e.first(), gz, norm_f)
        sum_r.cross_again(sent_r)
        sum_e.cross(sent_e)
    gqkv, sums_s, *grad_s = net.space_backward(gz, normed_s, qkv_s, p_s, o_s, ws)
    if pieced:
        sum_s = Reduction(*grad_s)
        kept_r, sent_e, gqkv, sums_s, sum_s.keep = tie(jnp.concatenate(sum_r.finish(), axis=0), sum_e.second(), gqkv, sums_s, sum_s.keep)
        sum_e.cross_again(sent_e)
        got_r = inward(kept_r)
    gy, norm_s = net.norm_backward(12, gqkv, y, gz, small, ws, "space_norm")
    if pieced:
        got_r, sum_e.last_x, sum_e.last_y, gy, norm_s = tie(got_r, sum_e.last_x, sum_e.last_y, gy, norm_s)
        kept_e = jnp.concatenate(sum_e.finish(), axis=0)
        kept_r, kept_e, sent_s, gy, norm_s = tie(total(kept_r, got_r), kept_e, sum_s.first(), gy, norm_s)
        sum_s.cross(sent_s)
        got_r, got_e = across(kept_r), inward(kept_e)
        sums_s = jnp.concatenate([sums_s[0:3], norm_s[0:2], sums_s[5:]], axis=0)
        sums_f = jnp.concatenate([sums_f[0:1], norm_f[0:2], sums_f[3:]], axis=0)
    others = (sums_s, sums_f, ghb) if pieced else ()
    go, sums_m, *grad_m = net.mixer_backward(gy, o_t, e_t, wt)
    if pieced:
        sum_m = Reduction(*grad_m)
        sent = [beside(last, both) for last, both in zip(sum_s.second(), sum_m.first())]
        kept_r, kept_e, sent, go, sums_m, sum_m.keep = tie(total(kept_r, got_r), total(kept_e, got_e), sent, go, sums_m, sum_m.keep)
        arrived = (along_x(sent[0]), along_y(sent[1]), outward(kept_r), across(kept_e))
    gx, sums_t, *grad_t = net.time_backward(go, qkv_t, p_t, normed_t, x, gy, small, sums_m, others, wt)

    if pieced:
        group = lax.axis_index("grp")
        even = group % 2 == 0
        inner = (group == 1) | (group == 2)
        (came_x, came_y, got_r, got_e), grad_t, gx, sums_t = tie(arrived, grad_t, gx, sums_t)
        widths = (sum_s.keep.shape[2], sum_m.keep.shape[2], sum_m.keep.shape[2])
        sum_s.last_x, *from_x = apart(came_x, widths)
        sum_s.last_y, *from_y = apart(came_y, widths)
        sum_m.from_x, sum_m.from_y = jnp.concatenate(from_x, axis=0), jnp.concatenate(from_y, axis=0)
        sum_t = Reduction(*grad_t)
        low_s, high_s = sum_s.finish()
        kept_e = total(kept_e, got_e)
        sent_s, kept_e = tie(jnp.where(even, high_s, low_s), kept_e)
        got_s, got_e = swap_z(sent_s), outward(kept_e)
        sent_x, sent_y = (beside(last, both) for last, both in zip(sum_m.second(), sum_t.first()))
        came_x, came_y = along_x(sent_x), along_y(sent_y)
        held_s = total(jnp.where(even, low_s, high_s), got_s)
        held_s, came_x, came_y = tie(held_s, came_x, came_y)
        got_s = across_pairs(held_s)
        widths = (sum_m.keep.shape[2], sum_t.keep.shape[2], sum_t.keep.shape[2])
        sum_m.last_x, *from_x = apart(came_x, widths)
        sum_m.last_y, *from_y = apart(came_y, widths)
        sum_t.from_x, sum_t.from_y = jnp.concatenate(from_x, axis=0), jnp.concatenate(from_y, axis=0)
        sum_t.cross_again(tie(*sum_t.second()))
        low_t, high_t = (jnp.concatenate(pair, axis=1) for pair in zip(sum_m.finish(), sum_t.finish()))
        sent_t, held_t, got_s, got_e = tie(jnp.where(even, high_t, low_t), jnp.where(even, low_t, high_t), got_s, got_e)
        got_t = swap_z(sent_t)
        held_s = total(held_s, got_s)
        got_s = swap_z(held_s)
        held_t, got_s = tie(total(held_t, got_t), got_s)
        held_t = total(held_t, across_pairs(held_t))
        got_t = swap_z(held_t)
        rt = jnp.concatenate([jnp.where(even, held_t, got_t), jnp.where(even, got_t, held_t)], axis=0).astype(F32)
        rs = jnp.concatenate([jnp.where(even, held_s, got_s), jnp.where(even, got_s, held_s)], axis=0).astype(F32)
        re = jnp.where(inner, kept_e, got_e).astype(F32)
        rr = jnp.where(inner, kept_r, got_r).astype(F32)
        rr = jnp.concatenate([rr[:, k * columns : (k + 1) * columns] for k in range(share)], axis=0)
        rm, rt = rt[:, : 2 * columns], rt[:, 2 * columns :]
        narrow = rt[:, 3 * columns :]
        biases, rows_hidden = narrow[0:8, :part], narrow[8:11].reshape(-1)
        gains, shifts = narrow[11:14, :part], narrow[14:17, :part]
    else:
        re, rr, rs, rm, rt = (
            lax.psum(lax.psum_scatter(v, "shard", scatter_dimension=0, tiled=True), "grp").astype(F32)
            for v in (*grad_e, *grad_r, *grad_s, *grad_m, *grad_t)
        )
        rows = [sums_t[0:4], sums_s[0:3], sums_f[0:1], sums_t[4:5], norm_s[0:1], norm_f[0:1], sums_t[5:6], norm_s[1:2], norm_f[1:2]]
        cut = lax.dynamic_slice_in_dim(lax.psum(jnp.concatenate(rows, axis=0), BOTH), mine * part, part, axis=1)
        biases, gains, shifts = cut[0:8], cut[8:11], cut[11:14]
        rows_hidden = lax.dynamic_slice_in_dim(lax.psum(ghb[0], BOTH), mine * hidden_bias.shape[0], hidden_bias.shape[0])
    return (
        (unpack_rows(out, clips) * flags)[:, None],
        unpack_rows(gx, clips)[:, None],
        rt[:, : 3 * columns],
        rm[:, :columns],
        rm[:, columns:],
        rs[:, : 3 * columns],
        rs[:, 3 * columns :],
        re,
        rr,
        biases,
        rows_hidden,
        gains,
        shifts,
    )


def solution(mesh):
    clips = P(None, ("grp", "shard"), None, None)
    rows = P("shard", None)
    cols = P(None, "shard")
    return jax.shard_map(
        local,
        mesh=mesh,
        in_specs=(clips, clips, P(None, ("grp", "shard"))) + (rows,) * 7 + (cols, P("shard"), cols, cols),
        out_specs=(clips, clips) + (rows,) * 7 + (cols, P("shard"), cols, cols),
        check_vma=False,
    )
```

```python
import functools
import math

import jax
import jax.numpy as jnp
from jax import lax
from jax.experimental import pallas as pl
from jax.experimental.pallas import tpu as pltpu
from jax.sharding import PartitionSpec as P

FRAMES = 2
PLACES = 196
HD = 64
EPSILON = 1e-06
BLOCK = 208
EDGE = 192
CLASS = PLACES - EDGE
CHUNK = 2 * BLOCK
WIDE = 256
BF = jnp.bfloat16
F32 = jnp.float32
SMALL = 32
MICRO = 4_000_000_000
SPARE = 12 * 1024 * 1024
VMEM_LIMIT = 60 * 1024 * 1024


def nn(a, b):
    return lax.dot_general(a, b, (((1,), (0,)), ((), ())), preferred_element_type=F32)


def nt(a, b):
    return lax.dot_general(a, b, (((1,), (1,)), ((), ())), preferred_element_type=F32)


def tn(a, b):
    return lax.dot_general(a, b, (((0,), (0,)), ((), ())), preferred_element_type=F32)


def loop(count, body):
    for i in range(count):
        body(i)


def rows_of(i, size):
    return slice(i * size, (i + 1) * size)


def cols_of(i, size, base=0):
    return slice(base + i * size, base + (i + 1) * size)


def unit(x):
    center = x - jnp.mean(x, axis=-1, keepdims=True)
    factor = lax.rsqrt(jnp.mean(center * center, axis=-1, keepdims=True) + EPSILON)
    return center * factor, factor


def norm_chunks(src, dst, gain, shift):
    def body(i):
        at = rows_of(i, CHUNK)
        w, _ = unit(src[at, :].astype(F32))
        dst[at, :] = (w * gain + shift).astype(BF)

    loop(src.shape[0] // CHUNK, body)


def fold(x):
    return jnp.sum(x.reshape(x.shape[0] // 8, 8, x.shape[1]), axis=0)


def norm_back_chunks(gn_ref, x_ref, gain, base_of, store):
    columns = x_ref.shape[1]

    def body(i, carry):
        gain_sum, shift_sum = carry
        at = rows_of(i, CHUNK)
        gn = gn_ref[at, :]
        w, factor = unit(x_ref[at, :].astype(F32))
        scaled = gn * gain
        plain = jnp.mean(scaled, axis=-1, keepdims=True)
        cross = jnp.mean(scaled * w, axis=-1, keepdims=True)
        store(at, base_of(at) + factor * (scaled - plain - w * cross))
        return gain_sum + fold(gn * w), shift_sum + fold(gn)

    zero = jnp.zeros((8, columns), F32)
    gain_sum, shift_sum = zero, zero
    for i in range(x_ref.shape[0] // CHUNK):
        gain_sum, shift_sum = body(i, (gain_sum, shift_sum))
    return jnp.sum(gain_sum, axis=0, keepdims=True), jnp.sum(shift_sum, axis=0, keepdims=True)


def column_sums(ref, start, size):
    def body(i, total):
        return total + fold(ref[rows_of(i, CHUNK), start : start + size].astype(F32))

    total = jnp.zeros((8, size), F32)
    for i in range(ref.shape[0] // CHUNK):
        total = body(i, total)
    return jnp.sum(total, axis=0, keepdims=True)


def head_map(columns):
    feature = lax.broadcasted_iota(jnp.int32, (columns, 128), 0) // HD
    head = lax.broadcasted_iota(jnp.int32, (columns, 128), 1)
    return (feature == head).astype(BF)


def head_sums(a_ref, a_rows, a_base, b_ref, b_rows, b_base, heads):
    total = None
    for j in range(heads.shape[0] // WIDE):
        a = a_ref[a_rows, a_base + j * WIDE : a_base + (j + 1) * WIDE].astype(F32)
        b = b_ref[b_rows, b_base + j * WIDE : b_base + (j + 1) * WIDE].astype(F32)
        top = (a * b).astype(BF)
        rest = (a * b - top.astype(F32)).astype(BF)
        part = heads[j * WIDE : (j + 1) * WIDE, :]
        term = nn(top, part) + nn(rest, part)
        total = term if total is None else total + term
    return total


def row_in_block(i, size, columns):
    return (i * size + lax.broadcasted_iota(jnp.int32, (size, columns), 0)) % BLOCK


def start(pairs, sems):
    copies = [pltpu.make_async_copy(s, d, sems.at[n]) for n, (s, d) in enumerate(pairs)]
    for copy in copies:
        copy.start()
    return copies


def wait(copies):
    for copy in copies:
        copy.wait()


def piece_views(bufs):
    rows = bufs[2].shape[0]
    return [b.at[k * rows : (k + 1) * rows] for b in bufs for k in range(b.shape[0] // rows)]


def rows_at(place, rows, share=1, k=0):
    return pl.ds(pl.multiple_of((place * share + k) * rows, 16), rows)


def load(bufs, place_ref, w, sems):
    if len(bufs) == 1:
        return start([(bufs[0], w)], sems)
    views = piece_views(bufs)
    rows = views[0].shape[0]
    return start([(v, w.at[rows_at(place_ref[n], rows), :]) for n, v in enumerate(views)], sems)


ORDER = ((3, 0), (1, 0), (3, 1), (2, 1), (1, 1), (2, 0), (0, 0), (0, 1))


def store_pieces(dw, outs, place_ref, sems, share=1, base=0):
    if len(outs) == 1:
        return start([(dw, outs[0])], sems)
    half, columns = outs[0].shape[1], dw.shape[1]
    pairs = []
    for side, out in enumerate(outs):
        for n, (chip, top) in enumerate(ORDER):
            place = place_ref[8 + side * 4 + chip]
            for k in range(share):
                source = dw.at[pl.ds(pl.multiple_of(((place * share + k) * 2 + top) * half, 16), half), :]
                pairs.append((source, out.at[n, :, base + k * columns : base + (k + 1) * columns]))
    return start(pairs, sems)


def piece_select(piece, rows, columns):
    lane = lax.broadcasted_iota(jnp.int32, (128, columns), 0)
    column = lax.broadcasted_iota(jnp.int32, (128, columns), 1)
    return ((lane < rows) & (column == piece * rows + lane)).astype(BF)


def spread_small(w, small_ref, hb_ref):
    columns = small_ref.shape[1]
    rows = columns // 8
    start = w.shape[1] - 128
    total = jnp.zeros((SMALL, columns), F32)
    for piece in range(8):
        block = w[piece * rows : piece * rows + SMALL, start:]
        total = total + nn(block, piece_select(piece, rows, columns))
        wide = block.astype(F32)
        for r in range(3):
            at = (piece * 3 + r) * 128
            hb_ref[0:1, at : at + 128] = wide[8 + r : 9 + r, :]
    small_ref[...] = total


def gather_small(dw, sums):
    sums_t, sums_s, sums_f, ghb = sums
    columns = sums_t.shape[1]
    rows = columns // 8
    start = dw.shape[1] - 128
    zero = jnp.zeros((3, columns), F32)
    order = [sums_t[0:4, :], sums_s[0:3, :], sums_f[0:1, :], zero, sums_t[4:5, :], sums_s[3:4, :], sums_f[1:2, :]]
    order += [sums_t[5:6, :], sums_s[4:5, :], sums_f[2:3, :], jnp.zeros((SMALL - 17, columns), F32)]
    values = jnp.concatenate(order, axis=0).astype(BF)
    for piece in range(8):
        block = nt(values, piece_select(piece, rows, columns))
        hidden = [ghb[0:1, (piece * 3 + r) * 128 : (piece * 3 + r + 1) * 128] for r in range(3)]
        block = jnp.concatenate([block[0:8, :]] + hidden + [block[11:, :]], axis=0)
        dw[piece * rows : piece * rows + SMALL, start:] = block.astype(BF)
        dw[piece * rows + SMALL : (piece + 1) * rows, start:] = jnp.zeros((rows - SMALL, 128), BF)


def load_feed(bufs, place_ref, we, wr, sems):
    if len(bufs) == 2:
        return start([(bufs[0], we)], sems), start([(bufs[1], wr)], sems.at[8:])
    views = piece_views(bufs)
    rows, units, columns = views[0].shape[0], we.shape[1], wr.shape[1]
    share = units // columns
    first = start([(v.at[:, 0:units], we.at[rows_at(place_ref[n], rows), :]) for n, v in enumerate(views)], sems)
    pairs = []
    for n, v in enumerate(views):
        for k in range(share):
            to = rows_at(place_ref[n], rows, share, k)
            pairs.append((v.at[:, units + k * columns : units + (k + 1) * columns], wr.at[to, :]))
    return first, start(pairs, sems.at[8:])


class Late:
    def __init__(self, source, target, sem):
        self.target = target
        self.copy = pltpu.make_async_copy(source, target, sem)
        self.copy.start()

    def get(self):
        if self.copy is not None:
            self.copy.wait()
            self.copy = None
        return self.target


class Early:
    def __init__(self, ref, target, sem):
        self.ref = ref
        self.copy = pltpu.make_async_copy(ref, target, sem)

    def send(self):
        self.copy.start()


SPACES = {
    "v": pl.BlockSpec(memory_space=pltpu.VMEM),
    "a": pl.BlockSpec(memory_space=pl.ANY),
    "l": pl.BlockSpec(memory_space=pl.ANY),
    "e": pl.BlockSpec(memory_space=pl.ANY),
    "s": pl.BlockSpec(memory_space=pltpu.SMEM),
}


def call(body, operands, spaces, outs, out_spaces, scratch, micros, name, tight=True):
    late = [n for n, space in enumerate(spaces) if space == "l"]
    early = [n for n, space in enumerate(out_spaces) if space == "e"]
    n_in, n_out, n_scratch = len(operands), len(outs), len(scratch)

    def kernel(*refs):
        ins, refs = list(refs[:n_in]), refs[n_in:]
        results, refs = list(refs[:n_out]), refs[n_out:]
        own, refs = refs[:n_scratch], refs[n_scratch:]
        held, refs = refs[: len(late)], refs[len(late) :]
        filled, refs = refs[: len(early)], refs[len(early) :]
        late_sems, early_sems = refs
        for k, n in enumerate(late):
            ins[n] = Late(ins[n], held[k], late_sems.at[k])
        for k, n in enumerate(early):
            results[n] = Early(filled[k], results[n], early_sems.at[k])
        body(ins, results, own)
        for n in late:
            ins[n].get()
        for n in early:
            results[n].copy.wait()

    held = [operands[n].size * operands[n].dtype.itemsize for n, space in enumerate(spaces) if space in "vl"]
    held += [math.prod(outs[n][0]) * jnp.dtype(outs[n][1]).itemsize for n, space in enumerate(out_spaces) if space in "ve"]
    held += [math.prod(ref.shape) * jnp.dtype(ref.dtype).itemsize for ref in scratch if "semaphore" not in str(ref.memory_space)]
    limit = min(VMEM_LIMIT, sum(held) + SPARE) if tight else VMEM_LIMIT
    more = [pltpu.VMEM(operands[n].shape, operands[n].dtype) for n in late]
    more += [pltpu.VMEM(*outs[n]) for n in early]
    more += [pltpu.SemaphoreType.DMA((max(1, len(late)),)), pltpu.SemaphoreType.DMA((max(1, len(early)),))]
    return pl.pallas_call(
        kernel,
        out_shape=[jax.ShapeDtypeStruct(s, d) for s, d in outs],
        in_specs=[SPACES[space] for space in spaces],
        out_specs=[SPACES[space] for space in out_spaces],
        scratch_shapes=list(scratch) + more,
        compiler_params=pltpu.CompilerParams(vmem_limit_bytes=limit),
        cost_estimate=pl.CostEstimate(flops=micros * MICRO, bytes_accessed=0, transcendentals=0),
        name=name,
    )(*operands)


def blocks_of(count):
    return [slice(j * WIDE, (j + 1) * WIDE) for j in range(count // WIDE)]


def shifted(at, base):
    return slice(at.start + base, at.stop + base)


def entry(normed, w, qkv, query_bias, value_bias):
    columns = normed.shape[1]
    for part, bias in enumerate((query_bias, None, value_bias)):
        for at in blocks_of(columns):
            to = shifted(at, part * columns)
            packed = nn(normed[...], w[:, to])
            qkv[:, to] = (packed if bias is None else packed + bias[:, at]).astype(BF)


def time_forward(n, ins, results, own):
    place_ref, x_ref, *rest = ins
    given, bufs = rest[: len(rest) - n], rest[len(rest) - n :]
    nt_out, qkv_out, o_out, e_out, p_out, y_ref, small_ref, hb_ref = results
    w, sems = own
    columns = x_ref.shape[1]
    wait(load(bufs, place_ref, w, sems))
    if given:
        small_ref[...] = given[0][...]
        hb_ref[...] = given[1][...]
    else:
        spread_small(w, small_ref, hb_ref)
    norm_chunks(x_ref, nt_out.ref, small_ref[11:12, :], small_ref[14:15, :])
    nt_out.send()
    qkv_ref, o_ref, e_ref, p_ref = qkv_out.ref, o_out.ref, e_out.ref, p_out.ref
    entry(nt_out.ref, w, qkv_ref, small_ref[0:1, :], small_ref[1:2, :])
    qkv_out.send()
    heads = head_map(columns)
    for clip in range(x_ref.shape[0] // (FRAMES * BLOCK)):
        at = [slice((clip * FRAMES + f) * BLOCK, (clip * FRAMES + f + 1) * BLOCK) for f in range(FRAMES)]
        weights = []
        for f in range(FRAMES):
            s = [head_sums(qkv_ref, at[f], 0, qkv_ref, at[g], columns, heads) * HD ** (-0.5) for g in range(FRAMES)]
            peak = jnp.maximum(s[0], s[1])
            powered = [jnp.exp(score - peak) for score in s]
            inverse = 1.0 / (powered[0] + powered[1])
            for g in range(FRAMES):
                m = (clip * FRAMES + f) * FRAMES + g
                p = powered[g] * inverse
                p_ref[m * BLOCK : (m + 1) * BLOCK, :] = p
                weights.append(p.astype(BF))
        for to in blocks_of(columns):
            v = [qkv_ref[a, shifted(to, 2 * columns)].astype(F32) for a in at]
            for f in range(FRAMES):
                spread = [nt(weights[FRAMES * f + g], heads[to, :]) for g in range(FRAMES)]
                o_ref[at[f], to] = (spread[0] * v[0] + spread[1] * v[1]).astype(BF)
    p_out.send()
    o_out.send()
    for at in blocks_of(columns):
        e_ref[:, at] = (nn(o_ref[...], w[:, shifted(at, 3 * columns)]) + small_ref[2:3, at]).astype(BF)
    e_out.send()
    patch = row_in_block(0, x_ref.shape[0], WIDE) < PLACES
    for at in blocks_of(columns):
        branch = nn(e_ref[...], w[:, shifted(at, 4 * columns)]) + small_ref[3:4, at]
        y_ref[:, at] = x_ref[:, at].astype(F32) + jnp.where(patch, branch, 0.0)


def half_masks():
    lane = lax.broadcasted_iota(jnp.int32, (1, 128), 1)
    return (lane < HD).astype(BF), (lane >= HD).astype(BF)


def space_forward(n, ins, results, own):
    place_ref, y_ref, small_ref, *bufs = ins
    ns_out, qkv_out, p_out, o_out, z_ref = results
    w, sems = own
    columns = y_ref.shape[1]
    blocks = y_ref.shape[0] // BLOCK
    pairs = columns // 128
    copies = load(bufs, place_ref, w, sems)
    norm_chunks(y_ref, ns_out.ref, small_ref[12:13, :], small_ref[15:16, :])
    ns_out.send()
    wait(copies)
    qkv_ref, p_ref, o_ref = qkv_out.ref, p_out.ref, o_out.ref
    entry(ns_out.ref, w, qkv_ref, small_ref[4:5, :], small_ref[5:6, :])
    qkv_out.send()
    masks = half_masks()
    first = lax.broadcasted_iota(jnp.int32, (BLOCK, 128), 1) < HD
    column = lax.broadcasted_iota(jnp.int32, (1, BLOCK), 1)
    hidden = jnp.where(column <= PLACES, 0.0, -1e30)

    def attend(block):
        at = rows_of(block, BLOCK)
        columns_of = [[slice(part * columns + k * 128, part * columns + (k + 1) * 128) for k in range(pairs)] for part in range(3)]
        scores = []
        for k in range(pairs):
            query, key = qkv_ref[at, columns_of[0][k]], qkv_ref[at, columns_of[1][k]]
            scores += [nt(query * mask, key) * HD ** (-0.5) + hidden for mask in masks]
        powered = [jnp.exp(s - jnp.max(s, axis=-1, keepdims=True)) for s in scores]
        weights = [(e * (1.0 / jnp.sum(e, axis=-1, keepdims=True))).astype(BF) for e in powered]
        for k in range(pairs):
            value = qkv_ref[at, columns_of[2][k]]
            for half in range(2):
                p_ref[(block * pairs + k) * 2 + half] = weights[2 * k + half]
            mixed = jnp.where(first, nn(weights[2 * k], value), nn(weights[2 * k + 1], value))
            o_ref[at, columns_of[0][k]] = mixed.astype(BF)

    loop(blocks, attend)
    p_out.send()
    o_out.send()
    is_class = lax.broadcasted_iota(jnp.int32, (BLOCK - EDGE, WIDE), 0) == CLASS
    for at in blocks_of(columns):
        branch = nn(o_ref[...], w[:, shifted(at, 3 * columns)]) + small_ref[6:7, at]
        z_ref[:, at] = y_ref[:, at] + branch
        for clip in range(blocks // FRAMES):
            edges = [slice((clip * FRAMES + f) * BLOCK + EDGE, (clip * FRAMES + f + 1) * BLOCK) for f in range(FRAMES)]
            mean = (branch[edges[0], :] + branch[edges[1], :]) * (1.0 / FRAMES)
            for edge in edges:
                z_ref[edge, at] = y_ref[edge, at] + jnp.where(is_class, mean, branch[edge, :])


def gelu_both(h):
    cdf = 0.5 * (1.0 + lax.erf(h * 0.5**0.5))
    density = jnp.exp(h * h * -0.5) * 0.3989422804014327
    return h * cdf, cdf + h * density


def feed_out(ins, results, own):
    place_ref, z_ref, g_ref, small_ref, hb_ref, *bufs = ins
    out_ref, nm_out, gh_out, *outs = results
    we, wr, dwr, a, sems, out_sems = own
    nm, gh = nm_out.ref, gh_out.ref
    columns = z_ref.shape[1]
    units = we.shape[1]
    copies, more = load_feed(bufs, place_ref, we, wr, sems)
    norm_chunks(z_ref, nm, small_ref[13:14, :], small_ref[16:17, :])
    nm_out.send()
    wait(copies + more)

    def inner(j):
        at = cols_of(j, WIDE)
        h = nn(nm[...], we[:, at]) + hb_ref[0:1, at]
        active, slope = gelu_both(h)
        a[:, at] = active.astype(BF)
        gh[:, at] = (nt(g_ref[...], wr[rows_of(j, WIDE), :]) * slope).astype(BF)

    loop(units // WIDE, inner)
    gh_out.send()

    def left(j):
        dwr[rows_of(j, WIDE), :] = tn(a[:, cols_of(j, WIDE)], g_ref[...]).astype(BF)

    loop(units // WIDE, left)
    copies = store_pieces(dwr, outs, place_ref, out_sems, units // columns)
    for at in blocks_of(columns):
        out_ref[:, at] = (z_ref[:, at] + (nn(a[...], wr[:, at]) + small_ref[7:8, at])).astype(BF)
    wait(copies)


def feed_in(ins, results, own):
    place_ref, gh, nm, g_in = ins
    sums_ref, ghb_ref, *outs = results
    dwe, out_sems = own
    units = gh.shape[1]

    def right(j):
        at = cols_of(j, WIDE)
        block = gh[:, at]
        dwe[:, at] = tn(nm[...], block).astype(BF)
        ghb_ref[0:1, at] = jnp.sum(block.astype(F32), axis=0, keepdims=True)

    loop(units // WIDE, right)
    copies = store_pieces(dwe, outs, place_ref, out_sems)
    sums_ref[0:1, :] = column_sums(g_in.get(), 0, nm.shape[1])
    wait(copies)


def norm_backward(row, n, ins, results, own):
    place_ref, gh_ref, x_in, base_in, small_ref, *bufs = ins
    gz_ref, sums_ref = results
    w, gn, sems = own
    columns = gz_ref.shape[1]
    views = [b.at[:, 0 : w.shape[1]] for b in bufs]
    wait(load(views, place_ref, w, sems))
    for at in blocks_of(columns):
        gn[:, at] = nt(gh_ref[...], w[at, :])
    x_ref, base = x_in.get(), base_in.get()

    def store(at, value):
        gz_ref[at, :] = value

    gain_sum, shift_sum = norm_back_chunks(
        gn, x_ref, small_ref[row : row + 1, :], lambda at: base[at, :].astype(F32), store
    )
    sums_ref[0:1, :] = gain_sum
    sums_ref[1:2, :] = shift_sum


def space_backward(n, ins, results, own):
    place_ref, gz_ref, ns_in, qkv_in, p_in, o_in, *rest = ins
    bufs = rest[:n]
    gqkv_out, sums_ref, *outs = results
    w, dw_ref, gbs, go, sems, out_sems = own
    columns = gz_ref.shape[1]
    rows = gz_ref.shape[0]
    clips = rows // (BLOCK * FRAMES)
    pairs = columns // 128
    copies = load([b.at[:, 3 * columns : 4 * columns] for b in bufs], place_ref, w, sems)

    def lower(i):
        at = rows_of(i, CHUNK)
        gbs[at, :] = gz_ref[at, :].astype(BF)

    loop(rows // CHUNK, lower)
    is_class = lax.broadcasted_iota(jnp.int32, (BLOCK - EDGE, columns), 0) == CLASS
    for clip in range(clips):
        edges = [slice((clip * FRAMES + f) * BLOCK + EDGE, (clip * FRAMES + f + 1) * BLOCK) for f in range(FRAMES)]
        share = gz_ref[edges[0], :] * (1.0 / FRAMES)
        for edge in edges:
            gbs[edge, :] = jnp.where(is_class, share, gz_ref[edge, :]).astype(BF)
    wait(copies)
    for at in blocks_of(columns):
        go[:, at] = nt(gbs[...], w[at, :]).astype(BF)
    o_ref, qkv_ref, p_ref, gqkv = o_in.get(), qkv_in.get(), p_in.get(), gqkv_out.ref
    for at in blocks_of(columns):
        dw_ref[:, shifted(at, 3 * columns)] = tn(o_ref[...], gbs[:, at]).astype(BF)
    masks = half_masks()
    first = lax.broadcasted_iota(jnp.int32, (BLOCK, 128), 1) < HD
    class_row = lax.broadcasted_iota(jnp.int32, (BLOCK - EDGE, 128), 0) == CLASS
    together = 2

    def attend(step):
        parts = []
        for u in range(together):
            clip, pair = (step * together + u) // pairs, (step * together + u) % pairs
            for f in range(FRAMES):
                block = clip * FRAMES + f
                at = rows_of(block, BLOCK)
                q, k, v = (qkv_ref[at, cols_of(pair, 128, part * columns)] for part in range(3))
                grad = go[at, cols_of(pair, 128)]
                parts += [(q, k, v, grad, mask, p_ref[2 * (block * pairs + pair) + half]) for half, mask in enumerate(masks)]
        gp = [nt(grad * mask, v) for _, _, v, grad, mask, _ in parts]
        p = [part[5].astype(F32) for part in parts]
        shared = [jnp.sum(a * b, axis=-1, keepdims=True) for a, b in zip(gp, p)]
        gs = [(b * (a - c)).astype(BF) for a, b, c in zip(gp, p, shared)]
        scale = HD ** (-0.5)
        gq = [nn(a, part[1]) * scale for a, part in zip(gs, parts)]
        gv = [tn(part[5], part[3]) for part in parts]
        gk = [tn(a, part[0]) * scale for a, part in zip(gs, parts)]
        for u in range(together):
            clip, pair = (step * together + u) // pairs, (step * together + u) % pairs
            for part, values in enumerate((gq, gk, gv)):
                to = cols_of(pair, 128, part * columns)
                one, two = (jnp.where(first, values[4 * u + 2 * f], values[4 * u + 2 * f + 1]) for f in range(FRAMES))
                top = clip * FRAMES * BLOCK
                gqkv[pl.ds(top, EDGE), to] = one[:EDGE].astype(BF)
                gqkv[pl.ds(top + BLOCK, EDGE), to] = two[:EDGE].astype(BF)
                both = jnp.where(class_row, one[EDGE:] + two[EDGE:], one[EDGE:])
                gqkv[pl.ds(top + EDGE, BLOCK - EDGE), to] = both.astype(BF)
                rest = jnp.where(class_row, 0.0, two[EDGE:])
                gqkv[pl.ds(top + BLOCK + EDGE, BLOCK - EDGE), to] = rest.astype(BF)

    loop(clips * pairs // together, attend)
    gqkv_out.send()
    ns_ref = ns_in.get()
    for at in blocks_of(3 * columns):
        dw_ref[:, at] = tn(ns_ref[...], gqkv[:, at]).astype(BF)
    copies = store_pieces(dw_ref, outs, place_ref, out_sems)
    sums_ref[0:1, :] = column_sums(gqkv, 0, columns)
    sums_ref[1:2, :] = column_sums(gqkv, 2 * columns, columns)
    sums_ref[2:3, :] = column_sums(gbs, 0, columns)
    wait(copies)


def mixer_backward(n, ins, results, own):
    place_ref, gy_ref, o_in, e_in, *bufs = ins
    go_out, sums_ref, *outs = results
    w, dw_ref, grt, get, sems, out_sems = own
    columns = gy_ref.shape[1]
    rows = gy_ref.shape[0]
    copies = load([b.at[:, 3 * columns : 5 * columns] for b in bufs], place_ref, w, sems)

    def lower(i):
        at = rows_of(i, CHUNK)
        patch = row_in_block(i, CHUNK, columns) < PLACES
        grt[at, :] = jnp.where(patch, gy_ref[at, :], 0.0).astype(BF)

    loop(rows // CHUNK, lower)
    wait(copies)
    go = go_out.ref
    for at in blocks_of(columns):
        get[:, at] = nt(grt[...], w[at, columns : 2 * columns]).astype(BF)
    e_ref, o_ref = e_in.get(), o_in.get()
    for at in blocks_of(columns):
        dw_ref[:, shifted(at, columns)] = tn(e_ref[...], grt[:, at]).astype(BF)
    for at in blocks_of(columns):
        dw_ref[:, at] = tn(o_ref[...], get[:, at]).astype(BF)
    copies = store_pieces(dw_ref, outs, place_ref, out_sems)
    for at in blocks_of(columns):
        go[:, at] = nt(get[...], w[at, 0:columns]).astype(BF)
    go_out.send()
    sums_ref[2:3, :] = column_sums(get, 0, columns)
    sums_ref[3:4, :] = column_sums(grt, 0, columns)
    wait(copies)


def time_backward(n, ins, results, own):
    place_ref, go, qkv_ref, p_ref, nt_in, x_in, gy_in, small_ref, before, *others = ins
    others, bufs = others[: len(others) - n], others[len(others) - n :]
    gx_ref, sums_ref, *outs = results
    w, dw_ref, gqkv, gn, sems, out_sems = own
    columns = gx_ref.shape[1]
    rows = gx_ref.shape[0]
    copies = load([b.at[:, 0 : 3 * columns] for b in bufs], place_ref, w, sems)
    heads = head_map(columns)
    for clip in range(rows // (FRAMES * BLOCK)):
        at = [slice((clip * FRAMES + f) * BLOCK, (clip * FRAMES + f + 1) * BLOCK) for f in range(FRAMES)]
        gs, kept = [], []
        for f in range(FRAMES):
            gp = [head_sums(go, at[f], 0, qkv_ref, at[g], 2 * columns, heads) for g in range(FRAMES)]
            first = ((clip * FRAMES + f) * FRAMES) * BLOCK
            p = [p_ref[first + g * BLOCK : first + (g + 1) * BLOCK, :] for g in range(FRAMES)]
            shared = gp[0] * p[0] + gp[1] * p[1]
            gs += [(p[g] * (gp[g] - shared)).astype(BF) for g in range(FRAMES)]
            kept += [p[g].astype(BF) for g in range(FRAMES)]
        for block in blocks_of(columns):
            to = [shifted(block, part * columns) for part in range(3)]
            q, k = ([qkv_ref[a, to[part]].astype(F32) for a in at] for part in range(2))
            grad = [go[a, block].astype(F32) for a in at]
            scaled = heads[block, :] * BF(HD ** (-0.5))
            spread = [nt(value, scaled) for value in gs]
            for f in range(FRAMES):
                gqkv[at[f], to[0]] = (spread[2 * f] * k[0] + spread[2 * f + 1] * k[1]).astype(BF)
                gqkv[at[f], to[1]] = (spread[f] * q[0] + spread[2 + f] * q[1]).astype(BF)
            spread = [nt(value, heads[block, :]) for value in kept]
            for f in range(FRAMES):
                gqkv[at[f], to[2]] = (spread[f] * grad[0] + spread[2 + f] * grad[1]).astype(BF)
    nt_ref = nt_in.get()
    for at in blocks_of(3 * columns):
        dw_ref[:, at] = tn(nt_ref[...], gqkv[:, at]).astype(BF)
    main = slice(0, 3 * columns)
    stores = store_pieces(dw_ref.at[:, main], [out.at[..., main] for out in outs], place_ref, out_sems)
    wait(copies)
    for at in blocks_of(columns):
        gn[:, at] = nt(gqkv[...], w[at, :])
    x_ref, gy_ref = x_in.get(), gy_in.get()

    def store(at, value):
        gx_ref[at, :] = value.astype(BF)

    gain_sum, shift_sum = norm_back_chunks(gn, x_ref, small_ref[11:12, :], lambda at: gy_ref[at, :], store)
    sums_ref[0:1, :] = column_sums(gqkv, 0, columns)
    sums_ref[1:2, :] = column_sums(gqkv, 2 * columns, columns)
    sums_ref[2:4, :] = before[2:4, :]
    sums_ref[4:5, :] = gain_sum
    sums_ref[5:6, :] = shift_sum
    wait(stores)
    if others:
        gather_small(dw_ref, (sums_ref, *others))
        last = slice(3 * columns, 3 * columns + 128)
        wait(store_pieces(dw_ref.at[:, last], [out.at[..., last] for out in outs], place_ref, out_sems))


def pack_rows(tokens, once):
    clips, _, columns = tokens.shape
    frames = []
    for f in range(FRAMES):
        places = tokens[:, 1 + f * PLACES : 1 + (f + 1) * PLACES]
        head = tokens[:, :1] if f == 0 or not once else jnp.zeros_like(tokens[:, :1])
        frames.append(jnp.concatenate([places, head, jnp.zeros((clips, BLOCK - PLACES - 1, columns), tokens.dtype)], axis=1))
    return jnp.stack(frames, axis=1).reshape(clips * FRAMES * BLOCK, columns)


def unpack_rows(rows, clips):
    framed = rows.reshape(clips, FRAMES, BLOCK, rows.shape[-1])
    return jnp.concatenate(
        [framed[:, 0, PLACES : PLACES + 1]] + [framed[:, f, :PLACES] for f in range(FRAMES)], axis=1
    )


class Layer:
    def __init__(self, rows, columns, units, shards, pieced, place):
        self.rows, self.columns, self.units = rows, columns, units
        self.pieced, self.place = pieced, place
        self.piece = columns // shards
        self.act = ((rows, columns), BF)
        self.act3 = ((rows, 3 * columns), BF)
        self.tall = ((rows, units), BF)
        self.wide = ((rows, columns), F32)
        self.sums = ((8, columns), F32)

    def grads(self, width):
        if self.pieced:
            return [((8, self.piece // 2, width), BF)] * 2
        return [((self.columns, width), BF)]

    def vmem(self, *shapes):
        return [pltpu.VMEM(s, d) for s, d in shapes]

    def sems(self, *counts):
        return [pltpu.SemaphoreType.DMA((count,)) for count in counts]

    def time_forward(self, x, given, bufs):
        c, n = self.columns, len(bufs)
        extra = [((SMALL, c), F32), ((8, self.units), F32)]
        return call(
            functools.partial(time_forward, n), (self.place, x, *given, *bufs), "sv" + "v" * len(given) + "a" * n,
            [self.act, self.act3, self.act, self.act, ((self.rows * FRAMES, 128), F32), self.wide] + extra, "eeeeevvv",
            self.vmem(((c, bufs[0].shape[1]), BF)) + self.sems(8), 14, "time_forward", False,
        )

    def space_forward(self, y, small, bufs):
        c, n = self.columns, len(bufs)
        probs = ((self.rows // BLOCK * (c // 128) * 2, BLOCK, BLOCK), BF)
        return call(
            functools.partial(space_forward, n), (self.place, y, small, *bufs), "svv" + "a" * n,
            [self.act, self.act3, probs, self.act, self.wide], "eeeev",
            self.vmem(((c, 4 * c), BF)) + self.sems(8), 16, "space_forward", False,
        )

    def feed_out(self, z, g, small, hb, bufs):
        c, u, n = self.columns, self.units, len(bufs)
        outs = self.grads(u) if self.pieced else [((u, c), BF)]
        return call(
            feed_out, (self.place, z, g, small, hb, *bufs), "svvvv" + "a" * n,
            [self.act, self.act, self.tall] + outs, "vee" + "a" * len(outs),
            self.vmem(((c, u), BF), ((u, c), BF), ((u, c), BF), self.tall) + self.sems(40, 64), 30, "feed_out", False,
        )

    def feed_in(self, gh, normed, g):
        c, u = self.columns, self.units
        outs = self.grads(u)
        return call(
            feed_in, (self.place, gh, normed, g), "svvl", [self.sums, ((8, u), F32)] + outs, "vv" + "a" * len(outs),
            self.vmem(((c, u), BF)) + self.sems(16), 8, "feed_in",
        )

    def norm_backward(self, row, gh, x, base, small, bufs, name):
        c, n, wide = self.columns, len(bufs), gh.shape[1]
        return call(
            functools.partial(norm_backward, row, n), (self.place, gh, x, base, small, *bufs), "svllv" + "a" * n,
            [self.wide, self.sums], "vv", self.vmem(((c, wide), BF), self.wide) + self.sems(8), 10, name,
        )

    def space_backward(self, gz, normed, qkv, p, o, bufs):
        c, n = self.columns, len(bufs)
        outs = self.grads(4 * c)
        return call(
            functools.partial(space_backward, n), (self.place, gz, normed, qkv, p, o, *bufs), "svllll" + "a" * n,
            [self.act3, self.sums] + outs, "ev" + "a" * len(outs),
            self.vmem(((c, c), BF), ((c, 4 * c), BF), self.act, self.act) + self.sems(8, 16), 20, "space_backward",
        )

    def mixer_backward(self, gy, o, e, bufs):
        c, n = self.columns, len(bufs)
        outs = self.grads(2 * c)
        return call(
            functools.partial(mixer_backward, n), (self.place, gy, o, e, *bufs), "svll" + "a" * n,
            [self.act, self.sums] + outs, "ev" + "a" * len(outs),
            self.vmem(((c, 2 * c), BF), ((c, 2 * c), BF), self.act, self.act) + self.sems(8, 16), 8, "mixer_backward",
        )

    def time_backward(self, go, qkv, p, normed, x, gy, small, before, others, bufs):
        c, n = self.columns, len(bufs)
        width = 3 * c + (128 if others else 0)
        outs = self.grads(width)
        return call(
            functools.partial(time_backward, n), (self.place, go, qkv, p, normed, x, gy, small, before, *others, *bufs),
            "svvvlllvv" + "v" * len(others) + "a" * n, [self.act, self.sums] + outs, "vv" + "a" * len(outs),
            self.vmem(((c, 3 * c), BF), ((c, width), BF), self.act3, self.wide) + self.sems(8, 16), 20, "time_backward",
        )


BOTH = ("grp", "shard")


def permute(value, target):
    shards = lax.axis_size("shard")
    pairs = [(z * shards + s, z * shards + target(s)) for z in range(lax.axis_size("grp")) for s in range(shards)]
    return lax.ppermute(value, BOTH, pairs)


def to_sibling(value):
    return permute(value, lambda s: s ^ 1)


def along_x(value):
    return permute(value, lambda s: s ^ 2)


def along_y(value):
    return permute(value, lambda s: s ^ 4)


def gather_start(own):
    return jnp.concatenate([own, to_sibling(own)], axis=0)


def gather_hop(both):
    return permute(both, lambda s: s ^ (2 if s % 2 == 0 else 4))


def gather_second(hop):
    return permute(hop[: hop.shape[0] // 2], lambda s: s ^ (4 if s % 2 == 0 else 2))


def places(s):
    near = jnp.where(s % 2 == 0, 2, 4)
    far = 6 - near
    gathered = [s, s ^ 1, s ^ near, s ^ near ^ 1, s ^ 6, s ^ 1 ^ far, s ^ far, s ^ 7]
    kept = [s, s ^ 2, s ^ 4, s ^ 6]
    return jnp.stack(gathered + kept + [k ^ 1 for k in kept]).astype(jnp.int32)


def total(*terms):
    return sum(t.astype(F32) for t in terms).astype(BF)


class Reduction:
    def __init__(self, keep, give):
        self.keep = keep
        self.got = to_sibling(give)

    def own(self, start, stop):
        return self.keep[start:stop], self.got[start:stop]

    def first(self):
        return total(*self.own(0, 2)), total(*self.own(2, 4))

    def cross(self, sent):
        self.from_x, self.from_y = along_x(sent[0]), along_y(sent[1])

    def second(self):
        return total(*self.own(4, 5), self.from_y[:1]), total(*self.own(5, 6), self.from_x[:1])

    def cross_again(self, sent):
        self.last_x, self.last_y = along_x(sent[0]), along_y(sent[1])

    def finish(self):
        top = total(*self.own(6, 7), self.from_x[1:], self.last_y)
        bottom = total(*self.own(7, 8), self.from_y[1:], self.last_x)
        return top[0], bottom[0]


def beside(*values):
    return jnp.concatenate([v[n : n + 1] for v in values for n in range(v.shape[0])], axis=2)


def apart(value, widths):
    stops = [sum(widths[: n + 1]) for n in range(len(widths))]
    return [value[..., stop - width : stop] for stop, width in zip(stops, widths)]


def hand_over(arrived, ahead, behind):
    widths = (ahead.keep.shape[2], behind.keep.shape[2], behind.keep.shape[2])
    ahead.last_x, *from_x = apart(arrived[0], widths)
    ahead.last_y, *from_y = apart(arrived[1], widths)
    behind.from_x, behind.from_y = jnp.concatenate(from_x, axis=0), jnp.concatenate(from_y, axis=0)


def tie(*values):
    leaves, shape = jax.tree.flatten(values)
    return jax.tree.unflatten(shape, lax.optimization_barrier(tuple(leaves)))


def swap_z(value):
    shards = lax.axis_size("shard")
    pairs = [(z * shards + s, (z ^ 1) * shards + s) for z in range(lax.axis_size("grp")) for s in range(shards)]
    return lax.ppermute(value, BOTH, pairs)


def across_pairs(value):
    return lax.ppermute(value, "grp", [(z, z ^ 2) for z in range(4)])


def split_groups(halves, even):
    low, high = halves
    return jnp.where(even, low, high), jnp.where(even, high, low)


def join_groups(held, other, even):
    return jnp.concatenate([jnp.where(even, held, other), jnp.where(even, other, held)], axis=0)


def local(video, cotangent, live, time_entry, time_exit, time_mixer, space_entry, space_exit, hidden_expand, hidden_reduce, bias_rows, hidden_bias, norm_gain, norm_shift):
    clips, _, tokens, columns = video.shape
    shards, groups = lax.axis_size("shard"), lax.axis_size("grp")
    mine = lax.axis_index("shard")
    part = columns // shards
    units = hidden_bias.shape[0] * shards
    share = units // columns
    pieced = shards == 8 and groups == 4

    def gather(value):
        return lax.all_gather(value, "shard", axis=0, tiled=True)

    flags = live.astype(BF)[:, :, None]

    own_t = jnp.concatenate([time_entry, time_exit, time_mixer], axis=1)
    own_s = jnp.concatenate([space_entry, space_exit], axis=1)
    if pieced:
        narrow = jnp.concatenate([norm_gain, norm_shift], axis=0)
        narrow = jnp.concatenate(
            [jnp.pad(bias_rows, ((0, 0), (0, 128 - part))), hidden_bias.reshape(-1, 128), jnp.pad(narrow, ((0, 0), (0, 128 - part)))], axis=0
        )
        own_t = jnp.concatenate([own_t, jnp.pad(narrow, ((0, part - narrow.shape[0]), (0, 0)))], axis=1)
        own_f = jnp.concatenate([hidden_expand] + [hidden_reduce[k * part : (k + 1) * part] for k in range(share)], axis=1)
        net = Layer(clips * FRAMES * BLOCK, columns, units, shards, pieced, places(mine))
        both_t = gather_start(own_t)
        both_t, video, own_s, own_f = tie(both_t, video, own_s, own_f)
        hop_t = gather_hop(both_t)
        x = pack_rows(video[:, 0], False)
        both_s, both_f = gather_start(own_s), gather_start(own_f)
        hop_t, both_s, both_f, x = tie(hop_t, both_s, both_f, x)
        second_t, both_s, both_f = tie(gather_second(hop_t), both_s, both_f)
        wt = (both_t, hop_t, second_t, to_sibling(hop_t), to_sibling(second_t))
        hop_s, hop_f = gather_hop(both_s), gather_hop(both_f)
        normed_t, qkv_t, o_t, e_t, p_t, y, small, hb = net.time_forward(x, (), wt)
        hop_s, y, cotangent = tie(hop_s, y, cotangent)
        g = pack_rows(cotangent[:, 0] * flags, True)
        second_s = gather_second(hop_s)
        ws = (both_s, hop_s, second_s, to_sibling(hop_s), to_sibling(second_s))
        hop_f, y, ws, g = tie(hop_f, y, ws, g)
        normed_s, qkv_s, p_s, o_s, z = net.space_forward(y, small, ws)
        second_f, z = tie(gather_second(hop_f), z)
        wf = (both_f, hop_f, second_f, to_sibling(hop_f), to_sibling(second_f))
    else:
        x, g = pack_rows(video[:, 0], False), pack_rows(cotangent[:, 0] * flags, True)
        net = Layer(clips * FRAMES * BLOCK, columns, units, shards, pieced, jnp.zeros((16,), jnp.int32))
        packed = jnp.concatenate([bias_rows, norm_gain, norm_shift], axis=0)
        spread = lax.all_gather(packed, "shard", axis=0).transpose(1, 0, 2).reshape(-1, columns).astype(F32)
        small = jnp.concatenate([spread[:8], jnp.zeros((3, columns), F32), spread[8:], jnp.zeros((SMALL - 17, columns), F32)], axis=0)
        given = (small, jnp.pad(gather(hidden_bias).astype(F32)[None], ((0, 7), (0, 0))))
        wt, ws, wf = (gather(own_t),), (gather(own_s),), (gather(hidden_expand), gather(hidden_reduce))
        normed_t, qkv_t, o_t, e_t, p_t, y, small, hb = net.time_forward(x, given, wt)
        normed_s, qkv_s, p_s, o_s, z = net.space_forward(y, small, ws)

    out, normed_f, gh, *grad_r = net.feed_out(z, g, small, hb, wf)
    if pieced:
        sum_r = Reduction(*grad_r)
    sums_f, ghb, *grad_e = net.feed_in(gh, normed_f, g)
    if pieced:
        sum_e = Reduction(*grad_e)
        sent_r, gh, ghb, sums_f, sum_e.keep = tie(sum_r.first(), gh, ghb, sums_f, sum_e.keep)
        sum_r.cross(sent_r)
    gz, norm_f = net.norm_backward(13, gh, z, g, small, wf if pieced else wf[:1], "feed_norm")
    if pieced:
        sent = [beside(last, both) for last, both in zip(sum_r.second(), sum_e.first())]
        sent, gz, norm_f = tie(sent, gz, norm_f)
        arrived = (along_x(sent[0]), along_y(sent[1]))
    gqkv, sums_s, *grad_s = net.space_backward(gz, normed_s, qkv_s, p_s, o_s, ws)
    if pieced:
        sum_s = Reduction(*grad_s)
        hand_over(arrived, sum_r, sum_e)
        even = lax.axis_index("grp") % 2 == 0
        held_r, sent_r = split_groups(sum_r.finish(), even)
        held_r, sent_r, sent_e, gqkv, sums_s, sum_s.keep = tie(held_r, sent_r, sum_e.second(), gqkv, sums_s, sum_s.keep)
        sum_e.cross_again(sent_e)
        got_r = swap_z(sent_r)
    gy, norm_s = net.norm_backward(12, gqkv, y, gz, small, ws, "space_norm")
    if pieced:
        got_r, sum_e.last_x, sum_e.last_y, gy, norm_s = tie(got_r, sum_e.last_x, sum_e.last_y, gy, norm_s)
        held_e, sent_e = split_groups(sum_e.finish(), even)
        held_r, held_e, sent_e, sent_s, gy, norm_s = tie(total(held_r, got_r), held_e, sent_e, sum_s.first(), gy, norm_s)
        sum_s.cross(sent_s)
        got_r, got_e = across_pairs(held_r), swap_z(sent_e)
        sums_s = jnp.concatenate([sums_s[0:3], norm_s[0:2], sums_s[5:]], axis=0)
        sums_f = jnp.concatenate([sums_f[0:1], norm_f[0:2], sums_f[3:]], axis=0)
    others = (sums_s, sums_f, ghb) if pieced else ()
    go, sums_m, *grad_m = net.mixer_backward(gy, o_t, e_t, wt)
    if pieced:
        sum_m = Reduction(*grad_m)
        arrived = (got_r, got_e, sum_s.from_x, sum_s.from_y)
        arrived, go, sums_m, sum_m.keep = tie(arrived, go, sums_m, sum_m.keep)
        got_r, got_e, sum_s.from_x, sum_s.from_y = arrived
        sent = [beside(last, both) for last, both in zip(sum_s.second(), sum_m.first())]
        held_r, held_e, sent, go = tie(total(held_r, got_r), total(held_e, got_e), sent, go)
        arrived = (along_x(sent[0]), along_y(sent[1]), swap_z(held_r), across_pairs(held_e))
    gx, sums_t, *grad_t = net.time_backward(go, qkv_t, p_t, normed_t, x, gy, small, sums_m, others, wt)

    if pieced:
        (came_x, came_y, got_r, got_e), grad_t, gx, sums_t, out = tie(arrived, grad_t, gx, sums_t, out)
        hand_over((came_x, came_y), sum_s, sum_m)
        sum_t = Reduction(*grad_t)
        held_e = total(held_e, got_e)
        sent = [beside(last, both) for last, both in zip(sum_m.second(), sum_t.first())]
        held_s, sent_s = split_groups(sum_s.finish(), even)
        sent, held_s, sent_s, held_e = tie(sent, held_s, sent_s, held_e)
        came_x, came_y = along_x(sent[0]), along_y(sent[1])
        got_s, got_e = swap_z(sent_s), swap_z(held_e)
        came_x, came_y, got_s = tie(came_x, came_y, got_s)
        hand_over((came_x, came_y), sum_m, sum_t)
        sum_t.cross_again(tie(*sum_t.second()))
        held_s = total(held_s, got_s)
        sum_t.last_x, sum_t.last_y, held_s = tie(sum_t.last_x, sum_t.last_y, held_s)
        halves = [jnp.concatenate(pair, axis=1) for pair in zip(sum_m.finish(), sum_t.finish())]
        held_t, sent_t = split_groups(halves, even)
        sent_t, held_t, held_s, got_e = tie(sent_t, held_t, held_s, got_e)
        got_t, got_s = swap_z(sent_t), across_pairs(held_s)
        got_t, got_s = tie(got_t, got_s)
        held_t, held_s = tie(total(held_t, got_t), total(held_s, got_s))
        got_t, got_s = across_pairs(held_t), swap_z(held_s)
        got_t, got_s = tie(got_t, got_s)
        held_t = total(held_t, got_t)
        got_t = swap_z(held_t)
        rt = join_groups(held_t, got_t, even).astype(F32)
        rs = join_groups(held_s, got_s, even).astype(F32)
        re = join_groups(held_e, got_e, even).astype(F32)
        rr = join_groups(held_r, got_r, even).astype(F32)
        rr = jnp.concatenate([rr[:, k * columns : (k + 1) * columns] for k in range(share)], axis=0)
        rm, rt = rt[:, : 2 * columns], rt[:, 2 * columns :]
        narrow = rt[:, 3 * columns :]
        biases, rows_hidden = narrow[0:8, :part], narrow[8:11].reshape(-1)
        gains, shifts = narrow[11:14, :part], narrow[14:17, :part]
    else:
        re, rr, rs, rm, rt = (
            lax.psum(lax.psum_scatter(v, "shard", scatter_dimension=0, tiled=True), "grp").astype(F32)
            for v in (*grad_e, *grad_r, *grad_s, *grad_m, *grad_t)
        )
        rows = [sums_t[0:4], sums_s[0:3], sums_f[0:1], sums_t[4:5], norm_s[0:1], norm_f[0:1], sums_t[5:6], norm_s[1:2], norm_f[1:2]]
        cut = lax.dynamic_slice_in_dim(lax.psum(jnp.concatenate(rows, axis=0), BOTH), mine * part, part, axis=1)
        biases, gains, shifts = cut[0:8], cut[8:11], cut[11:14]
        rows_hidden = lax.dynamic_slice_in_dim(lax.psum(ghb[0], BOTH), mine * hidden_bias.shape[0], hidden_bias.shape[0])
    return (
        (unpack_rows(out, clips) * flags)[:, None],
        unpack_rows(gx, clips)[:, None],
        rt[:, : 3 * columns],
        rm[:, :columns],
        rm[:, columns:],
        rs[:, : 3 * columns],
        rs[:, 3 * columns :],
        re,
        rr,
        biases,
        rows_hidden,
        gains,
        shifts,
    )


def solution(mesh):
    clips = P(None, ("grp", "shard"), None, None)
    rows = P("shard", None)
    cols = P(None, "shard")
    return jax.shard_map(
        local,
        mesh=mesh,
        in_specs=(clips, clips, P(None, ("grp", "shard"))) + (rows,) * 7 + (cols, P("shard"), cols, cols),
        out_specs=(clips, clips) + (rows,) * 7 + (cols, P("shard"), cols, cols),
        check_vma=False,
    )
```

```python
import functools
import math

import jax
import jax.numpy as jnp
from jax import lax
from jax.experimental import pallas as pl
from jax.experimental.pallas import tpu as pltpu
from jax.sharding import PartitionSpec as P

FRAMES = 2
PLACES = 196
HD = 64
EPSILON = 1e-06
BLOCK = 208
EDGE = 192
CLASS = PLACES - EDGE
CHUNK = 2 * BLOCK
WIDE = 256
BF = jnp.bfloat16
F32 = jnp.float32
SMALL = 32
MICRO = 4_000_000_000
SPARE = 12 * 1024 * 1024
VMEM_LIMIT = 60 * 1024 * 1024


def nn(a, b):
    return lax.dot_general(a, b, (((1,), (0,)), ((), ())), preferred_element_type=F32)


def nt(a, b):
    return lax.dot_general(a, b, (((1,), (1,)), ((), ())), preferred_element_type=F32)


def tn(a, b):
    return lax.dot_general(a, b, (((0,), (0,)), ((), ())), preferred_element_type=F32)


def loop(count, body):
    for i in range(count):
        body(i)


def rows_of(i, size):
    return slice(i * size, (i + 1) * size)


def cols_of(i, size, base=0):
    return slice(base + i * size, base + (i + 1) * size)


def unit(x):
    center = x - jnp.mean(x, axis=-1, keepdims=True)
    factor = lax.rsqrt(jnp.mean(center * center, axis=-1, keepdims=True) + EPSILON)
    return center * factor, factor


def norm_chunks(src, dst, gain, shift):
    def body(i):
        at = rows_of(i, CHUNK)
        w, _ = unit(src[at, :].astype(F32))
        dst[at, :] = (w * gain + shift).astype(BF)

    loop(src.shape[0] // CHUNK, body)


def fold(x):
    return jnp.sum(x.reshape(x.shape[0] // 8, 8, x.shape[1]), axis=0)


def norm_back_chunks(gn_ref, x_ref, gain, base_of, store):
    columns = x_ref.shape[1]

    def body(i, carry):
        gain_sum, shift_sum = carry
        at = rows_of(i, CHUNK)
        gn = gn_ref[at, :]
        w, factor = unit(x_ref[at, :].astype(F32))
        scaled = gn * gain
        plain = jnp.mean(scaled, axis=-1, keepdims=True)
        cross = jnp.mean(scaled * w, axis=-1, keepdims=True)
        store(at, base_of(at) + factor * (scaled - plain - w * cross))
        return gain_sum + fold(gn * w), shift_sum + fold(gn)

    zero = jnp.zeros((8, columns), F32)
    gain_sum, shift_sum = zero, zero
    for i in range(x_ref.shape[0] // CHUNK):
        gain_sum, shift_sum = body(i, (gain_sum, shift_sum))
    return jnp.sum(gain_sum, axis=0, keepdims=True), jnp.sum(shift_sum, axis=0, keepdims=True)


def column_sums(ref, start, size):
    def body(i, total):
        return total + fold(ref[rows_of(i, CHUNK), start : start + size].astype(F32))

    total = jnp.zeros((8, size), F32)
    for i in range(ref.shape[0] // CHUNK):
        total = body(i, total)
    return jnp.sum(total, axis=0, keepdims=True)


def head_map(columns):
    feature = lax.broadcasted_iota(jnp.int32, (columns, 128), 0) // HD
    head = lax.broadcasted_iota(jnp.int32, (columns, 128), 1)
    return (feature == head).astype(BF)


def head_sums(a_ref, a_rows, a_base, b_ref, b_rows, b_base, heads):
    total = None
    for j in range(heads.shape[0] // WIDE):
        a = a_ref[a_rows, a_base + j * WIDE : a_base + (j + 1) * WIDE].astype(F32)
        b = b_ref[b_rows, b_base + j * WIDE : b_base + (j + 1) * WIDE].astype(F32)
        top = (a * b).astype(BF)
        rest = (a * b - top.astype(F32)).astype(BF)
        part = heads[j * WIDE : (j + 1) * WIDE, :]
        term = nn(top, part) + nn(rest, part)
        total = term if total is None else total + term
    return total


def row_in_block(i, size, columns):
    return (i * size + lax.broadcasted_iota(jnp.int32, (size, columns), 0)) % BLOCK


def start(pairs, sems):
    copies = [pltpu.make_async_copy(s, d, sems.at[n]) for n, (s, d) in enumerate(pairs)]
    for copy in copies:
        copy.start()
    return copies


def wait(copies):
    for copy in copies:
        copy.wait()


def piece_views(bufs):
    return list(bufs)


def rows_at(place, rows, share=1, k=0):
    return pl.ds(pl.multiple_of((place * share + k) * rows, 16), rows)


def load(bufs, place_ref, w, sems):
    if len(bufs) == 1:
        return start([(bufs[0], w)], sems)
    views = piece_views(bufs)
    rows = views[0].shape[0]
    return start([(v, w.at[rows_at(place_ref[n], rows), :]) for n, v in enumerate(views)], sems)


ORDER = ((3, 0), (1, 0), (3, 1), (2, 1), (1, 1), (2, 0), (0, 0), (0, 1))


def store_pieces(dw, outs, place_ref, sems, share=1, base=0):
    if len(outs) == 1:
        return start([(dw, outs[0])], sems)
    half, columns = outs[0].shape[1], dw.shape[1]
    pairs = []
    for side, out in enumerate(outs):
        for n, (chip, top) in enumerate(ORDER):
            place = place_ref[8 + side * 4 + chip]
            for k in range(share):
                source = dw.at[pl.ds(pl.multiple_of(((place * share + k) * 2 + top) * half, 16), half), :]
                pairs.append((source, out.at[n, :, base + k * columns : base + (k + 1) * columns]))
    return start(pairs, sems)


def piece_select(piece, rows, columns):
    lane = lax.broadcasted_iota(jnp.int32, (128, columns), 0)
    column = lax.broadcasted_iota(jnp.int32, (128, columns), 1)
    return ((lane < rows) & (column == piece * rows + lane)).astype(BF)


def spread_small(w, small_ref, hb_ref):
    columns = small_ref.shape[1]
    rows = columns // 8
    start = w.shape[1] - 128
    total = jnp.zeros((SMALL, columns), F32)
    for piece in range(8):
        block = w[piece * rows : piece * rows + SMALL, start:]
        total = total + nn(block, piece_select(piece, rows, columns))
        wide = block.astype(F32)
        for r in range(3):
            at = (piece * 3 + r) * 128
            hb_ref[0:1, at : at + 128] = wide[8 + r : 9 + r, :]
    small_ref[...] = total


def gather_small(dw, sums):
    sums_t, sums_s, sums_f, ghb = sums
    columns = sums_t.shape[1]
    rows = columns // 8
    start = dw.shape[1] - 128
    zero = jnp.zeros((3, columns), F32)
    order = [sums_t[0:4, :], sums_s[0:3, :], sums_f[0:1, :], zero, sums_t[4:5, :], sums_s[3:4, :], sums_f[1:2, :]]
    order += [sums_t[5:6, :], sums_s[4:5, :], sums_f[2:3, :], jnp.zeros((SMALL - 17, columns), F32)]
    values = jnp.concatenate(order, axis=0).astype(BF)
    for piece in range(8):
        block = nt(values, piece_select(piece, rows, columns))
        hidden = [ghb[0:1, (piece * 3 + r) * 128 : (piece * 3 + r + 1) * 128] for r in range(3)]
        block = jnp.concatenate([block[0:8, :]] + hidden + [block[11:, :]], axis=0)
        dw[piece * rows : piece * rows + SMALL, start:] = block.astype(BF)
        dw[piece * rows + SMALL : (piece + 1) * rows, start:] = jnp.zeros((rows - SMALL, 128), BF)


def load_feed(bufs, place_ref, we, wr, sems):
    if len(bufs) == 2:
        return start([(bufs[0], we)], sems), start([(bufs[1], wr)], sems.at[8:])
    views = piece_views(bufs)
    rows, units, columns = views[0].shape[0], we.shape[1], wr.shape[1]
    share = units // columns
    first = start([(v.at[:, 0:units], we.at[rows_at(place_ref[n], rows), :]) for n, v in enumerate(views)], sems)
    pairs = []
    for n, v in enumerate(views):
        for k in range(share):
            to = rows_at(place_ref[n], rows, share, k)
            pairs.append((v.at[:, units + k * columns : units + (k + 1) * columns], wr.at[to, :]))
    return first, start(pairs, sems.at[8:])


class Late:
    def __init__(self, source, target, sem):
        self.target = target
        self.copy = pltpu.make_async_copy(source, target, sem)
        self.copy.start()

    def get(self):
        if self.copy is not None:
            self.copy.wait()
            self.copy = None
        return self.target


class Early:
    def __init__(self, ref, target, sem):
        self.ref = ref
        self.copy = pltpu.make_async_copy(ref, target, sem)

    def send(self):
        self.copy.start()


SPACES = {
    "v": pl.BlockSpec(memory_space=pltpu.VMEM),
    "a": pl.BlockSpec(memory_space=pl.ANY),
    "l": pl.BlockSpec(memory_space=pl.ANY),
    "e": pl.BlockSpec(memory_space=pl.ANY),
    "s": pl.BlockSpec(memory_space=pltpu.SMEM),
}


def call(body, operands, spaces, outs, out_spaces, scratch, micros, name, tight=True):
    late = [n for n, space in enumerate(spaces) if space == "l"]
    early = [n for n, space in enumerate(out_spaces) if space == "e"]
    n_in, n_out, n_scratch = len(operands), len(outs), len(scratch)

    def kernel(*refs):
        ins, refs = list(refs[:n_in]), refs[n_in:]
        results, refs = list(refs[:n_out]), refs[n_out:]
        own, refs = refs[:n_scratch], refs[n_scratch:]
        held, refs = refs[: len(late)], refs[len(late) :]
        filled, refs = refs[: len(early)], refs[len(early) :]
        late_sems, early_sems = refs
        for k, n in enumerate(late):
            ins[n] = Late(ins[n], held[k], late_sems.at[k])
        for k, n in enumerate(early):
            results[n] = Early(filled[k], results[n], early_sems.at[k])
        body(ins, results, own)
        for n in late:
            ins[n].get()
        for n in early:
            results[n].copy.wait()

    held = [operands[n].size * operands[n].dtype.itemsize for n, space in enumerate(spaces) if space in "vl"]
    held += [math.prod(outs[n][0]) * jnp.dtype(outs[n][1]).itemsize for n, space in enumerate(out_spaces) if space in "ve"]
    held += [math.prod(ref.shape) * jnp.dtype(ref.dtype).itemsize for ref in scratch if "semaphore" not in str(ref.memory_space)]
    limit = min(VMEM_LIMIT, sum(held) + SPARE) if tight else VMEM_LIMIT
    more = [pltpu.VMEM(operands[n].shape, operands[n].dtype) for n in late]
    more += [pltpu.VMEM(*outs[n]) for n in early]
    more += [pltpu.SemaphoreType.DMA((max(1, len(late)),)), pltpu.SemaphoreType.DMA((max(1, len(early)),))]
    return pl.pallas_call(
        kernel,
        out_shape=[jax.ShapeDtypeStruct(s, d) for s, d in outs],
        in_specs=[SPACES[space] for space in spaces],
        out_specs=[SPACES[space] for space in out_spaces],
        scratch_shapes=list(scratch) + more,
        compiler_params=pltpu.CompilerParams(vmem_limit_bytes=limit),
        cost_estimate=pl.CostEstimate(flops=micros * MICRO, bytes_accessed=0, transcendentals=0),
        name=name,
    )(*operands)


def blocks_of(count):
    return [slice(j * WIDE, (j + 1) * WIDE) for j in range(count // WIDE)]


def shifted(at, base):
    return slice(at.start + base, at.stop + base)


def entry(normed, w, qkv, query_bias, value_bias):
    columns = normed.shape[1]
    for part, bias in enumerate((query_bias, None, value_bias)):
        for at in blocks_of(columns):
            to = shifted(at, part * columns)
            packed = nn(normed[...], w[:, to])
            qkv[:, to] = (packed if bias is None else packed + bias[:, at]).astype(BF)


def time_forward(n, ins, results, own):
    place_ref, x_ref, *rest = ins
    given, bufs = rest[: len(rest) - n], rest[len(rest) - n :]
    nt_out, qkv_out, o_out, e_out, p_out, y_ref, small_ref, hb_ref = results
    w, sems = own
    columns = x_ref.shape[1]
    wait(load(bufs, place_ref, w, sems))
    if given:
        small_ref[...] = given[0][...]
        hb_ref[...] = given[1][...]
    else:
        spread_small(w, small_ref, hb_ref)
    norm_chunks(x_ref, nt_out.ref, small_ref[11:12, :], small_ref[14:15, :])
    nt_out.send()
    qkv_ref, o_ref, e_ref, p_ref = qkv_out.ref, o_out.ref, e_out.ref, p_out.ref
    entry(nt_out.ref, w, qkv_ref, small_ref[0:1, :], small_ref[1:2, :])
    qkv_out.send()
    heads = head_map(columns)
    for clip in range(x_ref.shape[0] // (FRAMES * BLOCK)):
        at = [slice((clip * FRAMES + f) * BLOCK, (clip * FRAMES + f + 1) * BLOCK) for f in range(FRAMES)]
        weights = []
        for f in range(FRAMES):
            s = [head_sums(qkv_ref, at[f], 0, qkv_ref, at[g], columns, heads) * HD ** (-0.5) for g in range(FRAMES)]
            peak = jnp.maximum(s[0], s[1])
            powered = [jnp.exp(score - peak) for score in s]
            inverse = 1.0 / (powered[0] + powered[1])
            for g in range(FRAMES):
                m = (clip * FRAMES + f) * FRAMES + g
                p = powered[g] * inverse
                p_ref[m * BLOCK : (m + 1) * BLOCK, :] = p
                weights.append(p.astype(BF))
        for to in blocks_of(columns):
            v = [qkv_ref[a, shifted(to, 2 * columns)].astype(F32) for a in at]
            for f in range(FRAMES):
                spread = [nt(weights[FRAMES * f + g], heads[to, :]) for g in range(FRAMES)]
                o_ref[at[f], to] = (spread[0] * v[0] + spread[1] * v[1]).astype(BF)
    p_out.send()
    o_out.send()
    for at in blocks_of(columns):
        e_ref[:, at] = (nn(o_ref[...], w[:, shifted(at, 3 * columns)]) + small_ref[2:3, at]).astype(BF)
    e_out.send()
    patch = row_in_block(0, x_ref.shape[0], WIDE) < PLACES
    for at in blocks_of(columns):
        branch = nn(e_ref[...], w[:, shifted(at, 4 * columns)]) + small_ref[3:4, at]
        y_ref[:, at] = x_ref[:, at].astype(F32) + jnp.where(patch, branch, 0.0)


def half_masks():
    lane = lax.broadcasted_iota(jnp.int32, (1, 128), 1)
    return (lane < HD).astype(BF), (lane >= HD).astype(BF)


def space_forward(n, ins, results, own):
    place_ref, y_ref, small_ref, *bufs = ins
    ns_out, qkv_out, p_out, o_out, z_ref = results
    w, sems = own
    columns = y_ref.shape[1]
    blocks = y_ref.shape[0] // BLOCK
    pairs = columns // 128
    copies = load(bufs, place_ref, w, sems)
    norm_chunks(y_ref, ns_out.ref, small_ref[12:13, :], small_ref[15:16, :])
    ns_out.send()
    wait(copies)
    qkv_ref, p_ref, o_ref = qkv_out.ref, p_out.ref, o_out.ref
    entry(ns_out.ref, w, qkv_ref, small_ref[4:5, :], small_ref[5:6, :])
    qkv_out.send()
    masks = half_masks()
    first = lax.broadcasted_iota(jnp.int32, (BLOCK, 128), 1) < HD
    column = lax.broadcasted_iota(jnp.int32, (1, BLOCK), 1)
    hidden = jnp.where(column <= PLACES, 0.0, -1e30)

    def attend(block):
        at = rows_of(block, BLOCK)
        columns_of = [[slice(part * columns + k * 128, part * columns + (k + 1) * 128) for k in range(pairs)] for part in range(3)]
        scores = []
        for k in range(pairs):
            query, key = qkv_ref[at, columns_of[0][k]], qkv_ref[at, columns_of[1][k]]
            scores += [nt(query * mask, key) * HD ** (-0.5) + hidden for mask in masks]
        powered = [jnp.exp(s - jnp.max(s, axis=-1, keepdims=True)) for s in scores]
        weights = [(e * (1.0 / jnp.sum(e, axis=-1, keepdims=True))).astype(BF) for e in powered]
        for k in range(pairs):
            value = qkv_ref[at, columns_of[2][k]]
            for half in range(2):
                p_ref[(block * pairs + k) * 2 + half] = weights[2 * k + half]
            mixed = jnp.where(first, nn(weights[2 * k], value), nn(weights[2 * k + 1], value))
            o_ref[at, columns_of[0][k]] = mixed.astype(BF)

    loop(blocks, attend)
    p_out.send()
    o_out.send()
    is_class = lax.broadcasted_iota(jnp.int32, (BLOCK - EDGE, WIDE), 0) == CLASS
    for at in blocks_of(columns):
        branch = nn(o_ref[...], w[:, shifted(at, 3 * columns)]) + small_ref[6:7, at]
        z_ref[:, at] = y_ref[:, at] + branch
        for clip in range(blocks // FRAMES):
            edges = [slice((clip * FRAMES + f) * BLOCK + EDGE, (clip * FRAMES + f + 1) * BLOCK) for f in range(FRAMES)]
            mean = (branch[edges[0], :] + branch[edges[1], :]) * (1.0 / FRAMES)
            for edge in edges:
                z_ref[edge, at] = y_ref[edge, at] + jnp.where(is_class, mean, branch[edge, :])


def gelu_both(h):
    cdf = 0.5 * (1.0 + lax.erf(h * 0.5**0.5))
    density = jnp.exp(h * h * -0.5) * 0.3989422804014327
    return h * cdf, cdf + h * density


def feed_out(ins, results, own):
    place_ref, z_ref, g_ref, small_ref, hb_ref, *bufs = ins
    out_ref, nm_out, gh_out, *outs = results
    we, wr, dwr, a, sems, out_sems = own
    nm, gh = nm_out.ref, gh_out.ref
    columns = z_ref.shape[1]
    units = we.shape[1]
    copies, more = load_feed(bufs, place_ref, we, wr, sems)
    norm_chunks(z_ref, nm, small_ref[13:14, :], small_ref[16:17, :])
    nm_out.send()
    wait(copies + more)

    def inner(j):
        at = cols_of(j, WIDE)
        h = nn(nm[...], we[:, at]) + hb_ref[0:1, at]
        active, slope = gelu_both(h)
        a[:, at] = active.astype(BF)
        gh[:, at] = (nt(g_ref[...], wr[rows_of(j, WIDE), :]) * slope).astype(BF)

    loop(units // WIDE, inner)
    gh_out.send()

    def left(j):
        dwr[rows_of(j, WIDE), :] = tn(a[:, cols_of(j, WIDE)], g_ref[...]).astype(BF)

    loop(units // WIDE, left)
    copies = store_pieces(dwr, outs, place_ref, out_sems, units // columns)
    for at in blocks_of(columns):
        out_ref[:, at] = (z_ref[:, at] + (nn(a[...], wr[:, at]) + small_ref[7:8, at])).astype(BF)
    wait(copies)


def feed_in(ins, results, own):
    place_ref, gh, nm, g_in = ins
    sums_ref, ghb_ref, *outs = results
    dwe, out_sems = own
    units = gh.shape[1]

    def right(j):
        at = cols_of(j, WIDE)
        block = gh[:, at]
        dwe[:, at] = tn(nm[...], block).astype(BF)
        ghb_ref[0:1, at] = jnp.sum(block.astype(F32), axis=0, keepdims=True)

    loop(units // WIDE, right)
    copies = store_pieces(dwe, outs, place_ref, out_sems)
    sums_ref[0:1, :] = column_sums(g_in.get(), 0, nm.shape[1])
    wait(copies)


def norm_backward(row, n, ins, results, own):
    place_ref, gh_ref, x_in, base_in, small_ref, *bufs = ins
    gz_ref, sums_ref = results
    w, gn, sems = own
    columns = gz_ref.shape[1]
    views = [b.at[:, 0 : w.shape[1]] for b in bufs]
    wait(load(views, place_ref, w, sems))
    for at in blocks_of(columns):
        gn[:, at] = nt(gh_ref[...], w[at, :])
    x_ref, base = x_in.get(), base_in.get()

    def store(at, value):
        gz_ref[at, :] = value

    gain_sum, shift_sum = norm_back_chunks(
        gn, x_ref, small_ref[row : row + 1, :], lambda at: base[at, :].astype(F32), store
    )
    sums_ref[0:1, :] = gain_sum
    sums_ref[1:2, :] = shift_sum


def space_backward(n, ins, results, own):
    place_ref, gz_ref, ns_in, qkv_in, p_in, o_in, *rest = ins
    bufs = rest[:n]
    gqkv_out, sums_ref, *outs = results
    w, dw_ref, gbs, go, sems, out_sems = own
    columns = gz_ref.shape[1]
    rows = gz_ref.shape[0]
    clips = rows // (BLOCK * FRAMES)
    pairs = columns // 128
    copies = load([b.at[:, 3 * columns : 4 * columns] for b in bufs], place_ref, w, sems)

    def lower(i):
        at = rows_of(i, CHUNK)
        gbs[at, :] = gz_ref[at, :].astype(BF)

    loop(rows // CHUNK, lower)
    is_class = lax.broadcasted_iota(jnp.int32, (BLOCK - EDGE, columns), 0) == CLASS
    for clip in range(clips):
        edges = [slice((clip * FRAMES + f) * BLOCK + EDGE, (clip * FRAMES + f + 1) * BLOCK) for f in range(FRAMES)]
        share = gz_ref[edges[0], :] * (1.0 / FRAMES)
        for edge in edges:
            gbs[edge, :] = jnp.where(is_class, share, gz_ref[edge, :]).astype(BF)
    wait(copies)
    for at in blocks_of(columns):
        go[:, at] = nt(gbs[...], w[at, :]).astype(BF)
    o_ref, qkv_ref, p_ref, gqkv = o_in.get(), qkv_in.get(), p_in.get(), gqkv_out.ref
    for at in blocks_of(columns):
        dw_ref[:, shifted(at, 3 * columns)] = tn(o_ref[...], gbs[:, at]).astype(BF)
    masks = half_masks()
    first = lax.broadcasted_iota(jnp.int32, (BLOCK, 128), 1) < HD
    class_row = lax.broadcasted_iota(jnp.int32, (BLOCK - EDGE, 128), 0) == CLASS
    together = 2

    def attend(step):
        parts = []
        for u in range(together):
            clip, pair = (step * together + u) // pairs, (step * together + u) % pairs
            for f in range(FRAMES):
                block = clip * FRAMES + f
                at = rows_of(block, BLOCK)
                q, k, v = (qkv_ref[at, cols_of(pair, 128, part * columns)] for part in range(3))
                grad = go[at, cols_of(pair, 128)]
                parts += [(q, k, v, grad, mask, p_ref[2 * (block * pairs + pair) + half]) for half, mask in enumerate(masks)]
        gp = [nt(grad * mask, v) for _, _, v, grad, mask, _ in parts]
        p = [part[5].astype(F32) for part in parts]
        shared = [jnp.sum(a * b, axis=-1, keepdims=True) for a, b in zip(gp, p)]
        gs = [(b * (a - c)).astype(BF) for a, b, c in zip(gp, p, shared)]
        scale = HD ** (-0.5)
        gq = [nn(a, part[1]) * scale for a, part in zip(gs, parts)]
        gv = [tn(part[5], part[3]) for part in parts]
        gk = [tn(a, part[0]) * scale for a, part in zip(gs, parts)]
        for u in range(together):
            clip, pair = (step * together + u) // pairs, (step * together + u) % pairs
            for part, values in enumerate((gq, gk, gv)):
                to = cols_of(pair, 128, part * columns)
                one, two = (jnp.where(first, values[4 * u + 2 * f], values[4 * u + 2 * f + 1]) for f in range(FRAMES))
                top = clip * FRAMES * BLOCK
                gqkv[pl.ds(top, EDGE), to] = one[:EDGE].astype(BF)
                gqkv[pl.ds(top + BLOCK, EDGE), to] = two[:EDGE].astype(BF)
                both = jnp.where(class_row, one[EDGE:] + two[EDGE:], one[EDGE:])
                gqkv[pl.ds(top + EDGE, BLOCK - EDGE), to] = both.astype(BF)
                rest = jnp.where(class_row, 0.0, two[EDGE:])
                gqkv[pl.ds(top + BLOCK + EDGE, BLOCK - EDGE), to] = rest.astype(BF)

    loop(clips * pairs // together, attend)
    gqkv_out.send()
    ns_ref = ns_in.get()
    for at in blocks_of(3 * columns):
        dw_ref[:, at] = tn(ns_ref[...], gqkv[:, at]).astype(BF)
    copies = store_pieces(dw_ref, outs, place_ref, out_sems)
    sums_ref[0:1, :] = column_sums(gqkv, 0, columns)
    sums_ref[1:2, :] = column_sums(gqkv, 2 * columns, columns)
    sums_ref[2:3, :] = column_sums(gbs, 0, columns)
    wait(copies)


def mixer_backward(n, ins, results, own):
    place_ref, gy_ref, o_in, e_in, *bufs = ins
    go_out, sums_ref, *outs = results
    w, dw_ref, grt, get, sems, out_sems = own
    columns = gy_ref.shape[1]
    rows = gy_ref.shape[0]
    copies = load([b.at[:, 3 * columns : 5 * columns] for b in bufs], place_ref, w, sems)

    def lower(i):
        at = rows_of(i, CHUNK)
        patch = row_in_block(i, CHUNK, columns) < PLACES
        grt[at, :] = jnp.where(patch, gy_ref[at, :], 0.0).astype(BF)

    loop(rows // CHUNK, lower)
    wait(copies)
    go = go_out.ref
    for at in blocks_of(columns):
        get[:, at] = nt(grt[...], w[at, columns : 2 * columns]).astype(BF)
    e_ref, o_ref = e_in.get(), o_in.get()
    for at in blocks_of(columns):
        dw_ref[:, shifted(at, columns)] = tn(e_ref[...], grt[:, at]).astype(BF)
    for at in blocks_of(columns):
        dw_ref[:, at] = tn(o_ref[...], get[:, at]).astype(BF)
    copies = store_pieces(dw_ref, outs, place_ref, out_sems)
    for at in blocks_of(columns):
        go[:, at] = nt(get[...], w[at, 0:columns]).astype(BF)
    go_out.send()
    sums_ref[2:3, :] = column_sums(get, 0, columns)
    sums_ref[3:4, :] = column_sums(grt, 0, columns)
    wait(copies)


def time_backward(n, ins, results, own):
    place_ref, go, qkv_ref, p_ref, nt_in, x_in, gy_in, small_ref, before, *others = ins
    others, bufs = others[: len(others) - n], others[len(others) - n :]
    gx_ref, sums_ref, *outs = results
    w, dw_ref, gqkv, gn, sems, out_sems = own
    columns = gx_ref.shape[1]
    rows = gx_ref.shape[0]
    copies = load([b.at[:, 0 : 3 * columns] for b in bufs], place_ref, w, sems)
    heads = head_map(columns)
    for clip in range(rows // (FRAMES * BLOCK)):
        at = [slice((clip * FRAMES + f) * BLOCK, (clip * FRAMES + f + 1) * BLOCK) for f in range(FRAMES)]
        gs, kept = [], []
        for f in range(FRAMES):
            gp = [head_sums(go, at[f], 0, qkv_ref, at[g], 2 * columns, heads) for g in range(FRAMES)]
            first = ((clip * FRAMES + f) * FRAMES) * BLOCK
            p = [p_ref[first + g * BLOCK : first + (g + 1) * BLOCK, :] for g in range(FRAMES)]
            shared = gp[0] * p[0] + gp[1] * p[1]
            gs += [(p[g] * (gp[g] - shared)).astype(BF) for g in range(FRAMES)]
            kept += [p[g].astype(BF) for g in range(FRAMES)]
        for block in blocks_of(columns):
            to = [shifted(block, part * columns) for part in range(3)]
            q, k = ([qkv_ref[a, to[part]].astype(F32) for a in at] for part in range(2))
            grad = [go[a, block].astype(F32) for a in at]
            scaled = heads[block, :] * BF(HD ** (-0.5))
            spread = [nt(value, scaled) for value in gs]
            for f in range(FRAMES):
                gqkv[at[f], to[0]] = (spread[2 * f] * k[0] + spread[2 * f + 1] * k[1]).astype(BF)
                gqkv[at[f], to[1]] = (spread[f] * q[0] + spread[2 + f] * q[1]).astype(BF)
            spread = [nt(value, heads[block, :]) for value in kept]
            for f in range(FRAMES):
                gqkv[at[f], to[2]] = (spread[f] * grad[0] + spread[2 + f] * grad[1]).astype(BF)
    nt_ref = nt_in.get()
    for at in blocks_of(3 * columns):
        dw_ref[:, at] = tn(nt_ref[...], gqkv[:, at]).astype(BF)
    main = slice(0, 3 * columns)
    stores = store_pieces(dw_ref.at[:, main], [out.at[..., main] for out in outs], place_ref, out_sems)
    wait(copies)
    for at in blocks_of(columns):
        gn[:, at] = nt(gqkv[...], w[at, :])
    x_ref, gy_ref = x_in.get(), gy_in.get()

    def store(at, value):
        gx_ref[at, :] = value.astype(BF)

    gain_sum, shift_sum = norm_back_chunks(gn, x_ref, small_ref[11:12, :], lambda at: gy_ref[at, :], store)
    sums_ref[0:1, :] = column_sums(gqkv, 0, columns)
    sums_ref[1:2, :] = column_sums(gqkv, 2 * columns, columns)
    sums_ref[2:4, :] = before[2:4, :]
    sums_ref[4:5, :] = gain_sum
    sums_ref[5:6, :] = shift_sum
    wait(stores)
    if others:
        gather_small(dw_ref, (sums_ref, *others))
        last = slice(3 * columns, 3 * columns + 128)
        wait(store_pieces(dw_ref.at[:, last], [out.at[..., last] for out in outs], place_ref, out_sems))


def pack_rows(tokens, once):
    clips, _, columns = tokens.shape
    frames = []
    for f in range(FRAMES):
        places = tokens[:, 1 + f * PLACES : 1 + (f + 1) * PLACES]
        head = tokens[:, :1] if f == 0 or not once else jnp.zeros_like(tokens[:, :1])
        frames.append(jnp.concatenate([places, head, jnp.zeros((clips, BLOCK - PLACES - 1, columns), tokens.dtype)], axis=1))
    return jnp.stack(frames, axis=1).reshape(clips * FRAMES * BLOCK, columns)


def unpack_rows(rows, clips):
    framed = rows.reshape(clips, FRAMES, BLOCK, rows.shape[-1])
    return jnp.concatenate(
        [framed[:, 0, PLACES : PLACES + 1]] + [framed[:, f, :PLACES] for f in range(FRAMES)], axis=1
    )


class Layer:
    def __init__(self, rows, columns, units, shards, pieced, place):
        self.rows, self.columns, self.units = rows, columns, units
        self.pieced, self.place = pieced, place
        self.piece = columns // shards
        self.act = ((rows, columns), BF)
        self.act3 = ((rows, 3 * columns), BF)
        self.tall = ((rows, units), BF)
        self.wide = ((rows, columns), F32)
        self.sums = ((8, columns), F32)

    def grads(self, width):
        if self.pieced:
            return [((8, self.piece // 2, width), BF)] * 2
        return [((self.columns, width), BF)]

    def vmem(self, *shapes):
        return [pltpu.VMEM(s, d) for s, d in shapes]

    def sems(self, *counts):
        return [pltpu.SemaphoreType.DMA((count,)) for count in counts]

    def time_forward(self, x, given, bufs):
        c, n = self.columns, len(bufs)
        extra = [((SMALL, c), F32), ((8, self.units), F32)]
        return call(
            functools.partial(time_forward, n), (self.place, x, *given, *bufs), "sv" + "v" * len(given) + "a" * n,
            [self.act, self.act3, self.act, self.act, ((self.rows * FRAMES, 128), F32), self.wide] + extra, "eeeeevvv",
            self.vmem(((c, bufs[0].shape[1]), BF)) + self.sems(8), 14, "time_forward", False,
        )

    def space_forward(self, y, small, bufs):
        c, n = self.columns, len(bufs)
        probs = ((self.rows // BLOCK * (c // 128) * 2, BLOCK, BLOCK), BF)
        return call(
            functools.partial(space_forward, n), (self.place, y, small, *bufs), "svv" + "a" * n,
            [self.act, self.act3, probs, self.act, self.wide], "eeeev",
            self.vmem(((c, 4 * c), BF)) + self.sems(8), 16, "space_forward", False,
        )

    def feed_out(self, z, g, small, hb, bufs):
        c, u, n = self.columns, self.units, len(bufs)
        outs = self.grads(u) if self.pieced else [((u, c), BF)]
        return call(
            feed_out, (self.place, z, g, small, hb, *bufs), "svvvv" + "a" * n,
            [self.act, self.act, self.tall] + outs, "vee" + "a" * len(outs),
            self.vmem(((c, u), BF), ((u, c), BF), ((u, c), BF), self.tall) + self.sems(40, 64), 30, "feed_out", False,
        )

    def feed_in(self, gh, normed, g):
        c, u = self.columns, self.units
        outs = self.grads(u)
        return call(
            feed_in, (self.place, gh, normed, g), "svvl", [self.sums, ((8, u), F32)] + outs, "vv" + "a" * len(outs),
            self.vmem(((c, u), BF)) + self.sems(16), 8, "feed_in",
        )

    def norm_backward(self, row, gh, x, base, small, bufs, name):
        c, n, wide = self.columns, len(bufs), gh.shape[1]
        return call(
            functools.partial(norm_backward, row, n), (self.place, gh, x, base, small, *bufs), "svllv" + "a" * n,
            [self.wide, self.sums], "vv", self.vmem(((c, wide), BF), self.wide) + self.sems(8), 10, name,
        )

    def space_backward(self, gz, normed, qkv, p, o, bufs):
        c, n = self.columns, len(bufs)
        outs = self.grads(4 * c)
        return call(
            functools.partial(space_backward, n), (self.place, gz, normed, qkv, p, o, *bufs), "svllll" + "a" * n,
            [self.act3, self.sums] + outs, "ev" + "a" * len(outs),
            self.vmem(((c, c), BF), ((c, 4 * c), BF), self.act, self.act) + self.sems(8, 16), 20, "space_backward",
        )

    def mixer_backward(self, gy, o, e, bufs):
        c, n = self.columns, len(bufs)
        outs = self.grads(2 * c)
        return call(
            functools.partial(mixer_backward, n), (self.place, gy, o, e, *bufs), "svll" + "a" * n,
            [self.act, self.sums] + outs, "ev" + "a" * len(outs),
            self.vmem(((c, 2 * c), BF), ((c, 2 * c), BF), self.act, self.act) + self.sems(8, 16), 8, "mixer_backward",
        )

    def time_backward(self, go, qkv, p, normed, x, gy, small, before, others, bufs):
        c, n = self.columns, len(bufs)
        width = 3 * c + (128 if others else 0)
        outs = self.grads(width)
        return call(
            functools.partial(time_backward, n), (self.place, go, qkv, p, normed, x, gy, small, before, *others, *bufs),
            "svvvlllvv" + "v" * len(others) + "a" * n, [self.act, self.sums] + outs, "vv" + "a" * len(outs),
            self.vmem(((c, 3 * c), BF), ((c, width), BF), self.act3, self.wide) + self.sems(8, 16), 20, "time_backward",
        )


BOTH = ("grp", "shard")


def permute(value, target):
    shards = lax.axis_size("shard")
    pairs = [(z * shards + s, z * shards + target(s)) for z in range(lax.axis_size("grp")) for s in range(shards)]
    return lax.ppermute(value, BOTH, pairs)


def to_sibling(value):
    return permute(value, lambda s: s ^ 1)


def along_x(value):
    return permute(value, lambda s: s ^ 2)


def along_y(value):
    return permute(value, lambda s: s ^ 4)


def near_hop(value):
    return permute(value, lambda s: s ^ (2 if s % 2 == 0 else 4))


def far_hop(value):
    return permute(value, lambda s: s ^ (4 if s % 2 == 0 else 2))


def places(s):
    near = jnp.where(s % 2 == 0, 2, 4)
    far = 6 - near
    gathered = [s, s ^ 1, s ^ near, s ^ near ^ 1, s ^ 6, s ^ 1 ^ far, s ^ far, s ^ 7]
    kept = [s, s ^ 2, s ^ 4, s ^ 6]
    return jnp.stack(gathered + kept + [k ^ 1 for k in kept]).astype(jnp.int32)


def total(*terms):
    return sum(t.astype(F32) for t in terms).astype(BF)


class Reduction:
    def __init__(self, keep, give):
        self.keep = keep
        self.got = to_sibling(give)

    def own(self, start, stop):
        return self.keep[start:stop], self.got[start:stop]

    def first(self):
        return total(*self.own(0, 2)), total(*self.own(2, 4))

    def cross(self, sent):
        self.from_x, self.from_y = along_x(sent[0]), along_y(sent[1])

    def second(self):
        return total(*self.own(4, 5), self.from_y[:1]), total(*self.own(5, 6), self.from_x[:1])

    def cross_again(self, sent):
        self.last_x, self.last_y = along_x(sent[0]), along_y(sent[1])

    def finish(self):
        top = total(*self.own(6, 7), self.from_x[1:], self.last_y)
        bottom = total(*self.own(7, 8), self.from_y[1:], self.last_x)
        return top[0], bottom[0]


def beside(*values):
    return jnp.concatenate([v[n : n + 1] for v in values for n in range(v.shape[0])], axis=2)


def apart(value, widths):
    stops = [sum(widths[: n + 1]) for n in range(len(widths))]
    return [value[..., stop - width : stop] for stop, width in zip(stops, widths)]


def hand_over(arrived, ahead, behind):
    widths = (ahead.keep.shape[2], behind.keep.shape[2], behind.keep.shape[2])
    ahead.last_x, *from_x = apart(arrived[0], widths)
    ahead.last_y, *from_y = apart(arrived[1], widths)
    behind.from_x, behind.from_y = jnp.concatenate(from_x, axis=0), jnp.concatenate(from_y, axis=0)


def tie(*values):
    leaves, shape = jax.tree.flatten(values)
    return jax.tree.unflatten(shape, lax.optimization_barrier(tuple(leaves)))


def swap_z(value):
    shards = lax.axis_size("shard")
    pairs = [(z * shards + s, (z ^ 1) * shards + s) for z in range(lax.axis_size("grp")) for s in range(shards)]
    return lax.ppermute(value, BOTH, pairs)


def across_pairs(value):
    return lax.ppermute(value, "grp", [(z, z ^ 2) for z in range(4)])


def split_groups(halves, even):
    low, high = halves
    return jnp.where(even, low, high), jnp.where(even, high, low)


def join_groups(held, other, even):
    return jnp.concatenate([jnp.where(even, held, other), jnp.where(even, other, held)], axis=0)


def local(video, cotangent, live, time_entry, time_exit, time_mixer, space_entry, space_exit, hidden_expand, hidden_reduce, bias_rows, hidden_bias, norm_gain, norm_shift):
    clips, _, tokens, columns = video.shape
    shards, groups = lax.axis_size("shard"), lax.axis_size("grp")
    mine = lax.axis_index("shard")
    part = columns // shards
    units = hidden_bias.shape[0] * shards
    share = units // columns
    pieced = shards == 8 and groups == 4

    def gather(value):
        return lax.all_gather(value, "shard", axis=0, tiled=True)

    flags = live.astype(BF)[:, :, None]

    own_t = jnp.concatenate([time_entry, time_exit, time_mixer], axis=1)
    own_s = jnp.concatenate([space_entry, space_exit], axis=1)
    if pieced:
        narrow = jnp.concatenate([norm_gain, norm_shift], axis=0)
        narrow = jnp.concatenate(
            [jnp.pad(bias_rows, ((0, 0), (0, 128 - part))), hidden_bias.reshape(-1, 128), jnp.pad(narrow, ((0, 0), (0, 128 - part)))], axis=0
        )
        own_t = jnp.concatenate([own_t, jnp.pad(narrow, ((0, part - narrow.shape[0]), (0, 0)))], axis=1)
        own_f = jnp.concatenate([hidden_expand] + [hidden_reduce[k * part : (k + 1) * part] for k in range(share)], axis=1)
        net = Layer(clips * FRAMES * BLOCK, columns, units, shards, pieced, places(mine))
        pair_t = to_sibling(own_t)
        pair_t, own_t, video, own_s, own_f = tie(pair_t, own_t, video, own_s, own_f)
        hop_t = (near_hop(own_t), near_hop(pair_t))
        x = pack_rows(video[:, 0], False)
        pair_s, pair_f = to_sibling(own_s), to_sibling(own_f)
        first_t, x, pair_s, pair_f = tie(hop_t[0], x, pair_s, pair_f)
        second_t, own_s, own_f, pair_s, pair_f = tie(far_hop(first_t), own_s, own_f, pair_s, pair_f)
        gone_t = tuple(to_sibling(v) for v in (first_t, hop_t[1], second_t))
        wt = (own_t, pair_t, first_t, hop_t[1], second_t, *gone_t)
        hop_s, hop_f = ((near_hop(own), near_hop(pair)) for own, pair in ((own_s, pair_s), (own_f, pair_f)))
        normed_t, qkv_t, o_t, e_t, p_t, y, small, hb = net.time_forward(x, (), wt)
        first_s, y, cotangent = tie(hop_s[0], y, cotangent)
        g = pack_rows(cotangent[:, 0] * flags, True)
        second_s = far_hop(first_s)
        ws = (own_s, pair_s, first_s, hop_s[1], second_s, *(to_sibling(v) for v in (first_s, hop_s[1], second_s)))
        first_f, y, ws, g = tie(hop_f[0], y, ws, g)
        normed_s, qkv_s, p_s, o_s, z = net.space_forward(y, small, ws)
        second_f, last_f, z = tie(far_hop(first_f), hop_f[1], z)
        wf = (own_f, pair_f, first_f, last_f, second_f, *(to_sibling(v) for v in (first_f, last_f, second_f)))
    else:
        x, g = pack_rows(video[:, 0], False), pack_rows(cotangent[:, 0] * flags, True)
        net = Layer(clips * FRAMES * BLOCK, columns, units, shards, pieced, jnp.zeros((16,), jnp.int32))
        packed = jnp.concatenate([bias_rows, norm_gain, norm_shift], axis=0)
        spread = lax.all_gather(packed, "shard", axis=0).transpose(1, 0, 2).reshape(-1, columns).astype(F32)
        small = jnp.concatenate([spread[:8], jnp.zeros((3, columns), F32), spread[8:], jnp.zeros((SMALL - 17, columns), F32)], axis=0)
        given = (small, jnp.pad(gather(hidden_bias).astype(F32)[None], ((0, 7), (0, 0))))
        wt, ws, wf = (gather(own_t),), (gather(own_s),), (gather(hidden_expand), gather(hidden_reduce))
        normed_t, qkv_t, o_t, e_t, p_t, y, small, hb = net.time_forward(x, given, wt)
        normed_s, qkv_s, p_s, o_s, z = net.space_forward(y, small, ws)

    out, normed_f, gh, *grad_r = net.feed_out(z, g, small, hb, wf)
    if pieced:
        sum_r = Reduction(*grad_r)
    sums_f, ghb, *grad_e = net.feed_in(gh, normed_f, g)
    if pieced:
        sum_e = Reduction(*grad_e)
        sent_r, gh, ghb, sums_f, sum_e.keep = tie(sum_r.first(), gh, ghb, sums_f, sum_e.keep)
        sum_r.cross(sent_r)
    gz, norm_f = net.norm_backward(13, gh, z, g, small, wf if pieced else wf[:1], "feed_norm")
    if pieced:
        sent = [beside(last, both) for last, both in zip(sum_r.second(), sum_e.first())]
        sent, gz, norm_f = tie(sent, gz, norm_f)
        arrived = (along_x(sent[0]), along_y(sent[1]))
    gqkv, sums_s, *grad_s = net.space_backward(gz, normed_s, qkv_s, p_s, o_s, ws)
    if pieced:
        sum_s = Reduction(*grad_s)
        hand_over(arrived, sum_r, sum_e)
        even = lax.axis_index("grp") % 2 == 0
        held_r, sent_r = split_groups(sum_r.finish(), even)
        held_r, sent_r, sent_e, gqkv, sums_s, sum_s.keep = tie(held_r, sent_r, sum_e.second(), gqkv, sums_s, sum_s.keep)
        sum_e.cross_again(sent_e)
        got_r = swap_z(sent_r)
    gy, norm_s = net.norm_backward(12, gqkv, y, gz, small, ws, "space_norm")
    if pieced:
        got_r, sum_e.last_x, sum_e.last_y, gy, norm_s = tie(got_r, sum_e.last_x, sum_e.last_y, gy, norm_s)
        held_e, sent_e = split_groups(sum_e.finish(), even)
        held_r, held_e, sent_e, sent_s, gy, norm_s = tie(total(held_r, got_r), held_e, sent_e, sum_s.first(), gy, norm_s)
        sum_s.cross(sent_s)
        got_r, got_e = across_pairs(held_r), swap_z(sent_e)
        sums_s = jnp.concatenate([sums_s[0:3], norm_s[0:2], sums_s[5:]], axis=0)
        sums_f = jnp.concatenate([sums_f[0:1], norm_f[0:2], sums_f[3:]], axis=0)
    others = (sums_s, sums_f, ghb) if pieced else ()
    go, sums_m, *grad_m = net.mixer_backward(gy, o_t, e_t, wt)
    if pieced:
        sum_m = Reduction(*grad_m)
        arrived = (got_r, got_e, sum_s.from_x, sum_s.from_y)
        arrived, go, sums_m, sum_m.keep = tie(arrived, go, sums_m, sum_m.keep)
        got_r, got_e, sum_s.from_x, sum_s.from_y = arrived
        sent = [beside(last, both) for last, both in zip(sum_s.second(), sum_m.first())]
        held_r, held_e, sent, go = tie(total(held_r, got_r), total(held_e, got_e), sent, go)
        arrived = (along_x(sent[0]), along_y(sent[1]), swap_z(held_r), across_pairs(held_e))
    gx, sums_t, *grad_t = net.time_backward(go, qkv_t, p_t, normed_t, x, gy, small, sums_m, others, wt)

    if pieced:
        (came_x, came_y, got_r, got_e), grad_t, gx, sums_t, out = tie(arrived, grad_t, gx, sums_t, out)
        hand_over((came_x, came_y), sum_s, sum_m)
        sum_t = Reduction(*grad_t)
        held_e = total(held_e, got_e)
        sent = [beside(last, both) for last, both in zip(sum_m.second(), sum_t.first())]
        held_s, sent_s = split_groups(sum_s.finish(), even)
        sent, held_s, sent_s, held_e, gx, out = tie(sent, held_s, sent_s, held_e, gx, out)
        came_x, came_y = along_x(sent[0]), along_y(sent[1])
        got_s, got_e = swap_z(sent_s), swap_z(held_e)
        hand_over((came_x, came_y), sum_m, sum_t)
        sum_t.cross_again(tie(*sum_t.second()))
        held_s = total(held_s, got_s)
        got_s = across_pairs(held_s)
        halves = [jnp.concatenate(pair, axis=1) for pair in zip(sum_m.finish(), sum_t.finish())]
        held_t, sent_t = split_groups(halves, even)
        sent_t, held_t, got_e = tie(sent_t, held_t, got_e)
        got_t = swap_z(sent_t)
        got_t, got_s = tie(got_t, got_s)
        held_t, held_s = tie(total(held_t, got_t), total(held_s, got_s))
        got_t, got_s = across_pairs(held_t), swap_z(held_s)
        got_t, got_s = tie(got_t, got_s)
        held_t = total(held_t, got_t)
        got_t = swap_z(held_t)
        rt = join_groups(held_t, got_t, even).astype(F32)
        rs = join_groups(held_s, got_s, even).astype(F32)
        re = join_groups(held_e, got_e, even).astype(F32)
        rr = join_groups(held_r, got_r, even).astype(F32)
        rr = jnp.concatenate([rr[:, k * columns : (k + 1) * columns] for k in range(share)], axis=0)
        rm, rt = rt[:, : 2 * columns], rt[:, 2 * columns :]
        narrow = rt[:, 3 * columns :]
        biases, rows_hidden = narrow[0:8, :part], narrow[8:11].reshape(-1)
        gains, shifts = narrow[11:14, :part], narrow[14:17, :part]
    else:
        re, rr, rs, rm, rt = (
            lax.psum(lax.psum_scatter(v, "shard", scatter_dimension=0, tiled=True), "grp").astype(F32)
            for v in (*grad_e, *grad_r, *grad_s, *grad_m, *grad_t)
        )
        rows = [sums_t[0:4], sums_s[0:3], sums_f[0:1], sums_t[4:5], norm_s[0:1], norm_f[0:1], sums_t[5:6], norm_s[1:2], norm_f[1:2]]
        cut = lax.dynamic_slice_in_dim(lax.psum(jnp.concatenate(rows, axis=0), BOTH), mine * part, part, axis=1)
        biases, gains, shifts = cut[0:8], cut[8:11], cut[11:14]
        rows_hidden = lax.dynamic_slice_in_dim(lax.psum(ghb[0], BOTH), mine * hidden_bias.shape[0], hidden_bias.shape[0])
    return (
        (unpack_rows(out, clips) * flags)[:, None],
        unpack_rows(gx, clips)[:, None],
        rt[:, : 3 * columns],
        rm[:, :columns],
        rm[:, columns:],
        rs[:, : 3 * columns],
        rs[:, 3 * columns :],
        re,
        rr,
        biases,
        rows_hidden,
        gains,
        shifts,
    )


def solution(mesh):
    clips = P(None, ("grp", "shard"), None, None)
    rows = P("shard", None)
    cols = P(None, "shard")
    return jax.shard_map(
        local,
        mesh=mesh,
        in_specs=(clips, clips, P(None, ("grp", "shard"))) + (rows,) * 7 + (cols, P("shard"), cols, cols),
        out_specs=(clips, clips) + (rows,) * 7 + (cols, P("shard"), cols, cols),
        check_vma=False,
    )
```

```python
import functools
import math

import jax
import jax.numpy as jnp
from jax import lax
from jax.experimental import pallas as pl
from jax.experimental.pallas import tpu as pltpu
from jax.sharding import PartitionSpec as P

FRAMES = 2
PLACES = 196
HD = 64
EPSILON = 1e-06
BLOCK = 208
EDGE = 192
CLASS = PLACES - EDGE
CHUNK = 2 * BLOCK
WIDE = 256
BF = jnp.bfloat16
F32 = jnp.float32
SMALL = 32
MICRO = 4_000_000_000
SPARE = 12 * 1024 * 1024
VMEM_LIMIT = 60 * 1024 * 1024


def nn(a, b):
    return lax.dot_general(a, b, (((1,), (0,)), ((), ())), preferred_element_type=F32)


def nt(a, b):
    return lax.dot_general(a, b, (((1,), (1,)), ((), ())), preferred_element_type=F32)


def tn(a, b):
    return lax.dot_general(a, b, (((0,), (0,)), ((), ())), preferred_element_type=F32)


def loop(count, body):
    for i in range(count):
        body(i)


def rows_of(i, size):
    return slice(i * size, (i + 1) * size)


def cols_of(i, size, base=0):
    return slice(base + i * size, base + (i + 1) * size)


def unit(x):
    center = x - jnp.mean(x, axis=-1, keepdims=True)
    factor = lax.rsqrt(jnp.mean(center * center, axis=-1, keepdims=True) + EPSILON)
    return center * factor, factor


def norm_chunks(src, dst, gain, shift):
    def body(i):
        at = rows_of(i, CHUNK)
        w, _ = unit(src[at, :].astype(F32))
        dst[at, :] = (w * gain + shift).astype(BF)

    loop(src.shape[0] // CHUNK, body)


def fold(x):
    return jnp.sum(x.reshape(x.shape[0] // 8, 8, x.shape[1]), axis=0)


def norm_back_chunks(gn_ref, x_ref, gain, base_of, store):
    columns = x_ref.shape[1]

    def body(i, carry):
        gain_sum, shift_sum = carry
        at = rows_of(i, CHUNK)
        gn = gn_ref[at, :]
        w, factor = unit(x_ref[at, :].astype(F32))
        scaled = gn * gain
        plain = jnp.mean(scaled, axis=-1, keepdims=True)
        cross = jnp.mean(scaled * w, axis=-1, keepdims=True)
        store(at, base_of(at) + factor * (scaled - plain - w * cross))
        return gain_sum + fold(gn * w), shift_sum + fold(gn)

    zero = jnp.zeros((8, columns), F32)
    gain_sum, shift_sum = zero, zero
    for i in range(x_ref.shape[0] // CHUNK):
        gain_sum, shift_sum = body(i, (gain_sum, shift_sum))
    return jnp.sum(gain_sum, axis=0, keepdims=True), jnp.sum(shift_sum, axis=0, keepdims=True)


def column_sums(ref, start, size):
    def body(i, total):
        return total + fold(ref[rows_of(i, CHUNK), start : start + size].astype(F32))

    total = jnp.zeros((8, size), F32)
    for i in range(ref.shape[0] // CHUNK):
        total = body(i, total)
    return jnp.sum(total, axis=0, keepdims=True)


def head_map(columns):
    feature = lax.broadcasted_iota(jnp.int32, (columns, 128), 0) // HD
    head = lax.broadcasted_iota(jnp.int32, (columns, 128), 1)
    return (feature == head).astype(BF)


def head_sums(a_ref, a_rows, a_base, b_ref, b_rows, b_base, heads):
    total = None
    for j in range(heads.shape[0] // WIDE):
        a = a_ref[a_rows, a_base + j * WIDE : a_base + (j + 1) * WIDE].astype(F32)
        b = b_ref[b_rows, b_base + j * WIDE : b_base + (j + 1) * WIDE].astype(F32)
        top = (a * b).astype(BF)
        rest = (a * b - top.astype(F32)).astype(BF)
        part = heads[j * WIDE : (j + 1) * WIDE, :]
        term = nn(top, part) + nn(rest, part)
        total = term if total is None else total + term
    return total


def places_only(value):
    return jnp.where(lax.broadcasted_iota(jnp.int32, value.shape, 0) < PLACES, value, 0.0)


def start(pairs, sems):
    copies = [pltpu.make_async_copy(s, d, sems.at[n]) for n, (s, d) in enumerate(pairs)]
    for copy in copies:
        copy.start()
    return copies


def wait(copies):
    for copy in copies:
        copy.wait()


def piece_views(bufs):
    return list(bufs)


def rows_at(place, rows, share=1, k=0):
    return pl.ds(pl.multiple_of((place * share + k) * rows, 16), rows)


def load(bufs, place_ref, w, sems):
    if len(bufs) == 1:
        return start([(bufs[0], w)], sems)
    views = piece_views(bufs)
    rows = views[0].shape[0]
    return start([(v, w.at[rows_at(place_ref[n], rows), :]) for n, v in enumerate(views)], sems)


ORDER = ((3, 0), (1, 0), (3, 1), (2, 1), (1, 1), (2, 0), (0, 0), (0, 1))


def store_pieces(dw, outs, place_ref, sems, share=1, base=0):
    if len(outs) == 1:
        return start([(dw, outs[0])], sems)
    half, columns = outs[0].shape[1], dw.shape[1]
    pairs = []
    for side, out in enumerate(outs):
        for n, (chip, top) in enumerate(ORDER):
            place = place_ref[8 + side * 4 + chip]
            for k in range(share):
                source = dw.at[pl.ds(pl.multiple_of(((place * share + k) * 2 + top) * half, 16), half), :]
                pairs.append((source, out.at[n, :, base + k * columns : base + (k + 1) * columns]))
    return start(pairs, sems)


def piece_select(piece, rows, columns):
    lane = lax.broadcasted_iota(jnp.int32, (128, columns), 0)
    column = lax.broadcasted_iota(jnp.int32, (128, columns), 1)
    return ((lane < rows) & (column == piece * rows + lane)).astype(BF)


def spread_small(w, small_ref, hb_ref):
    columns = small_ref.shape[1]
    rows = columns // 8
    start = w.shape[1] - 128
    total = jnp.zeros((SMALL, columns), F32)
    for piece in range(8):
        block = w[piece * rows : piece * rows + SMALL, start:]
        total = total + nn(block, piece_select(piece, rows, columns))
        wide = block.astype(F32)
        for r in range(3):
            at = (piece * 3 + r) * 128
            hb_ref[0:1, at : at + 128] = wide[8 + r : 9 + r, :]
    small_ref[...] = total


def gather_small(dw, sums):
    sums_t, sums_s, sums_f, ghb = sums
    columns = sums_t.shape[1]
    rows = columns // 8
    start = dw.shape[1] - 128
    zero = jnp.zeros((3, columns), F32)
    order = [sums_t[0:4, :], sums_s[0:3, :], sums_f[0:1, :], zero, sums_t[4:5, :], sums_s[3:4, :], sums_f[1:2, :]]
    order += [sums_t[5:6, :], sums_s[4:5, :], sums_f[2:3, :], jnp.zeros((SMALL - 17, columns), F32)]
    values = jnp.concatenate(order, axis=0).astype(BF)
    for piece in range(8):
        block = nt(values, piece_select(piece, rows, columns))
        hidden = [ghb[0:1, (piece * 3 + r) * 128 : (piece * 3 + r + 1) * 128] for r in range(3)]
        block = jnp.concatenate([block[0:8, :]] + hidden + [block[11:, :]], axis=0)
        dw[piece * rows : piece * rows + SMALL, start:] = block.astype(BF)
        dw[piece * rows + SMALL : (piece + 1) * rows, start:] = jnp.zeros((rows - SMALL, 128), BF)


def load_feed(bufs, place_ref, we, wr, sems):
    if len(bufs) == 2:
        return start([(bufs[0], we)], sems), start([(bufs[1], wr)], sems.at[8:])
    views = piece_views(bufs)
    rows, units, columns = views[0].shape[0], we.shape[1], wr.shape[1]
    share = units // columns
    first = start([(v.at[:, 0:units], we.at[rows_at(place_ref[n], rows), :]) for n, v in enumerate(views)], sems)
    pairs = []
    for n, v in enumerate(views):
        for k in range(share):
            to = rows_at(place_ref[n], rows, share, k)
            pairs.append((v.at[:, units + k * columns : units + (k + 1) * columns], wr.at[to, :]))
    return first, start(pairs, sems.at[8:])


class Late:
    def __init__(self, source, target, sem):
        self.target = target
        self.copy = pltpu.make_async_copy(source, target, sem)
        self.copy.start()

    def get(self):
        if self.copy is not None:
            self.copy.wait()
            self.copy = None
        return self.target


class Early:
    def __init__(self, ref, target, sem):
        self.ref = ref
        self.copy = pltpu.make_async_copy(ref, target, sem)

    def send(self):
        self.copy.start()


SPACES = {
    "v": pl.BlockSpec(memory_space=pltpu.VMEM),
    "a": pl.BlockSpec(memory_space=pl.ANY),
    "l": pl.BlockSpec(memory_space=pl.ANY),
    "e": pl.BlockSpec(memory_space=pl.ANY),
    "s": pl.BlockSpec(memory_space=pltpu.SMEM),
}


def call(body, operands, spaces, outs, out_spaces, scratch, micros, name, tight=True):
    late = [n for n, space in enumerate(spaces) if space == "l"]
    early = [n for n, space in enumerate(out_spaces) if space == "e"]
    n_in, n_out, n_scratch = len(operands), len(outs), len(scratch)

    def kernel(*refs):
        ins, refs = list(refs[:n_in]), refs[n_in:]
        results, refs = list(refs[:n_out]), refs[n_out:]
        own, refs = refs[:n_scratch], refs[n_scratch:]
        held, refs = refs[: len(late)], refs[len(late) :]
        filled, refs = refs[: len(early)], refs[len(early) :]
        late_sems, early_sems = refs
        for k, n in enumerate(late):
            ins[n] = Late(ins[n], held[k], late_sems.at[k])
        for k, n in enumerate(early):
            results[n] = Early(filled[k], results[n], early_sems.at[k])
        body(ins, results, own)
        for n in late:
            ins[n].get()
        for n in early:
            results[n].copy.wait()

    held = [operands[n].size * operands[n].dtype.itemsize for n, space in enumerate(spaces) if space in "vl"]
    held += [math.prod(outs[n][0]) * jnp.dtype(outs[n][1]).itemsize for n, space in enumerate(out_spaces) if space in "ve"]
    held += [math.prod(ref.shape) * jnp.dtype(ref.dtype).itemsize for ref in scratch if "semaphore" not in str(ref.memory_space)]
    limit = min(VMEM_LIMIT, sum(held) + SPARE) if tight else VMEM_LIMIT
    more = [pltpu.VMEM(operands[n].shape, operands[n].dtype) for n in late]
    more += [pltpu.VMEM(*outs[n]) for n in early]
    more += [pltpu.SemaphoreType.DMA((max(1, len(late)),)), pltpu.SemaphoreType.DMA((max(1, len(early)),))]
    return pl.pallas_call(
        kernel,
        out_shape=[jax.ShapeDtypeStruct(s, d) for s, d in outs],
        in_specs=[SPACES[space] for space in spaces],
        out_specs=[SPACES[space] for space in out_spaces],
        scratch_shapes=list(scratch) + more,
        compiler_params=pltpu.CompilerParams(vmem_limit_bytes=limit),
        cost_estimate=pl.CostEstimate(flops=micros * MICRO, bytes_accessed=0, transcendentals=0),
        name=name,
    )(*operands)


def blocks_of(count):
    return [slice(j * WIDE, (j + 1) * WIDE) for j in range(count // WIDE)]


def shifted(at, base):
    return slice(at.start + base, at.stop + base)


def entry(normed, w, qkv, query_bias, value_bias):
    columns = normed.shape[1]
    for part, bias in enumerate((query_bias, None, value_bias)):
        for at in blocks_of(columns):
            to = shifted(at, part * columns)
            packed = nn(normed[...], w[:, to])
            qkv[:, to] = (packed if bias is None else packed + bias[:, at]).astype(BF)


def time_forward(n, ins, results, own):
    place_ref, x_ref, *rest = ins
    given, bufs = rest[: len(rest) - n], rest[len(rest) - n :]
    nt_out, qkv_out, o_out, e_out, p_out, y_ref, small_ref, hb_ref = results
    w, sems = own
    columns = x_ref.shape[1]
    wait(load(bufs, place_ref, w, sems))
    if given:
        small_ref[...] = given[0][...]
        hb_ref[...] = given[1][...]
    else:
        spread_small(w, small_ref, hb_ref)
    norm_chunks(x_ref, nt_out.ref, small_ref[11:12, :], small_ref[14:15, :])
    nt_out.send()
    qkv_ref, o_ref, e_ref, p_ref = qkv_out.ref, o_out.ref, e_out.ref, p_out.ref
    entry(nt_out.ref, w, qkv_ref, small_ref[0:1, :], small_ref[1:2, :])
    qkv_out.send()
    heads = head_map(columns)
    for clip in range(x_ref.shape[0] // (FRAMES * BLOCK)):
        at = [slice((clip * FRAMES + f) * BLOCK, (clip * FRAMES + f + 1) * BLOCK) for f in range(FRAMES)]
        weights = []
        for f in range(FRAMES):
            s = [head_sums(qkv_ref, at[f], 0, qkv_ref, at[g], columns, heads) * HD ** (-0.5) for g in range(FRAMES)]
            peak = jnp.maximum(s[0], s[1])
            powered = [jnp.exp(score - peak) for score in s]
            inverse = 1.0 / (powered[0] + powered[1])
            for g in range(FRAMES):
                m = (clip * FRAMES + f) * FRAMES + g
                p = powered[g] * inverse
                p_ref[m * BLOCK : (m + 1) * BLOCK, :] = p
                weights.append(p.astype(BF))
        for to in blocks_of(columns):
            v = [qkv_ref[a, shifted(to, 2 * columns)].astype(F32) for a in at]
            for f in range(FRAMES):
                spread = [nt(weights[FRAMES * f + g], heads[to, :]) for g in range(FRAMES)]
                o_ref[at[f], to] = (spread[0] * v[0] + spread[1] * v[1]).astype(BF)
    p_out.send()
    o_out.send()
    for at in blocks_of(columns):
        e_ref[:, at] = (nn(o_ref[...], w[:, shifted(at, 3 * columns)]) + small_ref[2:3, at]).astype(BF)
    e_out.send()
    for at in blocks_of(columns):
        branch = nn(e_ref[...], w[:, shifted(at, 4 * columns)]) + small_ref[3:4, at]
        for block in range(x_ref.shape[0] // BLOCK):
            rows = rows_of(block, BLOCK)
            y_ref[rows, at] = x_ref[rows, at].astype(F32) + places_only(branch[rows, :])


def half_masks():
    lane = lax.broadcasted_iota(jnp.int32, (1, 128), 1)
    return (lane < HD).astype(BF), (lane >= HD).astype(BF)


def space_forward(n, ins, results, own):
    place_ref, y_ref, small_ref, *bufs = ins
    ns_out, qkv_out, p_out, o_out, z_ref = results
    w, sems = own
    columns = y_ref.shape[1]
    blocks = y_ref.shape[0] // BLOCK
    pairs = columns // 128
    copies = load(bufs, place_ref, w, sems)
    norm_chunks(y_ref, ns_out.ref, small_ref[12:13, :], small_ref[15:16, :])
    ns_out.send()
    wait(copies)
    qkv_ref, p_ref, o_ref = qkv_out.ref, p_out.ref, o_out.ref
    entry(ns_out.ref, w, qkv_ref, small_ref[4:5, :], small_ref[5:6, :])
    qkv_out.send()
    masks = half_masks()
    first = lax.broadcasted_iota(jnp.int32, (BLOCK, 128), 1) < HD
    column = lax.broadcasted_iota(jnp.int32, (1, BLOCK), 1)
    hidden = jnp.where(column <= PLACES, 0.0, -1e30)

    def attend(block):
        at = rows_of(block, BLOCK)
        columns_of = [[slice(part * columns + k * 128, part * columns + (k + 1) * 128) for k in range(pairs)] for part in range(3)]
        scores = []
        for k in range(pairs):
            query, key = qkv_ref[at, columns_of[0][k]], qkv_ref[at, columns_of[1][k]]
            scores += [nt(query * mask, key) * HD ** (-0.5) + hidden for mask in masks]
        powered = [jnp.exp(s - jnp.max(s, axis=-1, keepdims=True)) for s in scores]
        weights = [(e * (1.0 / jnp.sum(e, axis=-1, keepdims=True))).astype(BF) for e in powered]
        for k in range(pairs):
            value = qkv_ref[at, columns_of[2][k]]
            for half in range(2):
                p_ref[(block * pairs + k) * 2 + half] = weights[2 * k + half]
            mixed = jnp.where(first, nn(weights[2 * k], value), nn(weights[2 * k + 1], value))
            o_ref[at, columns_of[0][k]] = mixed.astype(BF)

    loop(blocks, attend)
    p_out.send()
    o_out.send()
    is_class = lax.broadcasted_iota(jnp.int32, (BLOCK - EDGE, WIDE), 0) == CLASS
    for at in blocks_of(columns):
        branch = nn(o_ref[...], w[:, shifted(at, 3 * columns)]) + small_ref[6:7, at]
        z_ref[:, at] = y_ref[:, at] + branch
        for clip in range(blocks // FRAMES):
            edges = [slice((clip * FRAMES + f) * BLOCK + EDGE, (clip * FRAMES + f + 1) * BLOCK) for f in range(FRAMES)]
            mean = (branch[edges[0], :] + branch[edges[1], :]) * (1.0 / FRAMES)
            for edge in edges:
                z_ref[edge, at] = y_ref[edge, at] + jnp.where(is_class, mean, branch[edge, :])


def gelu_both(h):
    cdf = 0.5 * (1.0 + lax.erf(h * 0.5**0.5))
    density = jnp.exp(h * h * -0.5) * 0.3989422804014327
    return h * cdf, cdf + h * density


def feed_out(ins, results, own):
    place_ref, z_ref, g_ref, small_ref, hb_ref, *bufs = ins
    out_ref, nm_out, gh_out, sums_ref, *outs = results
    we, wr, dwr, a, sems, out_sems = own
    nm, gh = nm_out.ref, gh_out.ref
    columns = z_ref.shape[1]
    units = we.shape[1]
    copies, more = load_feed(bufs, place_ref, we, wr, sems)
    norm_chunks(z_ref, nm, small_ref[13:14, :], small_ref[16:17, :])
    nm_out.send()
    wait(copies + more)

    def inner(j):
        at = cols_of(j, WIDE)
        h = nn(nm[...], we[:, at]) + hb_ref[0:1, at]
        active, slope = gelu_both(h)
        a[:, at] = active.astype(BF)
        gh[:, at] = (nt(g_ref[...], wr[rows_of(j, WIDE), :]) * slope).astype(BF)

    loop(units // WIDE, inner)
    gh_out.send()

    def left(j):
        dwr[rows_of(j, WIDE), :] = tn(a[:, cols_of(j, WIDE)], g_ref[...]).astype(BF)

    loop(units // WIDE, left)
    copies = store_pieces(dwr, outs, place_ref, out_sems, units // columns)
    for at in blocks_of(columns):
        out_ref[:, at] = (z_ref[:, at] + (nn(a[...], wr[:, at]) + small_ref[7:8, at])).astype(BF)
    sums_ref[0:1, :] = column_sums(g_ref, 0, columns)
    wait(copies)


def feed_in(ins, results, own):
    place_ref, gh, nm = ins
    ghb_ref, *outs = results
    dwe, out_sems = own
    units = gh.shape[1]

    def right(j):
        at = cols_of(j, WIDE)
        block = gh[:, at]
        dwe[:, at] = tn(nm[...], block).astype(BF)
        ghb_ref[0:1, at] = jnp.sum(block.astype(F32), axis=0, keepdims=True)

    loop(units // WIDE, right)
    wait(store_pieces(dwe, outs, place_ref, out_sems))


def norm_backward(row, n, ins, results, own):
    place_ref, gh_ref, x_in, base_in, small_ref, *bufs = ins
    gz_ref, sums_ref = results
    w, gn, sems = own
    columns = gz_ref.shape[1]
    views = [b.at[:, 0 : w.shape[1]] for b in bufs]
    wait(load(views, place_ref, w, sems))
    for at in blocks_of(columns):
        gn[:, at] = nt(gh_ref[...], w[at, :])
    x_ref, base = x_in.get(), base_in.get()

    def store(at, value):
        gz_ref[at, :] = value

    gain_sum, shift_sum = norm_back_chunks(
        gn, x_ref, small_ref[row : row + 1, :], lambda at: base[at, :].astype(F32), store
    )
    sums_ref[0:1, :] = gain_sum
    sums_ref[1:2, :] = shift_sum


def space_backward(n, ins, results, own):
    place_ref, gz_ref, ns_in, qkv_in, p_in, o_in, *rest = ins
    bufs = rest[:n]
    gqkv_out, sums_ref, *outs = results
    w, dw_ref, gbs, go, sems, out_sems = own
    columns = gz_ref.shape[1]
    rows = gz_ref.shape[0]
    clips = rows // (BLOCK * FRAMES)
    pairs = columns // 128
    copies = load([b.at[:, 3 * columns : 4 * columns] for b in bufs], place_ref, w, sems)

    def lower(i):
        at = rows_of(i, CHUNK)
        gbs[at, :] = gz_ref[at, :].astype(BF)

    loop(rows // CHUNK, lower)
    is_class = lax.broadcasted_iota(jnp.int32, (BLOCK - EDGE, columns), 0) == CLASS
    for clip in range(clips):
        edges = [slice((clip * FRAMES + f) * BLOCK + EDGE, (clip * FRAMES + f + 1) * BLOCK) for f in range(FRAMES)]
        share = gz_ref[edges[0], :] * (1.0 / FRAMES)
        for edge in edges:
            gbs[edge, :] = jnp.where(is_class, share, gz_ref[edge, :]).astype(BF)
    wait(copies)
    for at in blocks_of(columns):
        go[:, at] = nt(gbs[...], w[at, :]).astype(BF)
    o_ref, qkv_ref, p_ref, gqkv = o_in.get(), qkv_in.get(), p_in.get(), gqkv_out.ref
    for at in blocks_of(columns):
        dw_ref[:, shifted(at, 3 * columns)] = tn(o_ref[...], gbs[:, at]).astype(BF)
    masks = half_masks()
    first = lax.broadcasted_iota(jnp.int32, (BLOCK, 128), 1) < HD
    class_row = lax.broadcasted_iota(jnp.int32, (BLOCK - EDGE, 128), 0) == CLASS
    together = 2

    def attend(step):
        parts = []
        for u in range(together):
            clip, pair = (step * together + u) // pairs, (step * together + u) % pairs
            for f in range(FRAMES):
                block = clip * FRAMES + f
                at = rows_of(block, BLOCK)
                q, k, v = (qkv_ref[at, cols_of(pair, 128, part * columns)] for part in range(3))
                grad = go[at, cols_of(pair, 128)]
                parts += [(q, k, v, grad, mask, p_ref[2 * (block * pairs + pair) + half]) for half, mask in enumerate(masks)]
        gp = [nt(grad * mask, v) for _, _, v, grad, mask, _ in parts]
        p = [part[5].astype(F32) for part in parts]
        shared = [jnp.sum(a * b, axis=-1, keepdims=True) for a, b in zip(gp, p)]
        gs = [(b * (a - c)).astype(BF) for a, b, c in zip(gp, p, shared)]
        scale = HD ** (-0.5)
        gq = [nn(a, part[1]) * scale for a, part in zip(gs, parts)]
        gv = [tn(part[5], part[3]) for part in parts]
        gk = [tn(a, part[0]) * scale for a, part in zip(gs, parts)]
        for u in range(together):
            clip, pair = (step * together + u) // pairs, (step * together + u) % pairs
            for part, values in enumerate((gq, gk, gv)):
                to = cols_of(pair, 128, part * columns)
                one, two = (jnp.where(first, values[4 * u + 2 * f], values[4 * u + 2 * f + 1]) for f in range(FRAMES))
                top = clip * FRAMES * BLOCK
                gqkv[pl.ds(top, EDGE), to] = one[:EDGE].astype(BF)
                gqkv[pl.ds(top + BLOCK, EDGE), to] = two[:EDGE].astype(BF)
                both = jnp.where(class_row, one[EDGE:] + two[EDGE:], one[EDGE:])
                gqkv[pl.ds(top + EDGE, BLOCK - EDGE), to] = both.astype(BF)
                rest = jnp.where(class_row, 0.0, two[EDGE:])
                gqkv[pl.ds(top + BLOCK + EDGE, BLOCK - EDGE), to] = rest.astype(BF)

    loop(clips * pairs // together, attend)
    gqkv_out.send()
    ns_ref = ns_in.get()
    for at in blocks_of(3 * columns):
        dw_ref[:, at] = tn(ns_ref[...], gqkv[:, at]).astype(BF)
    copies = store_pieces(dw_ref, outs, place_ref, out_sems)
    sums_ref[0:1, :] = column_sums(gqkv, 0, columns)
    sums_ref[1:2, :] = column_sums(gqkv, 2 * columns, columns)
    sums_ref[2:3, :] = column_sums(gbs, 0, columns)
    wait(copies)


def mixer_backward(n, ins, results, own):
    place_ref, gy_ref, o_in, e_in, *bufs = ins
    go_out, sums_ref, *outs = results
    w, dw_ref, grt, get, sems, out_sems = own
    columns = gy_ref.shape[1]
    rows = gy_ref.shape[0]
    copies = load([b.at[:, 3 * columns : 5 * columns] for b in bufs], place_ref, w, sems)

    def lower(block):
        at = rows_of(block, BLOCK)
        grt[at, :] = places_only(gy_ref[at, :]).astype(BF)

    loop(rows // BLOCK, lower)
    wait(copies)
    go = go_out.ref
    for at in blocks_of(columns):
        get[:, at] = nt(grt[...], w[at, columns : 2 * columns]).astype(BF)
    e_ref, o_ref = e_in.get(), o_in.get()
    for at in blocks_of(columns):
        dw_ref[:, shifted(at, columns)] = tn(e_ref[...], grt[:, at]).astype(BF)
    for at in blocks_of(columns):
        dw_ref[:, at] = tn(o_ref[...], get[:, at]).astype(BF)
    copies = store_pieces(dw_ref, outs, place_ref, out_sems)
    for at in blocks_of(columns):
        go[:, at] = nt(get[...], w[at, 0:columns]).astype(BF)
    go_out.send()
    sums_ref[2:3, :] = column_sums(get, 0, columns)
    sums_ref[3:4, :] = column_sums(grt, 0, columns)
    wait(copies)


def time_backward(n, ins, results, own):
    place_ref, go, qkv_ref, p_ref, x_in, gy_in, small_ref, before, *bufs = ins
    gqkv_out, gx_ref, sums_ref = results
    w, gn, sems = own
    columns = gx_ref.shape[1]
    rows = gx_ref.shape[0]
    gqkv = gqkv_out.ref
    copies = load([b.at[:, 0 : 3 * columns] for b in bufs], place_ref, w, sems)
    heads = head_map(columns)
    for clip in range(rows // (FRAMES * BLOCK)):
        at = [slice((clip * FRAMES + f) * BLOCK, (clip * FRAMES + f + 1) * BLOCK) for f in range(FRAMES)]
        gs, kept = [], []
        for f in range(FRAMES):
            gp = [head_sums(go, at[f], 0, qkv_ref, at[g], 2 * columns, heads) for g in range(FRAMES)]
            first = ((clip * FRAMES + f) * FRAMES) * BLOCK
            p = [p_ref[first + g * BLOCK : first + (g + 1) * BLOCK, :] for g in range(FRAMES)]
            shared = gp[0] * p[0] + gp[1] * p[1]
            gs += [(p[g] * (gp[g] - shared)).astype(BF) for g in range(FRAMES)]
            kept += [p[g].astype(BF) for g in range(FRAMES)]
        for block in blocks_of(columns):
            to = [shifted(block, part * columns) for part in range(3)]
            q, k = ([qkv_ref[a, to[part]].astype(F32) for a in at] for part in range(2))
            grad = [go[a, block].astype(F32) for a in at]
            scaled = heads[block, :] * BF(HD ** (-0.5))
            spread = [nt(value, scaled) for value in gs]
            for f in range(FRAMES):
                gqkv[at[f], to[0]] = (spread[2 * f] * k[0] + spread[2 * f + 1] * k[1]).astype(BF)
                gqkv[at[f], to[1]] = (spread[f] * q[0] + spread[2 + f] * q[1]).astype(BF)
            spread = [nt(value, heads[block, :]) for value in kept]
            for f in range(FRAMES):
                gqkv[at[f], to[2]] = (spread[f] * grad[0] + spread[2 + f] * grad[1]).astype(BF)
    gqkv_out.send()
    wait(copies)
    for at in blocks_of(columns):
        gn[:, at] = nt(gqkv[...], w[at, :])
    x_ref, gy_ref = x_in.get(), gy_in.get()

    def store(at, value):
        gx_ref[at, :] = value.astype(BF)

    gain_sum, shift_sum = norm_back_chunks(gn, x_ref, small_ref[11:12, :], lambda at: gy_ref[at, :], store)
    sums_ref[0:1, :] = column_sums(gqkv, 0, columns)
    sums_ref[1:2, :] = column_sums(gqkv, 2 * columns, columns)
    sums_ref[2:4, :] = before[2:4, :]
    sums_ref[4:5, :] = gain_sum
    sums_ref[5:6, :] = shift_sum


def time_weights(ins, results, own):
    place_ref, gqkv, nt_ref, *sums = ins
    dw_ref, out_sems = own
    columns = nt_ref.shape[1]
    for at in blocks_of(3 * columns):
        dw_ref[:, at] = tn(nt_ref[...], gqkv[:, at]).astype(BF)
    if sums:
        gather_small(dw_ref, sums)
    wait(store_pieces(dw_ref, results, place_ref, out_sems))


def pack_rows(tokens, once):
    clips, _, columns = tokens.shape
    frames = []
    for f in range(FRAMES):
        places = tokens[:, 1 + f * PLACES : 1 + (f + 1) * PLACES]
        head = tokens[:, :1] if f == 0 or not once else jnp.zeros_like(tokens[:, :1])
        frames.append(jnp.concatenate([places, head, jnp.zeros((clips, BLOCK - PLACES - 1, columns), tokens.dtype)], axis=1))
    return jnp.stack(frames, axis=1).reshape(clips * FRAMES * BLOCK, columns)


def unpack_rows(rows, clips):
    framed = rows.reshape(clips, FRAMES, BLOCK, rows.shape[-1])
    return jnp.concatenate(
        [framed[:, 0, PLACES : PLACES + 1]] + [framed[:, f, :PLACES] for f in range(FRAMES)], axis=1
    )


class Layer:
    def __init__(self, rows, columns, units, shards, pieced, place):
        self.rows, self.columns, self.units = rows, columns, units
        self.pieced, self.place = pieced, place
        self.piece = columns // shards
        self.act = ((rows, columns), BF)
        self.act3 = ((rows, 3 * columns), BF)
        self.tall = ((rows, units), BF)
        self.wide = ((rows, columns), F32)
        self.sums = ((8, columns), F32)

    def grads(self, width):
        if self.pieced:
            return [((8, self.piece // 2, width), BF)] * 2
        return [((self.columns, width), BF)]

    def vmem(self, *shapes):
        return [pltpu.VMEM(s, d) for s, d in shapes]

    def sems(self, *counts):
        return [pltpu.SemaphoreType.DMA((count,)) for count in counts]

    def time_forward(self, x, given, bufs):
        c, n = self.columns, len(bufs)
        extra = [((SMALL, c), F32), ((8, self.units), F32)]
        return call(
            functools.partial(time_forward, n), (self.place, x, *given, *bufs), "sv" + "v" * len(given) + "a" * n,
            [self.act, self.act3, self.act, self.act, ((self.rows * FRAMES, 128), F32), self.wide] + extra, "eeeeevvv",
            self.vmem(((c, bufs[0].shape[1]), BF)) + self.sems(8), 14, "time_forward", False,
        )

    def space_forward(self, y, small, bufs):
        c, n = self.columns, len(bufs)
        probs = ((self.rows // BLOCK * (c // 128) * 2, BLOCK, BLOCK), BF)
        return call(
            functools.partial(space_forward, n), (self.place, y, small, *bufs), "svv" + "a" * n,
            [self.act, self.act3, probs, self.act, self.wide], "eeeev",
            self.vmem(((c, 4 * c), BF)) + self.sems(8), 16, "space_forward", False,
        )

    def feed_out(self, z, g, small, hb, bufs):
        c, u, n = self.columns, self.units, len(bufs)
        outs = self.grads(u) if self.pieced else [((u, c), BF)]
        return call(
            feed_out, (self.place, z, g, small, hb, *bufs), "svvvv" + "a" * n,
            [self.act, self.act, self.tall, self.sums] + outs, "veev" + "a" * len(outs),
            self.vmem(((c, u), BF), ((u, c), BF), ((u, c), BF), self.tall) + self.sems(40, 64), 30, "feed_out", False,
        )

    def feed_in(self, gh, normed):
        c, u = self.columns, self.units
        outs = self.grads(u)
        return call(
            feed_in, (self.place, gh, normed), "svv", [((8, u), F32)] + outs, "v" + "a" * len(outs),
            self.vmem(((c, u), BF)) + self.sems(16), 8, "feed_in",
        )

    def norm_backward(self, row, gh, x, base, small, bufs, name):
        c, n, wide = self.columns, len(bufs), gh.shape[1]
        return call(
            functools.partial(norm_backward, row, n), (self.place, gh, x, base, small, *bufs), "svllv" + "a" * n,
            [self.wide, self.sums], "vv", self.vmem(((c, wide), BF), self.wide) + self.sems(8), 10, name,
        )

    def space_backward(self, gz, normed, qkv, p, o, bufs):
        c, n = self.columns, len(bufs)
        outs = self.grads(4 * c)
        return call(
            functools.partial(space_backward, n), (self.place, gz, normed, qkv, p, o, *bufs), "svllll" + "a" * n,
            [self.act3, self.sums] + outs, "ev" + "a" * len(outs),
            self.vmem(((c, c), BF), ((c, 4 * c), BF), self.act, self.act) + self.sems(8, 16), 20, "space_backward",
        )

    def mixer_backward(self, gy, o, e, bufs):
        c, n = self.columns, len(bufs)
        outs = self.grads(2 * c)
        return call(
            functools.partial(mixer_backward, n), (self.place, gy, o, e, *bufs), "svll" + "a" * n,
            [self.act, self.sums] + outs, "ev" + "a" * len(outs),
            self.vmem(((c, 2 * c), BF), ((c, 2 * c), BF), self.act, self.act) + self.sems(8, 16), 8, "mixer_backward",
        )

    def time_backward(self, go, qkv, p, x, gy, small, before, bufs):
        c, n = self.columns, len(bufs)
        return call(
            functools.partial(time_backward, n), (self.place, go, qkv, p, x, gy, small, before, *bufs),
            "svvvllvv" + "a" * n, [self.act3, self.act, self.sums], "evv",
            self.vmem(((c, 3 * c), BF), self.wide) + self.sems(8), 12, "time_backward",
        )

    def time_weights(self, gqkv, normed, sums):
        c = self.columns
        width = 3 * c + (128 if sums else 0)
        outs = self.grads(width)
        return call(
            time_weights, (self.place, gqkv, normed, *sums), "svv" + "v" * len(sums), outs, "a" * len(outs),
            self.vmem(((c, width), BF)) + self.sems(16), 8, "time_weights",
        )


BOTH = ("grp", "shard")


def permute(value, target):
    shards = lax.axis_size("shard")
    pairs = [(z * shards + s, z * shards + target(s)) for z in range(lax.axis_size("grp")) for s in range(shards)]
    return lax.ppermute(value, BOTH, pairs)


def to_sibling(value):
    return permute(value, lambda s: s ^ 1)


def along_x(value):
    return permute(value, lambda s: s ^ 2)


def along_y(value):
    return permute(value, lambda s: s ^ 4)


def near_hop(value):
    return permute(value, lambda s: s ^ (2 if s % 2 == 0 else 4))


def far_hop(value):
    return permute(value, lambda s: s ^ (4 if s % 2 == 0 else 2))


def places(s):
    near = jnp.where(s % 2 == 0, 2, 4)
    far = 6 - near
    gathered = [s, s ^ 1, s ^ near, s ^ near ^ 1, s ^ 6, s ^ 1 ^ far, s ^ far, s ^ 7]
    kept = [s, s ^ 2, s ^ 4, s ^ 6]
    return jnp.stack(gathered + kept + [k ^ 1 for k in kept]).astype(jnp.int32)


def total(*terms):
    return sum(t.astype(F32) for t in terms).astype(BF)


class Reduction:
    def __init__(self, keep, give):
        self.keep = keep
        self.got = to_sibling(give)

    def own(self, start, stop):
        return self.keep[start:stop], self.got[start:stop]

    def first(self):
        return total(*self.own(0, 2)), total(*self.own(2, 4))

    def cross(self, sent):
        self.from_x, self.from_y = along_x(sent[0]), along_y(sent[1])

    def second(self):
        return total(*self.own(4, 5), self.from_y[:1]), total(*self.own(5, 6), self.from_x[:1])

    def cross_again(self, sent):
        self.last_x, self.last_y = along_x(sent[0]), along_y(sent[1])

    def finish(self):
        top = total(*self.own(6, 7), self.from_x[1:], self.last_y)
        bottom = total(*self.own(7, 8), self.from_y[1:], self.last_x)
        return top[0], bottom[0]


def beside(*values):
    return jnp.concatenate([v[n : n + 1] for v in values for n in range(v.shape[0])], axis=2)


def apart(value, widths):
    stops = [sum(widths[: n + 1]) for n in range(len(widths))]
    return [value[..., stop - width : stop] for stop, width in zip(stops, widths)]


def hand_over(arrived, ahead, behind):
    widths = (ahead.keep.shape[2], behind.keep.shape[2], behind.keep.shape[2])
    ahead.last_x, *from_x = apart(arrived[0], widths)
    ahead.last_y, *from_y = apart(arrived[1], widths)
    behind.from_x, behind.from_y = jnp.concatenate(from_x, axis=0), jnp.concatenate(from_y, axis=0)


def tie(*values):
    leaves, shape = jax.tree.flatten(values)
    return jax.tree.unflatten(shape, lax.optimization_barrier(tuple(leaves)))


def swap_z(value):
    shards = lax.axis_size("shard")
    pairs = [(z * shards + s, (z ^ 1) * shards + s) for z in range(lax.axis_size("grp")) for s in range(shards)]
    return lax.ppermute(value, BOTH, pairs)


def across_pairs(value):
    return lax.ppermute(value, "grp", [(z, z ^ 2) for z in range(4)])


def split_groups(halves, even):
    low, high = halves
    return jnp.where(even, low, high), jnp.where(even, high, low)


def join_groups(held, other, even):
    return jnp.concatenate([jnp.where(even, held, other), jnp.where(even, other, held)], axis=0)


def local(video, cotangent, live, time_entry, time_exit, time_mixer, space_entry, space_exit, hidden_expand, hidden_reduce, bias_rows, hidden_bias, norm_gain, norm_shift):
    clips, _, tokens, columns = video.shape
    shards, groups = lax.axis_size("shard"), lax.axis_size("grp")
    mine = lax.axis_index("shard")
    part = columns // shards
    units = hidden_bias.shape[0] * shards
    share = units // columns
    pieced = shards == 8 and groups == 4

    def gather(value):
        return lax.all_gather(value, "shard", axis=0, tiled=True)

    flags = live.astype(BF)[:, :, None]

    own_t = jnp.concatenate([time_entry, time_exit, time_mixer], axis=1)
    own_s = jnp.concatenate([space_entry, space_exit], axis=1)
    if pieced:
        narrow = jnp.concatenate([norm_gain, norm_shift], axis=0)
        narrow = jnp.concatenate(
            [jnp.pad(bias_rows, ((0, 0), (0, 128 - part))), hidden_bias.reshape(-1, 128), jnp.pad(narrow, ((0, 0), (0, 128 - part)))], axis=0
        )
        own_t = jnp.concatenate([own_t, jnp.pad(narrow, ((0, part - narrow.shape[0]), (0, 0)))], axis=1)
        own_f = jnp.concatenate([hidden_expand] + [hidden_reduce[k * part : (k + 1) * part] for k in range(share)], axis=1)
        net = Layer(clips * FRAMES * BLOCK, columns, units, shards, pieced, places(mine))
        pair_t = to_sibling(own_t)
        pair_t, own_t, video, own_s, own_f = tie(pair_t, own_t, video, own_s, own_f)
        hop_t = (near_hop(own_t), near_hop(pair_t))
        x = pack_rows(video[:, 0], False)
        pair_s, pair_f = to_sibling(own_s), to_sibling(own_f)
        first_t, x, pair_s, pair_f = tie(hop_t[0], x, pair_s, pair_f)
        second_t, own_s, own_f, pair_s, pair_f = tie(far_hop(first_t), own_s, own_f, pair_s, pair_f)
        gone_t = tuple(to_sibling(v) for v in (first_t, hop_t[1], second_t))
        wt = (own_t, pair_t, first_t, hop_t[1], second_t, *gone_t)
        hop_s, hop_f = ((near_hop(own), near_hop(pair)) for own, pair in ((own_s, pair_s), (own_f, pair_f)))
        normed_t, qkv_t, o_t, e_t, p_t, y, small, hb = net.time_forward(x, (), wt)
        first_s, last_s, y, cotangent = tie(*hop_s, y, cotangent)
        g = pack_rows(cotangent[:, 0] * flags, True)
        second_s = far_hop(first_s)
        ws = (own_s, pair_s, first_s, last_s, second_s, *(to_sibling(v) for v in (first_s, last_s, second_s)))
        first_f, y, ws, g = tie(hop_f[0], y, ws, g)
        normed_s, qkv_s, p_s, o_s, z = net.space_forward(y, small, ws)
        second_f, last_f, z = tie(far_hop(first_f), hop_f[1], z)
        wf = (own_f, pair_f, first_f, last_f, second_f, *(to_sibling(v) for v in (first_f, last_f, second_f)))
    else:
        x, g = pack_rows(video[:, 0], False), pack_rows(cotangent[:, 0] * flags, True)
        net = Layer(clips * FRAMES * BLOCK, columns, units, shards, pieced, jnp.zeros((16,), jnp.int32))
        packed = jnp.concatenate([bias_rows, norm_gain, norm_shift], axis=0)
        spread = lax.all_gather(packed, "shard", axis=0).transpose(1, 0, 2).reshape(-1, columns).astype(F32)
        small = jnp.concatenate([spread[:8], jnp.zeros((3, columns), F32), spread[8:], jnp.zeros((SMALL - 17, columns), F32)], axis=0)
        given = (small, jnp.pad(gather(hidden_bias).astype(F32)[None], ((0, 7), (0, 0))))
        wt, ws, wf = (gather(own_t),), (gather(own_s),), (gather(hidden_expand), gather(hidden_reduce))
        normed_t, qkv_t, o_t, e_t, p_t, y, small, hb = net.time_forward(x, given, wt)
        normed_s, qkv_s, p_s, o_s, z = net.space_forward(y, small, ws)

    out, normed_f, gh, sums_f, *grad_r = net.feed_out(z, g, small, hb, wf)
    if pieced:
        sum_r = Reduction(*grad_r)
    ghb, *grad_e = net.feed_in(gh, normed_f)
    if pieced:
        sum_e = Reduction(*grad_e)
        sent_r, gh, ghb, sums_f, sum_e.keep = tie(sum_r.first(), gh, ghb, sums_f, sum_e.keep)
        sum_r.cross(sent_r)
    gz, norm_f = net.norm_backward(13, gh, z, g, small, wf if pieced else wf[:1], "feed_norm")
    if pieced:
        sent = [beside(last, both) for last, both in zip(sum_r.second(), sum_e.first())]
        sent, gz, norm_f = tie(sent, gz, norm_f)
        arrived = (along_x(sent[0]), along_y(sent[1]))
    gqkv, sums_s, *grad_s = net.space_backward(gz, normed_s, qkv_s, p_s, o_s, ws)
    if pieced:
        sum_s = Reduction(*grad_s)
        hand_over(arrived, sum_r, sum_e)
        even = lax.axis_index("grp") % 2 == 0
        held_r, sent_r = split_groups(sum_r.finish(), even)
        held_r, sent_r, sent_e, gqkv, sums_s, sum_s.keep = tie(held_r, sent_r, sum_e.second(), gqkv, sums_s, sum_s.keep)
        sum_e.cross_again(sent_e)
        got_r = swap_z(sent_r)
    gy, norm_s = net.norm_backward(12, gqkv, y, gz, small, ws, "space_norm")
    if pieced:
        got_r, sum_e.last_x, sum_e.last_y, gy, norm_s = tie(got_r, sum_e.last_x, sum_e.last_y, gy, norm_s)
        held_e, sent_e = split_groups(sum_e.finish(), even)
        held_r, held_e, sent_e, sent_s, gy, norm_s = tie(total(held_r, got_r), held_e, sent_e, sum_s.first(), gy, norm_s)
        sum_s.cross(sent_s)
        got_r, got_e = across_pairs(held_r), swap_z(sent_e)
        sums_s = jnp.concatenate([sums_s[0:3], norm_s[0:2], sums_s[5:]], axis=0)
        sums_f = jnp.concatenate([sums_f[0:1], norm_f[0:2], sums_f[3:]], axis=0)
    go, sums_m, *grad_m = net.mixer_backward(gy, o_t, e_t, wt)
    if pieced:
        sum_m = Reduction(*grad_m)
        arrived = (got_r, got_e, sum_s.from_x, sum_s.from_y)
        arrived, go, sums_m, sum_m.keep = tie(arrived, go, sums_m, sum_m.keep)
        got_r, got_e, sum_s.from_x, sum_s.from_y = arrived
        sent = [beside(last, both) for last, both in zip(sum_s.second(), sum_m.first())]
        held_r, held_e, sent, go = tie(total(held_r, got_r), total(held_e, got_e), sent, go)
        arrived = (along_x(sent[0]), along_y(sent[1]), swap_z(held_r), across_pairs(held_e))
    gqkv, gx, sums_t = net.time_backward(go, qkv_t, p_t, x, gy, small, sums_m, wt)
    if pieced:
        arrived, gqkv, gx, sums_t, out = tie(arrived, gqkv, gx, sums_t, out)
        came_x, came_y, got_r, got_e = arrived
        hand_over((came_x, came_y), sum_s, sum_m)
        held_s, sent_s = split_groups(sum_s.finish(), even)
        held_s, sent_s, sent_m, gqkv = tie(held_s, sent_s, sum_m.second(), gqkv)
        sum_m.cross_again(sent_m)
        got_s = swap_z(sent_s)
    grad_t = net.time_weights(gqkv, normed_t, (sums_t, sums_s, sums_f, ghb) if pieced else ())

    if pieced:
        got_s, sum_m.last_x, sum_m.last_y, grad_t = tie(got_s, sum_m.last_x, sum_m.last_y, grad_t)
        sum_t = Reduction(*grad_t)
        held_s, held_e = total(held_s, got_s), total(held_e, got_e)
        held_m, sent_m = split_groups(sum_m.finish(), even)
        sent_t, held_s, held_e, held_m, sent_m, gx, out = tie(sum_t.first(), held_s, held_e, held_m, sent_m, gx, out)
        sum_t.cross(sent_t)
        got_s, got_m, got_e = across_pairs(held_s), swap_z(sent_m), swap_z(held_e)
        sum_t.from_x, sum_t.from_y, got_m = tie(sum_t.from_x, sum_t.from_y, got_m)
        held_m, sent_t = tie(total(held_m, got_m), sum_t.second())
        sum_t.cross_again(sent_t)
        got_m = across_pairs(held_m)
        sum_t.last_x, sum_t.last_y, got_s = tie(sum_t.last_x, sum_t.last_y, got_s)
        held_t, sent_t = split_groups(sum_t.finish(), even)
        held_t, sent_t, held_s = tie(held_t, sent_t, total(held_s, got_s))
        got_t, got_s = swap_z(sent_t), swap_z(held_s)
        got_t, got_m = tie(got_t, got_m)
        held_t, held_m = tie(total(held_t, got_t), total(held_m, got_m))
        got_t, got_m = across_pairs(held_t), swap_z(held_m)
        got_t, got_m, got_s, got_e = tie(got_t, got_m, got_s, got_e)
        held_t = total(held_t, got_t)
        got_t = swap_z(held_t)
        rt = join_groups(held_t, got_t, even).astype(F32)
        rs = join_groups(held_s, got_s, even).astype(F32)
        re = join_groups(held_e, got_e, even).astype(F32)
        rr = join_groups(held_r, got_r, even).astype(F32)
        rr = jnp.concatenate([rr[:, k * columns : (k + 1) * columns] for k in range(share)], axis=0)
        rm = join_groups(held_m, got_m, even).astype(F32)
        narrow = rt[:, 3 * columns :]
        biases, rows_hidden = narrow[0:8, :part], narrow[8:11].reshape(-1)
        gains, shifts = narrow[11:14, :part], narrow[14:17, :part]
    else:
        re, rr, rs, rm, rt = (
            lax.psum(lax.psum_scatter(v, "shard", scatter_dimension=0, tiled=True), "grp").astype(F32)
            for v in (*grad_e, *grad_r, *grad_s, *grad_m, *grad_t)
        )
        rows = [sums_t[0:4], sums_s[0:3], sums_f[0:1], sums_t[4:5], norm_s[0:1], norm_f[0:1], sums_t[5:6], norm_s[1:2], norm_f[1:2]]
        cut = lax.dynamic_slice_in_dim(lax.psum(jnp.concatenate(rows, axis=0), BOTH), mine * part, part, axis=1)
        biases, gains, shifts = cut[0:8], cut[8:11], cut[11:14]
        rows_hidden = lax.dynamic_slice_in_dim(lax.psum(ghb[0], BOTH), mine * hidden_bias.shape[0], hidden_bias.shape[0])
    return (
        (unpack_rows(out, clips) * flags)[:, None],
        unpack_rows(gx, clips)[:, None],
        rt[:, : 3 * columns],
        rm[:, :columns],
        rm[:, columns:],
        rs[:, : 3 * columns],
        rs[:, 3 * columns :],
        re,
        rr,
        biases,
        rows_hidden,
        gains,
        shifts,
    )


def solution(mesh):
    clips = P(None, ("grp", "shard"), None, None)
    rows = P("shard", None)
    cols = P(None, "shard")
    return jax.shard_map(
        local,
        mesh=mesh,
        in_specs=(clips, clips, P(None, ("grp", "shard"))) + (rows,) * 7 + (cols, P("shard"), cols, cols),
        out_specs=(clips, clips) + (rows,) * 7 + (cols, P("shard"), cols, cols),
        check_vma=False,
    )
```

```python
import functools
import math

import jax
import jax.numpy as jnp
from jax import lax
from jax.experimental import pallas as pl
from jax.experimental.pallas import tpu as pltpu
from jax.sharding import PartitionSpec as P

FRAMES = 2
PLACES = 196
HD = 64
EPSILON = 1e-06
BLOCK = 208
EDGE = 192
CLASS = PLACES - EDGE
CHUNK = 2 * BLOCK
WIDE = 256
BF = jnp.bfloat16
F32 = jnp.float32
SMALL = 32
MICRO = 4_000_000_000
SPARE = 12 * 1024 * 1024
VMEM_LIMIT = 60 * 1024 * 1024


def nn(a, b):
    return lax.dot_general(a, b, (((1,), (0,)), ((), ())), preferred_element_type=F32)


def nt(a, b):
    return lax.dot_general(a, b, (((1,), (1,)), ((), ())), preferred_element_type=F32)


def tn(a, b):
    return lax.dot_general(a, b, (((0,), (0,)), ((), ())), preferred_element_type=F32)


def loop(count, body):
    for i in range(count):
        body(i)


def rows_of(i, size):
    return slice(i * size, (i + 1) * size)


def cols_of(i, size, base=0):
    return slice(base + i * size, base + (i + 1) * size)


def unit(x):
    center = x - jnp.mean(x, axis=-1, keepdims=True)
    factor = lax.rsqrt(jnp.mean(center * center, axis=-1, keepdims=True) + EPSILON)
    return center * factor, factor


def norm_chunks(src, dst, gain, shift):
    def body(i):
        at = rows_of(i, CHUNK)
        w, _ = unit(src[at, :].astype(F32))
        dst[at, :] = (w * gain + shift).astype(BF)

    loop(src.shape[0] // CHUNK, body)


def fold(x):
    return jnp.sum(x.reshape(x.shape[0] // 8, 8, x.shape[1]), axis=0)


def norm_back_chunks(gn_ref, x_ref, gain, base_of, store):
    columns = x_ref.shape[1]

    def body(i, carry):
        gain_sum, shift_sum = carry
        at = rows_of(i, CHUNK)
        gn = gn_ref[at, :]
        w, factor = unit(x_ref[at, :].astype(F32))
        scaled = gn * gain
        plain = jnp.mean(scaled, axis=-1, keepdims=True)
        cross = jnp.mean(scaled * w, axis=-1, keepdims=True)
        store(at, base_of(at) + factor * (scaled - plain - w * cross))
        return gain_sum + fold(gn * w), shift_sum + fold(gn)

    zero = jnp.zeros((8, columns), F32)
    gain_sum, shift_sum = zero, zero
    for i in range(x_ref.shape[0] // CHUNK):
        gain_sum, shift_sum = body(i, (gain_sum, shift_sum))
    return jnp.sum(gain_sum, axis=0, keepdims=True), jnp.sum(shift_sum, axis=0, keepdims=True)


def column_sums(ref, start, size):
    def body(i, total):
        return total + fold(ref[rows_of(i, CHUNK), start : start + size].astype(F32))

    total = jnp.zeros((8, size), F32)
    for i in range(ref.shape[0] // CHUNK):
        total = body(i, total)
    return jnp.sum(total, axis=0, keepdims=True)


def head_map(columns):
    feature = lax.broadcasted_iota(jnp.int32, (columns, 128), 0) // HD
    head = lax.broadcasted_iota(jnp.int32, (columns, 128), 1)
    return (feature == head).astype(BF)


def head_sums(a_ref, a_rows, a_base, b_ref, b_rows, b_base, heads):
    total = None
    for j in range(heads.shape[0] // WIDE):
        a = a_ref[a_rows, a_base + j * WIDE : a_base + (j + 1) * WIDE].astype(F32)
        b = b_ref[b_rows, b_base + j * WIDE : b_base + (j + 1) * WIDE].astype(F32)
        top = (a * b).astype(BF)
        rest = (a * b - top.astype(F32)).astype(BF)
        part = heads[j * WIDE : (j + 1) * WIDE, :]
        term = nn(top, part) + nn(rest, part)
        total = term if total is None else total + term
    return total


def places_only(value):
    return jnp.where(lax.broadcasted_iota(jnp.int32, value.shape, 0) < PLACES, value, 0.0)


def start(pairs, sems):
    copies = [pltpu.make_async_copy(s, d, sems.at[n]) for n, (s, d) in enumerate(pairs)]
    for copy in copies:
        copy.start()
    return copies


def wait(copies):
    for copy in copies:
        copy.wait()


def piece_views(bufs):
    return list(bufs)


def rows_at(place, rows, share=1, k=0):
    return pl.ds(pl.multiple_of((place * share + k) * rows, 16), rows)


def load(bufs, place_ref, w, sems):
    if len(bufs) == 1:
        return start([(bufs[0], w)], sems)
    views = piece_views(bufs)
    rows = views[0].shape[0]
    return start([(v, w.at[rows_at(place_ref[n], rows), :]) for n, v in enumerate(views)], sems)


ORDER = ((3, 0), (1, 0), (3, 1), (2, 1), (1, 1), (2, 0), (0, 0), (0, 1))


def store_pieces(dw, outs, place_ref, sems, share=1, base=0):
    if len(outs) == 1:
        return start([(dw, outs[0])], sems)
    half, columns = outs[0].shape[1], dw.shape[1]
    pairs = []
    for side, out in enumerate(outs):
        for n, (chip, top) in enumerate(ORDER):
            place = place_ref[8 + side * 4 + chip]
            for k in range(share):
                source = dw.at[pl.ds(pl.multiple_of(((place * share + k) * 2 + top) * half, 16), half), :]
                pairs.append((source, out.at[n, :, base + k * columns : base + (k + 1) * columns]))
    return start(pairs, sems)


def piece_select(piece, rows, columns):
    lane = lax.broadcasted_iota(jnp.int32, (128, columns), 0)
    column = lax.broadcasted_iota(jnp.int32, (128, columns), 1)
    return ((lane < rows) & (column == piece * rows + lane)).astype(BF)


def spread_small(w, small_ref, hb_ref):
    columns = small_ref.shape[1]
    rows = columns // 8
    start = w.shape[1] - 128
    total = jnp.zeros((SMALL, columns), F32)
    for piece in range(8):
        block = w[piece * rows : piece * rows + SMALL, start:]
        total = total + nn(block, piece_select(piece, rows, columns))
        wide = block.astype(F32)
        for r in range(3):
            at = (piece * 3 + r) * 128
            hb_ref[0:1, at : at + 128] = wide[8 + r : 9 + r, :]
    small_ref[...] = total


def gather_small(dw, sums):
    sums_t, sums_s, norm_s, sums_f, norm_f, ghb = sums
    columns = sums_t.shape[1]
    rows = columns // 8
    start = dw.shape[1] - 128
    zero = jnp.zeros((3, columns), F32)
    order = [sums_t[0:4, :], sums_s[0:3, :], sums_f[0:1, :], zero, sums_t[4:5, :], norm_s[0:1, :], norm_f[0:1, :]]
    order += [sums_t[5:6, :], norm_s[1:2, :], norm_f[1:2, :], jnp.zeros((SMALL - 17, columns), F32)]
    values = jnp.concatenate(order, axis=0).astype(BF)
    for piece in range(8):
        block = nt(values, piece_select(piece, rows, columns))
        hidden = [ghb[0:1, (piece * 3 + r) * 128 : (piece * 3 + r + 1) * 128] for r in range(3)]
        block = jnp.concatenate([block[0:8, :]] + hidden + [block[11:, :]], axis=0)
        dw[piece * rows : piece * rows + SMALL, start:] = block.astype(BF)
        dw[piece * rows + SMALL : (piece + 1) * rows, start:] = jnp.zeros((rows - SMALL, 128), BF)


def load_feed(bufs, place_ref, we, wr, sems):
    if len(bufs) == 2:
        return start([(bufs[0], we)], sems), start([(bufs[1], wr)], sems.at[8:])
    views = piece_views(bufs)
    rows, units, columns = views[0].shape[0], we.shape[1], wr.shape[1]
    share = units // columns
    first = start([(v.at[:, 0:units], we.at[rows_at(place_ref[n], rows), :]) for n, v in enumerate(views)], sems)
    pairs = []
    for n, v in enumerate(views):
        for k in range(share):
            to = rows_at(place_ref[n], rows, share, k)
            pairs.append((v.at[:, units + k * columns : units + (k + 1) * columns], wr.at[to, :]))
    return first, start(pairs, sems.at[8:])


class Late:
    def __init__(self, source, target, sem):
        self.target = target
        self.copy = pltpu.make_async_copy(source, target, sem)
        self.copy.start()

    def get(self):
        if self.copy is not None:
            self.copy.wait()
            self.copy = None
        return self.target


class Early:
    def __init__(self, ref, target, sem):
        self.ref = ref
        self.copy = pltpu.make_async_copy(ref, target, sem)

    def send(self):
        self.copy.start()


SPACES = {
    "v": pl.BlockSpec(memory_space=pltpu.VMEM),
    "a": pl.BlockSpec(memory_space=pl.ANY),
    "l": pl.BlockSpec(memory_space=pl.ANY),
    "e": pl.BlockSpec(memory_space=pl.ANY),
    "s": pl.BlockSpec(memory_space=pltpu.SMEM),
}


def call(body, operands, spaces, outs, out_spaces, scratch, micros, name, tight=True):
    late = [n for n, space in enumerate(spaces) if space == "l"]
    early = [n for n, space in enumerate(out_spaces) if space == "e"]
    n_in, n_out, n_scratch = len(operands), len(outs), len(scratch)

    def kernel(*refs):
        ins, refs = list(refs[:n_in]), refs[n_in:]
        results, refs = list(refs[:n_out]), refs[n_out:]
        own, refs = refs[:n_scratch], refs[n_scratch:]
        held, refs = refs[: len(late)], refs[len(late) :]
        filled, refs = refs[: len(early)], refs[len(early) :]
        late_sems, early_sems = refs
        for k, n in enumerate(late):
            ins[n] = Late(ins[n], held[k], late_sems.at[k])
        for k, n in enumerate(early):
            results[n] = Early(filled[k], results[n], early_sems.at[k])
        body(ins, results, own)
        for n in late:
            ins[n].get()
        for n in early:
            results[n].copy.wait()

    held = [operands[n].size * operands[n].dtype.itemsize for n, space in enumerate(spaces) if space in "vl"]
    held += [math.prod(outs[n][0]) * jnp.dtype(outs[n][1]).itemsize for n, space in enumerate(out_spaces) if space in "ve"]
    held += [math.prod(ref.shape) * jnp.dtype(ref.dtype).itemsize for ref in scratch if "semaphore" not in str(ref.memory_space)]
    limit = min(VMEM_LIMIT, sum(held) + SPARE) if tight else VMEM_LIMIT
    more = [pltpu.VMEM(operands[n].shape, operands[n].dtype) for n in late]
    more += [pltpu.VMEM(*outs[n]) for n in early]
    more += [pltpu.SemaphoreType.DMA((max(1, len(late)),)), pltpu.SemaphoreType.DMA((max(1, len(early)),))]
    return pl.pallas_call(
        kernel,
        out_shape=[jax.ShapeDtypeStruct(s, d) for s, d in outs],
        in_specs=[SPACES[space] for space in spaces],
        out_specs=[SPACES[space] for space in out_spaces],
        scratch_shapes=list(scratch) + more,
        compiler_params=pltpu.CompilerParams(vmem_limit_bytes=limit),
        cost_estimate=pl.CostEstimate(flops=micros * MICRO, bytes_accessed=0, transcendentals=0),
        name=name,
    )(*operands)


def blocks_of(count):
    return [slice(j * WIDE, (j + 1) * WIDE) for j in range(count // WIDE)]


def shifted(at, base):
    return slice(at.start + base, at.stop + base)


def entry(normed, w, qkv, query_bias, value_bias):
    columns = normed.shape[1]
    for part, bias in enumerate((query_bias, None, value_bias)):
        for at in blocks_of(columns):
            to = shifted(at, part * columns)
            packed = nn(normed[...], w[:, to])
            qkv[:, to] = (packed if bias is None else packed + bias[:, at]).astype(BF)


def time_forward(n, ins, results, own):
    place_ref, x_ref, *rest = ins
    given, bufs = rest[: len(rest) - n], rest[len(rest) - n :]
    nt_out, qkv_out, o_out, e_out, p_out, y_ref, small_ref, hb_ref = results
    w, sems = own
    columns = x_ref.shape[1]
    wait(load(bufs, place_ref, w, sems))
    if given:
        small_ref[...] = given[0][...]
        hb_ref[...] = given[1][...]
    else:
        spread_small(w, small_ref, hb_ref)
    norm_chunks(x_ref, nt_out.ref, small_ref[11:12, :], small_ref[14:15, :])
    nt_out.send()
    qkv_ref, o_ref, e_ref, p_ref = qkv_out.ref, o_out.ref, e_out.ref, p_out.ref
    entry(nt_out.ref, w, qkv_ref, small_ref[0:1, :], small_ref[1:2, :])
    qkv_out.send()
    heads = head_map(columns)
    for clip in range(x_ref.shape[0] // (FRAMES * BLOCK)):
        at = [slice((clip * FRAMES + f) * BLOCK, (clip * FRAMES + f + 1) * BLOCK) for f in range(FRAMES)]
        weights = []
        for f in range(FRAMES):
            s = [head_sums(qkv_ref, at[f], 0, qkv_ref, at[g], columns, heads) * HD ** (-0.5) for g in range(FRAMES)]
            peak = jnp.maximum(s[0], s[1])
            powered = [jnp.exp(score - peak) for score in s]
            inverse = 1.0 / (powered[0] + powered[1])
            for g in range(FRAMES):
                m = (clip * FRAMES + f) * FRAMES + g
                p = powered[g] * inverse
                p_ref[m * BLOCK : (m + 1) * BLOCK, :] = p
                weights.append(p.astype(BF))
        for to in blocks_of(columns):
            v = [qkv_ref[a, shifted(to, 2 * columns)].astype(F32) for a in at]
            for f in range(FRAMES):
                spread = [nt(weights[FRAMES * f + g], heads[to, :]) for g in range(FRAMES)]
                o_ref[at[f], to] = (spread[0] * v[0] + spread[1] * v[1]).astype(BF)
    p_out.send()
    o_out.send()
    for at in blocks_of(columns):
        e_ref[:, at] = (nn(o_ref[...], w[:, shifted(at, 3 * columns)]) + small_ref[2:3, at]).astype(BF)
    e_out.send()
    for at in blocks_of(columns):
        branch = nn(e_ref[...], w[:, shifted(at, 4 * columns)]) + small_ref[3:4, at]
        for block in range(x_ref.shape[0] // BLOCK):
            rows = rows_of(block, BLOCK)
            y_ref[rows, at] = x_ref[rows, at].astype(F32) + places_only(branch[rows, :])


def half_masks():
    lane = lax.broadcasted_iota(jnp.int32, (1, 128), 1)
    return (lane < HD).astype(BF), (lane >= HD).astype(BF)


def space_forward(n, ins, results, own):
    place_ref, y_ref, small_ref, *bufs = ins
    ns_out, qkv_out, p_out, o_out, z_ref = results
    w, sems = own
    columns = y_ref.shape[1]
    blocks = y_ref.shape[0] // BLOCK
    pairs = columns // 128
    copies = load(bufs, place_ref, w, sems)
    norm_chunks(y_ref, ns_out.ref, small_ref[12:13, :], small_ref[15:16, :])
    ns_out.send()
    wait(copies)
    qkv_ref, p_ref, o_ref = qkv_out.ref, p_out.ref, o_out.ref
    entry(ns_out.ref, w, qkv_ref, small_ref[4:5, :], small_ref[5:6, :])
    qkv_out.send()
    masks = half_masks()
    first = lax.broadcasted_iota(jnp.int32, (BLOCK, 128), 1) < HD
    column = lax.broadcasted_iota(jnp.int32, (1, BLOCK), 1)
    hidden = jnp.where(column <= PLACES, 0.0, -1e30)

    def attend(block):
        at = rows_of(block, BLOCK)
        columns_of = [[slice(part * columns + k * 128, part * columns + (k + 1) * 128) for k in range(pairs)] for part in range(3)]
        scores = []
        for k in range(pairs):
            query, key = qkv_ref[at, columns_of[0][k]], qkv_ref[at, columns_of[1][k]]
            scores += [nt(query * mask, key) * HD ** (-0.5) + hidden for mask in masks]
        powered = [jnp.exp(s - jnp.max(s, axis=-1, keepdims=True)) for s in scores]
        weights = [(e * (1.0 / jnp.sum(e, axis=-1, keepdims=True))).astype(BF) for e in powered]
        for k in range(pairs):
            value = qkv_ref[at, columns_of[2][k]]
            for half in range(2):
                p_ref[(block * pairs + k) * 2 + half] = weights[2 * k + half]
            mixed = jnp.where(first, nn(weights[2 * k], value), nn(weights[2 * k + 1], value))
            o_ref[at, columns_of[0][k]] = mixed.astype(BF)

    loop(blocks, attend)
    p_out.send()
    o_out.send()
    is_class = lax.broadcasted_iota(jnp.int32, (BLOCK - EDGE, WIDE), 0) == CLASS
    for at in blocks_of(columns):
        branch = nn(o_ref[...], w[:, shifted(at, 3 * columns)]) + small_ref[6:7, at]
        z_ref[:, at] = y_ref[:, at] + branch
        for clip in range(blocks // FRAMES):
            edges = [slice((clip * FRAMES + f) * BLOCK + EDGE, (clip * FRAMES + f + 1) * BLOCK) for f in range(FRAMES)]
            mean = (branch[edges[0], :] + branch[edges[1], :]) * (1.0 / FRAMES)
            for edge in edges:
                z_ref[edge, at] = y_ref[edge, at] + jnp.where(is_class, mean, branch[edge, :])


def gelu_both(h):
    cdf = 0.5 * (1.0 + lax.erf(h * 0.5**0.5))
    density = jnp.exp(h * h * -0.5) * 0.3989422804014327
    return h * cdf, cdf + h * density


def feed_out(ins, results, own):
    place_ref, z_ref, g_ref, small_ref, hb_ref, *bufs = ins
    out_ref, nm_out, gh_out, sums_ref, *outs = results
    we, wr, dwr, a, sems, out_sems = own
    nm, gh = nm_out.ref, gh_out.ref
    columns = z_ref.shape[1]
    units = we.shape[1]
    copies, more = load_feed(bufs, place_ref, we, wr, sems)
    norm_chunks(z_ref, nm, small_ref[13:14, :], small_ref[16:17, :])
    nm_out.send()
    wait(copies + more)

    def inner(j):
        at = cols_of(j, WIDE)
        h = nn(nm[...], we[:, at]) + hb_ref[0:1, at]
        active, slope = gelu_both(h)
        a[:, at] = active.astype(BF)
        gh[:, at] = (nt(g_ref[...], wr[rows_of(j, WIDE), :]) * slope).astype(BF)

    loop(units // WIDE, inner)
    gh_out.send()

    def left(j):
        dwr[rows_of(j, WIDE), :] = tn(a[:, cols_of(j, WIDE)], g_ref[...]).astype(BF)

    loop(units // WIDE, left)
    copies = store_pieces(dwr, outs, place_ref, out_sems, units // columns)
    for at in blocks_of(columns):
        out_ref[:, at] = (z_ref[:, at] + (nn(a[...], wr[:, at]) + small_ref[7:8, at])).astype(BF)
    sums_ref[0:1, :] = column_sums(g_ref, 0, columns)
    wait(copies)


def feed_in(ins, results, own):
    place_ref, gh, nm = ins
    ghb_ref, *outs = results
    dwe, out_sems = own
    units = gh.shape[1]

    def right(j):
        at = cols_of(j, WIDE)
        block = gh[:, at]
        dwe[:, at] = tn(nm[...], block).astype(BF)
        ghb_ref[0:1, at] = jnp.sum(block.astype(F32), axis=0, keepdims=True)

    loop(units // WIDE, right)
    wait(store_pieces(dwe, outs, place_ref, out_sems))


def norm_backward(row, n, ins, results, own):
    place_ref, gh_ref, x_in, base_in, small_ref, *bufs = ins
    gz_ref, sums_ref = results
    w, gn, sems = own
    columns = gz_ref.shape[1]
    views = [b.at[:, 0 : w.shape[1]] for b in bufs]
    wait(load(views, place_ref, w, sems))
    for at in blocks_of(columns):
        gn[:, at] = nt(gh_ref[...], w[at, :])
    x_ref, base = x_in.get(), base_in.get()

    def store(at, value):
        gz_ref[at, :] = value

    gain_sum, shift_sum = norm_back_chunks(
        gn, x_ref, small_ref[row : row + 1, :], lambda at: base[at, :].astype(F32), store
    )
    sums_ref[0:1, :] = gain_sum
    sums_ref[1:2, :] = shift_sum


def space_backward(n, ins, results, own):
    place_ref, gz_ref, ns_in, qkv_in, p_in, o_in, *rest = ins
    bufs = rest[:n]
    gqkv_out, sums_ref, *outs = results
    w, dw_ref, gbs, go, sems, out_sems = own
    columns = gz_ref.shape[1]
    rows = gz_ref.shape[0]
    clips = rows // (BLOCK * FRAMES)
    pairs = columns // 128
    copies = load([b.at[:, 3 * columns : 4 * columns] for b in bufs], place_ref, w, sems)

    def lower(i):
        at = rows_of(i, CHUNK)
        gbs[at, :] = gz_ref[at, :].astype(BF)

    loop(rows // CHUNK, lower)
    is_class = lax.broadcasted_iota(jnp.int32, (BLOCK - EDGE, columns), 0) == CLASS
    for clip in range(clips):
        edges = [slice((clip * FRAMES + f) * BLOCK + EDGE, (clip * FRAMES + f + 1) * BLOCK) for f in range(FRAMES)]
        share = gz_ref[edges[0], :] * (1.0 / FRAMES)
        for edge in edges:
            gbs[edge, :] = jnp.where(is_class, share, gz_ref[edge, :]).astype(BF)
    wait(copies)
    for at in blocks_of(columns):
        go[:, at] = nt(gbs[...], w[at, :]).astype(BF)
    o_ref, qkv_ref, p_ref, gqkv = o_in.get(), qkv_in.get(), p_in.get(), gqkv_out.ref
    for at in blocks_of(columns):
        dw_ref[:, shifted(at, 3 * columns)] = tn(o_ref[...], gbs[:, at]).astype(BF)
    masks = half_masks()
    first = lax.broadcasted_iota(jnp.int32, (BLOCK, 128), 1) < HD
    class_row = lax.broadcasted_iota(jnp.int32, (BLOCK - EDGE, 128), 0) == CLASS
    together = 2

    def attend(step):
        parts = []
        for u in range(together):
            clip, pair = (step * together + u) // pairs, (step * together + u) % pairs
            for f in range(FRAMES):
                block = clip * FRAMES + f
                at = rows_of(block, BLOCK)
                q, k, v = (qkv_ref[at, cols_of(pair, 128, part * columns)] for part in range(3))
                grad = go[at, cols_of(pair, 128)]
                parts += [(q, k, v, grad, mask, p_ref[2 * (block * pairs + pair) + half]) for half, mask in enumerate(masks)]
        gp = [nt(grad * mask, v) for _, _, v, grad, mask, _ in parts]
        p = [part[5].astype(F32) for part in parts]
        shared = [jnp.sum(a * b, axis=-1, keepdims=True) for a, b in zip(gp, p)]
        gs = [(b * (a - c)).astype(BF) for a, b, c in zip(gp, p, shared)]
        scale = HD ** (-0.5)
        gq = [nn(a, part[1]) * scale for a, part in zip(gs, parts)]
        gv = [tn(part[5], part[3]) for part in parts]
        gk = [tn(a, part[0]) * scale for a, part in zip(gs, parts)]
        for u in range(together):
            clip, pair = (step * together + u) // pairs, (step * together + u) % pairs
            for part, values in enumerate((gq, gk, gv)):
                to = cols_of(pair, 128, part * columns)
                one, two = (jnp.where(first, values[4 * u + 2 * f], values[4 * u + 2 * f + 1]) for f in range(FRAMES))
                top = clip * FRAMES * BLOCK
                gqkv[pl.ds(top, EDGE), to] = one[:EDGE].astype(BF)
                gqkv[pl.ds(top + BLOCK, EDGE), to] = two[:EDGE].astype(BF)
                both = jnp.where(class_row, one[EDGE:] + two[EDGE:], one[EDGE:])
                gqkv[pl.ds(top + EDGE, BLOCK - EDGE), to] = both.astype(BF)
                rest = jnp.where(class_row, 0.0, two[EDGE:])
                gqkv[pl.ds(top + BLOCK + EDGE, BLOCK - EDGE), to] = rest.astype(BF)

    loop(clips * pairs // together, attend)
    gqkv_out.send()
    ns_ref = ns_in.get()
    for at in blocks_of(3 * columns):
        dw_ref[:, at] = tn(ns_ref[...], gqkv[:, at]).astype(BF)
    copies = store_pieces(dw_ref, outs, place_ref, out_sems)
    sums_ref[0:1, :] = column_sums(gqkv, 0, columns)
    sums_ref[1:2, :] = column_sums(gqkv, 2 * columns, columns)
    sums_ref[2:3, :] = column_sums(gbs, 0, columns)
    wait(copies)


def mixer_backward(n, ins, results, own):
    place_ref, gy_ref, o_in, e_in, *bufs = ins
    go_out, sums_ref, *outs = results
    w, dw_ref, grt, get, sems, out_sems = own
    columns = gy_ref.shape[1]
    rows = gy_ref.shape[0]
    copies = load([b.at[:, 3 * columns : 5 * columns] for b in bufs], place_ref, w, sems)

    def lower(block):
        at = rows_of(block, BLOCK)
        grt[at, :] = places_only(gy_ref[at, :]).astype(BF)

    loop(rows // BLOCK, lower)
    wait(copies)
    go = go_out.ref
    for at in blocks_of(columns):
        get[:, at] = nt(grt[...], w[at, columns : 2 * columns]).astype(BF)
    e_ref, o_ref = e_in.get(), o_in.get()
    for at in blocks_of(columns):
        dw_ref[:, shifted(at, columns)] = tn(e_ref[...], grt[:, at]).astype(BF)
    for at in blocks_of(columns):
        dw_ref[:, at] = tn(o_ref[...], get[:, at]).astype(BF)
    copies = store_pieces(dw_ref, outs, place_ref, out_sems)
    for at in blocks_of(columns):
        go[:, at] = nt(get[...], w[at, 0:columns]).astype(BF)
    go_out.send()
    sums_ref[2:3, :] = column_sums(get, 0, columns)
    sums_ref[3:4, :] = column_sums(grt, 0, columns)
    wait(copies)


def time_backward(n, ins, results, own):
    place_ref, go, qkv_ref, p_ref, x_in, gy_in, small_ref, before, *bufs = ins
    gqkv_out, gx_ref, sums_ref = results
    w, gn, sems = own
    columns = gx_ref.shape[1]
    rows = gx_ref.shape[0]
    gqkv = gqkv_out.ref
    copies = load([b.at[:, 0 : 3 * columns] for b in bufs], place_ref, w, sems)
    heads = head_map(columns)
    for clip in range(rows // (FRAMES * BLOCK)):
        at = [slice((clip * FRAMES + f) * BLOCK, (clip * FRAMES + f + 1) * BLOCK) for f in range(FRAMES)]
        gs, kept = [], []
        for f in range(FRAMES):
            gp = [head_sums(go, at[f], 0, qkv_ref, at[g], 2 * columns, heads) for g in range(FRAMES)]
            first = ((clip * FRAMES + f) * FRAMES) * BLOCK
            p = [p_ref[first + g * BLOCK : first + (g + 1) * BLOCK, :] for g in range(FRAMES)]
            shared = gp[0] * p[0] + gp[1] * p[1]
            gs += [(p[g] * (gp[g] - shared)).astype(BF) for g in range(FRAMES)]
            kept += [p[g].astype(BF) for g in range(FRAMES)]
        for block in blocks_of(columns):
            to = [shifted(block, part * columns) for part in range(3)]
            q, k = ([qkv_ref[a, to[part]].astype(F32) for a in at] for part in range(2))
            grad = [go[a, block].astype(F32) for a in at]
            scaled = heads[block, :] * BF(HD ** (-0.5))
            spread = [nt(value, scaled) for value in gs]
            for f in range(FRAMES):
                gqkv[at[f], to[0]] = (spread[2 * f] * k[0] + spread[2 * f + 1] * k[1]).astype(BF)
                gqkv[at[f], to[1]] = (spread[f] * q[0] + spread[2 + f] * q[1]).astype(BF)
            spread = [nt(value, heads[block, :]) for value in kept]
            for f in range(FRAMES):
                gqkv[at[f], to[2]] = (spread[f] * grad[0] + spread[2 + f] * grad[1]).astype(BF)
    gqkv_out.send()
    wait(copies)
    for at in blocks_of(columns):
        gn[:, at] = nt(gqkv[...], w[at, :])
    x_ref, gy_ref = x_in.get(), gy_in.get()

    def store(at, value):
        gx_ref[at, :] = value.astype(BF)

    gain_sum, shift_sum = norm_back_chunks(gn, x_ref, small_ref[11:12, :], lambda at: gy_ref[at, :], store)
    sums_ref[0:1, :] = column_sums(gqkv, 0, columns)
    sums_ref[1:2, :] = column_sums(gqkv, 2 * columns, columns)
    sums_ref[2:4, :] = before[2:4, :]
    sums_ref[4:5, :] = gain_sum
    sums_ref[5:6, :] = shift_sum


def time_weights(ins, results, own):
    place_ref, gqkv, nt_ref, *sums = ins
    dw_ref, out_sems = own
    columns = nt_ref.shape[1]
    for at in blocks_of(3 * columns):
        dw_ref[:, at] = tn(nt_ref[...], gqkv[:, at]).astype(BF)
    if sums:
        gather_small(dw_ref, sums)
    wait(store_pieces(dw_ref, results, place_ref, out_sems))


def pack_rows(tokens, once):
    clips, _, columns = tokens.shape
    frames = []
    for f in range(FRAMES):
        places = tokens[:, 1 + f * PLACES : 1 + (f + 1) * PLACES]
        head = tokens[:, :1] if f == 0 or not once else jnp.zeros_like(tokens[:, :1])
        frames.append(jnp.concatenate([places, head, jnp.zeros((clips, BLOCK - PLACES - 1, columns), tokens.dtype)], axis=1))
    return jnp.stack(frames, axis=1).reshape(clips * FRAMES * BLOCK, columns)


def unpack_rows(rows, clips):
    framed = rows.reshape(clips, FRAMES, BLOCK, rows.shape[-1])
    return jnp.concatenate(
        [framed[:, 0, PLACES : PLACES + 1]] + [framed[:, f, :PLACES] for f in range(FRAMES)], axis=1
    )


class Layer:
    def __init__(self, rows, columns, units, shards, pieced, place):
        self.rows, self.columns, self.units = rows, columns, units
        self.pieced, self.place = pieced, place
        self.piece = columns // shards
        self.act = ((rows, columns), BF)
        self.act3 = ((rows, 3 * columns), BF)
        self.tall = ((rows, units), BF)
        self.wide = ((rows, columns), F32)
        self.sums = ((8, columns), F32)

    def grads(self, width):
        if self.pieced:
            return [((8, self.piece // 2, width), BF)] * 2
        return [((self.columns, width), BF)]

    def vmem(self, *shapes):
        return [pltpu.VMEM(s, d) for s, d in shapes]

    def sems(self, *counts):
        return [pltpu.SemaphoreType.DMA((count,)) for count in counts]

    def time_forward(self, x, given, bufs):
        c, n = self.columns, len(bufs)
        extra = [((SMALL, c), F32), ((8, self.units), F32)]
        return call(
            functools.partial(time_forward, n), (self.place, x, *given, *bufs), "sv" + "v" * len(given) + "a" * n,
            [self.act, self.act3, self.act, self.act, ((self.rows * FRAMES, 128), F32), self.wide] + extra, "eeeeevvv",
            self.vmem(((c, bufs[0].shape[1]), BF)) + self.sems(8), 14, "time_forward", False,
        )

    def space_forward(self, y, small, bufs):
        c, n = self.columns, len(bufs)
        probs = ((self.rows // BLOCK * (c // 128) * 2, BLOCK, BLOCK), BF)
        return call(
            functools.partial(space_forward, n), (self.place, y, small, *bufs), "svv" + "a" * n,
            [self.act, self.act3, probs, self.act, self.wide], "eeeev",
            self.vmem(((c, 4 * c), BF)) + self.sems(8), 16, "space_forward", False,
        )

    def feed_out(self, z, g, small, hb, bufs):
        c, u, n = self.columns, self.units, len(bufs)
        outs = self.grads(u) if self.pieced else [((u, c), BF)]
        return call(
            feed_out, (self.place, z, g, small, hb, *bufs), "svvvv" + "a" * n,
            [self.act, self.act, self.tall, self.sums] + outs, "veev" + "a" * len(outs),
            self.vmem(((c, u), BF), ((u, c), BF), ((u, c), BF), self.tall) + self.sems(40, 64), 30, "feed_out", False,
        )

    def feed_in(self, gh, normed):
        c, u = self.columns, self.units
        outs = self.grads(u)
        return call(
            feed_in, (self.place, gh, normed), "svv", [((8, u), F32)] + outs, "v" + "a" * len(outs),
            self.vmem(((c, u), BF)) + self.sems(16), 8, "feed_in",
        )

    def norm_backward(self, row, gh, x, base, small, bufs, name):
        c, n, wide = self.columns, len(bufs), gh.shape[1]
        return call(
            functools.partial(norm_backward, row, n), (self.place, gh, x, base, small, *bufs), "svllv" + "a" * n,
            [self.wide, self.sums], "vv", self.vmem(((c, wide), BF), self.wide) + self.sems(8), 10, name,
        )

    def space_backward(self, gz, normed, qkv, p, o, bufs):
        c, n = self.columns, len(bufs)
        outs = self.grads(4 * c)
        return call(
            functools.partial(space_backward, n), (self.place, gz, normed, qkv, p, o, *bufs), "svllll" + "a" * n,
            [self.act3, self.sums] + outs, "ev" + "a" * len(outs),
            self.vmem(((c, c), BF), ((c, 4 * c), BF), self.act, self.act) + self.sems(8, 16), 20, "space_backward",
        )

    def mixer_backward(self, gy, o, e, bufs):
        c, n = self.columns, len(bufs)
        outs = self.grads(2 * c)
        return call(
            functools.partial(mixer_backward, n), (self.place, gy, o, e, *bufs), "svll" + "a" * n,
            [self.act, self.sums] + outs, "ev" + "a" * len(outs),
            self.vmem(((c, 2 * c), BF), ((c, 2 * c), BF), self.act, self.act) + self.sems(8, 16), 8, "mixer_backward",
        )

    def time_backward(self, go, qkv, p, x, gy, small, before, bufs):
        c, n = self.columns, len(bufs)
        return call(
            functools.partial(time_backward, n), (self.place, go, qkv, p, x, gy, small, before, *bufs),
            "svvvllvv" + "a" * n, [self.act3, self.act, self.sums], "evv",
            self.vmem(((c, 3 * c), BF), self.wide) + self.sems(8), 12, "time_backward",
        )

    def time_weights(self, gqkv, normed, sums):
        c = self.columns
        width = 3 * c + (128 if sums else 0)
        outs = self.grads(width)
        return call(
            time_weights, (self.place, gqkv, normed, *sums), "svv" + "v" * len(sums), outs, "a" * len(outs),
            self.vmem(((c, width), BF)) + self.sems(16), 8, "time_weights",
        )


BOTH = ("grp", "shard")


def permute(value, target):
    shards = lax.axis_size("shard")
    pairs = [(z * shards + s, z * shards + target(s)) for z in range(lax.axis_size("grp")) for s in range(shards)]
    return lax.ppermute(value, BOTH, pairs)


def to_sibling(value):
    return permute(value, lambda s: s ^ 1)


def along_x(value):
    return permute(value, lambda s: s ^ 2)


def along_y(value):
    return permute(value, lambda s: s ^ 4)


def near_hop(value):
    return permute(value, lambda s: s ^ (2 if s % 2 == 0 else 4))


def far_hop(value):
    return permute(value, lambda s: s ^ (4 if s % 2 == 0 else 2))


def places(s):
    near = jnp.where(s % 2 == 0, 2, 4)
    far = 6 - near
    gathered = [s, s ^ 1, s ^ near, s ^ near ^ 1, s ^ 6, s ^ 1 ^ far, s ^ far, s ^ 7]
    kept = [s, s ^ 2, s ^ 4, s ^ 6]
    return jnp.stack(gathered + kept + [k ^ 1 for k in kept]).astype(jnp.int32)


def total(*terms):
    return sum(t.astype(F32) for t in terms).astype(BF)


class Reduction:
    def __init__(self, keep, give):
        self.keep = keep
        self.got = to_sibling(give)

    def own(self, start, stop):
        return self.keep[start:stop], self.got[start:stop]

    def first(self):
        return total(*self.own(0, 2)), total(*self.own(2, 4))

    def cross(self, sent):
        self.from_x, self.from_y = along_x(sent[0]), along_y(sent[1])

    def second(self):
        return total(*self.own(4, 5), self.from_y[:1]), total(*self.own(5, 6), self.from_x[:1])

    def cross_again(self, sent):
        self.last_x, self.last_y = along_x(sent[0]), along_y(sent[1])

    def finish(self):
        top = total(*self.own(6, 7), self.from_x[1:], self.last_y)
        bottom = total(*self.own(7, 8), self.from_y[1:], self.last_x)
        return top[0], bottom[0]


def beside(*values):
    return jnp.concatenate([v[n : n + 1] for v in values for n in range(v.shape[0])], axis=2)


def apart(value, widths):
    stops = [sum(widths[: n + 1]) for n in range(len(widths))]
    return [value[..., stop - width : stop] for stop, width in zip(stops, widths)]


def hand_over(arrived, ahead, behind):
    widths = (ahead.keep.shape[2], behind.keep.shape[2], behind.keep.shape[2])
    ahead.last_x, *from_x = apart(arrived[0], widths)
    ahead.last_y, *from_y = apart(arrived[1], widths)
    behind.from_x, behind.from_y = jnp.concatenate(from_x, axis=0), jnp.concatenate(from_y, axis=0)


def tie(*values):
    leaves, shape = jax.tree.flatten(values)
    return jax.tree.unflatten(shape, lax.optimization_barrier(tuple(leaves)))


def swap_z(value):
    shards = lax.axis_size("shard")
    pairs = [(z * shards + s, (z ^ 1) * shards + s) for z in range(lax.axis_size("grp")) for s in range(shards)]
    return lax.ppermute(value, BOTH, pairs)


def across_pairs(value):
    return lax.ppermute(value, "grp", [(z, z ^ 2) for z in range(4)])


def split_groups(halves, even):
    low, high = halves
    return jnp.where(even, low, high), jnp.where(even, high, low)


def join_groups(held, other, even):
    return jnp.concatenate([jnp.where(even, held, other), jnp.where(even, other, held)], axis=0)


def local(video, cotangent, live, time_entry, time_exit, time_mixer, space_entry, space_exit, hidden_expand, hidden_reduce, bias_rows, hidden_bias, norm_gain, norm_shift):
    clips, _, tokens, columns = video.shape
    shards, groups = lax.axis_size("shard"), lax.axis_size("grp")
    mine = lax.axis_index("shard")
    part = columns // shards
    units = hidden_bias.shape[0] * shards
    share = units // columns
    pieced = shards == 8 and groups == 4

    def gather(value):
        return lax.all_gather(value, "shard", axis=0, tiled=True)

    flags = live.astype(BF)[:, :, None]

    own_t = jnp.concatenate([time_entry, time_exit, time_mixer], axis=1)
    own_s = jnp.concatenate([space_entry, space_exit], axis=1)
    if pieced:
        narrow = jnp.concatenate([norm_gain, norm_shift], axis=0)
        narrow = jnp.concatenate(
            [jnp.pad(bias_rows, ((0, 0), (0, 128 - part))), hidden_bias.reshape(-1, 128), jnp.pad(narrow, ((0, 0), (0, 128 - part)))], axis=0
        )
        own_t = jnp.concatenate([own_t, jnp.pad(narrow, ((0, part - narrow.shape[0]), (0, 0)))], axis=1)
        own_f = jnp.concatenate([hidden_expand] + [hidden_reduce[k * part : (k + 1) * part] for k in range(share)], axis=1)
        net = Layer(clips * FRAMES * BLOCK, columns, units, shards, pieced, places(mine))
        pair_t = to_sibling(own_t)
        pair_t, own_t, video, own_s, own_f = tie(pair_t, own_t, video, own_s, own_f)
        hop_t = (near_hop(own_t), near_hop(pair_t))
        x = pack_rows(video[:, 0], False)
        pair_s, pair_f = to_sibling(own_s), to_sibling(own_f)
        first_t, x, pair_s, pair_f = tie(hop_t[0], x, pair_s, pair_f)
        second_t, own_s, own_f, pair_s, pair_f = tie(far_hop(first_t), own_s, own_f, pair_s, pair_f)
        gone_t = tuple(to_sibling(v) for v in (first_t, hop_t[1], second_t))
        wt = (own_t, pair_t, first_t, hop_t[1], second_t, *gone_t)
        hop_s, hop_f = ((near_hop(own), near_hop(pair)) for own, pair in ((own_s, pair_s), (own_f, pair_f)))
        normed_t, qkv_t, o_t, e_t, p_t, y, small, hb = net.time_forward(x, (), wt)
        first_s, last_s, y, cotangent = tie(*hop_s, y, cotangent)
        g = pack_rows(cotangent[:, 0] * flags, True)
        second_s = far_hop(first_s)
        ws = (own_s, pair_s, first_s, last_s, second_s, *(to_sibling(v) for v in (first_s, last_s, second_s)))
        first_f, y, ws, g = tie(hop_f[0], y, ws, g)
        normed_s, qkv_s, p_s, o_s, z = net.space_forward(y, small, ws)
        second_f, last_f, z = tie(far_hop(first_f), hop_f[1], z)
        wf = (own_f, pair_f, first_f, last_f, second_f, *(to_sibling(v) for v in (first_f, last_f, second_f)))
    else:
        x, g = pack_rows(video[:, 0], False), pack_rows(cotangent[:, 0] * flags, True)
        net = Layer(clips * FRAMES * BLOCK, columns, units, shards, pieced, jnp.zeros((16,), jnp.int32))
        packed = jnp.concatenate([bias_rows, norm_gain, norm_shift], axis=0)
        spread = lax.all_gather(packed, "shard", axis=0).transpose(1, 0, 2).reshape(-1, columns).astype(F32)
        small = jnp.concatenate([spread[:8], jnp.zeros((3, columns), F32), spread[8:], jnp.zeros((SMALL - 17, columns), F32)], axis=0)
        given = (small, jnp.pad(gather(hidden_bias).astype(F32)[None], ((0, 7), (0, 0))))
        wt, ws, wf = (gather(own_t),), (gather(own_s),), (gather(hidden_expand), gather(hidden_reduce))
        normed_t, qkv_t, o_t, e_t, p_t, y, small, hb = net.time_forward(x, given, wt)
        normed_s, qkv_s, p_s, o_s, z = net.space_forward(y, small, ws)

    out, normed_f, gh, sums_f, *grad_r = net.feed_out(z, g, small, hb, wf)
    if pieced:
        sum_r = Reduction(*grad_r)
    ghb, *grad_e = net.feed_in(gh, normed_f)
    if pieced:
        sum_e = Reduction(*grad_e)
        sent_r, gh, ghb, sums_f, sum_e.keep = tie(sum_r.first(), gh, ghb, sums_f, sum_e.keep)
        sum_r.cross(sent_r)
    gz, norm_f = net.norm_backward(13, gh, z, g, small, wf if pieced else wf[:1], "feed_norm")
    if pieced:
        sent = [beside(last, both) for last, both in zip(sum_r.second(), sum_e.first())]
        sent, gz, norm_f = tie(sent, gz, norm_f)
        arrived = (along_x(sent[0]), along_y(sent[1]))
    gqkv, sums_s, *grad_s = net.space_backward(gz, normed_s, qkv_s, p_s, o_s, ws)
    if pieced:
        sum_s = Reduction(*grad_s)
        hand_over(arrived, sum_r, sum_e)
        even = lax.axis_index("grp") % 2 == 0
        held_r, sent_r = split_groups(sum_r.finish(), even)
        held_r, sent_r, sent_e, gqkv, sums_s, sum_s.keep = tie(held_r, sent_r, sum_e.second(), gqkv, sums_s, sum_s.keep)
        sum_e.cross_again(sent_e)
        got_r = swap_z(sent_r)
    gy, norm_s = net.norm_backward(12, gqkv, y, gz, small, ws, "space_norm")
    if pieced:
        got_r, sum_e.last_x, sum_e.last_y, gy, norm_s = tie(got_r, sum_e.last_x, sum_e.last_y, gy, norm_s)
        held_e, sent_e = split_groups(sum_e.finish(), even)
        held_r, held_e, sent_e, sent_s, gy, norm_s = tie(total(held_r, got_r), held_e, sent_e, sum_s.first(), gy, norm_s)
        sum_s.cross(sent_s)
        got_r, got_e = across_pairs(held_r), swap_z(sent_e)
    go, sums_m, *grad_m = net.mixer_backward(gy, o_t, e_t, wt)
    if pieced:
        sum_m = Reduction(*grad_m)
        arrived = (got_r, got_e, sum_s.from_x, sum_s.from_y)
        arrived, go, sums_m, sum_m.keep = tie(arrived, go, sums_m, sum_m.keep)
        got_r, got_e, sum_s.from_x, sum_s.from_y = arrived
        sent = [beside(last, both) for last, both in zip(sum_s.second(), sum_m.first())]
        held_r, held_e, sent, go = tie(total(held_r, got_r), total(held_e, got_e), sent, go)
        arrived = (along_x(sent[0]), along_y(sent[1]), swap_z(held_r), across_pairs(held_e))
    gqkv, gx, sums_t = net.time_backward(go, qkv_t, p_t, x, gy, small, sums_m, wt)
    if pieced:
        arrived, gqkv, gx, sums_t, out = tie(arrived, gqkv, gx, sums_t, out)
        came_x, came_y, got_r, got_e = arrived
        hand_over((came_x, came_y), sum_s, sum_m)
        held_s, sent_s = split_groups(sum_s.finish(), even)
        held_s, sent_s, sent_m, gqkv = tie(held_s, sent_s, sum_m.second(), gqkv)
        sum_m.cross_again(sent_m)
        got_s = swap_z(sent_s)
    grad_t = net.time_weights(gqkv, normed_t, (sums_t, sums_s, norm_s, sums_f, norm_f, ghb) if pieced else ())

    if pieced:
        got_s, sum_m.last_x, sum_m.last_y, grad_t = tie(got_s, sum_m.last_x, sum_m.last_y, grad_t)
        sum_t = Reduction(*grad_t)
        sent_t, got_s, got_e, sum_m.last_x, sum_m.last_y, gx, out = tie(
            sum_t.first(), got_s, got_e, sum_m.last_x, sum_m.last_y, gx, out
        )
        sum_t.cross(sent_t)
        held_s, held_e = total(held_s, got_s), total(held_e, got_e)
        held_m, sent_m = split_groups(sum_m.finish(), even)
        got_s, got_m, got_e = across_pairs(held_s), swap_z(sent_m), swap_z(held_e)
        sum_t.from_x, sum_t.from_y, got_m = tie(sum_t.from_x, sum_t.from_y, got_m)
        held_m, sent_t = tie(total(held_m, got_m), sum_t.second())
        sum_t.cross_again(sent_t)
        got_m = across_pairs(held_m)
        sum_t.last_x, sum_t.last_y, got_s = tie(sum_t.last_x, sum_t.last_y, got_s)
        held_t, sent_t = split_groups(sum_t.finish(), even)
        held_t, sent_t, held_s = tie(held_t, sent_t, total(held_s, got_s))
        got_t, got_s = swap_z(sent_t), swap_z(held_s)
        got_t, got_m = tie(got_t, got_m)
        held_t, held_m = tie(total(held_t, got_t), total(held_m, got_m))
        got_t, got_m = across_pairs(held_t), swap_z(held_m)
        got_t, got_m, got_s, got_e = tie(got_t, got_m, got_s, got_e)
        held_t = total(held_t, got_t)
        got_t = swap_z(held_t)
        rt = join_groups(held_t, got_t, even).astype(F32)
        rs = join_groups(held_s, got_s, even).astype(F32)
        re = join_groups(held_e, got_e, even).astype(F32)
        rr = join_groups(held_r, got_r, even).astype(F32)
        rr = jnp.concatenate([rr[:, k * columns : (k + 1) * columns] for k in range(share)], axis=0)
        rm = join_groups(held_m, got_m, even).astype(F32)
        narrow = rt[:, 3 * columns :]
        biases, rows_hidden = narrow[0:8, :part], narrow[8:11].reshape(-1)
        gains, shifts = narrow[11:14, :part], narrow[14:17, :part]
    else:
        re, rr, rs, rm, rt = (
            lax.psum(lax.psum_scatter(v, "shard", scatter_dimension=0, tiled=True), "grp").astype(F32)
            for v in (*grad_e, *grad_r, *grad_s, *grad_m, *grad_t)
        )
        rows = [sums_t[0:4], sums_s[0:3], sums_f[0:1], sums_t[4:5], norm_s[0:1], norm_f[0:1], sums_t[5:6], norm_s[1:2], norm_f[1:2]]
        cut = lax.dynamic_slice_in_dim(lax.psum(jnp.concatenate(rows, axis=0), BOTH), mine * part, part, axis=1)
        biases, gains, shifts = cut[0:8], cut[8:11], cut[11:14]
        rows_hidden = lax.dynamic_slice_in_dim(lax.psum(ghb[0], BOTH), mine * hidden_bias.shape[0], hidden_bias.shape[0])
    return (
        (unpack_rows(out, clips) * flags)[:, None],
        unpack_rows(gx, clips)[:, None],
        rt[:, : 3 * columns],
        rm[:, :columns],
        rm[:, columns:],
        rs[:, : 3 * columns],
        rs[:, 3 * columns :],
        re,
        rr,
        biases,
        rows_hidden,
        gains,
        shifts,
    )


def solution(mesh):
    clips = P(None, ("grp", "shard"), None, None)
    rows = P("shard", None)
    cols = P(None, "shard")
    return jax.shard_map(
        local,
        mesh=mesh,
        in_specs=(clips, clips, P(None, ("grp", "shard"))) + (rows,) * 7 + (cols, P("shard"), cols, cols),
        out_specs=(clips, clips) + (rows,) * 7 + (cols, P("shard"), cols, cols),
        check_vma=False,
    )
```

```python
import functools
import math

import jax
import jax.numpy as jnp
from jax import lax
from jax.experimental import pallas as pl
from jax.experimental.pallas import tpu as pltpu
from jax.sharding import PartitionSpec as P

FRAMES = 2
PLACES = 196
HD = 64
EPSILON = 1e-06
BLOCK = 208
EDGE = 192
CLASS = PLACES - EDGE
CHUNK = 2 * BLOCK
WIDE = 256
BF = jnp.bfloat16
F32 = jnp.float32
SMALL = 32
MICRO = 4_000_000_000
SPARE = 12 * 1024 * 1024
VMEM_LIMIT = 60 * 1024 * 1024


def nn(a, b):
    return lax.dot_general(a, b, (((1,), (0,)), ((), ())), preferred_element_type=F32)


def nt(a, b):
    return lax.dot_general(a, b, (((1,), (1,)), ((), ())), preferred_element_type=F32)


def tn(a, b):
    return lax.dot_general(a, b, (((0,), (0,)), ((), ())), preferred_element_type=F32)


def loop(count, body):
    for i in range(count):
        body(i)


def rows_of(i, size):
    return slice(i * size, (i + 1) * size)


def cols_of(i, size, base=0):
    return slice(base + i * size, base + (i + 1) * size)


def unit(x):
    center = x - jnp.mean(x, axis=-1, keepdims=True)
    factor = lax.rsqrt(jnp.mean(center * center, axis=-1, keepdims=True) + EPSILON)
    return center * factor, factor


def norm_chunks(src, dst, gain, shift):
    def body(i):
        at = rows_of(i, CHUNK)
        w, _ = unit(src[at, :].astype(F32))
        dst[at, :] = (w * gain + shift).astype(BF)

    loop(src.shape[0] // CHUNK, body)


def fold(x):
    return jnp.sum(x.reshape(x.shape[0] // 8, 8, x.shape[1]), axis=0)


def norm_back_chunks(gn_ref, x_ref, gain, base_of, store):
    columns = x_ref.shape[1]

    def body(i, carry):
        gain_sum, shift_sum = carry
        at = rows_of(i, CHUNK)
        gn = gn_ref[at, :]
        w, factor = unit(x_ref[at, :].astype(F32))
        scaled = gn * gain
        plain = jnp.mean(scaled, axis=-1, keepdims=True)
        cross = jnp.mean(scaled * w, axis=-1, keepdims=True)
        store(at, base_of(at) + factor * (scaled - plain - w * cross))
        return gain_sum + fold(gn * w), shift_sum + fold(gn)

    zero = jnp.zeros((8, columns), F32)
    gain_sum, shift_sum = zero, zero
    for i in range(x_ref.shape[0] // CHUNK):
        gain_sum, shift_sum = body(i, (gain_sum, shift_sum))
    return jnp.sum(gain_sum, axis=0, keepdims=True), jnp.sum(shift_sum, axis=0, keepdims=True)


def column_sums(ref, start, size):
    def body(i, total):
        return total + fold(ref[rows_of(i, CHUNK), start : start + size].astype(F32))

    total = jnp.zeros((8, size), F32)
    for i in range(ref.shape[0] // CHUNK):
        total = body(i, total)
    return jnp.sum(total, axis=0, keepdims=True)


def head_map(columns):
    feature = lax.broadcasted_iota(jnp.int32, (columns, 128), 0) // HD
    head = lax.broadcasted_iota(jnp.int32, (columns, 128), 1)
    return (feature == head).astype(BF)


def head_sums(a_ref, a_rows, a_base, b_ref, b_rows, b_base, heads):
    total = None
    for j in range(heads.shape[0] // WIDE):
        a = a_ref[a_rows, a_base + j * WIDE : a_base + (j + 1) * WIDE].astype(F32)
        b = b_ref[b_rows, b_base + j * WIDE : b_base + (j + 1) * WIDE].astype(F32)
        top = (a * b).astype(BF)
        rest = (a * b - top.astype(F32)).astype(BF)
        part = heads[j * WIDE : (j + 1) * WIDE, :]
        term = nn(top, part) + nn(rest, part)
        total = term if total is None else total + term
    return total


def places_only(value):
    return jnp.where(lax.broadcasted_iota(jnp.int32, value.shape, 0) < PLACES, value, 0.0)


def start(pairs, sems):
    copies = [pltpu.make_async_copy(s, d, sems.at[n]) for n, (s, d) in enumerate(pairs)]
    for copy in copies:
        copy.start()
    return copies


def wait(copies):
    for copy in copies:
        copy.wait()


def piece_views(bufs):
    return list(bufs)


def rows_at(place, rows, share=1, k=0):
    return pl.ds(pl.multiple_of((place * share + k) * rows, 16), rows)


def load(bufs, place_ref, w, sems):
    if len(bufs) == 1:
        return start([(bufs[0], w)], sems)
    views = piece_views(bufs)
    rows = views[0].shape[0]
    return start([(v, w.at[rows_at(place_ref[n], rows), :]) for n, v in enumerate(views)], sems)


ORDER = ((3, 0), (1, 0), (3, 1), (2, 1), (1, 1), (2, 0), (0, 0), (0, 1))


def store_pieces(dw, outs, place_ref, sems, share=1, base=0):
    if len(outs) == 1:
        return start([(dw, outs[0])], sems)
    half, columns = outs[0].shape[1], dw.shape[1]
    pairs = []
    for side, out in enumerate(outs):
        for n, (chip, top) in enumerate(ORDER):
            place = place_ref[8 + side * 4 + chip]
            for k in range(share):
                source = dw.at[pl.ds(pl.multiple_of(((place * share + k) * 2 + top) * half, 16), half), :]
                pairs.append((source, out.at[n, :, base + k * columns : base + (k + 1) * columns]))
    return start(pairs, sems)


def piece_select(piece, rows, columns):
    lane = lax.broadcasted_iota(jnp.int32, (128, columns), 0)
    column = lax.broadcasted_iota(jnp.int32, (128, columns), 1)
    return ((lane < rows) & (column == piece * rows + lane)).astype(BF)


def spread_small(w, small_ref, hb_ref):
    columns = small_ref.shape[1]
    rows = columns // 8
    start = w.shape[1] - 128
    total = jnp.zeros((SMALL, columns), F32)
    for piece in range(8):
        block = w[piece * rows : piece * rows + SMALL, start:]
        total = total + nn(block, piece_select(piece, rows, columns))
        wide = block.astype(F32)
        for r in range(3):
            at = (piece * 3 + r) * 128
            hb_ref[0:1, at : at + 128] = wide[8 + r : 9 + r, :]
    small_ref[...] = total


def gather_small(dw, sums):
    sums_t, sums_s, norm_s, sums_f, norm_f, ghb = sums
    columns = sums_t.shape[1]
    rows = columns // 8
    start = dw.shape[1] - 128
    zero = jnp.zeros((3, columns), F32)
    order = [sums_t[0:4, :], sums_s[0:3, :], sums_f[0:1, :], zero, sums_t[4:5, :], norm_s[0:1, :], norm_f[0:1, :]]
    order += [sums_t[5:6, :], norm_s[1:2, :], norm_f[1:2, :], jnp.zeros((SMALL - 17, columns), F32)]
    values = jnp.concatenate(order, axis=0).astype(BF)
    for piece in range(8):
        block = nt(values, piece_select(piece, rows, columns))
        hidden = [ghb[0:1, (piece * 3 + r) * 128 : (piece * 3 + r + 1) * 128] for r in range(3)]
        block = jnp.concatenate([block[0:8, :]] + hidden + [block[11:, :]], axis=0)
        dw[piece * rows : piece * rows + SMALL, start:] = block.astype(BF)
        dw[piece * rows + SMALL : (piece + 1) * rows, start:] = jnp.zeros((rows - SMALL, 128), BF)


def load_feed(bufs, place_ref, we, wr, sems):
    if len(bufs) == 2:
        return start([(bufs[0], we)], sems), start([(bufs[1], wr)], sems.at[8:])
    views = piece_views(bufs)
    rows, units, columns = views[0].shape[0], we.shape[1], wr.shape[1]
    share = units // columns
    first = start([(v.at[:, 0:units], we.at[rows_at(place_ref[n], rows), :]) for n, v in enumerate(views)], sems)
    pairs = []
    for n, v in enumerate(views):
        for k in range(share):
            to = rows_at(place_ref[n], rows, share, k)
            pairs.append((v.at[:, units + k * columns : units + (k + 1) * columns], wr.at[to, :]))
    return first, start(pairs, sems.at[8:])


class Late:
    def __init__(self, source, target, sem):
        self.target = target
        self.copy = pltpu.make_async_copy(source, target, sem)
        self.copy.start()

    def get(self):
        if self.copy is not None:
            self.copy.wait()
            self.copy = None
        return self.target


class Early:
    def __init__(self, ref, target, sem):
        self.ref = ref
        self.copy = pltpu.make_async_copy(ref, target, sem)

    def send(self):
        self.copy.start()


SPACES = {
    "v": pl.BlockSpec(memory_space=pltpu.VMEM),
    "a": pl.BlockSpec(memory_space=pl.ANY),
    "l": pl.BlockSpec(memory_space=pl.ANY),
    "e": pl.BlockSpec(memory_space=pl.ANY),
    "s": pl.BlockSpec(memory_space=pltpu.SMEM),
}


def call(body, operands, spaces, outs, out_spaces, scratch, micros, name, tight=True):
    late = [n for n, space in enumerate(spaces) if space == "l"]
    early = [n for n, space in enumerate(out_spaces) if space == "e"]
    n_in, n_out, n_scratch = len(operands), len(outs), len(scratch)

    def kernel(*refs):
        ins, refs = list(refs[:n_in]), refs[n_in:]
        results, refs = list(refs[:n_out]), refs[n_out:]
        own, refs = refs[:n_scratch], refs[n_scratch:]
        held, refs = refs[: len(late)], refs[len(late) :]
        filled, refs = refs[: len(early)], refs[len(early) :]
        late_sems, early_sems = refs
        for k, n in enumerate(late):
            ins[n] = Late(ins[n], held[k], late_sems.at[k])
        for k, n in enumerate(early):
            results[n] = Early(filled[k], results[n], early_sems.at[k])
        body(ins, results, own)
        for n in late:
            ins[n].get()
        for n in early:
            results[n].copy.wait()

    held = [operands[n].size * operands[n].dtype.itemsize for n, space in enumerate(spaces) if space in "vl"]
    held += [math.prod(outs[n][0]) * jnp.dtype(outs[n][1]).itemsize for n, space in enumerate(out_spaces) if space in "ve"]
    held += [math.prod(ref.shape) * jnp.dtype(ref.dtype).itemsize for ref in scratch if "semaphore" not in str(ref.memory_space)]
    limit = min(VMEM_LIMIT, sum(held) + SPARE) if tight else VMEM_LIMIT
    more = [pltpu.VMEM(operands[n].shape, operands[n].dtype) for n in late]
    more += [pltpu.VMEM(*outs[n]) for n in early]
    more += [pltpu.SemaphoreType.DMA((max(1, len(late)),)), pltpu.SemaphoreType.DMA((max(1, len(early)),))]
    return pl.pallas_call(
        kernel,
        out_shape=[jax.ShapeDtypeStruct(s, d) for s, d in outs],
        in_specs=[SPACES[space] for space in spaces],
        out_specs=[SPACES[space] for space in out_spaces],
        scratch_shapes=list(scratch) + more,
        compiler_params=pltpu.CompilerParams(vmem_limit_bytes=limit),
        cost_estimate=pl.CostEstimate(flops=micros * MICRO, bytes_accessed=0, transcendentals=0),
        name=name,
    )(*operands)


def blocks_of(count):
    return [slice(j * WIDE, (j + 1) * WIDE) for j in range(count // WIDE)]


def shifted(at, base):
    return slice(at.start + base, at.stop + base)


def entry(normed, w, qkv, query_bias, value_bias):
    columns = normed.shape[1]
    for part, bias in enumerate((query_bias, None, value_bias)):
        for at in blocks_of(columns):
            to = shifted(at, part * columns)
            packed = nn(normed[...], w[:, to])
            qkv[:, to] = (packed if bias is None else packed + bias[:, at]).astype(BF)


def time_forward(n, ins, results, own):
    place_ref, x_ref, *rest = ins
    given, bufs = rest[: len(rest) - n], rest[len(rest) - n :]
    nt_out, qkv_out, o_out, e_out, p_out, y_ref, small_ref, hb_ref = results
    w, sems = own
    columns = x_ref.shape[1]
    wait(load(bufs, place_ref, w, sems))
    if given:
        small_ref[...] = given[0][...]
        hb_ref[...] = given[1][...]
    else:
        spread_small(w, small_ref, hb_ref)
    norm_chunks(x_ref, nt_out.ref, small_ref[11:12, :], small_ref[14:15, :])
    nt_out.send()
    qkv_ref, o_ref, e_ref, p_ref = qkv_out.ref, o_out.ref, e_out.ref, p_out.ref
    entry(nt_out.ref, w, qkv_ref, small_ref[0:1, :], small_ref[1:2, :])
    qkv_out.send()
    heads = head_map(columns)
    for clip in range(x_ref.shape[0] // (FRAMES * BLOCK)):
        at = [slice((clip * FRAMES + f) * BLOCK, (clip * FRAMES + f + 1) * BLOCK) for f in range(FRAMES)]
        weights = []
        for f in range(FRAMES):
            s = [head_sums(qkv_ref, at[f], 0, qkv_ref, at[g], columns, heads) * HD ** (-0.5) for g in range(FRAMES)]
            peak = jnp.maximum(s[0], s[1])
            powered = [jnp.exp(score - peak) for score in s]
            inverse = 1.0 / (powered[0] + powered[1])
            for g in range(FRAMES):
                m = (clip * FRAMES + f) * FRAMES + g
                p = powered[g] * inverse
                p_ref[m * BLOCK : (m + 1) * BLOCK, :] = p
                weights.append(p.astype(BF))
        for to in blocks_of(columns):
            v = [qkv_ref[a, shifted(to, 2 * columns)].astype(F32) for a in at]
            for f in range(FRAMES):
                spread = [nt(weights[FRAMES * f + g], heads[to, :]) for g in range(FRAMES)]
                o_ref[at[f], to] = (spread[0] * v[0] + spread[1] * v[1]).astype(BF)
    p_out.send()
    o_out.send()
    for at in blocks_of(columns):
        e_ref[:, at] = (nn(o_ref[...], w[:, shifted(at, 3 * columns)]) + small_ref[2:3, at]).astype(BF)
    e_out.send()
    for at in blocks_of(columns):
        branch = nn(e_ref[...], w[:, shifted(at, 4 * columns)]) + small_ref[3:4, at]
        for block in range(x_ref.shape[0] // BLOCK):
            rows = rows_of(block, BLOCK)
            y_ref[rows, at] = x_ref[rows, at].astype(F32) + places_only(branch[rows, :])


def half_masks():
    lane = lax.broadcasted_iota(jnp.int32, (1, 128), 1)
    return (lane < HD).astype(BF), (lane >= HD).astype(BF)


def space_forward(n, ins, results, own):
    place_ref, y_ref, small_ref, *bufs = ins
    ns_out, qkv_out, p_out, o_out, z_ref = results
    w, sems = own
    columns = y_ref.shape[1]
    blocks = y_ref.shape[0] // BLOCK
    pairs = columns // 128
    copies = load(bufs, place_ref, w, sems)
    norm_chunks(y_ref, ns_out.ref, small_ref[12:13, :], small_ref[15:16, :])
    ns_out.send()
    wait(copies)
    qkv_ref, p_ref, o_ref = qkv_out.ref, p_out.ref, o_out.ref
    entry(ns_out.ref, w, qkv_ref, small_ref[4:5, :], small_ref[5:6, :])
    qkv_out.send()
    masks = half_masks()
    first = lax.broadcasted_iota(jnp.int32, (BLOCK, 128), 1) < HD
    column = lax.broadcasted_iota(jnp.int32, (1, BLOCK), 1)
    hidden = jnp.where(column <= PLACES, 0.0, -1e30)

    def attend(block):
        at = rows_of(block, BLOCK)
        columns_of = [[slice(part * columns + k * 128, part * columns + (k + 1) * 128) for k in range(pairs)] for part in range(3)]
        scores = []
        for k in range(pairs):
            query, key = qkv_ref[at, columns_of[0][k]], qkv_ref[at, columns_of[1][k]]
            scores += [nt(query * mask, key) * HD ** (-0.5) + hidden for mask in masks]
        powered = [jnp.exp(s - jnp.max(s, axis=-1, keepdims=True)) for s in scores]
        weights = [(e * (1.0 / jnp.sum(e, axis=-1, keepdims=True))).astype(BF) for e in powered]
        for k in range(pairs):
            value = qkv_ref[at, columns_of[2][k]]
            for half in range(2):
                p_ref[(block * pairs + k) * 2 + half] = weights[2 * k + half]
            mixed = jnp.where(first, nn(weights[2 * k], value), nn(weights[2 * k + 1], value))
            o_ref[at, columns_of[0][k]] = mixed.astype(BF)

    loop(blocks, attend)
    p_out.send()
    o_out.send()
    is_class = lax.broadcasted_iota(jnp.int32, (BLOCK - EDGE, WIDE), 0) == CLASS
    for at in blocks_of(columns):
        branch = nn(o_ref[...], w[:, shifted(at, 3 * columns)]) + small_ref[6:7, at]
        z_ref[:, at] = y_ref[:, at] + branch
        for clip in range(blocks // FRAMES):
            edges = [slice((clip * FRAMES + f) * BLOCK + EDGE, (clip * FRAMES + f + 1) * BLOCK) for f in range(FRAMES)]
            mean = (branch[edges[0], :] + branch[edges[1], :]) * (1.0 / FRAMES)
            for edge in edges:
                z_ref[edge, at] = y_ref[edge, at] + jnp.where(is_class, mean, branch[edge, :])


def gelu_both(h):
    cdf = 0.5 * (1.0 + lax.erf(h * 0.5**0.5))
    density = jnp.exp(h * h * -0.5) * 0.3989422804014327
    return h * cdf, cdf + h * density


def feed_out(ins, results, own):
    place_ref, z_ref, g_ref, small_ref, hb_ref, *bufs = ins
    out_ref, nm_out, gh_out, sums_ref, *outs = results
    we, wr, dwr, a, sems, out_sems = own
    nm, gh = nm_out.ref, gh_out.ref
    columns = z_ref.shape[1]
    units = we.shape[1]
    copies, more = load_feed(bufs, place_ref, we, wr, sems)
    norm_chunks(z_ref, nm, small_ref[13:14, :], small_ref[16:17, :])
    nm_out.send()
    wait(copies + more)

    def inner(j):
        at = cols_of(j, WIDE)
        h = nn(nm[...], we[:, at]) + hb_ref[0:1, at]
        active, slope = gelu_both(h)
        a[:, at] = active.astype(BF)
        gh[:, at] = (nt(g_ref[...], wr[rows_of(j, WIDE), :]) * slope).astype(BF)

    loop(units // WIDE, inner)
    gh_out.send()

    def left(j):
        dwr[rows_of(j, WIDE), :] = tn(a[:, cols_of(j, WIDE)], g_ref[...]).astype(BF)

    loop(units // WIDE, left)
    copies = store_pieces(dwr, outs, place_ref, out_sems, units // columns)
    for at in blocks_of(columns):
        out_ref[:, at] = (z_ref[:, at] + (nn(a[...], wr[:, at]) + small_ref[7:8, at])).astype(BF)
    sums_ref[0:1, :] = column_sums(g_ref, 0, columns)
    wait(copies)


def feed_in(ins, results, own):
    place_ref, gh, nm = ins
    ghb_ref, *outs = results
    dwe, out_sems = own
    units = gh.shape[1]

    def right(j):
        at = cols_of(j, WIDE)
        block = gh[:, at]
        dwe[:, at] = tn(nm[...], block).astype(BF)
        ghb_ref[0:1, at] = jnp.sum(block.astype(F32), axis=0, keepdims=True)

    loop(units // WIDE, right)
    wait(store_pieces(dwe, outs, place_ref, out_sems))


def norm_backward(row, n, ins, results, own):
    place_ref, gh_ref, x_in, base_in, small_ref, *bufs = ins
    gz_ref, sums_ref = results
    w, gn, sems = own
    columns = gz_ref.shape[1]
    views = [b.at[:, 0 : w.shape[1]] for b in bufs]
    wait(load(views, place_ref, w, sems))
    for at in blocks_of(columns):
        gn[:, at] = nt(gh_ref[...], w[at, :])
    x_ref, base = x_in.get(), base_in.get()

    def store(at, value):
        gz_ref[at, :] = value

    gain_sum, shift_sum = norm_back_chunks(
        gn, x_ref, small_ref[row : row + 1, :], lambda at: base[at, :].astype(F32), store
    )
    sums_ref[0:1, :] = gain_sum
    sums_ref[1:2, :] = shift_sum


def space_backward(n, ins, results, own):
    place_ref, gz_ref, ns_in, qkv_in, p_in, o_in, *rest = ins
    bufs = rest[:n]
    gqkv_out, sums_ref, *outs = results
    w, dw_ref, gbs, go, sems, out_sems = own
    columns = gz_ref.shape[1]
    rows = gz_ref.shape[0]
    clips = rows // (BLOCK * FRAMES)
    pairs = columns // 128
    copies = load([b.at[:, 3 * columns : 4 * columns] for b in bufs], place_ref, w, sems)

    def lower(i):
        at = rows_of(i, CHUNK)
        gbs[at, :] = gz_ref[at, :].astype(BF)

    loop(rows // CHUNK, lower)
    is_class = lax.broadcasted_iota(jnp.int32, (BLOCK - EDGE, columns), 0) == CLASS
    for clip in range(clips):
        edges = [slice((clip * FRAMES + f) * BLOCK + EDGE, (clip * FRAMES + f + 1) * BLOCK) for f in range(FRAMES)]
        share = gz_ref[edges[0], :] * (1.0 / FRAMES)
        for edge in edges:
            gbs[edge, :] = jnp.where(is_class, share, gz_ref[edge, :]).astype(BF)
    wait(copies)
    for at in blocks_of(columns):
        go[:, at] = nt(gbs[...], w[at, :]).astype(BF)
    o_ref, qkv_ref, p_ref, gqkv = o_in.get(), qkv_in.get(), p_in.get(), gqkv_out.ref
    for at in blocks_of(columns):
        dw_ref[:, shifted(at, 3 * columns)] = tn(o_ref[...], gbs[:, at]).astype(BF)
    masks = half_masks()
    first = lax.broadcasted_iota(jnp.int32, (BLOCK, 128), 1) < HD
    class_row = lax.broadcasted_iota(jnp.int32, (BLOCK - EDGE, 128), 0) == CLASS
    together = 2

    def attend(step):
        parts = []
        for u in range(together):
            clip, pair = (step * together + u) // pairs, (step * together + u) % pairs
            for f in range(FRAMES):
                block = clip * FRAMES + f
                at = rows_of(block, BLOCK)
                q, k, v = (qkv_ref[at, cols_of(pair, 128, part * columns)] for part in range(3))
                grad = go[at, cols_of(pair, 128)]
                parts += [(q, k, v, grad, mask, p_ref[2 * (block * pairs + pair) + half]) for half, mask in enumerate(masks)]
        gp = [nt(grad * mask, v) for _, _, v, grad, mask, _ in parts]
        p = [part[5].astype(F32) for part in parts]
        shared = [jnp.sum(a * b, axis=-1, keepdims=True) for a, b in zip(gp, p)]
        gs = [(b * (a - c)).astype(BF) for a, b, c in zip(gp, p, shared)]
        scale = HD ** (-0.5)
        gq = [nn(a, part[1]) * scale for a, part in zip(gs, parts)]
        gv = [tn(part[5], part[3]) for part in parts]
        gk = [tn(a, part[0]) * scale for a, part in zip(gs, parts)]
        for u in range(together):
            clip, pair = (step * together + u) // pairs, (step * together + u) % pairs
            for part, values in enumerate((gq, gk, gv)):
                to = cols_of(pair, 128, part * columns)
                one, two = (jnp.where(first, values[4 * u + 2 * f], values[4 * u + 2 * f + 1]) for f in range(FRAMES))
                top = clip * FRAMES * BLOCK
                gqkv[pl.ds(top, EDGE), to] = one[:EDGE].astype(BF)
                gqkv[pl.ds(top + BLOCK, EDGE), to] = two[:EDGE].astype(BF)
                both = jnp.where(class_row, one[EDGE:] + two[EDGE:], one[EDGE:])
                gqkv[pl.ds(top + EDGE, BLOCK - EDGE), to] = both.astype(BF)
                rest = jnp.where(class_row, 0.0, two[EDGE:])
                gqkv[pl.ds(top + BLOCK + EDGE, BLOCK - EDGE), to] = rest.astype(BF)

    loop(clips * pairs // together, attend)
    gqkv_out.send()
    ns_ref = ns_in.get()
    for at in blocks_of(3 * columns):
        dw_ref[:, at] = tn(ns_ref[...], gqkv[:, at]).astype(BF)
    copies = store_pieces(dw_ref, outs, place_ref, out_sems)
    sums_ref[0:1, :] = column_sums(gqkv, 0, columns)
    sums_ref[1:2, :] = column_sums(gqkv, 2 * columns, columns)
    sums_ref[2:3, :] = column_sums(gbs, 0, columns)
    wait(copies)


def mixer_backward(n, ins, results, own):
    place_ref, gy_ref, o_in, e_in, *bufs = ins
    go_out, sums_ref, *outs = results
    w, dw_ref, grt, get, sems, out_sems = own
    columns = gy_ref.shape[1]
    rows = gy_ref.shape[0]
    copies = load([b.at[:, 3 * columns : 5 * columns] for b in bufs], place_ref, w, sems)

    def lower(block):
        at = rows_of(block, BLOCK)
        grt[at, :] = places_only(gy_ref[at, :]).astype(BF)

    loop(rows // BLOCK, lower)
    wait(copies)
    go = go_out.ref
    for at in blocks_of(columns):
        get[:, at] = nt(grt[...], w[at, columns : 2 * columns]).astype(BF)
    e_ref, o_ref = e_in.get(), o_in.get()
    for at in blocks_of(columns):
        dw_ref[:, shifted(at, columns)] = tn(e_ref[...], grt[:, at]).astype(BF)
    for at in blocks_of(columns):
        dw_ref[:, at] = tn(o_ref[...], get[:, at]).astype(BF)
    copies = store_pieces(dw_ref, outs, place_ref, out_sems)
    for at in blocks_of(columns):
        go[:, at] = nt(get[...], w[at, 0:columns]).astype(BF)
    go_out.send()
    sums_ref[2:3, :] = column_sums(get, 0, columns)
    sums_ref[3:4, :] = column_sums(grt, 0, columns)
    wait(copies)


def time_backward(n, ins, results, own):
    place_ref, go, qkv_ref, p_ref, x_in, gy_in, small_ref, before, *bufs = ins
    gqkv_out, gx_ref, sums_ref = results
    w, gn, sems = own
    columns = gx_ref.shape[1]
    rows = gx_ref.shape[0]
    gqkv = gqkv_out.ref
    copies = load([b.at[:, 0 : 3 * columns] for b in bufs], place_ref, w, sems)
    heads = head_map(columns)
    for clip in range(rows // (FRAMES * BLOCK)):
        at = [slice((clip * FRAMES + f) * BLOCK, (clip * FRAMES + f + 1) * BLOCK) for f in range(FRAMES)]
        gs, kept = [], []
        for f in range(FRAMES):
            gp = [head_sums(go, at[f], 0, qkv_ref, at[g], 2 * columns, heads) for g in range(FRAMES)]
            first = ((clip * FRAMES + f) * FRAMES) * BLOCK
            p = [p_ref[first + g * BLOCK : first + (g + 1) * BLOCK, :] for g in range(FRAMES)]
            shared = gp[0] * p[0] + gp[1] * p[1]
            gs += [(p[g] * (gp[g] - shared)).astype(BF) for g in range(FRAMES)]
            kept += [p[g].astype(BF) for g in range(FRAMES)]
        for block in blocks_of(columns):
            to = [shifted(block, part * columns) for part in range(3)]
            q, k = ([qkv_ref[a, to[part]].astype(F32) for a in at] for part in range(2))
            grad = [go[a, block].astype(F32) for a in at]
            scaled = heads[block, :] * BF(HD ** (-0.5))
            spread = [nt(value, scaled) for value in gs]
            for f in range(FRAMES):
                gqkv[at[f], to[0]] = (spread[2 * f] * k[0] + spread[2 * f + 1] * k[1]).astype(BF)
                gqkv[at[f], to[1]] = (spread[f] * q[0] + spread[2 + f] * q[1]).astype(BF)
            spread = [nt(value, heads[block, :]) for value in kept]
            for f in range(FRAMES):
                gqkv[at[f], to[2]] = (spread[f] * grad[0] + spread[2 + f] * grad[1]).astype(BF)
    gqkv_out.send()
    wait(copies)
    for at in blocks_of(columns):
        gn[:, at] = nt(gqkv[...], w[at, :])
    x_ref, gy_ref = x_in.get(), gy_in.get()

    def store(at, value):
        gx_ref[at, :] = value.astype(BF)

    gain_sum, shift_sum = norm_back_chunks(gn, x_ref, small_ref[11:12, :], lambda at: gy_ref[at, :], store)
    sums_ref[0:1, :] = column_sums(gqkv, 0, columns)
    sums_ref[1:2, :] = column_sums(gqkv, 2 * columns, columns)
    sums_ref[2:4, :] = before[2:4, :]
    sums_ref[4:5, :] = gain_sum
    sums_ref[5:6, :] = shift_sum


def time_weights(ins, results, own):
    place_ref, gqkv, nt_ref, *sums = ins
    dw_ref, out_sems = own
    columns = nt_ref.shape[1]
    for at in blocks_of(3 * columns):
        dw_ref[:, at] = tn(nt_ref[...], gqkv[:, at]).astype(BF)
    if sums:
        gather_small(dw_ref, sums)
    wait(store_pieces(dw_ref, results, place_ref, out_sems))


def pack_rows(tokens, once):
    clips, _, columns = tokens.shape
    frames = []
    for f in range(FRAMES):
        places = tokens[:, 1 + f * PLACES : 1 + (f + 1) * PLACES]
        head = tokens[:, :1] if f == 0 or not once else jnp.zeros_like(tokens[:, :1])
        frames.append(jnp.concatenate([places, head, jnp.zeros((clips, BLOCK - PLACES - 1, columns), tokens.dtype)], axis=1))
    return jnp.stack(frames, axis=1).reshape(clips * FRAMES * BLOCK, columns)


def unpack_rows(rows, clips):
    framed = rows.reshape(clips, FRAMES, BLOCK, rows.shape[-1])
    return jnp.concatenate(
        [framed[:, 0, PLACES : PLACES + 1]] + [framed[:, f, :PLACES] for f in range(FRAMES)], axis=1
    )


class Layer:
    def __init__(self, rows, columns, units, shards, pieced, place):
        self.rows, self.columns, self.units = rows, columns, units
        self.pieced, self.place = pieced, place
        self.piece = columns // shards
        self.act = ((rows, columns), BF)
        self.act3 = ((rows, 3 * columns), BF)
        self.tall = ((rows, units), BF)
        self.wide = ((rows, columns), F32)
        self.sums = ((8, columns), F32)

    def grads(self, width):
        if self.pieced:
            return [((8, self.piece // 2, width), BF)] * 2
        return [((self.columns, width), BF)]

    def vmem(self, *shapes):
        return [pltpu.VMEM(s, d) for s, d in shapes]

    def sems(self, *counts):
        return [pltpu.SemaphoreType.DMA((count,)) for count in counts]

    def time_forward(self, x, given, bufs):
        c, n = self.columns, len(bufs)
        extra = [((SMALL, c), F32), ((8, self.units), F32)]
        return call(
            functools.partial(time_forward, n), (self.place, x, *given, *bufs), "sv" + "v" * len(given) + "a" * n,
            [self.act, self.act3, self.act, self.act, ((self.rows * FRAMES, 128), F32), self.wide] + extra, "eeeeevvv",
            self.vmem(((c, bufs[0].shape[1]), BF)) + self.sems(8), 14, "time_forward", False,
        )

    def space_forward(self, y, small, bufs):
        c, n = self.columns, len(bufs)
        probs = ((self.rows // BLOCK * (c // 128) * 2, BLOCK, BLOCK), BF)
        return call(
            functools.partial(space_forward, n), (self.place, y, small, *bufs), "svv" + "a" * n,
            [self.act, self.act3, probs, self.act, self.wide], "eeeev",
            self.vmem(((c, 4 * c), BF)) + self.sems(8), 16, "space_forward", False,
        )

    def feed_out(self, z, g, small, hb, bufs):
        c, u, n = self.columns, self.units, len(bufs)
        outs = self.grads(u) if self.pieced else [((u, c), BF)]
        return call(
            feed_out, (self.place, z, g, small, hb, *bufs), "svvvv" + "a" * n,
            [self.act, self.act, self.tall, self.sums] + outs, "veev" + "a" * len(outs),
            self.vmem(((c, u), BF), ((u, c), BF), ((u, c), BF), self.tall) + self.sems(40, 64), 30, "feed_out", False,
        )

    def feed_in(self, gh, normed):
        c, u = self.columns, self.units
        outs = self.grads(u)
        return call(
            feed_in, (self.place, gh, normed), "svv", [((8, u), F32)] + outs, "v" + "a" * len(outs),
            self.vmem(((c, u), BF)) + self.sems(16), 8, "feed_in",
        )

    def norm_backward(self, row, gh, x, base, small, bufs, name):
        c, n, wide = self.columns, len(bufs), gh.shape[1]
        return call(
            functools.partial(norm_backward, row, n), (self.place, gh, x, base, small, *bufs), "svllv" + "a" * n,
            [self.wide, self.sums], "vv", self.vmem(((c, wide), BF), self.wide) + self.sems(8), 10, name,
        )

    def space_backward(self, gz, normed, qkv, p, o, bufs):
        c, n = self.columns, len(bufs)
        outs = self.grads(4 * c)
        return call(
            functools.partial(space_backward, n), (self.place, gz, normed, qkv, p, o, *bufs), "svllll" + "a" * n,
            [self.act3, self.sums] + outs, "ev" + "a" * len(outs),
            self.vmem(((c, c), BF), ((c, 4 * c), BF), self.act, self.act) + self.sems(8, 16), 20, "space_backward",
        )

    def mixer_backward(self, gy, o, e, bufs):
        c, n = self.columns, len(bufs)
        outs = self.grads(2 * c)
        return call(
            functools.partial(mixer_backward, n), (self.place, gy, o, e, *bufs), "svll" + "a" * n,
            [self.act, self.sums] + outs, "ev" + "a" * len(outs),
            self.vmem(((c, 2 * c), BF), ((c, 2 * c), BF), self.act, self.act) + self.sems(8, 16), 8, "mixer_backward",
        )

    def time_backward(self, go, qkv, p, x, gy, small, before, bufs):
        c, n = self.columns, len(bufs)
        return call(
            functools.partial(time_backward, n), (self.place, go, qkv, p, x, gy, small, before, *bufs),
            "svvvllvv" + "a" * n, [self.act3, self.act, self.sums], "evv",
            self.vmem(((c, 3 * c), BF), self.wide) + self.sems(8), 12, "time_backward",
        )

    def time_weights(self, gqkv, normed, sums):
        c = self.columns
        width = 3 * c + (128 if sums else 0)
        outs = self.grads(width)
        return call(
            time_weights, (self.place, gqkv, normed, *sums), "svv" + "v" * len(sums), outs, "a" * len(outs),
            self.vmem(((c, width), BF)) + self.sems(16), 8, "time_weights",
        )


BOTH = ("grp", "shard")


def permute(value, target):
    shards = lax.axis_size("shard")
    pairs = [(z * shards + s, z * shards + target(s)) for z in range(lax.axis_size("grp")) for s in range(shards)]
    return lax.ppermute(value, BOTH, pairs)


def to_sibling(value):
    return permute(value, lambda s: s ^ 1)


def along_x(value):
    return permute(value, lambda s: s ^ 2)


def along_y(value):
    return permute(value, lambda s: s ^ 4)


def near_hop(value):
    return permute(value, lambda s: s ^ (2 if s % 2 == 0 else 4))


def far_hop(value):
    return permute(value, lambda s: s ^ (4 if s % 2 == 0 else 2))


def places(s):
    near = jnp.where(s % 2 == 0, 2, 4)
    far = 6 - near
    gathered = [s, s ^ 1, s ^ near, s ^ near ^ 1, s ^ 6, s ^ 1 ^ far, s ^ far, s ^ 7]
    kept = [s, s ^ 2, s ^ 4, s ^ 6]
    return jnp.stack(gathered + kept + [k ^ 1 for k in kept]).astype(jnp.int32)


def total(*terms):
    return sum(t.astype(F32) for t in terms).astype(BF)


class Reduction:
    def __init__(self, keep, give):
        self.keep = keep
        self.got = to_sibling(give)

    def own(self, start, stop):
        return self.keep[start:stop], self.got[start:stop]

    def first(self):
        return total(*self.own(0, 2)), total(*self.own(2, 4))

    def cross(self, sent):
        self.from_x, self.from_y = along_x(sent[0]), along_y(sent[1])

    def second(self):
        return total(*self.own(4, 5), self.from_y[:1]), total(*self.own(5, 6), self.from_x[:1])

    def cross_again(self, sent):
        self.last_x, self.last_y = along_x(sent[0]), along_y(sent[1])

    def finish(self):
        top = total(*self.own(6, 7), self.from_x[1:], self.last_y)
        bottom = total(*self.own(7, 8), self.from_y[1:], self.last_x)
        return top[0], bottom[0]


def beside(*values):
    return jnp.concatenate([v[n : n + 1] for v in values for n in range(v.shape[0])], axis=2)


def apart(value, widths):
    stops = [sum(widths[: n + 1]) for n in range(len(widths))]
    return [value[..., stop - width : stop] for stop, width in zip(stops, widths)]


def hand_over(arrived, ahead, behind):
    widths = (ahead.keep.shape[2], behind.keep.shape[2], behind.keep.shape[2])
    ahead.last_x, *from_x = apart(arrived[0], widths)
    ahead.last_y, *from_y = apart(arrived[1], widths)
    behind.from_x, behind.from_y = jnp.concatenate(from_x, axis=0), jnp.concatenate(from_y, axis=0)


def tie(*values):
    leaves, shape = jax.tree.flatten(values)
    return jax.tree.unflatten(shape, lax.optimization_barrier(tuple(leaves)))


def swap_z(value):
    shards = lax.axis_size("shard")
    pairs = [(z * shards + s, (z ^ 1) * shards + s) for z in range(lax.axis_size("grp")) for s in range(shards)]
    return lax.ppermute(value, BOTH, pairs)


def across_pairs(value):
    return lax.ppermute(value, "grp", [(z, z ^ 2) for z in range(4)])


def split_groups(halves, even):
    low, high = halves
    return jnp.where(even, low, high), jnp.where(even, high, low)


def join_groups(held, other, even):
    return jnp.concatenate([jnp.where(even, held, other), jnp.where(even, other, held)], axis=0)


def local(video, cotangent, live, time_entry, time_exit, time_mixer, space_entry, space_exit, hidden_expand, hidden_reduce, bias_rows, hidden_bias, norm_gain, norm_shift):
    clips, _, tokens, columns = video.shape
    shards, groups = lax.axis_size("shard"), lax.axis_size("grp")
    mine = lax.axis_index("shard")
    part = columns // shards
    units = hidden_bias.shape[0] * shards
    share = units // columns
    pieced = shards == 8 and groups == 4

    def gather(value):
        return lax.all_gather(value, "shard", axis=0, tiled=True)

    flags = live.astype(BF)[:, :, None]

    own_t = jnp.concatenate([time_entry, time_exit, time_mixer], axis=1)
    own_s = jnp.concatenate([space_entry, space_exit], axis=1)
    if pieced:
        narrow = jnp.concatenate([norm_gain, norm_shift], axis=0)
        narrow = jnp.concatenate(
            [jnp.pad(bias_rows, ((0, 0), (0, 128 - part))), hidden_bias.reshape(-1, 128), jnp.pad(narrow, ((0, 0), (0, 128 - part)))], axis=0
        )
        own_t = jnp.concatenate([own_t, jnp.pad(narrow, ((0, part - narrow.shape[0]), (0, 0)))], axis=1)
        own_f = jnp.concatenate([hidden_expand] + [hidden_reduce[k * part : (k + 1) * part] for k in range(share)], axis=1)
        net = Layer(clips * FRAMES * BLOCK, columns, units, shards, pieced, places(mine))
        pair_t = to_sibling(own_t)
        pair_t, own_t, video, own_s, own_f = tie(pair_t, own_t, video, own_s, own_f)
        hop_t = (near_hop(own_t), near_hop(pair_t))
        x = pack_rows(video[:, 0], False)
        pair_s, pair_f = to_sibling(own_s), to_sibling(own_f)
        first_t, x, pair_s, pair_f = tie(hop_t[0], x, pair_s, pair_f)
        second_t, own_s, own_f, pair_s, pair_f = tie(far_hop(first_t), own_s, own_f, pair_s, pair_f)
        gone_t = tuple(to_sibling(v) for v in (first_t, hop_t[1], second_t))
        wt = (own_t, pair_t, first_t, hop_t[1], second_t, *gone_t)
        hop_s, hop_f = ((near_hop(own), near_hop(pair)) for own, pair in ((own_s, pair_s), (own_f, pair_f)))
        normed_t, qkv_t, o_t, e_t, p_t, y, small, hb = net.time_forward(x, (), wt)
        first_s, last_s, y, cotangent = tie(*hop_s, y, cotangent)
        g = pack_rows(cotangent[:, 0] * flags, True)
        second_s = far_hop(first_s)
        ws = (own_s, pair_s, first_s, last_s, second_s, *(to_sibling(v) for v in (first_s, last_s, second_s)))
        first_f, y, ws, g = tie(hop_f[0], y, ws, g)
        normed_s, qkv_s, p_s, o_s, z = net.space_forward(y, small, ws)
        second_f, last_f, z = tie(far_hop(first_f), hop_f[1], z)
        wf = (own_f, pair_f, first_f, last_f, second_f, *(to_sibling(v) for v in (first_f, last_f, second_f)))
    else:
        x, g = pack_rows(video[:, 0], False), pack_rows(cotangent[:, 0] * flags, True)
        net = Layer(clips * FRAMES * BLOCK, columns, units, shards, pieced, jnp.zeros((16,), jnp.int32))
        packed = jnp.concatenate([bias_rows, norm_gain, norm_shift], axis=0)
        spread = lax.all_gather(packed, "shard", axis=0).transpose(1, 0, 2).reshape(-1, columns).astype(F32)
        small = jnp.concatenate([spread[:8], jnp.zeros((3, columns), F32), spread[8:], jnp.zeros((SMALL - 17, columns), F32)], axis=0)
        given = (small, jnp.pad(gather(hidden_bias).astype(F32)[None], ((0, 7), (0, 0))))
        wt, ws, wf = (gather(own_t),), (gather(own_s),), (gather(hidden_expand), gather(hidden_reduce))
        normed_t, qkv_t, o_t, e_t, p_t, y, small, hb = net.time_forward(x, given, wt)
        normed_s, qkv_s, p_s, o_s, z = net.space_forward(y, small, ws)

    out, normed_f, gh, sums_f, *grad_r = net.feed_out(z, g, small, hb, wf)
    if pieced:
        sum_r = Reduction(*grad_r)
    ghb, *grad_e = net.feed_in(gh, normed_f)
    if pieced:
        sum_e = Reduction(*grad_e)
        sent_r, gh, ghb, sums_f, sum_e.keep = tie(sum_r.first(), gh, ghb, sums_f, sum_e.keep)
        sum_r.cross(sent_r)
    gz, norm_f = net.norm_backward(13, gh, z, g, small, wf if pieced else wf[:1], "feed_norm")
    if pieced:
        sent = [beside(last, both) for last, both in zip(sum_r.second(), sum_e.first())]
        sent, gz, norm_f = tie(sent, gz, norm_f)
        arrived = (along_x(sent[0]), along_y(sent[1]))
    gqkv, sums_s, *grad_s = net.space_backward(gz, normed_s, qkv_s, p_s, o_s, ws)
    if pieced:
        sum_s = Reduction(*grad_s)
        hand_over(arrived, sum_r, sum_e)
        even = lax.axis_index("grp") % 2 == 0
        held_r, sent_r = split_groups(sum_r.finish(), even)
        held_r, sent_r, sent_e, gqkv, sums_s, sum_s.keep = tie(held_r, sent_r, sum_e.second(), gqkv, sums_s, sum_s.keep)
        sum_e.cross_again(sent_e)
        got_r = swap_z(sent_r)
    gy, norm_s = net.norm_backward(12, gqkv, y, gz, small, ws, "space_norm")
    if pieced:
        got_r, sum_e.last_x, sum_e.last_y, gy, norm_s = tie(got_r, sum_e.last_x, sum_e.last_y, gy, norm_s)
        held_e, sent_e = split_groups(sum_e.finish(), even)
        held_r, held_e, sent_e, sent_s, gy, norm_s = tie(total(held_r, got_r), held_e, sent_e, sum_s.first(), gy, norm_s)
        sum_s.cross(sent_s)
        got_r, got_e = across_pairs(held_r), swap_z(sent_e)
    go, sums_m, *grad_m = net.mixer_backward(gy, o_t, e_t, wt)
    if pieced:
        sum_m = Reduction(*grad_m)
        arrived = (got_r, got_e, sum_s.from_x, sum_s.from_y)
        arrived, go, sums_m, sum_m.keep = tie(arrived, go, sums_m, sum_m.keep)
        got_r, got_e, sum_s.from_x, sum_s.from_y = arrived
        sent = [beside(last, both) for last, both in zip(sum_s.second(), sum_m.first())]
        held_r, held_e, sent, go = tie(total(held_r, got_r), total(held_e, got_e), sent, go)
        arrived = (along_x(sent[0]), along_y(sent[1]), swap_z(held_r), across_pairs(held_e))
    gqkv, gx, sums_t = net.time_backward(go, qkv_t, p_t, x, gy, small, sums_m, wt)
    if pieced:
        arrived, gqkv, gx, sums_t, out = tie(arrived, gqkv, gx, sums_t, out)
        came_x, came_y, got_r, got_e = arrived
        hand_over((came_x, came_y), sum_s, sum_m)
        held_s, sent_s = split_groups(sum_s.finish(), even)
        held_s, sent_s, sent_m, gqkv = tie(held_s, sent_s, sum_m.second(), gqkv)
        sum_m.cross_again(sent_m)
        got_s = swap_z(sent_s)
    grad_t = net.time_weights(gqkv, normed_t, (sums_t, sums_s, norm_s, sums_f, norm_f, ghb) if pieced else ())

    if pieced:
        got_s, sum_m.last_x, sum_m.last_y, grad_t = tie(got_s, sum_m.last_x, sum_m.last_y, grad_t)
        sum_t = Reduction(*grad_t)
        sent_t, got_s, got_e, sum_m.last_x, sum_m.last_y, gx, out = tie(
            sum_t.first(), got_s, got_e, sum_m.last_x, sum_m.last_y, gx, out
        )
        sum_t.cross(sent_t)
        input_grad = unpack_rows(gx, clips)
        input_grad, got_s, got_e, sum_m.last_x, sum_m.last_y = tie(input_grad, got_s, got_e, sum_m.last_x, sum_m.last_y)
        held_s, held_e = total(held_s, got_s), total(held_e, got_e)
        held_m, sent_m = split_groups(sum_m.finish(), even)
        got_s, got_m, got_e = across_pairs(held_s), swap_z(sent_m), swap_z(held_e)
        sum_t.from_x, sum_t.from_y, got_m = tie(sum_t.from_x, sum_t.from_y, got_m)
        held_m, sent_t = tie(total(held_m, got_m), sum_t.second())
        sum_t.cross_again(sent_t)
        got_m = across_pairs(held_m)
        held_t, sent_t = split_groups(sum_t.finish(), even)
        got_t = swap_z(sent_t)
        got_t, got_m, got_s = tie(got_t, got_m, got_s)
        held_t, held_m, held_s = tie(total(held_t, got_t), total(held_m, got_m), total(held_s, got_s))
        got_t, got_m, got_s = across_pairs(held_t), swap_z(held_m), swap_z(held_s)
        got_t, got_m, got_s, got_e = tie(got_t, got_m, got_s, got_e)
        held_t = total(held_t, got_t)
        got_t = swap_z(held_t)
        rt = join_groups(held_t, got_t, even).astype(F32)
        rs = join_groups(held_s, got_s, even).astype(F32)
        re = join_groups(held_e, got_e, even).astype(F32)
        rr = join_groups(held_r, got_r, even).astype(F32)
        rr = jnp.concatenate([rr[:, k * columns : (k + 1) * columns] for k in range(share)], axis=0)
        rm = join_groups(held_m, got_m, even).astype(F32)
        narrow = rt[:, 3 * columns :]
        biases, rows_hidden = narrow[0:8, :part], narrow[8:11].reshape(-1)
        gains, shifts = narrow[11:14, :part], narrow[14:17, :part]
    else:
        re, rr, rs, rm, rt = (
            lax.psum(lax.psum_scatter(v, "shard", scatter_dimension=0, tiled=True), "grp").astype(F32)
            for v in (*grad_e, *grad_r, *grad_s, *grad_m, *grad_t)
        )
        rows = [sums_t[0:4], sums_s[0:3], sums_f[0:1], sums_t[4:5], norm_s[0:1], norm_f[0:1], sums_t[5:6], norm_s[1:2], norm_f[1:2]]
        cut = lax.dynamic_slice_in_dim(lax.psum(jnp.concatenate(rows, axis=0), BOTH), mine * part, part, axis=1)
        biases, gains, shifts = cut[0:8], cut[8:11], cut[11:14]
        input_grad = unpack_rows(gx, clips)
        rows_hidden = lax.dynamic_slice_in_dim(lax.psum(ghb[0], BOTH), mine * hidden_bias.shape[0], hidden_bias.shape[0])
    return (
        (unpack_rows(out, clips) * flags)[:, None],
        input_grad[:, None],
        rt[:, : 3 * columns],
        rm[:, :columns],
        rm[:, columns:],
        rs[:, : 3 * columns],
        rs[:, 3 * columns :],
        re,
        rr,
        biases,
        rows_hidden,
        gains,
        shifts,
    )


def solution(mesh):
    clips = P(None, ("grp", "shard"), None, None)
    rows = P("shard", None)
    cols = P(None, "shard")
    return jax.shard_map(
        local,
        mesh=mesh,
        in_specs=(clips, clips, P(None, ("grp", "shard"))) + (rows,) * 7 + (cols, P("shard"), cols, cols),
        out_specs=(clips, clips) + (rows,) * 7 + (cols, P("shard"), cols, cols),
        check_vma=False,
    )
```
